32 devices in a mesh: dp: 2 (over x), seq: 16 (over z, y, core).
Axes of the slice: x: 2, y: 2, z: 4, core: 2. Of those that a mesh axis runs over, the one named last changes fastest.
Arguments:
- inputs: bfloat16 [4, 4096, 1536], P('dp', 'seq'), may hold values from -6 to 6
- skip_input: bfloat16 [4, 8192, 1536], P('dp', 'seq'), may hold values from -6 to 6
- lengths: int32 [4], P('dp'), may hold values from 1024 to 4096, as said below
- cotangent: bfloat16 [4, 8192, 1536], P('dp', 'seq'), may hold values from -6 to 6
- first_gain: bfloat16 [1536], P(('dp', 'seq')), may hold values from 0.099609375 to 1.8984375
- query_weight: bfloat16 [1536, 512], P(('dp', 'seq')), may hold values from -0.15625 to 0.15625
- key_weight: bfloat16 [1536, 512], P(('dp', 'seq')), may hold values from -0.15625 to 0.15625
- value_weight: bfloat16 [1536, 1536], P(('dp', 'seq')), may hold values from -0.15625 to 0.15625
- content_bias: bfloat16 [512], P(('dp', 'seq')), may hold values from -3 to 3
- position_bias: bfloat16 [512], P(('dp', 'seq')), may hold values from -3 to 3
- relative_weight: bfloat16 [512, 32], P(('dp', 'seq')), may hold values from -3 to 3
- mixing_weight: bfloat16 [1536, 1536], P(('dp', 'seq')), may hold values from -2.5 to 2.5
- second_gain: bfloat16 [1536], P(('dp', 'seq')), may hold values from 0.099609375 to 1.8984375
- inner_weight: bfloat16 [1536, 3072], P(('dp', 'seq')), may hold values from -0.15625 to 0.15625
- inner_bias: bfloat16 [3072], P(('dp', 'seq')), may hold values from -3 to 3
- outer_weight: bfloat16 [3072, 1536], P(('dp', 'seq')), may hold values from -0.15625 to 0.15625
- outer_bias: bfloat16 [1536], P(('dp', 'seq')), may hold values from -3 to 3
- third_gain: bfloat16 [1536], P(('dp', 'seq')), may hold values from 0.099609375 to 1.8984375
- upsample_weight: bfloat16 [1536, 1536], P(('dp', 'seq')), may hold values from -0.21875 to 0.21875
- skip_weight: bfloat16 [1536, 1536], P(('dp', 'seq')), may hold values from -0.15625 to 0.15625
- skip_bias: bfloat16 [1536], P(('dp', 'seq')), may hold values from -3 to 3
- depth_weight: bfloat16 [1536, 3], P(('dp', 'seq')), may hold values from -4 to 4
- point_weight: bfloat16 [1536, 1536], P(('dp', 'seq')), may hold values from -0.15625 to 0.15625
Outputs:
- outputs: bfloat16 [4, 8192, 1536], P('dp', 'seq')
- input_grad: bfloat16 [4, 4096, 1536], P('dp', 'seq')
- skip_grad: bfloat16 [4, 8192, 1536], P('dp', 'seq')
- first_gain_grad: float32 [1536], P(('dp', 'seq'))
- query_weight_grad: float32 [1536, 512], P(('dp', 'seq'))
- key_weight_grad: float32 [1536, 512], P(('dp', 'seq'))
- value_weight_grad: float32 [1536, 1536], P(('dp', 'seq'))
- content_bias_grad: float32 [512], P(('dp', 'seq'))
- position_bias_grad: float32 [512], P(('dp', 'seq'))
- relative_weight_grad: float32 [512, 32], P(('dp', 'seq'))
- mixing_weight_grad: float32 [1536, 1536], P(('dp', 'seq'))
- second_gain_grad: float32 [1536], P(('dp', 'seq'))
- inner_weight_grad: float32 [1536, 3072], P(('dp', 'seq'))
- inner_bias_grad: float32 [3072], P(('dp', 'seq'))
- outer_weight_grad: float32 [3072, 1536], P(('dp', 'seq'))
- outer_bias_grad: float32 [1536], P(('dp', 'seq'))
- third_gain_grad: float32 [1536], P(('dp', 'seq'))
- upsample_weight_grad: float32 [1536, 1536], P(('dp', 'seq'))
- skip_weight_grad: float32 [1536, 1536], P(('dp', 'seq'))
- skip_bias_grad: float32 [1536], P(('dp', 'seq'))
- depth_weight_grad: float32 [1536, 3], P(('dp', 'seq'))
- point_weight_grad: float32 [1536, 1536], P(('dp', 'seq'))
The draws below stay inside these ranges and needn't reach their ends.
Inputs may be any that keep to these rules, and one draw needn't show every extreme that they name: `lengths`: in each run of 2 windows on one index of dp, exactly one window has all 4096 bins valid; each other window has at most 3072 valid bins.
All inputs are finite; a program needn't handle non-finite values.
Results may differ from the reference program's by a relative error of at most 0.03.
Values may be sent and summed in bfloat16 or wider, within the bound.
A program may use at most 512 MiB of HBM per device.

```python
import math
import jax
import jax.numpy as jnp
from jax import lax

D = 1536
H = 8
KD = 64
VD = 192
FF = 3072
RPF = 32
LEN = 4096
WIN_DEV = 2
WINDOWS = 4


def draw_lengths(key, part):
    key = jax.random.fold_in(key, 11)
    first_key, second_key = jax.random.split(key)
    drawn = jax.random.randint(first_key, (WINDOWS,), LEN // 4, LEN - LEN // 4 + 1, dtype=jnp.int32)
    groups = WINDOWS // WIN_DEV
    chosen = jax.random.randint(second_key, (groups,), 0, WIN_DEV, dtype=jnp.int32)
    window_index = jnp.arange(WINDOWS, dtype=jnp.int32)
    group_pick = jnp.repeat(chosen, WIN_DEV)
    full_window = window_index % WIN_DEV == group_pick
    return jnp.where(full_window, LEN, drawn).astype(jnp.int32)


def levels(key, shape, cuts, least, largest):
    level, own = 1.0, jax.random.fold_in(key, 6)
    for dim, blocks in cuts:
        steps = jnp.exp(jax.random.uniform(jax.random.fold_in(own, dim), (blocks,), jnp.float32, least / len(cuts), largest / len(cuts)))
        level = level * jnp.repeat(steps, shape[dim] // blocks).reshape([-1 if axis == dim else 1 for axis in range(len(shape))])
    return level


def bell_draw(own_key, shape, scale, reach, pieces=(), kind=jnp.bfloat16):
    values = scale * jax.random.normal(own_key, shape, jnp.float32)
    if pieces:
        values = values * levels(own_key, shape, pieces, -0.22, 0.18)
    return jnp.clip(values, -reach, reach).astype(kind)


def setup_inputs(seed: int = 0) -> dict:
    key_list = jax.random.split(jax.random.key(seed), 24)
    inputs = bell_draw(key_list[0], (WINDOWS, LEN, D), 1.0, 6.0, ((0, 2), (1, 16)))
    skip_input = bell_draw(key_list[1], (WINDOWS, 2 * LEN, D), 1.0, 6.0, ((0, 2), (1, 16)))
    lengths = draw_lengths(jax.random.fold_in(key_list[23], 71), 0)
    cotangent = bell_draw(key_list[3], (WINDOWS, 2 * LEN, D), 1.0, 6.0, ((0, 2), (1, 16)))
    first_gain = jnp.clip(1.0 + 0.18 * jax.random.normal(key_list[4], (D,), jnp.float32), 0.099609375, 1.8984375).astype(jnp.bfloat16)
    query_weight = bell_draw(key_list[5], (D, H * KD), D ** -0.5, 0.15625, ((0, 32),))
    key_weight = bell_draw(key_list[6], (D, H * KD), D ** -0.5, 0.15625, ((0, 32),))
    value_weight = bell_draw(key_list[7], (D, H * VD), D ** -0.5, 0.15625, ((0, 32),))
    content_bias = bell_draw(key_list[8], (H * KD,), 0.5, 3.0, ((0, 32),))
    position_bias = bell_draw(key_list[9], (H * KD,), 0.5, 3.0, ((0, 32),))
    relative_weight = bell_draw(key_list[10], (H * KD, RPF), 4 ** -0.5, 3.0, ((0, 32),))
    mixing_weight = bell_draw(key_list[11], (H * VD, D), (H * VD // 256) ** -0.5, 2.5, ((0, 32),))
    second_gain = jnp.clip(1.0 + 0.18 * jax.random.normal(key_list[12], (D,), jnp.float32), 0.099609375, 1.8984375).astype(jnp.bfloat16)
    inner_weight = bell_draw(key_list[13], (D, FF), D ** -0.5, 0.15625, ((0, 32),))
    inner_bias = bell_draw(key_list[14], (FF,), 0.5, 3.0, ((0, 32),))
    outer_weight = bell_draw(key_list[15], (FF, D), (FF // 2) ** -0.5, 0.15625, ((0, 32),))
    outer_bias = bell_draw(key_list[16], (D,), 0.5, 3.0, ((0, 32),))
    third_gain = jnp.clip(1.0 + 0.18 * jax.random.normal(key_list[17], (D,), jnp.float32), 0.099609375, 1.8984375).astype(jnp.bfloat16)
    upsample_weight = bell_draw(key_list[18], (D, D), (D // 2) ** -0.5, 0.21875, ((0, 32),))
    skip_weight = bell_draw(key_list[19], (D, D), D ** -0.5, 0.15625, ((0, 32),))
    skip_bias = bell_draw(key_list[20], (D,), 0.5, 3.0, ((0, 32),))
    depth_weight = bell_draw(key_list[21], (D, 3), 2 ** -0.5, 4.0, ((0, 32),))
    point_weight = bell_draw(key_list[22], (D, D), D ** -0.5, 0.15625, ((0, 32),))
    return {"inputs": inputs, "skip_input": skip_input, "lengths": lengths, "cotangent": cotangent, "first_gain": first_gain, "query_weight": query_weight, "key_weight": key_weight, "value_weight": value_weight, "content_bias": content_bias, "position_bias": position_bias, "relative_weight": relative_weight, "mixing_weight": mixing_weight, "second_gain": second_gain, "inner_weight": inner_weight, "inner_bias": inner_bias, "outer_weight": outer_weight, "outer_bias": outer_bias, "third_gain": third_gain, "upsample_weight": upsample_weight, "skip_weight": skip_weight, "skip_bias": skip_bias, "depth_weight": depth_weight, "point_weight": point_weight}


highest = lax.Precision.HIGHEST
masked_score = -1e+30
epsilon = 1e-05

@jax.custom_vjp
def low(v):
    return lax.optimization_barrier(v.astype(jnp.bfloat16)).astype(jnp.float32)

@jax.custom_vjp
def low_back(v):
    return v

def low_keep(v):
    return (low(v), None)

def low_pass(kept, grad):
    return (grad,)

def back_keep(v):
    return (v, None)

def back_low(kept, grad):
    return (low(grad),)
low.defvjp(low_keep, low_pass)
low_back.defvjp(back_keep, back_low)

def product(left, right):
    return jnp.dot(left, right, precision=highest)

def layer_norm(values, gain):
    mean = lax.optimization_barrier(jnp.mean(values, axis=-1, keepdims=True))
    centered = values - mean
    spread = lax.optimization_barrier(jnp.mean(centered * centered, axis=-1, keepdims=True))
    return centered * lax.rsqrt(spread + epsilon) * gain

def smooth_gelu(values):
    return jax.nn.gelu(values, approximate=False)

def basis_line(first, count, features, extent):
    distance = (first - jnp.arange(count, dtype=jnp.int32)).astype(jnp.float32)
    half = features // 2
    lives = jnp.exp(jnp.linspace(math.log(3.0), math.log(extent), half, dtype=jnp.float32))
    decay = jnp.exp(-math.log(2.0) * jnp.abs(distance)[None, :] / lives[:, None])
    return jnp.concatenate([decay, jnp.sign(distance)[None, :] * decay], axis=0)

def relative_shift(matrix, keys):
    rows = matrix.shape[-2]
    lead = matrix.shape[:-2]
    width = matrix.shape[-1]
    padded = jnp.concatenate([matrix, jnp.zeros(lead + (rows, 1), matrix.dtype)], axis=-1)
    flat = padded.reshape(lead + (rows * (width + 1),))
    flat = flat[..., rows - 1:rows - 1 + rows * width]
    return flat.reshape(lead + (rows, width))[..., :keys]

def window_forward(params, inputs, skip_input, length):
    first_gain, query_weight, key_weight, value_weight, content_bias, position_bias, relative_weight, mixing_weight, second_gain, inner_weight, inner_bias, outer_weight, outer_bias, third_gain, upsample_weight, skip_weight, skip_bias, depth_weight, point_weight = params
    scale = float(KD) ** (-0.5)
    normed = low(layer_norm(inputs, first_gain))
    queries = low_back(product(normed, query_weight))
    keys = low(low_back(product(normed, key_weight))).reshape(LEN, H, KD)
    values = low(low_back(product(normed, value_weight))).reshape(LEN, H, VD)
    content = low((queries + content_bias) * scale).reshape(LEN, H, KD)
    positional = ((queries + position_bias) * scale).reshape(LEN, H, KD)
    projected = low(jnp.einsum('qhk,hkf->qhf', positional, relative_weight.reshape(H, KD, RPF), precision=highest))
    valid = jnp.arange(LEN) < length
    block_rows = min(512, LEN)

    def attend(start):
        block_content = lax.dynamic_slice_in_dim(content, start, block_rows, 0)
        block_projected = lax.dynamic_slice_in_dim(projected, start, block_rows, 0)
        line = low(basis_line(start + block_rows - 1, block_rows + LEN - 1, RPF, LEN))
        scores = jnp.einsum('qhk,thk->hqt', block_content, keys, precision=highest)
        wide = jnp.einsum('qhf,fc->hqc', block_projected, line, precision=highest)
        scores = low_back(scores + relative_shift(wide, LEN))
        scores = jnp.where(valid[None, None, :], scores, masked_score)
        top = lax.optimization_barrier(jnp.max(scores, axis=-1, keepdims=True))
        exponent = jnp.exp(scores - top)
        probs = low(exponent / lax.optimization_barrier(jnp.sum(exponent, axis=-1, keepdims=True)))
        mixed = jnp.einsum('hqt,thv->qhv', probs, values, precision=highest)
        return low(low_back(mixed)).reshape(block_rows, H * VD)
    starts = (jnp.arange(LEN // block_rows) * block_rows).astype(jnp.int32)
    mixed = lax.map(jax.checkpoint(attend), starts).reshape(LEN, H * VD)
    middle = inputs + low_back(product(mixed, mixing_weight))
    second = low(layer_norm(middle, second_gain))
    before = low_back(product(second, inner_weight) + inner_bias)
    hidden = low(smooth_gelu(before))
    block_out = middle + low_back(product(hidden, outer_weight)) + outer_bias
    third = low(smooth_gelu(layer_norm(block_out, third_gain)))
    lifted = low_back(product(third, upsample_weight))
    doubled = jnp.repeat(lifted, 2, axis=0)
    joined = low(doubled + low_back(product(skip_input, skip_weight)) + skip_bias)
    padded = jnp.pad(joined, ((1, 1), (0, 0)))
    conv = padded[:-2] * depth_weight[:, 0] + padded[1:-1] * depth_weight[:, 1] + padded[2:] * depth_weight[:, 2]
    conv = low(low_back(conv))
    result = low_back(product(conv, point_weight))
    keep = (jnp.arange(2 * LEN, dtype=jnp.int32) // 2 < length).astype(jnp.float32)
    return result * keep[:, None]

def reference(inputs, skip_input, lengths, cotangent, first_gain, query_weight, key_weight, value_weight, content_bias, position_bias, relative_weight, mixing_weight, second_gain, inner_weight, inner_bias, outer_weight, outer_bias, third_gain, upsample_weight, skip_weight, skip_bias, depth_weight, point_weight):
    params = tuple((entry.astype(jnp.float32) for entry in (first_gain, query_weight, key_weight, value_weight, content_bias, position_bias, relative_weight, mixing_weight, second_gain, inner_weight, inner_bias, outer_weight, outer_bias, third_gain, upsample_weight, skip_weight, skip_bias, depth_weight, point_weight)))

    def whole(params, inputs, skip_input):

        def single(items):
            return window_forward(params, items[0], items[1], items[2])
        return lax.map(jax.checkpoint(single), (inputs, skip_input, lengths))
    outputs, pullback = jax.vjp(whole, params, inputs.astype(jnp.float32), skip_input.astype(jnp.float32))
    grads, input_grad, skip_grad = pullback(cotangent.astype(jnp.float32))
    grad_first, grad_query, grad_key, grad_value, grad_content, grad_position, grad_relative, grad_mixing, grad_second, grad_inner, grad_inner_bias, grad_outer, grad_outer_bias, grad_third, grad_upsample, grad_skip, grad_skip_bias, grad_depth, grad_point = grads
    return (outputs.astype(jnp.bfloat16), input_grad.astype(jnp.bfloat16), skip_grad.astype(jnp.bfloat16), grad_first, grad_query, grad_key, grad_value, grad_content, grad_position, grad_relative, grad_mixing, grad_second, grad_inner, grad_inner_bias, grad_outer, grad_outer_bias, grad_third, grad_upsample, grad_skip, grad_skip_bias, grad_depth, grad_point)
```

```python
import functools
import math

import jax
import jax.numpy as jnp
from jax import lax
from jax.experimental import pallas as pl
from jax.experimental.pallas import tpu as pltpu
from jax.sharding import PartitionSpec as P

H = 8
KD = 64
VD = 192
RPF = 32
NEG = -1e30
BF = jnp.bfloat16
F32 = jnp.float32
epsilon = 1e-05


def extended_2(array, sides, width):
    for axis, dim in sides:
        peers, length = (lax.axis_size(axis), array.shape[dim])
        up = [(i, (i + 1) % peers) for i in range(peers - 1)]
        down = [(j, i) for i, j in up]
        last = lax.slice_in_dim(array, length - width, length, axis=dim)
        initial = lax.slice_in_dim(array, 0, width, axis=dim)
        before = lax.ppermute(last, axis, up)
        after = lax.ppermute(initial, axis, down)
        array = jnp.concatenate([before, array, after], axis=dim)
    return array


def layer_norm(values, gain):
    mean = jnp.mean(values, axis=-1, keepdims=True)
    centered = values - mean
    spread = jnp.mean(centered * centered, axis=-1, keepdims=True)
    return centered * lax.rsqrt(spread + epsilon) * gain


def smooth_gelu(values):
    return jax.nn.gelu(values, approximate=False)


def norm_gelu(values, gain):
    return smooth_gelu(layer_norm(values, gain))


def matmul(left, right):
    return jnp.dot(left, right, preferred_element_type=jnp.float32)


def times_transposed(left, right):
    return lax.dot_general(
        left, right, (((1,), (1,)), ((), ())), preferred_element_type=jnp.float32
    )


def transposed_times(left, right):
    return lax.dot_general(
        left, right, (((0,), (0,)), ((), ())), preferred_element_type=jnp.float32
    )


def depth_apply(extended, taps):
    return (
        extended[:, :-2] * taps[:, 0]
        + extended[:, 1:-1] * taps[:, 1]
        + extended[:, 2:] * taps[:, 2]
    )


def dot(a, b):
    return lax.dot_general(a, b, (((1,), (0,)), ((), ())), preferred_element_type=F32)


def dot32(a, b, dims=((1,), (0,))):
    return lax.dot_general(
        a, b, (dims, ((), ())), precision=lax.Precision.HIGHEST, preferred_element_type=F32
    )


def key_side(parts, part, rates, rows, groups, mine, other, store):
    half = RPF // 2
    spot = lax.broadcasted_iota(jnp.int32, (half, rows), 1).astype(F32)
    low = jnp.exp(-rates * (rows - 1 - spot)).astype(BF)
    high = jnp.exp(-rates * spot).astype(BF)
    pad = jnp.zeros((128 - KD - RPF, rows), BF)
    for slot in range(parts):
        theirs = lax.rem(part + slot, 2) if parts == 2 else slot_part(part, slot, parts)
        for g in range(groups):
            source = mine if slot == 0 else other
            if slot == 0:
                kt, vt = mine[g, 0, KD : 2 * KD, :], mine[g, 0, 2 * KD :, :]
            else:
                kt, vt = other[slot - 1, g, 0, :KD, :], other[slot - 1, g, 0, KD:, :]
            store(g * parts + theirs, jnp.concatenate([kt, low, high, pad], axis=0), vt)


def slot_part(part, slot, parts):
    out, bit = part, 1
    while bit < parts:
        if slot & bit:
            has = lax.rem(lax.div(part, bit), 2)
            out = out + bit - 2 * bit * has
        bit *= 2
    return out


def query_side(content, bias, relative, half):
    positional = content.astype(F32) + bias
    projected = dot32(relative, positional).astype(BF).astype(F32)
    return positional, projected[:half] + projected[half:], projected[:half] - projected[half:]


def block_query(content, plus, minus, rates, q_block, k_block, rows, kind):
    spot = lax.broadcasted_iota(jnp.int32, plus.shape, 1)
    query_pos = q_block * rows + spot
    zero = jnp.zeros(plus.shape, BF)
    below = above = zero
    if kind != "above":
        gap = (query_pos - (k_block * rows + rows - 1)).astype(F32)
        below = (plus * jnp.exp(jnp.minimum(-rates * gap, 60.0))).astype(BF)
    if kind != "below":
        gap = (k_block * rows - query_pos).astype(F32)
        above = (minus * jnp.exp(jnp.minimum(-rates * gap, 60.0))).astype(BF)
    rest = jnp.zeros((128 - KD - RPF, rows), BF)
    if kind == "below":
        return jnp.concatenate([content, below, zero, rest], axis=0)
    if kind == "above":
        return jnp.concatenate([content, zero, above, rest], axis=0)
    return (
        jnp.concatenate([content, below, zero, rest], axis=0),
        jnp.concatenate([content, zero, above, rest], axis=0),
    )


def signs(q_block, k_block, rows):
    i = q_block * rows + lax.broadcasted_iota(jnp.int32, (rows, rows), 1)
    j = k_block * rows + lax.broadcasted_iota(jnp.int32, (rows, rows), 0)
    return i, j


def block_scores(k_sc, content, plus, minus, rates, q_block, k_block, rows, kind, length):
    keys = k_sc[pl.ds(pl.multiple_of(k_block * rows, rows), rows), :]
    if kind != "both":
        return dot(keys, block_query(content, plus, minus, rates, q_block, k_block, rows, kind))
    below, above = block_query(content, plus, minus, rates, q_block, k_block, rows, kind)
    i, j = signs(q_block, k_block, rows)
    s_below, s_above = dot(keys, below), dot(keys, above)
    scores = jnp.where(i > j, s_below, jnp.where(i < j, s_above, 0.5 * (s_below + s_above)))
    return jnp.where(j < length, scores, NEG)


def visit_tiles(tile, q_block, length, rows, per, tiles):
    span = rows * per
    count = lax.div(length + span - 1, span)
    full = lax.div(length, span)
    own = lax.div(q_block, per)
    pl.loop(0, jnp.minimum(own, full))(functools.partial(tile, kind="below"))
    pl.loop(own + 1, full)(functools.partial(tile, kind="above"))

    @pl.loop(0, 2)
    def _(k):
        t = jnp.where(k == 0, own, full)
        go = (t < count) & ((k == 0) | (full != own))

        @pl.when(go)
        def _():
            tile(t, kind="both")


def forward_kernel(
    parts, per, info, rates_ref, bias_ref, rel_ref, mine, other, mixed, wide, lse, k_sc, v_sc, m_sc, l_sc, acc
):
    groups, rows = mine.shape[0], mine.shape[3]
    half = RPF // 2
    length = info[pl.program_id(0)]
    part = info[pl.num_programs(0)]
    rates = rates_ref[...]

    def store(block, kt, vt):
        spot = pl.multiple_of(block * rows, rows)
        k_sc[pl.ds(spot, rows), :] = kt.T
        v_sc[:, pl.ds(spot, rows)] = vt

    key_side(parts, part, rates, rows, groups, mine, other, store)

    @pl.loop(0, groups)
    def _(g):
        q_block = g * parts + part

        @pl.when(q_block * rows > length)
        def _():
            mixed[g, 0] = jnp.zeros(mixed.shape[2:], mixed.dtype)
            wide[g, 0] = jnp.zeros(wide.shape[2:], wide.dtype)
            lse[g, 0] = jnp.zeros(lse.shape[2:], lse.dtype)

        @pl.when(q_block * rows <= length)
        def _():
            content = mine[g, 0, :KD, :]
            _, plus, minus = query_side(content, bias_ref[...], rel_ref[...], half)
            m_sc[...] = jnp.full(m_sc.shape, NEG, F32)
            l_sc[...] = jnp.zeros(l_sc.shape, F32)
            acc[...] = jnp.zeros(acc.shape, F32)

            def tile(t, kind):
                scores = jnp.concatenate(
                    [
                        block_scores(
                            k_sc, content, plus, minus, rates, q_block, t * per + n, rows, kind, length
                        )
                        for n in range(per)
                    ],
                    axis=0,
                )
                old = m_sc[...]
                new = jnp.maximum(old, jnp.max(scores, axis=0, keepdims=True))
                alpha = jnp.exp(old - new)
                probs = jnp.exp(scores - new)
                m_sc[...] = new
                l_sc[...] = l_sc[...] * alpha + jnp.sum(probs, axis=0, keepdims=True)
                span = rows * per
                values = v_sc[:, pl.ds(pl.multiple_of(t * span, span), span)]
                acc[...] = acc[...] * alpha + dot(values, probs.astype(BF))

            visit_tiles(tile, q_block, length, rows, per, groups * parts // per)
            total = l_sc[...]
            out = acc[...] / total
            mixed[g, 0] = out.astype(BF)
            wide[g, 0] = out
            lse[g, 0] = jnp.broadcast_to(m_sc[...] + jnp.log(total), lse.shape[2:])


def backward_kernel(
    parts, per, info, rates_ref, bias_ref, rel_ref, mine, other, grad, wide, lse,
    dq, dkv_mine, dkv_other, sums, rel_grad,
    k_sc, kt_sc, v_sc, dk_sc, dv_sc, dq_sc, bias_sc,
):
    groups, rows = mine.shape[0], mine.shape[3]
    half = RPF // 2
    step = pl.program_id(0)
    length = info[step]
    part = info[pl.num_programs(0)]
    rates = rates_ref[...]
    scale = KD**-0.5

    def store(block, kt, vt):
        spot = pl.multiple_of(block * rows, rows)
        k_sc[pl.ds(spot, rows), :] = kt.T
        kt_sc[:, pl.ds(spot, rows)] = kt
        v_sc[pl.ds(spot, rows), :] = vt.T

    key_side(parts, part, rates, rows, groups, mine, other, store)
    dk_sc[...] = jnp.zeros(dk_sc.shape, F32)
    dv_sc[...] = jnp.zeros(dv_sc.shape, F32)

    @pl.when(step == 0)
    def _():
        bias_sc[...] = jnp.zeros(bias_sc.shape, F32)
        rel_grad[...] = jnp.zeros(rel_grad.shape, F32)

    @pl.loop(0, groups)
    def _(g):
        q_block = g * parts + part

        @pl.when(q_block * rows > length)
        def _():
            dq[g, 0] = jnp.zeros(dq.shape[2:], dq.dtype)

        @pl.when(q_block * rows <= length)
        def _():
            content = mine[g, 0, :KD, :]
            content_rows = content.T
            positional, plus, minus = query_side(content, bias_ref[...], rel_ref[...], half)
            grad_t = grad[g, 0]
            grad_rows = grad_t.T
            log_total = lse[g, 0, :1, :]
            row_sum = jnp.sum(grad_t.astype(F32) * wide[g, 0], axis=0, keepdims=True)
            dq_sc[...] = jnp.zeros(dq_sc.shape, F32)

            def tile(t, kind):
                span = rows * per
                spot = pl.multiple_of(t * span, span)
                scores = jnp.concatenate(
                    [
                        block_scores(
                            k_sc, content, plus, minus, rates, q_block, t * per + n, rows, kind, length
                        )
                        for n in range(per)
                    ],
                    axis=0,
                )
                exact = jnp.exp(scores - log_total)
                prob_grad = dot(v_sc[pl.ds(spot, span), :], grad_t)
                score_grad = exact * (prob_grad - row_sum)
                low = score_grad.astype(BF)
                dv_sc[pl.ds(spot, span), :] += dot(exact.astype(BF), grad_rows)
                dk_sc[pl.ds(spot, span), :] += dot(low, content_rows)
                for n in range(per):
                    k_block = t * per + n
                    piece = low[n * rows : (n + 1) * rows]
                    keys = kt_sc[:, pl.ds(pl.multiple_of(k_block * rows, rows), rows)]
                    place = q_block * rows + lax.broadcasted_iota(jnp.int32, (half, rows), 1)
                    down = -rates * (place - (k_block * rows + rows - 1)).astype(F32)
                    up = -rates * (k_block * rows - place).astype(F32)
                    if kind == "below":
                        part_sum = dot(keys[: KD + half], piece)
                        dq_sc[:KD] += part_sum[:KD]
                        dq_sc[KD : KD + half] += part_sum[KD:] * jnp.exp(down)
                    elif kind == "above":
                        part_sum = dot(keys[: KD + RPF], piece)
                        dq_sc[:KD] += part_sum[:KD]
                        dq_sc[KD + half :] += part_sum[KD + half :] * jnp.exp(up)
                    else:
                        i, j = signs(q_block, k_block, rows)
                        wide_piece = score_grad[n * rows : (n + 1) * rows]
                        equal = 0.5 * wide_piece
                        lower = jnp.where(i > j, wide_piece, jnp.where(i < j, 0.0, equal)).astype(BF)
                        upper = jnp.where(i < j, wide_piece, jnp.where(i > j, 0.0, equal)).astype(BF)
                        dq_sc[:KD] += dot(keys[:KD], piece)
                        dq_sc[KD : KD + half] += dot(keys[KD : KD + half], lower) * jnp.exp(
                            jnp.minimum(down, 60.0)
                        )
                        dq_sc[KD + half :] += dot(keys[KD + half : KD + RPF], upper) * jnp.exp(
                            jnp.minimum(up, 60.0)
                        )

            visit_tiles(tile, q_block, length, rows, per, groups * parts // per)
            content_grad = dq_sc[:KD]
            down, up = dq_sc[KD : KD + half], dq_sc[KD + half :]
            projected_grad = jnp.concatenate([down + up, down - up], axis=0)
            positional_grad = dot32(rel_ref[...], projected_grad, ((0,), (0,)))
            dq[g, 0] = (scale * (content_grad + positional_grad)).astype(BF)
            bias_sc[0] += content_grad
            bias_sc[1] += positional_grad
            rel_grad[...] += dot32(positional, projected_grad, ((1,), (1,)))

    for slot in range(parts):
        theirs = slot_part(part, slot, parts)
        for g in range(groups):
            spot = pl.multiple_of((g * parts + theirs) * rows, rows)
            dkt = dk_sc[pl.ds(spot, rows), :].astype(BF).T
            dvt = dv_sc[pl.ds(spot, rows), :].astype(BF).T
            both = jnp.concatenate([dkt, dvt], axis=0)
            if slot == 0:
                dkv_mine[g, 0] = both
            else:
                dkv_other[slot - 1, g, 0] = both

    @pl.when(step == pl.num_programs(0) - 1)
    def _():
        sums[...] = scale * jnp.sum(bias_sc[...], axis=-1, keepdims=True)


def attention_cost(windows, groups, rows, parts, wide):
    pairs = windows * groups * rows * groups * parts * rows
    return pl.CostEstimate(
        flops=int(pairs * 2 * wide * 0.75), bytes_accessed=20_000_000, transcendentals=int(pairs)
    )


def whole(*shape):
    return pl.BlockSpec(shape, lambda w: (0,) * len(shape))


def per_window(*shape):
    lead = len(shape) - 3
    return pl.BlockSpec(shape, lambda w: (0,) * lead + (w, 0, 0))


def tile_blocks(rows, groups, parts, target):
    per = max(1, target // rows)
    while (groups * parts) % per:
        per -= 1
    return per


def attention_forward(info, rates, bias, rel, mine, other, parts):
    groups, windows, _, rows = mine.shape
    per = tile_blocks(rows, groups, parts, 512)
    total = groups * parts * rows
    return pl.pallas_call(
        functools.partial(forward_kernel, parts, per),
        grid=(windows,),
        out_shape=(
            jax.ShapeDtypeStruct((groups, windows, VD, rows), BF),
            jax.ShapeDtypeStruct((groups, windows, VD, rows), F32),
            jax.ShapeDtypeStruct((groups, windows, 8, rows), F32),
        ),
        in_specs=[
            pl.BlockSpec(memory_space=pltpu.SMEM),
            whole(*rates.shape),
            whole(*bias.shape),
            whole(*rel.shape),
            per_window(groups, 1, 2 * KD + VD, rows),
            per_window(parts - 1, groups, 1, KD + VD, rows),
        ],
        out_specs=(
            per_window(groups, 1, VD, rows),
            per_window(groups, 1, VD, rows),
            per_window(groups, 1, 8, rows),
        ),
        scratch_shapes=[
            pltpu.VMEM((total, 128), BF),
            pltpu.VMEM((VD, total), BF),
            pltpu.VMEM((1, rows), F32),
            pltpu.VMEM((1, rows), F32),
            pltpu.VMEM((VD, rows), F32),
        ],
        compiler_params=pltpu.CompilerParams(vmem_limit_bytes=56 * 2**20),
        cost_estimate=attention_cost(windows, groups, rows, parts, 128 + 256),
        name="attention_forward",
    )(info, rates, bias, rel, mine, other)


def attention_backward(info, rates, bias, rel, mine, other, grad, wide, lse, parts):
    groups, windows, _, rows = mine.shape
    per = tile_blocks(rows, groups, parts, 512)
    total = groups * parts * rows
    return pl.pallas_call(
        functools.partial(backward_kernel, parts, per),
        grid=(windows,),
        out_shape=(
            jax.ShapeDtypeStruct((groups, windows, KD, rows), BF),
            jax.ShapeDtypeStruct((groups, windows, KD + VD, rows), BF),
            jax.ShapeDtypeStruct((parts - 1, groups, windows, KD + VD, rows), BF),
            jax.ShapeDtypeStruct((2, KD, 1), F32),
            jax.ShapeDtypeStruct((KD, RPF), F32),
        ),
        in_specs=[
            pl.BlockSpec(memory_space=pltpu.SMEM),
            whole(*rates.shape),
            whole(*bias.shape),
            whole(*rel.shape),
            per_window(groups, 1, 2 * KD + VD, rows),
            per_window(parts - 1, groups, 1, KD + VD, rows),
            per_window(groups, 1, VD, rows),
            per_window(groups, 1, VD, rows),
            per_window(groups, 1, 8, rows),
        ],
        out_specs=(
            per_window(groups, 1, KD, rows),
            per_window(groups, 1, KD + VD, rows),
            per_window(parts - 1, groups, 1, KD + VD, rows),
            whole(2, KD, 1),
            whole(KD, RPF),
        ),
        scratch_shapes=[
            pltpu.VMEM((total, 128), BF),
            pltpu.VMEM((128, total), BF),
            pltpu.VMEM((total, VD), BF),
            pltpu.VMEM((total, KD), F32),
            pltpu.VMEM((total, VD), F32),
            pltpu.VMEM((KD + RPF, rows), F32),
            pltpu.VMEM((2, KD, rows), F32),
        ],
        compiler_params=pltpu.CompilerParams(vmem_limit_bytes=56 * 2**20),
        cost_estimate=attention_cost(windows, groups, rows, parts, 3 * 256 + 2 * 256),
        name="attention_backward",
    )(info, rates, bias, rel, mine, other, grad, wide, lse)

MESH = pl.DeviceIdType.MESH


def gather_kernel(pairs, nhi, ndp, *refs):
    count = 1 + max(chunk[0] for pair in pairs for side in pair for chunk in side)
    refs_in, refs_out, sems = refs[:count], refs[count : 2 * count], refs[2 * count :]
    local_sem, send_hi, recv_hi, send_y, recv_y, send_dp, recv_dp, send_c, recv_c = sems
    dp, seq = lax.axis_index("dp"), lax.axis_index("seq")
    hi, low = lax.div(seq, 4), lax.rem(seq, 4)
    y, c = lax.div(low, 2), lax.rem(low, 2)

    def place(dp_to, hi_to, y_to, c_to):
        return (dp_to, hi_to * 4 + y_to * 2 + c_to)

    hi_peers = [place(dp, lax.rem(hi + k, nhi), y, c) for k in range(1, nhi)]
    y_peers = [place(dp, hi, 1 - y, c)]
    dp_peers = [place(lax.rem(dp + k, ndp), hi, y, c) for k in range(1, ndp)]
    c_peers = [place(dp, hi, y, 1 - c)]

    barrier = pltpu.get_barrier_semaphore()
    everyone = hi_peers + y_peers + dp_peers + c_peers
    for peer in everyone:
        pl.semaphore_signal(barrier, inc=1, device_id=peer, device_id_type=MESH)
    pl.semaphore_wait(barrier, len(everyone))

    chunks = [
        [(n, side) + chunk for n, (side, chunk) in enumerate(flat)]
        for flat in [[(s, ch) for s in (0, 1) for ch in pair[s]] for pair in pairs]
    ]
    serial, step_chunks = 0, []
    for group in chunks:
        step_chunks.append([])
        for _, side, array, first, columns in group:
            step_chunks[-1].append((serial, side, array, first, columns))
            serial += 1

    def copies(chunk, stage):
        n, side, array, first, columns = chunk
        cols = pl.ds(first, columns)
        shard, out = refs_in[array], refs_out[array]
        which = (("hi", "y", "dp", "c"), ("hi", "dp", "y", "c"))[side][stage]
        if which == "hi":
            target = out.at[dp, hi, y, c, :, cols]
            source = shard.at[:, cols]
            peers, ss, rs = hi_peers, send_hi, recv_hi
        else:
            if which == "c":
                target = out.at[:, :, :, c, :, cols]
                peers, ss, rs = c_peers, send_c, recv_c
            elif which == "y":
                target = (
                    out.at[dp, :, y, c, :, cols] if stage == 1 else out.at[:, :, y, c, :, cols]
                )
                peers, ss, rs = y_peers, send_y, recv_y
            else:
                target = (
                    out.at[dp, :, y, c, :, cols] if stage == 1 else out.at[dp, :, :, c, :, cols]
                )
                peers, ss, rs = dp_peers, send_dp, recv_dp
            source = target
        return [
            pltpu.make_async_remote_copy(
                src_ref=source,
                dst_ref=target,
                send_sem=ss.at[n, k],
                recv_sem=rs.at[n, k],
                device_id=peer,
                device_id_type=MESH,
            )
            for k, peer in enumerate(peers)
        ]

    def own(array):
        return pltpu.make_async_copy(
            refs_in[array], refs_out[array].at[dp, hi, y, c], local_sem.at[array]
        )

    for group in step_chunks:
        for chunk in group:
            for copy in copies(chunk, 0):
                copy.start()
    for array in range(count):
        own(array).start()
    for array in range(count):
        own(array).wait()
    for step in range(len(pairs) + 2):
        for stage in (3, 2, 1):
            if 0 <= step + 1 - stage < len(pairs):
                for chunk in step_chunks[step + 1 - stage]:
                    for copy in copies(chunk, stage - 1):
                        copy.wait_recv()
                    for copy in copies(chunk, stage):
                        copy.start()
    for group in step_chunks:
        for chunk in group:
            for copy in copies(chunk, 3):
                copy.wait_recv()
    for group in step_chunks:
        for chunk in group:
            for stage in range(4):
                for copy in copies(chunk, stage):
                    copy.wait_send()


def gather_weights(shards, pairs):
    ndp, nseq = lax.axis_size("dp"), lax.axis_size("seq")
    nhi, count = nseq // 4, len(shards)
    chunks = sum(len(side) for pair in pairs for side in pair)
    return pl.pallas_call(
        functools.partial(gather_kernel, pairs, nhi, ndp),
        out_shape=[
            jax.ShapeDtypeStruct((ndp, nhi, 2, 2) + shard.shape, shard.dtype) for shard in shards
        ],
        in_specs=[pl.BlockSpec(memory_space=pl.ANY)] * count,
        out_specs=[pl.BlockSpec(memory_space=pl.ANY)] * count,
        scratch_shapes=[pltpu.SemaphoreType.DMA((count,))]
        + [
            pltpu.SemaphoreType.DMA((chunks, size))
            for size in (nhi - 1, nhi - 1, 1, 1, ndp - 1, ndp - 1, 1, 1)
        ],
        compiler_params=pltpu.CompilerParams(collective_id=1, has_side_effects=True),
        name="gather_weights",
    )(*shards)


def flat_index():
    return lax.axis_index("dp") * lax.axis_size("seq") + lax.axis_index("seq")


def swap(array, mask):
    devices = lax.axis_size("dp") * lax.axis_size("seq")
    return lax.ppermute(array, ("dp", "seq"), [(i, i ^ mask) for i in range(devices)])


def tie(*values):
    return lax.optimization_barrier(values)


def tie_tree(tree):
    leaves, shape = jax.tree.flatten(tree)
    arrays = [k for k, leaf in enumerate(leaves) if isinstance(leaf, jax.Array)]
    for k, value in zip(arrays, tie(*[leaves[k] for k in arrays]), strict=True):
        leaves[k] = value
    return jax.tree.unflatten(shape, leaves)


def bit_of(mask):
    return lax.rem(lax.div(flat_index(), mask), 2)


def halve(arrays, left, mask):
    spot, bit = left.index(mask), bit_of(mask)

    def pick(which):
        return jnp.concatenate(
            [lax.dynamic_index_in_dim(a, which, spot, keepdims=False) for a in arrays], axis=-2
        )

    theirs = swap(pick(1 - bit), mask)
    total = pick(bit).astype(jnp.float32) + theirs.astype(jnp.float32)
    return total.astype(arrays[0].dtype), [m for m in left if m != mask]


def chip_term(left, right):
    half, core = right.shape[1] // 2, bit_of(1)
    theirs = lax.dynamic_slice_in_dim(right, (1 - core) * half, half, 1)
    mine = lax.dynamic_slice_in_dim(right, core * half, half, 1)
    arrived = swap(transposed_times(left, theirs).astype(jnp.bfloat16), 1)
    return (transposed_times(left, mine) + arrived.astype(jnp.float32)).astype(jnp.bfloat16)


def mask_lists():
    nseq, ndp = lax.axis_size("seq"), lax.axis_size("dp")
    left, mask = [], nseq * ndp // 2
    while mask > 1:
        left.append(mask)
        mask //= 2
    across = [m for m in left if m >= nseq]
    return left, across, [m for m in left if 2 < m < nseq]


def plane_orders():
    _, across, _ = mask_lists()
    return (across + [2], [2] + across)


def plane_start(terms, columns):
    left, _, _ = mask_lists()
    chips = 2 ** len(left)
    pieces = []
    for t in terms:
        t = t.reshape((2,) * len(left) + (t.shape[0] // chips, t.shape[1]))
        pieces += [t[..., k : k + columns] for k in range(0, t.shape[-1], columns)]
    half = columns // 2
    return [([p[..., :half] for p in pieces], left), ([p[..., half:] for p in pieces], left)]


def plane_step(state, step, last):
    out = []
    for (arrays, left), order in zip(state, plane_orders(), strict=True):
        hops = order[step:] if last else order[step : step + 1]
        for mask in hops:
            total, left = halve(arrays, left, mask)
            arrays = [total]
        out.append((arrays, left))
    return out


def line_sum(state):
    arrays = [pieces[0] for pieces, _ in state]
    whole_line = jnp.concatenate(arrays, axis=-1)
    _, _, line = mask_lists()
    count = 2 ** len(line)
    blocks = whole_line.reshape((count,) + whole_line.shape[len(line) :])
    here = lax.div(lax.axis_index("seq"), 4)
    total = lax.dynamic_index_in_dim(blocks, here, 0, keepdims=False).astype(jnp.float32)
    for k in range(1, count):
        there = here ^ k
        arrived = swap(lax.dynamic_index_in_dim(blocks, there, 0, keepdims=False), 4 * k)
        total = total + arrived.astype(jnp.float32)
    return total


def to_owner(total, rows):
    core = bit_of(1)
    out, spot = [], 0
    for r in rows:
        piece = total[spot : spot + 2 * r]
        spot += 2 * r
        out.append(piece.reshape(2, r, piece.shape[1]))
    mine = [lax.dynamic_index_in_dim(p, core, 0, keepdims=False) for p in out]
    theirs = jnp.concatenate(
        [lax.dynamic_index_in_dim(p, 1 - core, 0, keepdims=False) for p in out], axis=0
    )
    arrived = swap(theirs, 1)
    done, spot = [], 0
    for r, m in zip(rows, mine, strict=True):
        a = arrived[spot : spot + r]
        spot += r
        done.append((jnp.where(core == 0, m, a), jnp.where(core == 0, a, m)))
    return done


def scatter_small(pieces):
    devices = lax.axis_size("dp") * lax.axis_size("seq")
    packed = jnp.concatenate([p.reshape(devices, -1) for p in pieces], axis=1)
    count = packed.shape[1]
    total = jnp.pad(packed, ((0, 0), (0, -count % 1024))).reshape(devices, -1, 128)
    left, _, _ = mask_lists()
    left = left + [1]
    total = total.reshape((2,) * len(left) + total.shape[1:])
    for mask in left[::-1]:
        total, left = halve([total], left, mask)
    total = total.reshape(-1)
    out, spot = [], 0
    for p in pieces:
        size = p.size // devices
        out.append(total[spot : spot + size].reshape((p.shape[0] // devices,) + p.shape[1:]))
        spot += size
    return out


def on_device(
    inputs,
    skip_input,
    lengths,
    cotangent,
    first_gain,
    query_weight,
    key_weight,
    value_weight,
    content_bias,
    position_bias,
    relative_weight,
    mixing_weight,
    second_gain,
    inner_weight,
    inner_bias,
    outer_weight,
    outer_bias,
    third_gain,
    upsample_weight,
    skip_weight,
    skip_bias,
    depth_weight,
    point_weight,
):
    windows, rows, width = inputs.shape
    scale = float(KD) ** (-0.5)
    wide = 2 * KD + VD
    nseq, ndp = lax.axis_size("seq"), lax.axis_size("dp")
    devices = nseq * ndp
    parts = nseq // H
    keys_total = rows * nseq
    seq = lax.axis_index("seq")
    head, part = lax.div(seq, parts), lax.rem(seq, parts)
    first = seq * rows
    hidden_width = inner_weight.shape[1]

    shard_rows = query_weight.shape[0]
    packed_shard = jnp.concatenate(
        [
            query_weight.reshape(shard_rows, H, KD),
            key_weight.reshape(shard_rows, H, KD),
            value_weight.reshape(shard_rows, H, VD),
        ],
        axis=2,
    ).reshape(shard_rows, H * wide)
    small_shards = (
        first_gain,
        content_bias,
        position_bias,
        relative_weight,
        second_gain,
        inner_bias,
        outer_bias,
        third_gain,
        skip_bias,
        depth_weight,
    )
    small_shard = jnp.concatenate([s.reshape(-1) for s in small_shards])
    small_count = small_shard.shape[0]
    small_shard = jnp.pad(small_shard, (0, -small_count % 2048)).reshape(-1, 128)
    half_wide, half_hidden, half_width = H * wide // 2, hidden_width // 2, width // 2
    gathered = gather_weights(
        [
            small_shard,
            packed_shard,
            skip_weight,
            mixing_weight,
            inner_weight,
            outer_weight,
            upsample_weight,
            point_weight,
        ],
        (
            (((0, 0, 128), (1, 0, half_wide)), ((1, half_wide, half_wide),)),
            (((2, 0, width),), ((3, 0, width),)),
            (((4, 0, half_hidden),), ((5, 0, half_width),)),
            (((4, half_hidden, half_hidden),), ((5, half_width, half_width),)),
            (((6, 0, width),), ((7, 0, width),)),
        ),
    )
    small_full = gathered[0].reshape(devices, -1)
    (
        weight_packed,
        weight_skip,
        weight_mixing,
        weight_inner,
        weight_outer,
        weight_upsample,
        weight_point,
    ) = (g.reshape(-1, g.shape[-1]) for g in gathered[1:])
    small, spot = [], 0
    for s in small_shards:
        small.append(
            small_full[:, spot : spot + s.size].reshape((devices * s.shape[0],) + s.shape[1:])
        )
        spot += s.size
    (
        gain_first,
        bias_content,
        bias_position,
        weight_relative,
        gain_second,
        bias_inner,
        bias_outer,
        gain_third,
        bias_skip,
        weight_depth,
    ) = (s.astype(jnp.float32) for s in small)

    lives = jnp.exp(
        jnp.linspace(math.log(3.0), math.log(keys_total), RPF // 2, dtype=jnp.float32)
    )
    rates = (math.log(2.0) / lives)[:, None]
    bias_gap = ((bias_position - bias_content) * scale).reshape(H, KD, 1)
    bias_gap = lax.dynamic_index_in_dim(bias_gap, head, 0, keepdims=False)
    relative = lax.dynamic_index_in_dim(
        weight_relative.reshape(H, KD, RPF), head, 0, keepdims=False
    ).T
    info = jnp.concatenate([lengths, part[None].astype(jnp.int32)])
    groups = [[p + parts * g for g in range(H)] for p in range(parts)]

    def exchange(array):
        return lax.all_to_all(array, "seq", 0, 0, axis_index_groups=groups, tiled=True)

    def swap_part(array, slot):
        return lax.ppermute(array, "seq", [(i, i ^ slot) for i in range(nseq)])

    flat = inputs.reshape(windows * rows, width).astype(jnp.float32)
    normed, first_norm_back = jax.vjp(layer_norm, flat, gain_first)
    normed_low = normed.astype(jnp.bfloat16)
    per_head = jnp.concatenate(
        [bias_content.reshape(H, KD), jnp.zeros((H, KD + VD), jnp.float32)], axis=1
    ).reshape(H * wide)
    per_scale = jnp.tile(
        jnp.concatenate(
            [jnp.full((KD,), scale, jnp.float32), jnp.ones((KD + VD,), jnp.float32)]
        ),
        H,
    )

    def by_head(array, size):
        (array,) = tie(array)
        (array,) = tie(array.reshape(windows, rows, H, size).transpose(2, 0, 3, 1))
        return array

    def by_row(array):
        (array,) = tie(array.transpose(1, 3, 0, 2).reshape(windows * rows, -1))
        return array

    made = (matmul(normed_low, weight_packed) + per_head) * per_scale
    sent = by_head(made.astype(jnp.bfloat16), wide)
    mine = exchange(sent)
    other = jnp.stack([swap_part(mine[:, :, KD:, :], slot) for slot in range(1, parts)])
    mixed_own, mixed_wide, log_total = attention_forward(
        info, rates, bias_gap, relative, mine, other, parts
    )
    mixed_low = by_row(exchange(mixed_own))
    middle = flat + matmul(mixed_low, weight_mixing)
    second, second_norm_back = jax.vjp(layer_norm, middle, gain_second)
    second_low = second.astype(jnp.bfloat16)
    before = matmul(second_low, weight_inner) + bias_inner
    hidden, gelu_back = jax.vjp(smooth_gelu, before)
    hidden_low = hidden.astype(jnp.bfloat16)
    block_out = middle + matmul(hidden_low, weight_outer) + bias_outer
    third, third_back = jax.vjp(norm_gelu, block_out, gain_third)
    third_low = third.astype(jnp.bfloat16)
    fine = jnp.arange(2 * rows, dtype=jnp.int32)[:, None] // 2
    twice = (fine == jnp.arange(rows, dtype=jnp.int32)[None, :]).astype(jnp.bfloat16)
    third_twice = (
        jnp.einsum(
            "ts,wsd->wtd",
            twice,
            third_low.reshape(windows, rows, width),
            preferred_element_type=jnp.float32,
        )
        .astype(jnp.bfloat16)
        .reshape(windows * 2 * rows, width)
    )
    skip_flat = skip_input.reshape(windows * 2 * rows, width)
    skip_part = matmul(skip_flat, weight_skip) + bias_skip
    joined_low = (
        (matmul(third_twice, weight_upsample) + skip_part)
        .astype(jnp.bfloat16)
        .reshape(windows, 2 * rows, width)
    )
    joined_rim = extended_2(joined_low, (("seq", 1),), 1)
    taps = weight_depth
    joined_wide = joined_rim.astype(jnp.float32)
    conv_low = depth_apply(joined_wide, taps).astype(jnp.bfloat16)
    conv_flat = conv_low.reshape(windows * 2 * rows, width)
    bins = 2 * first + jnp.arange(2 * rows, dtype=jnp.int32)
    keep = (bins // 2)[None, :] < lengths[:, None]
    keep_wide = keep.astype(jnp.float32)[:, :, None]
    outputs = (
        matmul(conv_flat, weight_point).reshape(windows, 2 * rows, width) * keep_wide
    ).astype(jnp.bfloat16)

    out_grad = (cotangent * keep.astype(jnp.bfloat16)[:, :, None]).reshape(
        windows * 2 * rows, width
    )
    term_point = chip_term(conv_flat, out_grad)
    conv_grad = (
        times_transposed(out_grad, weight_point)
        .astype(jnp.bfloat16)
        .reshape(windows, 2 * rows, width)
    )
    grad_rim = extended_2(conv_grad, (("seq", 1),), 1).astype(jnp.float32)
    joined_grad = (
        grad_rim[:, 2:] * taps[:, 0]
        + grad_rim[:, 1:-1] * taps[:, 1]
        + grad_rim[:, :-2] * taps[:, 2]
    )
    conv_wide = conv_grad.astype(jnp.float32)
    grad_depth = jnp.stack(
        [
            jnp.sum(conv_wide * joined_wide[:, :-2], axis=(0, 1)),
            jnp.sum(conv_wide * joined_wide[:, 1:-1], axis=(0, 1)),
            jnp.sum(conv_wide * joined_wide[:, 2:], axis=(0, 1)),
        ],
        axis=1,
    )
    grad_skip_bias = jnp.sum(joined_grad, axis=(0, 1))
    joined_back = joined_grad.astype(jnp.bfloat16)
    joined_flat = joined_back.reshape(windows * 2 * rows, width)
    term_skip = chip_term(skip_flat, joined_flat)
    skip_grad = (
        times_transposed(joined_flat, weight_skip)
        .astype(jnp.bfloat16)
        .reshape(windows, 2 * rows, width)
    )
    lifted_grad = (
        jnp.einsum("ts,wtd->wsd", twice, joined_back, preferred_element_type=jnp.float32)
        .astype(jnp.bfloat16)
        .reshape(windows * rows, width)
    )
    third_grad = times_transposed(lifted_grad, weight_upsample)
    last = [False, True]
    term_point, term_skip, lifted_grad, third_grad, skip_grad, outputs = tie(
        term_point, term_skip, lifted_grad, third_grad, skip_grad, outputs
    )

    sum_a = plane_step(plane_start([term_point, term_skip], half_width), 0, last[0])
    block_grad, grad_third = third_back(third_grad)
    block_low = block_grad.astype(jnp.bfloat16)
    term_upsample = chip_term(third_low, lifted_grad)
    term_outer = chip_term(hidden_low, block_low)
    grad_outer_bias = jnp.sum(block_grad, axis=0)
    (before_grad,) = gelu_back(times_transposed(block_low, weight_outer))
    before_low = before_grad.astype(jnp.bfloat16)
    sum_a, term_upsample, term_outer, before_low, block_grad = tie_tree(
        (sum_a, term_upsample, term_outer, before_low, block_grad)
    )

    sum_a = plane_step(sum_a, 1, last[1])
    sum_b = plane_step(plane_start([term_upsample, term_outer], half_width), 0, last[0])
    grad_inner_bias = jnp.sum(before_low.astype(jnp.float32), axis=0)
    middle_part, grad_second = second_norm_back(times_transposed(before_low, weight_inner))
    middle_grad = block_grad + middle_part
    middle_low = middle_grad.astype(jnp.bfloat16)
    mixed_grad = by_head(times_transposed(middle_low, weight_mixing).astype(jnp.bfloat16), VD)
    term_inner = chip_term(second_low, before_low)
    sum_a, sum_b, term_inner, mixed_grad, middle_low, middle_grad = tie_tree(
        (sum_a, sum_b, term_inner, mixed_grad, middle_low, middle_grad)
    )

    arrived_grad = exchange(mixed_grad)
    sum_b = plane_step(sum_b, 1, last[1])
    term_mixing = chip_term(mixed_low, middle_low)
    sum_b, term_mixing, arrived_grad = tie_tree((sum_b, term_mixing, arrived_grad))

    line_a, line_b = line_sum(sum_a), line_sum(sum_b)
    sum_c = plane_step(plane_start([term_inner, term_mixing], half_width), 0, last[0])
    query_own, own_side, other_side, bias_sums, relative_sum = attention_backward(
        info, rates, bias_gap, relative, mine, other, arrived_grad, mixed_wide, log_total, parts
    )
    line_a, line_b, sum_c, query_own, own_side, other_side = tie_tree(
        (line_a, line_b, sum_c, query_own, own_side, other_side)
    )

    own_side = own_side.astype(jnp.float32)
    for slot in range(1, parts):
        own_side = own_side + swap_part(other_side[slot - 1], slot).astype(jnp.float32)
    heads_grad = exchange(
        jnp.concatenate([query_own, own_side.astype(jnp.bfloat16)], axis=2)
    )
    sum_c = plane_step(sum_c, 1, last[1])
    r = shard_rows
    own_point, own_skip = to_owner(line_a, [r, r])
    own_upsample, own_outer = to_owner(line_b, [r, outer_weight.shape[0]])
    sum_c, heads_grad = tie_tree((sum_c, heads_grad))

    line_c = line_sum(sum_c)
    packed_grad = by_row(heads_grad)
    term_packed = chip_term(normed_low, packed_grad)
    normed_grad = times_transposed(packed_grad, weight_packed)
    input_part, grad_first = first_norm_back(normed_grad)
    input_grad = (middle_grad + input_part).astype(jnp.bfloat16).reshape(windows, rows, width)
    sum_d = plane_start([term_packed], half_wide)
    sum_d = plane_step(plane_step(sum_d, 0, False), 1, True)
    own_inner_low, own_inner_high, own_mixing = to_owner(line_c, [r, r, r])
    (own_packed,) = to_owner(line_sum(sum_d), [r])

    def joined_columns(pair):
        return jnp.concatenate(pair, axis=1)

    def at_head(value):
        full = jnp.zeros((H,) + value.shape, jnp.float32)
        return lax.dynamic_update_index_in_dim(full, value, head, 0)

    small_grads = scatter_small(
        [
            grad_first,
            at_head(bias_sums[0, :, 0]).reshape(-1),
            at_head(bias_sums[1, :, 0]).reshape(-1),
            at_head(relative_sum).reshape(H * KD, RPF),
            grad_second,
            grad_inner_bias,
            grad_outer_bias,
            grad_third,
            grad_skip_bias,
            grad_depth,
        ]
    )
    (
        own_first,
        own_content,
        own_position,
        own_relative,
        own_second,
        own_inner_bias,
        own_outer_bias,
        own_third,
        own_skip_bias,
        own_depth,
    ) = small_grads
    own_heads = joined_columns(own_packed).reshape(r, H, wide)
    own_point, own_skip, own_upsample, own_outer, own_mixing = map(
        joined_columns, (own_point, own_skip, own_upsample, own_outer, own_mixing)
    )
    own_inner = jnp.concatenate(
        [own_inner_low[0], own_inner_high[0], own_inner_low[1], own_inner_high[1]], axis=1
    )
    return (
        outputs,
        input_grad,
        skip_grad,
        own_first,
        own_heads[:, :, :KD].reshape(r, H * KD),
        own_heads[:, :, KD : 2 * KD].reshape(r, H * KD),
        own_heads[:, :, 2 * KD :].reshape(r, H * VD),
        own_content,
        own_position,
        own_relative,
        own_mixing,
        own_second,
        own_inner,
        own_inner_bias,
        own_outer,
        own_outer_bias,
        own_third,
        own_upsample,
        own_skip,
        own_skip_bias,
        own_depth,
        own_point,
    )


def solution(mesh):
    in_specs = (
        P("dp", "seq", None),
        P("dp", "seq", None),
        P("dp"),
        P("dp", "seq", None),
        P(("dp", "seq")),
        P(("dp", "seq"), None),
        P(("dp", "seq"), None),
        P(("dp", "seq"), None),
        P(("dp", "seq")),
        P(("dp", "seq")),
        P(("dp", "seq"), None),
        P(("dp", "seq"), None),
        P(("dp", "seq")),
        P(("dp", "seq"), None),
        P(("dp", "seq")),
        P(("dp", "seq"), None),
        P(("dp", "seq")),
        P(("dp", "seq")),
        P(("dp", "seq"), None),
        P(("dp", "seq"), None),
        P(("dp", "seq")),
        P(("dp", "seq"), None),
        P(("dp", "seq"), None),
    )
    out_specs = (
        P("dp", "seq", None),
        P("dp", "seq", None),
        P("dp", "seq", None),
        P(("dp", "seq")),
        P(("dp", "seq"), None),
        P(("dp", "seq"), None),
        P(("dp", "seq"), None),
        P(("dp", "seq")),
        P(("dp", "seq")),
        P(("dp", "seq"), None),
        P(("dp", "seq"), None),
        P(("dp", "seq")),
        P(("dp", "seq"), None),
        P(("dp", "seq")),
        P(("dp", "seq"), None),
        P(("dp", "seq")),
        P(("dp", "seq")),
        P(("dp", "seq"), None),
        P(("dp", "seq"), None),
        P(("dp", "seq")),
        P(("dp", "seq"), None),
        P(("dp", "seq"), None),
    )
    return jax.shard_map(
        on_device, mesh=mesh, in_specs=in_specs, out_specs=out_specs, check_vma=False
    )
```

```python
import functools
import math

import jax
import jax.numpy as jnp
from jax import lax
from jax.experimental import pallas as pl
from jax.experimental.pallas import tpu as pltpu
from jax.sharding import PartitionSpec as P

H = 8
KD = 64
VD = 192
RPF = 32
NEG = -1e30
BF = jnp.bfloat16
F32 = jnp.float32
epsilon = 1e-05


def extended_2(array, sides, width):
    for axis, dim in sides:
        peers, length = (lax.axis_size(axis), array.shape[dim])
        up = [(i, (i + 1) % peers) for i in range(peers - 1)]
        down = [(j, i) for i, j in up]
        last = lax.slice_in_dim(array, length - width, length, axis=dim)
        initial = lax.slice_in_dim(array, 0, width, axis=dim)
        before = lax.ppermute(last, axis, up)
        after = lax.ppermute(initial, axis, down)
        array = jnp.concatenate([before, array, after], axis=dim)
    return array


def layer_norm(values, gain):
    mean = jnp.mean(values, axis=-1, keepdims=True)
    centered = values - mean
    spread = jnp.mean(centered * centered, axis=-1, keepdims=True)
    return centered * lax.rsqrt(spread + epsilon) * gain


def smooth_gelu(values):
    return jax.nn.gelu(values, approximate=False)


def norm_gelu(values, gain):
    return smooth_gelu(layer_norm(values, gain))


def matmul(left, right):
    return jnp.dot(left, right, preferred_element_type=jnp.float32)


def times_transposed(left, right):
    return lax.dot_general(
        left, right, (((1,), (1,)), ((), ())), preferred_element_type=jnp.float32
    )


def transposed_times(left, right):
    return lax.dot_general(
        left, right, (((0,), (0,)), ((), ())), preferred_element_type=jnp.float32
    )


def depth_apply(extended, taps):
    return (
        extended[:, :-2] * taps[:, 0]
        + extended[:, 1:-1] * taps[:, 1]
        + extended[:, 2:] * taps[:, 2]
    )


def dot(a, b):
    return lax.dot_general(a, b, (((1,), (0,)), ((), ())), preferred_element_type=F32)


def dot32(a, b, dims=((1,), (0,))):
    return lax.dot_general(
        a, b, (dims, ((), ())), precision=lax.Precision.HIGHEST, preferred_element_type=F32
    )


def key_side(parts, part, rates, rows, groups, mine, other, store):
    half = RPF // 2
    spot = lax.broadcasted_iota(jnp.int32, (half, rows), 1).astype(F32)
    low = jnp.exp(-rates * (rows - 1 - spot)).astype(BF)
    high = jnp.exp(-rates * spot).astype(BF)
    pad = jnp.zeros((128 - KD - RPF, rows), BF)
    for slot in range(parts):
        theirs = lax.rem(part + slot, 2) if parts == 2 else slot_part(part, slot, parts)
        for g in range(groups):
            source = mine if slot == 0 else other
            if slot == 0:
                kt, vt = mine[g, 0, KD : 2 * KD, :], mine[g, 0, 2 * KD :, :]
            else:
                kt, vt = other[slot - 1, g, 0, :KD, :], other[slot - 1, g, 0, KD:, :]
            store(g * parts + theirs, jnp.concatenate([kt, low, high, pad], axis=0), vt)


def slot_part(part, slot, parts):
    out, bit = part, 1
    while bit < parts:
        if slot & bit:
            has = lax.rem(lax.div(part, bit), 2)
            out = out + bit - 2 * bit * has
        bit *= 2
    return out


def query_side(content, bias, relative, half):
    positional = content.astype(F32) + bias
    projected = dot32(relative, positional).astype(BF).astype(F32)
    return positional, projected[:half] + projected[half:], projected[:half] - projected[half:]


def block_query(content, plus, minus, rates, q_block, k_block, rows, kind):
    spot = lax.broadcasted_iota(jnp.int32, plus.shape, 1)
    query_pos = q_block * rows + spot
    zero = jnp.zeros(plus.shape, BF)
    below = above = zero
    if kind != "above":
        gap = (query_pos - (k_block * rows + rows - 1)).astype(F32)
        below = (plus * jnp.exp(jnp.minimum(-rates * gap, 60.0))).astype(BF)
    if kind != "below":
        gap = (k_block * rows - query_pos).astype(F32)
        above = (minus * jnp.exp(jnp.minimum(-rates * gap, 60.0))).astype(BF)
    rest = jnp.zeros((128 - KD - RPF, rows), BF)
    if kind == "below":
        return jnp.concatenate([content, below, zero, rest], axis=0)
    if kind == "above":
        return jnp.concatenate([content, zero, above, rest], axis=0)
    return (
        jnp.concatenate([content, below, zero, rest], axis=0),
        jnp.concatenate([content, zero, above, rest], axis=0),
    )


def signs(q_block, k_block, rows):
    i = q_block * rows + lax.broadcasted_iota(jnp.int32, (rows, rows), 1)
    j = k_block * rows + lax.broadcasted_iota(jnp.int32, (rows, rows), 0)
    return i, j


def block_scores(k_sc, content, plus, minus, rates, q_block, k_block, rows, kind, length):
    keys = k_sc[pl.ds(pl.multiple_of(k_block * rows, rows), rows), :]
    if kind != "both":
        return dot(keys, block_query(content, plus, minus, rates, q_block, k_block, rows, kind))
    below, above = block_query(content, plus, minus, rates, q_block, k_block, rows, kind)
    i, j = signs(q_block, k_block, rows)
    s_below, s_above = dot(keys, below), dot(keys, above)
    scores = jnp.where(i > j, s_below, jnp.where(i < j, s_above, 0.5 * (s_below + s_above)))
    return jnp.where(j < length, scores, NEG)


def visit_tiles(tile, q_block, length, rows, per, tiles):
    span = rows * per
    count = lax.div(length + span - 1, span)
    full = lax.div(length, span)
    own = lax.div(q_block, per)
    pl.loop(0, jnp.minimum(own, full))(functools.partial(tile, kind="below"))
    pl.loop(own + 1, full)(functools.partial(tile, kind="above"))

    @pl.loop(0, 2)
    def _(k):
        t = jnp.where(k == 0, own, full)
        go = (t < count) & ((k == 0) | (full != own))

        @pl.when(go)
        def _():
            tile(t, kind="both")


def forward_kernel(
    parts, per, info, rates_ref, bias_ref, rel_ref, mine, other, mixed, wide, lse, k_sc, v_sc, m_sc, l_sc, acc
):
    groups, rows = mine.shape[0], mine.shape[3]
    half = RPF // 2
    length = info[pl.program_id(0)]
    part = info[pl.num_programs(0)]
    rates = rates_ref[...]

    def store(block, kt, vt):
        spot = pl.multiple_of(block * rows, rows)
        k_sc[pl.ds(spot, rows), :] = kt.T
        v_sc[:, pl.ds(spot, rows)] = vt

    key_side(parts, part, rates, rows, groups, mine, other, store)

    @pl.loop(0, groups)
    def _(g):
        q_block = g * parts + part

        @pl.when(q_block * rows > length)
        def _():
            mixed[g, 0] = jnp.zeros(mixed.shape[2:], mixed.dtype)
            wide[g, 0] = jnp.zeros(wide.shape[2:], wide.dtype)
            lse[g, 0] = jnp.zeros(lse.shape[2:], lse.dtype)

        @pl.when(q_block * rows <= length)
        def _():
            content = mine[g, 0, :KD, :]
            _, plus, minus = query_side(content, bias_ref[...], rel_ref[...], half)
            m_sc[...] = jnp.full(m_sc.shape, NEG, F32)
            l_sc[...] = jnp.zeros(l_sc.shape, F32)
            acc[...] = jnp.zeros(acc.shape, F32)

            def tile(t, kind):
                scores = jnp.concatenate(
                    [
                        block_scores(
                            k_sc, content, plus, minus, rates, q_block, t * per + n, rows, kind, length
                        )
                        for n in range(per)
                    ],
                    axis=0,
                )
                old = m_sc[...]
                new = jnp.maximum(old, jnp.max(scores, axis=0, keepdims=True))
                alpha = jnp.exp(old - new)
                probs = jnp.exp(scores - new)
                m_sc[...] = new
                l_sc[...] = l_sc[...] * alpha + jnp.sum(probs, axis=0, keepdims=True)
                span = rows * per
                values = v_sc[:, pl.ds(pl.multiple_of(t * span, span), span)]
                acc[...] = acc[...] * alpha + dot(values, probs.astype(BF))

            visit_tiles(tile, q_block, length, rows, per, groups * parts // per)
            total = l_sc[...]
            out = acc[...] / total
            mixed[g, 0] = out.astype(BF)
            wide[g, 0] = out
            lse[g, 0] = jnp.broadcast_to(m_sc[...] + jnp.log(total), lse.shape[2:])


def backward_kernel(
    parts, per, info, rates_ref, bias_ref, rel_ref, mine, other, grad, wide, lse,
    dq, dkv_mine, dkv_other, sums, rel_grad,
    k_sc, kt_sc, v_sc, dk_sc, dv_sc, dq_sc, bias_sc,
):
    groups, rows = mine.shape[0], mine.shape[3]
    half = RPF // 2
    step = pl.program_id(0)
    length = info[step]
    part = info[pl.num_programs(0)]
    rates = rates_ref[...]
    scale = KD**-0.5

    def store(block, kt, vt):
        spot = pl.multiple_of(block * rows, rows)
        k_sc[pl.ds(spot, rows), :] = kt.T
        kt_sc[:, pl.ds(spot, rows)] = kt
        v_sc[pl.ds(spot, rows), :] = vt.T

    key_side(parts, part, rates, rows, groups, mine, other, store)
    dk_sc[...] = jnp.zeros(dk_sc.shape, F32)
    dv_sc[...] = jnp.zeros(dv_sc.shape, F32)

    @pl.when(step == 0)
    def _():
        bias_sc[...] = jnp.zeros(bias_sc.shape, F32)
        rel_grad[...] = jnp.zeros(rel_grad.shape, F32)

    @pl.loop(0, groups)
    def _(g):
        q_block = g * parts + part

        @pl.when(q_block * rows > length)
        def _():
            dq[g, 0] = jnp.zeros(dq.shape[2:], dq.dtype)

        @pl.when(q_block * rows <= length)
        def _():
            content = mine[g, 0, :KD, :]
            content_rows = content.T
            positional, plus, minus = query_side(content, bias_ref[...], rel_ref[...], half)
            grad_t = grad[g, 0]
            grad_rows = grad_t.T
            log_total = lse[g, 0, :1, :]
            row_sum = jnp.sum(grad_t.astype(F32) * wide[g, 0], axis=0, keepdims=True)
            dq_sc[...] = jnp.zeros(dq_sc.shape, F32)

            def tile(t, kind):
                span = rows * per
                spot = pl.multiple_of(t * span, span)
                scores = jnp.concatenate(
                    [
                        block_scores(
                            k_sc, content, plus, minus, rates, q_block, t * per + n, rows, kind, length
                        )
                        for n in range(per)
                    ],
                    axis=0,
                )
                exact = jnp.exp(scores - log_total)
                prob_grad = dot(v_sc[pl.ds(spot, span), :], grad_t)
                score_grad = exact * (prob_grad - row_sum)
                low = score_grad.astype(BF)
                dv_sc[pl.ds(spot, span), :] += dot(exact.astype(BF), grad_rows)
                dk_sc[pl.ds(spot, span), :] += dot(low, content_rows)
                for n in range(per):
                    k_block = t * per + n
                    piece = low[n * rows : (n + 1) * rows]
                    keys = kt_sc[:, pl.ds(pl.multiple_of(k_block * rows, rows), rows)]
                    place = q_block * rows + lax.broadcasted_iota(jnp.int32, (half, rows), 1)
                    down = -rates * (place - (k_block * rows + rows - 1)).astype(F32)
                    up = -rates * (k_block * rows - place).astype(F32)
                    if kind == "below":
                        part_sum = dot(keys[: KD + half], piece)
                        dq_sc[:KD] += part_sum[:KD]
                        dq_sc[KD : KD + half] += part_sum[KD:] * jnp.exp(down)
                    elif kind == "above":
                        part_sum = dot(keys[: KD + RPF], piece)
                        dq_sc[:KD] += part_sum[:KD]
                        dq_sc[KD + half :] += part_sum[KD + half :] * jnp.exp(up)
                    else:
                        i, j = signs(q_block, k_block, rows)
                        wide_piece = score_grad[n * rows : (n + 1) * rows]
                        equal = 0.5 * wide_piece
                        lower = jnp.where(i > j, wide_piece, jnp.where(i < j, 0.0, equal)).astype(BF)
                        upper = jnp.where(i < j, wide_piece, jnp.where(i > j, 0.0, equal)).astype(BF)
                        dq_sc[:KD] += dot(keys[:KD], piece)
                        dq_sc[KD : KD + half] += dot(keys[KD : KD + half], lower) * jnp.exp(
                            jnp.minimum(down, 60.0)
                        )
                        dq_sc[KD + half :] += dot(keys[KD + half : KD + RPF], upper) * jnp.exp(
                            jnp.minimum(up, 60.0)
                        )

            visit_tiles(tile, q_block, length, rows, per, groups * parts // per)
            content_grad = dq_sc[:KD]
            down, up = dq_sc[KD : KD + half], dq_sc[KD + half :]
            projected_grad = jnp.concatenate([down + up, down - up], axis=0)
            positional_grad = dot32(rel_ref[...], projected_grad, ((0,), (0,)))
            dq[g, 0] = (scale * (content_grad + positional_grad)).astype(BF)
            bias_sc[0] += content_grad
            bias_sc[1] += positional_grad
            rel_grad[...] += dot32(positional, projected_grad, ((1,), (1,)))

    for slot in range(parts):
        theirs = slot_part(part, slot, parts)
        for g in range(groups):
            spot = pl.multiple_of((g * parts + theirs) * rows, rows)
            dkt = dk_sc[pl.ds(spot, rows), :].astype(BF).T
            dvt = dv_sc[pl.ds(spot, rows), :].astype(BF).T
            both = jnp.concatenate([dkt, dvt], axis=0)
            if slot == 0:
                dkv_mine[g, 0] = both
            else:
                dkv_other[slot - 1, g, 0] = both

    @pl.when(step == pl.num_programs(0) - 1)
    def _():
        sums[...] = scale * jnp.sum(bias_sc[...], axis=-1, keepdims=True)


def attention_cost(windows, groups, rows, parts, wide):
    pairs = windows * groups * rows * groups * parts * rows
    return pl.CostEstimate(
        flops=int(pairs * 2 * wide * 0.75), bytes_accessed=20_000_000, transcendentals=int(pairs)
    )


def whole(*shape):
    return pl.BlockSpec(shape, lambda w: (0,) * len(shape))


def per_window(*shape):
    lead = len(shape) - 3
    return pl.BlockSpec(shape, lambda w: (0,) * lead + (w, 0, 0))


def tile_blocks(rows, groups, parts, target):
    per = max(1, target // rows)
    while (groups * parts) % per:
        per -= 1
    return per


def attention_forward(info, rates, bias, rel, mine, other, parts):
    groups, windows, _, rows = mine.shape
    per = tile_blocks(rows, groups, parts, 512)
    total = groups * parts * rows
    return pl.pallas_call(
        functools.partial(forward_kernel, parts, per),
        grid=(windows,),
        out_shape=(
            jax.ShapeDtypeStruct((groups, windows, VD, rows), BF),
            jax.ShapeDtypeStruct((groups, windows, VD, rows), F32),
            jax.ShapeDtypeStruct((groups, windows, 8, rows), F32),
        ),
        in_specs=[
            pl.BlockSpec(memory_space=pltpu.SMEM),
            whole(*rates.shape),
            whole(*bias.shape),
            whole(*rel.shape),
            per_window(groups, 1, 2 * KD + VD, rows),
            per_window(parts - 1, groups, 1, KD + VD, rows),
        ],
        out_specs=(
            per_window(groups, 1, VD, rows),
            per_window(groups, 1, VD, rows),
            per_window(groups, 1, 8, rows),
        ),
        scratch_shapes=[
            pltpu.VMEM((total, 128), BF),
            pltpu.VMEM((VD, total), BF),
            pltpu.VMEM((1, rows), F32),
            pltpu.VMEM((1, rows), F32),
            pltpu.VMEM((VD, rows), F32),
        ],
        compiler_params=pltpu.CompilerParams(vmem_limit_bytes=56 * 2**20),
        cost_estimate=attention_cost(windows, groups, rows, parts, 128 + 256),
        name="attention_forward",
    )(info, rates, bias, rel, mine, other)


def attention_backward(info, rates, bias, rel, mine, other, grad, wide, lse, parts):
    groups, windows, _, rows = mine.shape
    per = tile_blocks(rows, groups, parts, 512)
    total = groups * parts * rows
    return pl.pallas_call(
        functools.partial(backward_kernel, parts, per),
        grid=(windows,),
        out_shape=(
            jax.ShapeDtypeStruct((groups, windows, KD, rows), BF),
            jax.ShapeDtypeStruct((groups, windows, KD + VD, rows), BF),
            jax.ShapeDtypeStruct((parts - 1, groups, windows, KD + VD, rows), BF),
            jax.ShapeDtypeStruct((2, KD, 1), F32),
            jax.ShapeDtypeStruct((KD, RPF), F32),
        ),
        in_specs=[
            pl.BlockSpec(memory_space=pltpu.SMEM),
            whole(*rates.shape),
            whole(*bias.shape),
            whole(*rel.shape),
            per_window(groups, 1, 2 * KD + VD, rows),
            per_window(parts - 1, groups, 1, KD + VD, rows),
            per_window(groups, 1, VD, rows),
            per_window(groups, 1, VD, rows),
            per_window(groups, 1, 8, rows),
        ],
        out_specs=(
            per_window(groups, 1, KD, rows),
            per_window(groups, 1, KD + VD, rows),
            per_window(parts - 1, groups, 1, KD + VD, rows),
            whole(2, KD, 1),
            whole(KD, RPF),
        ),
        scratch_shapes=[
            pltpu.VMEM((total, 128), BF),
            pltpu.VMEM((128, total), BF),
            pltpu.VMEM((total, VD), BF),
            pltpu.VMEM((total, KD), F32),
            pltpu.VMEM((total, VD), F32),
            pltpu.VMEM((KD + RPF, rows), F32),
            pltpu.VMEM((2, KD, rows), F32),
        ],
        compiler_params=pltpu.CompilerParams(vmem_limit_bytes=56 * 2**20),
        cost_estimate=attention_cost(windows, groups, rows, parts, 3 * 256 + 2 * 256),
        name="attention_backward",
    )(info, rates, bias, rel, mine, other, grad, wide, lse)

MESH = pl.DeviceIdType.MESH


def links_kernel(pairs, counts, parts, *refs):
    n_in, n_out = counts
    refs_in, refs = refs[:n_in], refs[n_in:]
    if parts:
        blocks, refs = refs[0], refs[1:]
    refs_out, refs = refs[:n_out], refs[n_out:]
    if parts:
        mine, other = refs[:2]
        refs = refs[2:]
    local_sem, send_hi, recv_hi, send_y, recv_y, send_dp, recv_dp, send_c, recv_c = refs[:9]
    dp, seq = lax.axis_index("dp"), lax.axis_index("seq")
    ndp, nhi = refs_out[0].shape[:2]
    hi, low = lax.div(seq, 4), lax.rem(seq, 4)
    y, c = lax.div(low, 2), lax.rem(low, 2)

    def place(dp_to, hi_to, y_to, c_to):
        return (dp_to, hi_to * 4 + y_to * 2 + c_to)

    hi_peers = [place(dp, lax.rem(hi + k, nhi), y, c) for k in range(1, nhi)]
    y_peers = [place(dp, hi, 1 - y, c)]
    dp_peers = [place(lax.rem(dp + k, ndp), hi, y, c) for k in range(1, ndp)]
    c_peers = [place(dp, hi, y, 1 - c)]
    everyone = hi_peers + y_peers + dp_peers + c_peers
    if parts:
        head, part = lax.div(seq, parts), lax.rem(seq, parts)
        head_of = [lax.rem(head + k, H) for k in range(1, H)]
        head_peers = [(dp, h * parts + part) for h in head_of]
        part_peers = [(dp, head * parts + slot_part(part, k, parts)) for k in range(1, parts)]
        everyone = everyone + head_peers + part_peers

    barrier = pltpu.get_barrier_semaphore()
    for peer in everyone:
        pl.semaphore_signal(barrier, inc=1, device_id=peer, device_id_type=MESH)
    pl.semaphore_wait(barrier, len(everyone))

    def remote(source, target, ss, rs, peer):
        return pltpu.make_async_remote_copy(
            src_ref=source,
            dst_ref=target,
            send_sem=ss,
            recv_sem=rs,
            device_id=peer,
            device_id_type=MESH,
        )

    step_chunks, serial = [], 0
    for pair in pairs:
        step_chunks.append([])
        for side in (0, 1):
            for chunk in pair[side]:
                step_chunks[-1].append((serial, side) + chunk)
                serial += 1

    def copies(chunk, stage):
        n, side, shard, shard_first, array, first, columns = chunk
        cols = pl.ds(first, columns)
        out = refs_out[array]
        which = (("hi", "y", "dp", "c"), ("hi", "dp", "y", "c"))[side][stage]
        if which == "hi":
            target = out.at[dp, hi, y, c, :, cols]
            source = refs_in[shard].at[:, pl.ds(shard_first, columns)]
            peers, ss, rs = hi_peers, send_hi, recv_hi
        else:
            if which == "c":
                target = out.at[:, :, :, c, :, cols]
                peers, ss, rs = c_peers, send_c, recv_c
            elif which == "y":
                target = (
                    out.at[dp, :, y, c, :, cols] if stage == 1 else out.at[:, :, y, c, :, cols]
                )
                peers, ss, rs = y_peers, send_y, recv_y
            else:
                target = (
                    out.at[dp, :, y, c, :, cols] if stage == 1 else out.at[dp, :, :, c, :, cols]
                )
                peers, ss, rs = dp_peers, send_dp, recv_dp
            source = target
        return [remote(source, target, ss.at[n, k], rs.at[n, k], p) for k, p in enumerate(peers)]

    def own(chunk):
        n, _, shard, shard_first, array, first, columns = chunk
        return pltpu.make_async_copy(
            refs_in[shard].at[:, pl.ds(shard_first, columns)],
            refs_out[array].at[dp, hi, y, c, :, pl.ds(first, columns)],
            local_sem.at[n],
        )

    everything = [chunk for group in step_chunks for chunk in group]
    if parts:
        head_local, head_send, head_recv, part_send, part_recv = refs[9:]
        head_copies = [
            remote(blocks.at[:, h], mine.at[head], head_send.at[k], head_recv.at[k], p)
            for k, (h, p) in enumerate(zip(head_of, head_peers, strict=True))
        ]
        head_own = pltpu.make_async_copy(blocks.at[:, head], mine.at[head], head_local.at[0])
        keys = mine.at[:, :, pl.ds(KD, KD + VD)]
        part_copies = [
            remote(keys, other.at[k], part_send.at[k], part_recv.at[k], p)
            for k, p in enumerate(part_peers)
        ]
        head_own.start()
    else:
        head_copies = []
    ahead, lag = 3, 2
    share = -(-len(head_copies) // len(pairs))

    def launch(step):
        for copy in head_copies[step * share : (step + 1) * share]:
            copy.start()
        for chunk in step_chunks[step]:
            for copy in copies(chunk, 0):
                copy.start()

    for step in range(min(ahead, len(pairs))):
        launch(step)
    for chunk in everything:
        own(chunk).start()
    for chunk in everything:
        own(chunk).wait()
    for step in range(len(pairs) + 2 * lag):
        for stage in (3, 2, 1):
            spot = step - lag * (stage - 1)
            if 0 <= spot < len(pairs):
                for chunk in step_chunks[spot]:
                    for copy in copies(chunk, stage - 1):
                        copy.wait_recv()
                    for copy in copies(chunk, stage):
                        copy.start()
        if step + ahead < len(pairs):
            launch(step + ahead)
    if parts:
        head_own.wait()
        for copy in head_copies:
            copy.wait_recv()
        for copy in part_copies:
            copy.start()
    for chunk in everything:
        for copy in copies(chunk, 3):
            copy.wait_recv()
    if parts:
        for copy in part_copies:
            copy.wait_recv()
        for copy in head_copies + part_copies:
            copy.wait_send()
    for chunk in everything:
        for stage in range(4):
            for copy in copies(chunk, stage):
                copy.wait_send()


def use_links(name, collective, shards, arrays, pairs, blocks=None):
    ndp, nseq = lax.axis_size("dp"), lax.axis_size("seq")
    nhi, parts = nseq // 4, nseq // H if blocks is not None else 0
    chunks = sum(len(side) for pair in pairs for side in pair)
    out_shape = [jax.ShapeDtypeStruct((ndp, nhi, 2, 2) + shape, BF) for shape in arrays]
    operands = list(shards)
    sizes = [(chunks,)] + [
        (chunks, size) for size in (nhi - 1, nhi - 1, 1, 1, ndp - 1, ndp - 1, 1, 1)
    ]
    if parts:
        windows, _, wide, rows = blocks.shape
        operands.append(blocks)
        out_shape += [
            jax.ShapeDtypeStruct((H, windows, wide, rows), BF),
            jax.ShapeDtypeStruct((parts - 1, H, windows, KD + VD, rows), BF),
        ]
        sizes += [(1,), (H - 1,), (H - 1,), (parts - 1,), (parts - 1,)]
    outs = pl.pallas_call(
        functools.partial(links_kernel, pairs, (len(shards), len(arrays)), parts),
        out_shape=out_shape,
        in_specs=[pl.BlockSpec(memory_space=pl.ANY)] * len(operands),
        out_specs=[pl.BlockSpec(memory_space=pl.ANY)] * len(out_shape),
        scratch_shapes=[pltpu.SemaphoreType.DMA(size) for size in sizes],
        compiler_params=pltpu.CompilerParams(collective_id=collective, has_side_effects=True),
        name=name,
    )(*operands)
    flat = [out.reshape(-1, out.shape[-1]) for out in outs[: len(arrays)]]
    return flat + list(outs[len(arrays) :])


def tie(*values):
    return lax.optimization_barrier(values)


def project_kernel(values, gain, content_bias, w_query, w_key, w_value, normed, sent, scratch):
    windows, rows, _ = values.shape

    @pl.when(pl.program_id(0) == 0)
    def _():
        for w in range(windows):
            low = layer_norm(values[w].astype(F32), gain[...]).astype(BF)
            scratch[w * rows : (w + 1) * rows, :] = low
            normed[w * rows : (w + 1) * rows, :] = low

    low = scratch[...]
    content = ((dot(low, w_query[...]) + content_bias[0]) * (KD**-0.5)).astype(BF).T
    keys = dot(low, w_key[...]).astype(BF).T
    mixable = dot(low, w_value[...]).astype(BF).T
    for h in range(2):
        for w in range(windows):
            span = slice(w * rows, (w + 1) * rows)
            sent[w, h, :KD, :] = content[h * KD : (h + 1) * KD, span]
            sent[w, h, KD : 2 * KD, :] = keys[h * KD : (h + 1) * KD, span]
            sent[w, h, 2 * KD :, :] = mixable[h * VD : (h + 1) * VD, span]


def project(values, gain, content_bias, weight_keys, weight_values):
    windows, rows, width = values.shape
    steps = H // 2
    return pl.pallas_call(
        project_kernel,
        grid=(steps,),
        out_shape=(
            jax.ShapeDtypeStruct((windows * rows, width), BF),
            jax.ShapeDtypeStruct((windows, H, 2 * KD + VD, rows), BF),
        ),
        in_specs=[
            pl.BlockSpec((windows, rows, width), lambda i: (0, 0, 0)),
            pl.BlockSpec((1, width), lambda i: (0, 0)),
            pl.BlockSpec((1, 1, 2 * KD), lambda i: (i, 0, 0)),
            pl.BlockSpec((width, 2 * KD), lambda i: (0, i)),
            pl.BlockSpec((width, 2 * KD), lambda i: (0, i + steps)),
            pl.BlockSpec((width, 2 * VD), lambda i: (0, i)),
        ],
        out_specs=(
            pl.BlockSpec((windows * rows, width), lambda i: (0, 0)),
            pl.BlockSpec((windows, 2, 2 * KD + VD, rows), lambda i: (0, i, 0, 0)),
        ),
        scratch_shapes=[pltpu.VMEM((windows * rows, width), BF)],
        compiler_params=pltpu.CompilerParams(vmem_limit_bytes=48 * 2**20),
        name="project",
    )(
        values,
        gain.reshape(1, width),
        content_bias.reshape(steps, 1, 2 * KD),
        weight_keys,
        weight_keys,
        weight_values,
    )


def sums_kernel(plan, refs_spec, *refs):
    groups, n_terms, mode, parts, n_small, made_here = plan
    refs = list(refs)

    def take(count):
        out, refs[:count] = refs[:count], []
        return out

    terms = take(n_terms * (2 if made_here else 1))
    head_in = take({None: 0, "in": 1, "out": 3}[mode])
    small_in = take(1 if n_small else 0)
    outs = take(n_terms)
    head_out = take(1 if mode else 0)
    small_out = take(1 if n_small else 0)
    own, arrived, result, back, hop1, hop2, line = [], [], [], [], [], [], []
    flat = [(side, unit) for group in groups for side in (0, 1) for unit in group[side]]
    count = len(flat)
    own = take(count)
    arrived = take(count)
    hop1 = take(count)
    hop2 = take(count)
    line = take(count)
    result = take(count)
    back = take(count)
    if made_here:
        slots = min(2, n_terms)
        lefts, rights, turned = take(slots), take(slots), take(slots)
        going, left_sem, right_sem = take(3)
    load_sem, c_send, c_recv, s1, r1, s2, r2, s3, r3, s4, r4 = take(11)
    dp, seq = lax.axis_index("dp"), lax.axis_index("seq")
    ndp, nhi = own[0].shape[:2]
    nseq = nhi * 4
    hi, low = lax.div(seq, 4), lax.rem(seq, 4)
    y, c = lax.div(low, 2), lax.rem(low, 2)

    def place(dp_to, hi_to, y_to, c_to):
        return (dp_to, hi_to * 4 + y_to * 2 + c_to)

    hi_index = [lax.rem(hi + k, nhi) for k in range(1, nhi)]
    dp_index = [lax.rem(dp + k, ndp) for k in range(1, ndp)]
    hi_peers = [place(dp, h, y, c) for h in hi_index]
    dp_peers = [place(d, hi, y, c) for d in dp_index]
    y_peer, c_peer = place(dp, hi, 1 - y, c), place(dp, hi, y, 1 - c)
    everyone = hi_peers + dp_peers + [y_peer, c_peer]
    if mode:
        head, part = lax.div(seq, parts), lax.rem(seq, parts)
        head_of = [lax.rem(head + k, H) for k in range(1, H)]
        head_peers = [(dp, h * parts + part) for h in head_of]
        part_peers = [(dp, head * parts + slot_part(part, k, parts)) for k in range(1, parts)]
        everyone = everyone + head_peers + part_peers

    barrier = pltpu.get_barrier_semaphore()
    for peer in everyone:
        pl.semaphore_signal(barrier, inc=1, device_id=peer, device_id_type=MESH)
    expected = len(everyone)
    me = dp * nseq + seq
    if n_small:

        def other_device(k):
            there = lax.rem(me + k, n_small)
            return (lax.div(there, nseq), lax.rem(there, nseq))

        @pl.loop(1, n_small)
        def _(k):
            pl.semaphore_signal(barrier, inc=1, device_id=other_device(k), device_id_type=MESH)

        expected += n_small - 1
    pl.semaphore_wait(barrier, expected)

    def remote(source, target, ss, rs, peer):
        return pltpu.make_async_remote_copy(
            src_ref=source,
            dst_ref=target,
            send_sem=ss,
            recv_sem=rs,
            device_id=peer,
            device_id_type=MESH,
        )

    def half_of(array):
        return outs[array].shape[1] // 2

    def columns_of(unit, core):
        array, row, rows, column, columns = unit
        half = half_of(array)
        spot = pl.multiple_of(core * half + column, 128)
        return terms[array].at[:, :, :, :, pl.ds(row, rows), pl.ds(spot, columns)]

    def load(n):
        return pltpu.make_async_copy(columns_of(flat[n][1], c), own[n], load_sem.at[n])

    def over_core(n):
        source = going_of(n) if made_here else columns_of(flat[n][1], 1 - c)
        return [remote(source, arrived[n], c_send.at[n], c_recv.at[n], c_peer)]

    def first_hop(n):
        if flat[n][0] == 0:
            return [
                remote(own[n].at[d], hop1[n].at[k], s1.at[n, k], r1.at[n, k], p)
                for k, (d, p) in enumerate(zip(dp_index, dp_peers, strict=True))
            ]
        return [remote(own[n].at[:, :, 1 - y], hop1[n], s1.at[n, 0], r1.at[n, 0], y_peer)]

    def second_hop(n):
        if flat[n][0] == 0:
            return [remote(own[n].at[dp, :, 1 - y], hop2[n], s2.at[n, 0], r2.at[n, 0], y_peer)]
        return [
            remote(own[n].at[d, :, y], hop2[n].at[k], s2.at[n, k], r2.at[n, k], p)
            for k, (d, p) in enumerate(zip(dp_index, dp_peers, strict=True))
        ]

    def along_line(n):
        return [
            remote(own[n].at[dp, h, y], line[n].at[k], s3.at[n, k], r3.at[n, k], p)
            for k, (h, p) in enumerate(zip(hi_index, hi_peers, strict=True))
        ]

    def back_home(n):
        return [remote(result[n].at[1 - c], back[n], s4.at[n], r4.at[n], c_peer)]

    hops = (over_core, first_hop, second_hop, along_line, back_home)

    def add(a, b):
        return (a.astype(F32) + b.astype(F32)).astype(BF)

    def absorb(n, stage):
        mine = own[n]
        if stage == 1:

            @pl.loop(0, ndp * nhi)
            def _(k):
                d, h = lax.div(k, nhi), lax.rem(k, nhi)
                mine[d, h] = add(mine[d, h], arrived[n][d, h])

        elif stage == 2 and flat[n][0] == 0:

            @pl.loop(0, nhi)
            def _(h):
                total = mine[dp, h].astype(F32)
                for k in range(ndp - 1):
                    total = total + hop1[n][k, h].astype(F32)
                mine[dp, h] = total.astype(BF)

        elif stage == 2:

            @pl.loop(0, ndp * nhi)
            def _(k):
                d, h = lax.div(k, nhi), lax.rem(k, nhi)
                mine[d, h, y] = add(mine[d, h, y], hop1[n][d, h])

        elif stage == 3 and flat[n][0] == 0:

            @pl.loop(0, nhi)
            def _(h):
                mine[dp, h, y] = add(mine[dp, h, y], hop2[n][h])

        elif stage == 3:

            @pl.loop(0, nhi)
            def _(h):
                total = mine[dp, h, y].astype(F32)
                for k in range(ndp - 1):
                    total = total + hop2[n][k, h].astype(F32)
                mine[dp, h, y] = total.astype(BF)

        elif stage == 4:
            total = mine[dp, hi, y].astype(F32)
            for k in range(nhi - 1):
                total = total + line[n][k].astype(F32)
            result[n][...] = total
        else:
            array, row, rows, column, columns = flat[n][1]
            half = half_of(array)
            here, there = result[n][c], back[n][...]
            outs[array][row : row + rows, column : column + columns] = jnp.where(
                c == 0, here, there
            )
            outs[array][row : row + rows, half + column : half + column + columns] = jnp.where(
                c == 0, there, here
            )

    numbers, serial = [], 0
    for group in groups:
        size = len(group[0]) + len(group[1])
        numbers.append(range(serial, serial + size))
        serial += size

    def going_of(n):
        step = next(k for k, some in enumerate(numbers) if n in some)
        unit = flat[n][1]
        side = numbers[step].index(n)
        return going.at[step % 2, side, :, :, :, :, pl.ds(0, unit[2]), pl.ds(0, unit[4])]

    def fetch(array):
        left, right = terms[2 * array], terms[2 * array + 1]
        tokens, slot = left.shape[0], array % 2
        return [
            pltpu.make_async_copy(
                left,
                lefts[slot].at[pl.ds(0, tokens), pl.ds(0, left.shape[1])],
                left_sem.at[array],
            ),
            pltpu.make_async_copy(
                right,
                rights[slot].at[pl.ds(0, tokens), pl.ds(0, right.shape[1])],
                right_sem.at[array],
            ),
        ]

    def make(step):
        units = [flat[n][1] for n in numbers[step]]
        array, rows = units[0][0], units[0][2]
        first, size = units[0][3], sum(u[4] for u in units)
        left = terms[2 * array]
        tokens, slot = left.shape[0], array % 2
        if step == 0 or flat[numbers[step - 1][0]][1][0] != array:
            for copy in fetch(array):
                copy.wait()
            if array >= 1 and array + 1 < n_terms:
                for copy in fetch(array + 1):
                    copy.start()

            @pl.loop(0, left.shape[1] // 256)
            def _(k):
                spot = pl.multiple_of(k * 256, 256)
                turned[slot][pl.ds(spot, 256), pl.ds(0, tokens)] = lefts[slot][
                    pl.ds(0, tokens), pl.ds(spot, 256)
                ].T

        if step >= 2:
            for n in numbers[step - 2]:
                for copy in over_core(n):
                    copy.wait_send()
        span = nhi * 4 * rows
        for whose in (1 - c, c):
            spot = pl.multiple_of(whose * half_of(array) + first, 128)
            part_right = rights[slot][pl.ds(0, tokens), pl.ds(spot, size)]
            for d in range(ndp):
                made = dot(turned[slot][pl.ds(d * span, span), pl.ds(0, tokens)], part_right)
                made = made.astype(BF).reshape(nhi, 2, 2, rows, size)
                at = 0
                for k, n in enumerate(numbers[step]):
                    piece = made[..., at : at + units[k][4]]
                    if whose is c:
                        own[n][d] = piece
                    else:
                        going[step % 2, k, d, :, :, :, pl.ds(0, rows), pl.ds(0, units[k][4])] = piece
                    at += units[k][4]
            if whose is not c:
                for n in numbers[step]:
                    for copy in over_core(n):
                        copy.start()

    def launch(step):
        if made_here:
            make(step)
        else:
            for n in numbers[step]:
                load(n).start()
                for copy in over_core(n):
                    copy.start()

    if made_here:
        for array in range(min(2, n_terms)):
            for copy in fetch(array):
                copy.start()

    if mode == "in":
        head_send, head_recv, head_local = take(3)
        blocks, gathered = head_in[0], head_out[0]
        head_copies = [
            remote(blocks.at[:, h], gathered.at[head], head_send.at[k], head_recv.at[k], p)
            for k, (h, p) in enumerate(zip(head_of, head_peers, strict=True))
        ]
        head_own = [
            pltpu.make_async_copy(blocks.at[:, head], gathered.at[head], head_local.at[0])
        ]
        for copy in head_copies + head_own:
            copy.start()
    if mode == "out":
        head_send, head_recv, head_local, part_send, part_recv, mine_kv, arrived_kv = take(7)
        query, pair_mine, pair_other = head_in
        gathered = head_out[0]
        part_copies = [
            remote(pair_other.at[k], arrived_kv.at[k], part_send.at[k], part_recv.at[k], p)
            for k, p in enumerate(part_peers)
        ]
        kv_load = pltpu.make_async_copy(pair_mine, mine_kv, head_local.at[0])
        for copy in part_copies + [kv_load]:
            copy.start()
    if n_small:
        small_send, small_recv, small_sc = take(3)
        small = small_in[0]

        def small_copy(k):
            there = lax.rem(me + k, n_small)
            return remote(
                small.at[there],
                small_sc.at[k - 1],
                small_send.at[k - 1],
                small_recv.at[k - 1],
                other_device(k),
            )

        @pl.loop(1, n_small)
        def _(k):
            small_copy(k).start()

    ahead = 3
    for step in range(min(ahead, len(groups))):
        launch(step)
    if mode == "out":
        for copy in part_copies:
            copy.wait_recv()
        kv_load.wait()

        @pl.loop(0, H)
        def _(g):
            total = mine_kv[g].astype(F32)
            for k in range(parts - 1):
                total = total + arrived_kv[k, g].astype(F32)
            mine_kv[g] = total.astype(BF)

        q_target = gathered.at[head, :, pl.ds(0, KD)]
        kv_target = gathered.at[head, :, pl.ds(KD, KD + VD)]
        head_copies = [
            remote(source.at[h], target, head_send.at[i, k], head_recv.at[i, k], p)
            for k, (h, p) in enumerate(zip(head_of, head_peers, strict=True))
            for i, (source, target) in enumerate(((query, q_target), (mine_kv, kv_target)))
        ]
        head_own = [
            pltpu.make_async_copy(query.at[head], q_target, head_local.at[1]),
            pltpu.make_async_copy(mine_kv.at[head], kv_target, head_local.at[2]),
        ]
        for copy in head_copies + head_own:
            copy.start()
    lag = 2
    for step in range(len(groups) + 4 * lag):
        for stage in (5, 4, 3, 2, 1):
            spot = step - lag * (stage - 1)
            if 0 <= spot < len(groups):
                for n in numbers[spot]:
                    if stage == 1 and not made_here:
                        load(n).wait()
                    for copy in hops[stage - 1](n):
                        copy.wait_recv()
                    absorb(n, stage)
                    if stage < 5:
                        for copy in hops[stage](n):
                            copy.start()
        if step + ahead < len(groups):
            launch(step + ahead)
    if n_small:

        @pl.loop(1, n_small)
        def _(k):
            small_copy(k).wait_recv()

        small_out[0][...] = small[me] + jnp.sum(small_sc[...], axis=0)

        @pl.loop(1, n_small)
        def _(k):
            small_copy(k).wait_send()

    if mode:
        for copy in head_own:
            copy.wait()
        for copy in head_copies:
            copy.wait_recv()
        for copy in head_copies:
            copy.wait_send()
    if mode == "out":
        for copy in part_copies:
            copy.wait_send()
    for n in range(count):
        for hop in hops:
            if hop is not over_core or not made_here or n in tuple(numbers[-1]) + tuple(numbers[-2]):
                for copy in hop(n):
                    copy.wait_send()


def sum_terms(name, collective, pairs, groups, mode=None, heads=(), small=None):
    ndp, nseq = lax.axis_size("dp"), lax.axis_size("seq")
    nhi, parts, devices = nseq // 4, nseq // H, ndp * nseq
    shares = [(left.shape[1] // devices, right.shape[1]) for left, right in pairs]
    made_here = all(rows % 16 == 0 for rows, _ in shares)
    if made_here:
        operands = [x for pair in pairs for x in pair]
    else:
        operands = [
            transposed_times(left, right).astype(BF).reshape((ndp, nhi, 2, 2) + share)
            for (left, right), share in zip(pairs, shares, strict=True)
        ]
    in_specs = [pl.BlockSpec(memory_space=pl.ANY)] * len(operands)
    out_shape = [jax.ShapeDtypeStruct(share, F32) for share in shares]
    out_specs = [pl.BlockSpec(memory_space=pltpu.VMEM)] * len(out_shape)
    flat = [(side, unit) for group in groups for side in (0, 1) for unit in group[side]]
    count = len(flat)
    shapes = [(unit[2], unit[4]) for _, unit in flat]
    sides = [side for side, _ in flat]
    scratch = [pltpu.VMEM((ndp, nhi, 2, 2) + s, BF) for s in shapes] * 2
    scratch += [
        pltpu.VMEM(((ndp, nhi, 2) if side else (ndp - 1, nhi, 2, 2)) + s, BF)
        if not side
        else pltpu.VMEM((ndp, nhi, 2) + s, BF)
        for side, s in zip(sides, shapes, strict=True)
    ]
    scratch += [
        pltpu.VMEM((ndp - 1, nhi, 2) + s if side else (nhi, 2) + s, BF)
        for side, s in zip(sides, shapes, strict=True)
    ]
    scratch += [pltpu.VMEM((nhi - 1, 2) + s, BF) for s in shapes]
    scratch += [pltpu.VMEM((2,) + s, F32) for s in shapes]
    scratch += [pltpu.VMEM(s, F32) for s in shapes]
    if made_here:
        slots = [pairs[k::2] for k in range(min(2, len(pairs)))]
        tokens = [max(left.shape[0] for left, _ in slot) for slot in slots]
        tall = [max(left.shape[1] for left, _ in slot) for slot in slots]
        wide = [max(right.shape[1] for _, right in slot) for slot in slots]
        unit_rows = max(rows for rows, _ in shapes)
        unit_columns = max(columns for _, columns in shapes)
        scratch += [
            *[pltpu.VMEM(s, BF) for s in zip(tokens, tall, strict=True)],
            *[pltpu.VMEM(s, BF) for s in zip(tokens, wide, strict=True)],
            *[pltpu.VMEM(s, BF) for s in zip(tall, tokens, strict=True)],
            pltpu.VMEM((2, 2, ndp, nhi, 2, 2, unit_rows, unit_columns), BF),
            pltpu.SemaphoreType.DMA((len(pairs),)),
            pltpu.SemaphoreType.DMA((len(pairs),)),
        ]
    hop = max(ndp - 1, 1)
    sizes = [(count,)] * 3 + [(count, hop)] * 4 + [(count, nhi - 1)] * 2 + [(count,)] * 2
    scratch += [pltpu.SemaphoreType.DMA(size) for size in sizes]
    if mode == "in":
        windows, _, size, rows = heads[0].shape
        operands.append(heads[0])
        in_specs.append(pl.BlockSpec(memory_space=pl.ANY))
        out_shape.append(jax.ShapeDtypeStruct((H, windows, size, rows), BF))
        out_specs.append(pl.BlockSpec(memory_space=pl.ANY))
        scratch += [pltpu.SemaphoreType.DMA((n,)) for n in (H - 1, H - 1, 1)]
    if mode == "out":
        _, windows, _, rows = heads[0].shape
        operands += list(heads)
        in_specs += [pl.BlockSpec(memory_space=pl.ANY)] * 3
        out_shape.append(jax.ShapeDtypeStruct((H, windows, 2 * KD + VD, rows), BF))
        out_specs.append(pl.BlockSpec(memory_space=pl.ANY))
        scratch += [
            pltpu.SemaphoreType.DMA(size)
            for size in ((2, H - 1), (2, H - 1), (3,), (parts - 1,), (parts - 1,))
        ]
        scratch += [pltpu.VMEM(heads[1].shape, BF), pltpu.VMEM(heads[2].shape, BF)]
    n_small = 0
    if small is not None:
        n_small = devices
        operands.append(small)
        in_specs.append(pl.BlockSpec(memory_space=pltpu.VMEM))
        out_shape.append(jax.ShapeDtypeStruct(small.shape[1:], F32))
        out_specs.append(pl.BlockSpec(memory_space=pltpu.VMEM))
        scratch += [
            pltpu.SemaphoreType.DMA((devices - 1,)),
            pltpu.SemaphoreType.DMA((devices - 1,)),
            pltpu.VMEM((devices - 1,) + small.shape[1:], F32),
        ]
    plan = (groups, len(pairs), mode, parts, n_small, made_here)
    return pl.pallas_call(
        functools.partial(sums_kernel, plan, None),
        out_shape=out_shape,
        in_specs=in_specs,
        out_specs=out_specs,
        scratch_shapes=scratch,
        compiler_params=pltpu.CompilerParams(
            collective_id=collective, has_side_effects=True, vmem_limit_bytes=60 * 2**20
        ),
        name=name,
    )(*operands)


def halves(array, rows, columns, size=128):
    out, spot = [], 0
    while spot < columns:
        size = min(size, (columns - spot) // 2)
        out.append((((array, 0, rows, spot, size),), ((array, 0, rows, spot + size, size),)))
        spot += 2 * size
    return tuple(out)


def weight_pairs(width, hidden_width):
    third = width // 3

    def pieces(array, total, size):
        return [(array, k, array, k, size) for k in range(0, total, size)]

    first = pieces(0, width, third) + pieces(2, hidden_width, third) + pieces(4, width, third)
    second = pieces(1, width, third) + pieces(3, width, third // 2) + pieces(5, width, third)
    return tuple(((a,), (b,)) for a, b in zip(first, second, strict=True))


def on_device(
    inputs,
    skip_input,
    lengths,
    cotangent,
    first_gain,
    query_weight,
    key_weight,
    value_weight,
    content_bias,
    position_bias,
    relative_weight,
    mixing_weight,
    second_gain,
    inner_weight,
    inner_bias,
    outer_weight,
    outer_bias,
    third_gain,
    upsample_weight,
    skip_weight,
    skip_bias,
    depth_weight,
    point_weight,
):
    windows, rows, width = inputs.shape
    scale = float(KD) ** (-0.5)
    nseq, ndp = lax.axis_size("seq"), lax.axis_size("dp")
    devices = nseq * ndp
    parts = nseq // H
    keys_total = rows * nseq
    seq = lax.axis_index("seq")
    head, part = lax.div(seq, parts), lax.rem(seq, parts)
    first = seq * rows
    hidden_width = inner_weight.shape[1]

    r = shard_rows = query_weight.shape[0]
    vectors = (
        first_gain,
        content_bias,
        position_bias,
        second_gain,
        inner_bias,
        outer_bias,
        third_gain,
        skip_bias,
    )
    small_rows = [v.reshape(1, -1) for v in vectors] + [depth_weight.T]
    small_rows = [jnp.pad(v, ((0, 0), (0, 128 - v.shape[1]))) for v in small_rows]
    small_rows.append(jnp.zeros((16 - len(vectors) - 3, 128), BF))
    relative_rows = relative_weight.shape[0]
    small_rows.append(
        jnp.pad(relative_weight, ((0, -relative_rows % 16), (0, 128 - relative_weight.shape[1])))
    )
    small_shard = jnp.concatenate(small_rows, axis=0)
    keys_width, values_width = 2 * H * KD, H * VD
    half_hidden, half_width = hidden_width // 2, width // 2
    small_full, weight_keys, weight_values = use_links(
        "gather_heads",
        1,
        [small_shard, query_weight, key_weight, value_weight],
        [small_shard.shape, (r, keys_width), (r, values_width)],
        (
            (((0, 0, 0, 0, 128), (1, 0, 1, 0, 256)), ((2, 0, 1, 512, 256),)),
            (((1, 256, 1, 256, 256),), ((2, 256, 1, 768, 256),)),
            (((3, 0, 2, 0, 256),), ((3, 256, 2, 256, 256),)),
            (((3, 512, 2, 512, 256),), ((3, 768, 2, 768, 256),)),
            (((3, 1024, 2, 1024, 256),), ((3, 1280, 2, 1280, 256),)),
        ),
    )
    small_full = small_full.reshape((devices,) + small_shard.shape).astype(jnp.float32)

    def vector(k):
        return small_full[:, k, : vectors[k].shape[0]].reshape(-1)

    (
        gain_first,
        bias_content,
        bias_position,
        gain_second,
        bias_inner,
        bias_outer,
        gain_third,
        bias_skip,
    ) = map(vector, range(len(vectors)))
    taken = len(vectors)
    weight_depth = (
        small_full[:, taken : taken + 3, :r].transpose(0, 2, 1).reshape(width, 3)
    )
    weight_relative = small_full[:, 16 : 16 + relative_rows, :RPF].reshape(H * KD, RPF)

    lives = jnp.exp(
        jnp.linspace(math.log(3.0), math.log(keys_total), RPF // 2, dtype=jnp.float32)
    )
    rates = (math.log(2.0) / lives)[:, None]
    bias_gap = ((bias_position - bias_content) * scale).reshape(H, KD, 1)
    bias_gap = lax.dynamic_index_in_dim(bias_gap, head, 0, keepdims=False)
    relative = lax.dynamic_index_in_dim(
        weight_relative.reshape(H, KD, RPF), head, 0, keepdims=False
    ).T
    info = jnp.concatenate([lengths, part[None].astype(jnp.int32)])
    groups = [[p + parts * g for g in range(H)] for p in range(parts)]

    def exchange(array):
        return lax.all_to_all(array, "seq", 0, 0, axis_index_groups=groups, tiled=True)

    def swap_part(array, slot):
        return lax.ppermute(array, "seq", [(i, i ^ slot) for i in range(nseq)])

    flat = inputs.reshape(windows * rows, width).astype(jnp.float32)
    _, first_norm_back = jax.vjp(layer_norm, flat, gain_first)
    normed_low, sent = project(inputs, gain_first, bias_content, weight_keys, weight_values)
    (
        weight_skip,
        weight_mixing,
        weight_inner,
        weight_outer,
        weight_upsample,
        weight_point,
        mine,
        other,
    ) = use_links(
        "gather_weights",
        2,
        [skip_weight, mixing_weight, inner_weight, outer_weight, upsample_weight, point_weight],
        [
            (r, width),
            (r, width),
            (r, hidden_width),
            (outer_weight.shape[0], width),
            (r, width),
            (r, width),
        ],
        weight_pairs(width, hidden_width),
        sent,
    )

    def by_row(array):
        (array,) = tie(array.transpose(1, 3, 0, 2).reshape(windows * rows, -1))
        return array

    mixed_own, mixed_wide, log_total = attention_forward(
        info, rates, bias_gap, relative, mine, other, parts
    )
    mixed_low = by_row(exchange(mixed_own))
    middle = flat + matmul(mixed_low, weight_mixing)
    second, second_norm_back = jax.vjp(layer_norm, middle, gain_second)
    second_low = second.astype(jnp.bfloat16)
    before = matmul(second_low, weight_inner) + bias_inner
    hidden, gelu_back = jax.vjp(smooth_gelu, before)
    hidden_low = hidden.astype(jnp.bfloat16)
    block_out = middle + matmul(hidden_low, weight_outer) + bias_outer
    third, third_back = jax.vjp(norm_gelu, block_out, gain_third)
    third_low = third.astype(jnp.bfloat16)
    fine = jnp.arange(2 * rows, dtype=jnp.int32)[:, None] // 2
    twice = (fine == jnp.arange(rows, dtype=jnp.int32)[None, :]).astype(jnp.bfloat16)
    third_twice = (
        jnp.einsum(
            "ts,wsd->wtd",
            twice,
            third_low.reshape(windows, rows, width),
            preferred_element_type=jnp.float32,
        )
        .astype(jnp.bfloat16)
        .reshape(windows * 2 * rows, width)
    )
    skip_flat = skip_input.reshape(windows * 2 * rows, width)
    skip_part = matmul(skip_flat, weight_skip) + bias_skip
    joined_low = (
        (matmul(third_twice, weight_upsample) + skip_part)
        .astype(jnp.bfloat16)
        .reshape(windows, 2 * rows, width)
    )
    joined_rim = extended_2(joined_low, (("seq", 1),), 1)
    taps = weight_depth
    joined_wide = joined_rim.astype(jnp.float32)
    conv_low = depth_apply(joined_wide, taps).astype(jnp.bfloat16)
    conv_flat = conv_low.reshape(windows * 2 * rows, width)
    bins = 2 * first + jnp.arange(2 * rows, dtype=jnp.int32)
    keep = (bins // 2)[None, :] < lengths[:, None]
    keep_wide = keep.astype(jnp.float32)[:, :, None]
    outputs = (
        matmul(conv_flat, weight_point).reshape(windows, 2 * rows, width) * keep_wide
    ).astype(jnp.bfloat16)

    out_grad = (cotangent * keep.astype(jnp.bfloat16)[:, :, None]).reshape(
        windows * 2 * rows, width
    )
    conv_grad = (
        times_transposed(out_grad, weight_point)
        .astype(jnp.bfloat16)
        .reshape(windows, 2 * rows, width)
    )
    grad_rim = extended_2(conv_grad, (("seq", 1),), 1).astype(jnp.float32)
    joined_grad = (
        grad_rim[:, 2:] * taps[:, 0]
        + grad_rim[:, 1:-1] * taps[:, 1]
        + grad_rim[:, :-2] * taps[:, 2]
    )
    conv_wide = conv_grad.astype(jnp.float32)
    grad_depth = jnp.stack(
        [
            jnp.sum(conv_wide * joined_wide[:, :-2], axis=(0, 1)),
            jnp.sum(conv_wide * joined_wide[:, 1:-1], axis=(0, 1)),
            jnp.sum(conv_wide * joined_wide[:, 2:], axis=(0, 1)),
        ],
        axis=1,
    )
    grad_skip_bias = jnp.sum(joined_grad, axis=(0, 1))
    joined_back = joined_grad.astype(jnp.bfloat16)
    joined_flat = joined_back.reshape(windows * 2 * rows, width)
    lifted_grad = (
        jnp.einsum("ts,wtd->wsd", twice, joined_back, preferred_element_type=jnp.float32)
        .astype(jnp.bfloat16)
        .reshape(windows * rows, width)
    )
    third_grad = times_transposed(lifted_grad, weight_upsample)
    skip_grad = (
        times_transposed(joined_flat, weight_skip)
        .astype(jnp.bfloat16)
        .reshape(windows, 2 * rows, width)
    )
    block_grad, grad_third = third_back(third_grad)
    block_low = block_grad.astype(jnp.bfloat16)
    grad_outer_bias = jnp.sum(block_grad, axis=0)
    (before_grad,) = gelu_back(times_transposed(block_low, weight_outer))
    before_low = before_grad.astype(jnp.bfloat16)
    grad_inner_bias = jnp.sum(before_low.astype(jnp.float32), axis=0)
    middle_part, grad_second = second_norm_back(times_transposed(before_low, weight_inner))
    middle_grad = block_grad + middle_part
    middle_low = middle_grad.astype(jnp.bfloat16)
    middle_rows = middle_low.reshape(windows, rows, width)
    mixed_grad = (
        jnp.einsum("vd,wrd->wvr", weight_mixing, middle_rows, preferred_element_type=jnp.float32)
        .astype(jnp.bfloat16)
        .reshape(windows, H, VD, rows)
    )
    own_point, own_outer, own_skip, own_upsample, arrived_grad = sum_terms(
        "sum_upper",
        3,
        [
            (conv_flat, out_grad),
            (hidden_low, block_low),
            (skip_flat, joined_flat),
            (third_low, lifted_grad),
        ],
        halves(0, r, half_width)
        + halves(1, outer_weight.shape[0], half_width)
        + halves(2, r, half_width)
        + halves(3, r, half_width),
        "in",
        (mixed_grad,),
    )
    query_own, own_side, other_side, bias_sums, relative_sum = attention_backward(
        info, rates, bias_gap, relative, mine, other, arrived_grad, mixed_wide, log_total, parts
    )
    own_inner, own_mixing, heads_grad = sum_terms(
        "sum_lower",
        4,
        [(second_low, before_low), (mixed_low, middle_low)],
        halves(0, r, half_hidden) + halves(1, r, half_width),
        "out",
        (query_own, own_side, other_side),
    )
    packed_grad = jnp.concatenate(
        [
            by_row(heads_grad[:, :, :KD]),
            by_row(heads_grad[:, :, KD : 2 * KD]),
            by_row(heads_grad[:, :, 2 * KD :]),
        ],
        axis=1,
    )
    (packed_grad,) = tie(packed_grad)
    normed_grad = times_transposed(packed_grad[:, :keys_width], weight_keys) + times_transposed(
        packed_grad[:, keys_width:], weight_values
    )
    input_part, grad_first = first_norm_back(normed_grad)
    input_grad = (middle_grad + input_part).astype(jnp.bfloat16).reshape(windows, rows, width)

    def at_head(value):
        full = jnp.zeros((H,) + value.shape, jnp.float32)
        return lax.dynamic_update_index_in_dim(full, value, head, 0)

    pieces = [
        grad_first,
        at_head(bias_sums[0, :, 0]).reshape(-1),
        at_head(bias_sums[1, :, 0]).reshape(-1),
        at_head(relative_sum).reshape(H * KD, RPF),
        grad_second,
        grad_inner_bias,
        grad_outer_bias,
        grad_third,
        grad_skip_bias,
        grad_depth,
    ]
    packed = jnp.concatenate([p.reshape(devices, -1) for p in pieces], axis=1)
    packed = jnp.pad(packed, ((0, 0), (0, -packed.shape[1] % 1024))).reshape(devices, -1, 128)
    own_heads, small_total = sum_terms(
        "sum_heads",
        5,
        [(normed_low, packed_grad)],
        halves(0, r, packed_grad.shape[1] // 2),
        small=packed,
    )
    small_total, spot, small_grads = small_total.reshape(-1), 0, []
    for p in pieces:
        size = p.size // devices
        small_grads.append(
            small_total[spot : spot + size].reshape((p.shape[0] // devices,) + p.shape[1:])
        )
        spot += size
    (
        own_first,
        own_content,
        own_position,
        own_relative,
        own_second,
        own_inner_bias,
        own_outer_bias,
        own_third,
        own_skip_bias,
        own_depth,
    ) = small_grads
    return (
        outputs,
        input_grad,
        skip_grad,
        own_first,
        own_heads[:, : H * KD],
        own_heads[:, H * KD : keys_width],
        own_heads[:, keys_width:],
        own_content,
        own_position,
        own_relative,
        own_mixing,
        own_second,
        own_inner,
        own_inner_bias,
        own_outer,
        own_outer_bias,
        own_third,
        own_upsample,
        own_skip,
        own_skip_bias,
        own_depth,
        own_point,
    )


def solution(mesh):
    in_specs = (
        P("dp", "seq", None),
        P("dp", "seq", None),
        P("dp"),
        P("dp", "seq", None),
        P(("dp", "seq")),
        P(("dp", "seq"), None),
        P(("dp", "seq"), None),
        P(("dp", "seq"), None),
        P(("dp", "seq")),
        P(("dp", "seq")),
        P(("dp", "seq"), None),
        P(("dp", "seq"), None),
        P(("dp", "seq")),
        P(("dp", "seq"), None),
        P(("dp", "seq")),
        P(("dp", "seq"), None),
        P(("dp", "seq")),
        P(("dp", "seq")),
        P(("dp", "seq"), None),
        P(("dp", "seq"), None),
        P(("dp", "seq")),
        P(("dp", "seq"), None),
        P(("dp", "seq"), None),
    )
    out_specs = (
        P("dp", "seq", None),
        P("dp", "seq", None),
        P("dp", "seq", None),
        P(("dp", "seq")),
        P(("dp", "seq"), None),
        P(("dp", "seq"), None),
        P(("dp", "seq"), None),
        P(("dp", "seq")),
        P(("dp", "seq")),
        P(("dp", "seq"), None),
        P(("dp", "seq"), None),
        P(("dp", "seq")),
        P(("dp", "seq"), None),
        P(("dp", "seq")),
        P(("dp", "seq"), None),
        P(("dp", "seq")),
        P(("dp", "seq")),
        P(("dp", "seq"), None),
        P(("dp", "seq"), None),
        P(("dp", "seq")),
        P(("dp", "seq"), None),
        P(("dp", "seq"), None),
    )
    return jax.shard_map(
        on_device, mesh=mesh, in_specs=in_specs, out_specs=out_specs, check_vma=False
    )
```

```python
import functools
import math

import jax
import jax.numpy as jnp
from jax import lax
from jax.experimental import pallas as pl
from jax.experimental.pallas import tpu as pltpu
from jax.sharding import PartitionSpec as P

H = 8
KD = 64
VD = 192
RPF = 32
NEG = -1e30
BF = jnp.bfloat16
F32 = jnp.float32
epsilon = 1e-05


def extended_2(array, sides, width):
    for axis, dim in sides:
        peers, length = (lax.axis_size(axis), array.shape[dim])
        up = [(i, (i + 1) % peers) for i in range(peers - 1)]
        down = [(j, i) for i, j in up]
        last = lax.slice_in_dim(array, length - width, length, axis=dim)
        initial = lax.slice_in_dim(array, 0, width, axis=dim)
        before = lax.ppermute(last, axis, up)
        after = lax.ppermute(initial, axis, down)
        array = jnp.concatenate([before, array, after], axis=dim)
    return array


def layer_norm(values, gain):
    mean = jnp.mean(values, axis=-1, keepdims=True)
    centered = values - mean
    spread = jnp.mean(centered * centered, axis=-1, keepdims=True)
    return centered * lax.rsqrt(spread + epsilon) * gain


def smooth_gelu(values):
    return jax.nn.gelu(values, approximate=False)


def norm_gelu(values, gain):
    return smooth_gelu(layer_norm(values, gain))


def matmul(left, right):
    return jnp.dot(left, right, preferred_element_type=jnp.float32)


def times_transposed(left, right):
    return lax.dot_general(
        left, right, (((1,), (1,)), ((), ())), preferred_element_type=jnp.float32
    )


def transposed_times(left, right):
    return lax.dot_general(
        left, right, (((0,), (0,)), ((), ())), preferred_element_type=jnp.float32
    )


def depth_apply(extended, taps):
    return (
        extended[:, :-2] * taps[:, 0]
        + extended[:, 1:-1] * taps[:, 1]
        + extended[:, 2:] * taps[:, 2]
    )


def dot(a, b):
    return lax.dot_general(a, b, (((1,), (0,)), ((), ())), preferred_element_type=F32)


def dot32(a, b, dims=((1,), (0,))):
    return lax.dot_general(
        a, b, (dims, ((), ())), precision=lax.Precision.HIGHEST, preferred_element_type=F32
    )


def key_side(parts, part, groups, mine, other, store):
    for slot in range(parts):
        theirs = slot_part(part, slot, parts)
        for g in range(groups):
            if slot == 0:
                kt, vt = mine[g, 0, KD : 2 * KD, :], mine[g, 0, 2 * KD :, :]
            else:
                kt, vt = other[slot - 1, g, 0, :KD, :], other[slot - 1, g, 0, KD:, :]
            store(g * parts + theirs, kt, vt)


def slot_part(part, slot, parts):
    out, bit = part, 1
    while bit < parts:
        if slot & bit:
            has = lax.rem(lax.div(part, bit), 2)
            out = out + bit - 2 * bit * has
        bit *= 2
    return out


def query_side(content, bias, relative, half):
    positional = content.astype(F32) + bias
    projected = dot32(relative, positional).astype(BF).astype(F32)
    return positional, projected[:half] + projected[half:], projected[:half] - projected[half:]


def query_block(content, plus, minus, rates):
    spot = lax.broadcasted_iota(jnp.int32, plus.shape, 1).astype(F32)
    last = plus.shape[1] - 1
    from_first, to_last = jnp.exp(-rates * spot), jnp.exp(-rates * (last - spot))
    rest = jnp.zeros((128 - KD - RPF, content.shape[1]), BF)
    block = jnp.concatenate(
        [content, (plus * from_first).astype(BF), (minus * to_last).astype(BF), rest], axis=0
    )
    return block, from_first, to_last


def lane_rates(rates_row):
    lane = lax.broadcasted_iota(jnp.int32, (1, 128), 1)
    half = RPF // 2
    below = (lane >= KD) & (lane < KD + half)
    above = (lane >= KD + half) & (lane < KD + RPF)
    return rates_row, below, above


def decay_table(rates_row, span):
    rates_row, below, above = lane_rates(rates_row)
    spot = lax.broadcasted_iota(jnp.int32, (span, 128), 0).astype(F32)
    table = jnp.where(below, jnp.exp(-rates_row * (span - 1 - spot)), 0.0)
    return jnp.where(above, jnp.exp(-rates_row * spot), table)


def key_decays(table, rates_row, first_query, last_query, first_key, span, kind):
    rates_row, below, above = lane_rates(rates_row)
    if kind == "plain":
        before = first_key < first_query
        gap = jnp.where(before, first_query - (first_key + span - 1), first_key - last_query)
        used = (below & before) | (above & jnp.logical_not(before))
        return (table * jnp.where(used, jnp.exp(-rates_row * gap.astype(F32)), 0.0)).astype(BF)
    key = first_key + lax.broadcasted_iota(jnp.int32, (span, 128), 0)
    down = jnp.exp(jnp.minimum(-rates_row * (first_query - key).astype(F32), 60.0))
    up = jnp.exp(jnp.minimum(-rates_row * (key - last_query).astype(F32), 60.0))
    return jnp.where(below, down, 0.0).astype(BF), jnp.where(above, up, 0.0).astype(BF)


def order_of(first_query, first_key, span, rows):
    i = first_query + lax.broadcasted_iota(jnp.int32, (span, rows), 1)
    j = first_key + lax.broadcasted_iota(jnp.int32, (span, rows), 0)
    return i, j


def tile_scores(keys, decays, query, first_query, first_key, length, kind):
    if kind != "both":
        return dot(keys + decays, query)
    s_below, s_above = dot(keys + decays[0], query), dot(keys + decays[1], query)
    i, j = order_of(first_query, first_key, *s_below.shape)
    scores = jnp.where(i > j, s_below, jnp.where(i < j, s_above, 0.5 * (s_below + s_above)))
    return jnp.where(j < length, scores, NEG)


def visit_tiles(scores_into, use, slots, whole_tile, q_block, length, rows, per):
    span = rows * per
    count = lax.div(length + span - 1, span)
    full = lax.div(length, span)
    own = lax.div(q_block, per)
    plain = full - jnp.where(own < full, 1, 0)

    def tile_of(k):
        return k + jnp.where(k >= own, 1, 0)

    @pl.when(plain > 0)
    def _():
        scores_into(slots[0], tile_of(0), own)

    @pl.loop(0, lax.div(plain, 2))
    def _(k):
        first = 2 * k
        scores_into(slots[1], tile_of(first + 1), own)
        use(slots[0], tile_of(first), own)
        scores_into(slots[0], tile_of(jnp.minimum(first + 2, plain - 1)), own)
        use(slots[1], tile_of(first + 1), own)

    @pl.when(lax.rem(plain, 2) == 1)
    def _():
        use(slots[0], tile_of(plain - 1), own)

    @pl.loop(0, 2)
    def _(k):
        t = jnp.where(k == 0, own, full)
        go = (t < count) & ((k == 0) | (full != own))

        @pl.when(go)
        def _():
            whole_tile(t)


def forward_kernel(
    parts, per, info, rates_ref, lanes_ref, bias_ref, rel_ref, mine, other, mixed, wide, lse, k_sc, v_sc, table_sc, s0_sc, s1_sc, m_sc, l_sc, acc
):
    groups, rows = mine.shape[0], mine.shape[3]
    half = RPF // 2
    length = info[pl.program_id(0)]
    part = info[pl.num_programs(0)]
    rates = rates_ref[...]

    def store(block, kt, vt):
        spot = pl.multiple_of(block * rows, rows)
        k_sc[pl.ds(spot, rows), :] = jnp.concatenate([kt, jnp.zeros_like(kt)], axis=0).T
        v_sc[:, pl.ds(spot, rows)] = vt

    key_side(parts, part, groups, mine, other, store)
    span = rows * per
    table_sc[...] = decay_table(lanes_ref[...], span)

    @pl.loop(0, groups)
    def _(g):
        q_block = g * parts + part

        @pl.when(q_block * rows > length)
        def _():
            mixed[g, 0] = jnp.zeros(mixed.shape[2:], mixed.dtype)
            wide[g, 0] = jnp.zeros(wide.shape[2:], wide.dtype)
            lse[g, 0] = jnp.zeros(lse.shape[2:], lse.dtype)

        @pl.when(q_block * rows <= length)
        def _():
            content = mine[g, 0, :KD, :]
            _, plus, minus = query_side(content, bias_ref[...], rel_ref[...], half)
            query, _, _ = query_block(content, plus, minus, rates)
            first_query = q_block * rows
            m_sc[...] = jnp.full(m_sc.shape, NEG, F32)
            l_sc[...] = jnp.zeros(l_sc.shape, F32)
            acc[...] = jnp.zeros(acc.shape, F32)

            def scores_of(t, kind):
                first_key = pl.multiple_of(t * span, span)
                decays = key_decays(
                    table_sc[...], lanes_ref[...], first_query, first_query + rows - 1, first_key, span, kind
                )
                keys = k_sc[pl.ds(first_key, span), :]
                return tile_scores(keys, decays, query, first_query, first_key, length, kind)

            def scores_into(slot, t, own):
                slot[...] = scores_of(t, "plain")

            def use(slot, t, own):
                scores = slot[...]
                old = m_sc[...]
                new = jnp.maximum(old, jnp.max(scores, axis=0, keepdims=True))
                alpha = jnp.exp(old - new)
                probs = jnp.exp(scores - new)
                m_sc[...] = new
                l_sc[...] = l_sc[...] * alpha + jnp.sum(probs, axis=0, keepdims=True)
                values = v_sc[:, pl.ds(pl.multiple_of(t * span, span), span)]
                acc[...] = acc[...] * alpha + dot(values, probs.astype(BF))

            def whole_tile(t):
                s0_sc[...] = scores_of(t, "both")
                use(s0_sc, t, None)

            visit_tiles(scores_into, use, (s0_sc, s1_sc), whole_tile, q_block, length, rows, per)
            total = l_sc[...]
            out = acc[...] / total
            mixed[g, 0] = out.astype(BF)
            wide[g, 0] = out
            lse[g, 0] = jnp.broadcast_to(m_sc[...] + jnp.log(total), lse.shape[2:])


def backward_kernel(
    parts, per, info, rates_ref, lanes_ref, bias_ref, rel_ref, mine, other, grad, wide, lse,
    dq, dkv_mine, dkv_other, sums, rel_grad,
    k_sc, kt_sc, v_sc, table_sc, turned_sc, s0_sc, s1_sc, dk_sc, dv_sc, dq_sc, bias_sc,
):
    groups, rows = mine.shape[0], mine.shape[3]
    half = RPF // 2
    step = pl.program_id(0)
    length = info[step]
    part = info[pl.num_programs(0)]
    rates = rates_ref[...]
    scale = KD**-0.5

    def store(block, kt, vt):
        spot = pl.multiple_of(block * rows, rows)
        k_sc[pl.ds(spot, rows), :] = jnp.concatenate([kt, jnp.zeros_like(kt)], axis=0).T
        kt_sc[:, pl.ds(spot, rows)] = kt
        v_sc[pl.ds(spot, rows), :] = vt.T

    key_side(parts, part, groups, mine, other, store)
    span = rows * per
    table_sc[...] = decay_table(lanes_ref[...], span)
    turned_sc[...] = table_sc[...].T[KD : KD + RPF]
    dk_sc[...] = jnp.zeros(dk_sc.shape, F32)
    dv_sc[...] = jnp.zeros(dv_sc.shape, F32)

    @pl.when(step == 0)
    def _():
        bias_sc[...] = jnp.zeros(bias_sc.shape, F32)
        rel_grad[...] = jnp.zeros(rel_grad.shape, F32)

    @pl.loop(0, groups)
    def _(g):
        q_block = g * parts + part

        @pl.when(q_block * rows > length)
        def _():
            dq[g, 0] = jnp.zeros(dq.shape[2:], dq.dtype)

        @pl.when(q_block * rows <= length)
        def _():
            content = mine[g, 0, :KD, :]
            content_rows = content.T
            positional, plus, minus = query_side(content, bias_ref[...], rel_ref[...], half)
            query, from_first, to_last = query_block(content, plus, minus, rates)
            first_query = q_block * rows
            last_query = first_query + rows - 1
            grad_t = grad[g, 0]
            grad_rows = grad_t.T
            log_total = lse[g, 0, :1, :]
            row_sum = jnp.sum(grad_t.astype(F32) * wide[g, 0], axis=0, keepdims=True)
            dq_sc[...] = jnp.zeros(dq_sc.shape, F32)

            def decays_of(first_key, kind):
                return key_decays(
                    table_sc[...], lanes_ref[...], first_query, last_query, first_key, span, kind
                )

            def scores_of(t, decays, kind):
                first_key = pl.multiple_of(t * span, span)
                keys = k_sc[pl.ds(first_key, span), :]
                return tile_scores(keys, decays, query, first_query, first_key, length, kind)

            def scores_into(slot, t, own):
                first_key = pl.multiple_of(t * span, span)
                slot[0] = scores_of(t, decays_of(first_key, "plain"), "plain")
                slot[1] = dot(v_sc[pl.ds(first_key, span), :], grad_t)

            def use(slot, t, own):
                absorb(slot, t, "plain", None)

            def whole_tile(t):
                first_key = pl.multiple_of(t * span, span)
                decays = decays_of(first_key, "both")
                s0_sc[0] = scores_of(t, decays, "both")
                s0_sc[1] = dot(v_sc[pl.ds(first_key, span), :], grad_t)
                absorb(s0_sc, t, "both", decays)

            def absorb(slot, t, kind, decays):
                first_key = spot = pl.multiple_of(t * span, span)
                scores, prob_grad = slot[0], slot[1]
                exact = jnp.exp(scores - log_total)
                score_grad = exact * (prob_grad - row_sum)
                low = score_grad.astype(BF)
                dv_sc[pl.ds(spot, span), :] += dot(exact.astype(BF), grad_rows)
                dk_sc[pl.ds(spot, span), :] += dot(low, content_rows)
                keys_turned = kt_sc[:, pl.ds(spot, span)]
                if kind == "both":
                    i, j = order_of(first_query, first_key, span, rows)
                    equal = 0.5 * score_grad
                    lower = jnp.where(i > j, score_grad, jnp.where(i < j, 0.0, equal)).astype(BF)
                    upper = jnp.where(i < j, score_grad, jnp.where(i > j, 0.0, equal)).astype(BF)
                    dq_sc[:KD] += dot(keys_turned, low)
                    below, above = decays
                    dq_sc[KD : KD + half] += dot(below.T[KD : KD + half], lower)
                    dq_sc[KD + half : KD + RPF] += dot(above.T[KD + half : KD + RPF], upper)
                else:
                    before = first_key < first_query
                    gap = jnp.where(before, first_query - (first_key + span - 1), first_key - last_query)
                    faded = jnp.exp(-rates * gap.astype(F32))
                    down = turned_sc[:half] * jnp.where(before, faded, 0.0)
                    up = turned_sc[half:] * jnp.where(before, 0.0, faded)
                    pos = jnp.concatenate([down, up], axis=0).astype(BF)
                    dq_sc[...] += dot(jnp.concatenate([keys_turned, pos], axis=0), low)

            visit_tiles(scores_into, use, (s0_sc, s1_sc), whole_tile, q_block, length, rows, per)
            content_grad = dq_sc[:KD]
            down, up = dq_sc[KD : KD + half] * from_first, dq_sc[KD + half :] * to_last
            projected_grad = jnp.concatenate([down + up, down - up], axis=0)
            positional_grad = dot32(rel_ref[...], projected_grad, ((0,), (0,)))
            dq[g, 0] = (scale * (content_grad + positional_grad)).astype(BF)
            bias_sc[0] += content_grad
            bias_sc[1] += positional_grad
            rel_grad[...] += dot32(positional, projected_grad, ((1,), (1,)))

    for slot in range(parts):
        theirs = slot_part(part, slot, parts)
        for g in range(groups):
            spot = pl.multiple_of((g * parts + theirs) * rows, rows)
            dkt = dk_sc[pl.ds(spot, rows), :].astype(BF).T
            dvt = dv_sc[pl.ds(spot, rows), :].astype(BF).T
            both = jnp.concatenate([dkt, dvt], axis=0)
            if slot == 0:
                dkv_mine[g, 0] = both
            else:
                dkv_other[slot - 1, g, 0] = both

    @pl.when(step == pl.num_programs(0) - 1)
    def _():
        sums[...] = scale * jnp.sum(bias_sc[...], axis=-1, keepdims=True)


def attention_cost(windows, groups, rows, parts, wide):
    pairs = windows * groups * rows * groups * parts * rows
    return pl.CostEstimate(
        flops=int(pairs * 2 * wide * 0.75), bytes_accessed=20_000_000, transcendentals=int(pairs)
    )


def whole(*shape):
    return pl.BlockSpec(shape, lambda w: (0,) * len(shape))


def per_window(*shape):
    lead = len(shape) - 3
    return pl.BlockSpec(shape, lambda w: (0,) * lead + (w, 0, 0))


def tile_blocks(rows, groups, parts, target):
    per = max(1, target // rows)
    while (groups * parts) % per:
        per -= 1
    return per


def lanes_of(rates):
    line = rates.reshape(1, -1)
    return jnp.pad(jnp.concatenate([line, line], axis=1), ((0, 0), (KD, 128 - KD - RPF)))


def attention_forward(info, rates, bias, rel, mine, other, parts):
    groups, windows, _, rows = mine.shape
    per = tile_blocks(rows, groups, parts, 1024)
    total = groups * parts * rows
    return pl.pallas_call(
        functools.partial(forward_kernel, parts, per),
        grid=(windows,),
        out_shape=(
            jax.ShapeDtypeStruct((groups, windows, VD, rows), BF),
            jax.ShapeDtypeStruct((groups, windows, VD, rows), F32),
            jax.ShapeDtypeStruct((groups, windows, 8, rows), F32),
        ),
        in_specs=[
            pl.BlockSpec(memory_space=pltpu.SMEM),
            whole(*rates.shape),
            whole(1, 128),
            whole(*bias.shape),
            whole(*rel.shape),
            per_window(groups, 1, 2 * KD + VD, rows),
            per_window(parts - 1, groups, 1, KD + VD, rows),
        ],
        out_specs=(
            per_window(groups, 1, VD, rows),
            per_window(groups, 1, VD, rows),
            per_window(groups, 1, 8, rows),
        ),
        scratch_shapes=[
            pltpu.VMEM((total, 128), BF),
            pltpu.VMEM((VD, total), BF),
            pltpu.VMEM((rows * per, 128), F32),
            pltpu.VMEM((rows * per, rows), F32),
            pltpu.VMEM((rows * per, rows), F32),
            pltpu.VMEM((1, rows), F32),
            pltpu.VMEM((1, rows), F32),
            pltpu.VMEM((VD, rows), F32),
        ],
        compiler_params=pltpu.CompilerParams(vmem_limit_bytes=56 * 2**20),
        cost_estimate=attention_cost(windows, groups, rows, parts, 128 + 256),
        name="attention_forward",
    )(info, rates, lanes_of(rates), bias, rel, mine, other)


def attention_backward(info, rates, bias, rel, mine, other, grad, wide, lse, parts):
    groups, windows, _, rows = mine.shape
    per = tile_blocks(rows, groups, parts, 1024)
    total = groups * parts * rows
    return pl.pallas_call(
        functools.partial(backward_kernel, parts, per),
        grid=(windows,),
        out_shape=(
            jax.ShapeDtypeStruct((groups, windows, KD, rows), BF),
            jax.ShapeDtypeStruct((groups, windows, KD + VD, rows), BF),
            jax.ShapeDtypeStruct((parts - 1, groups, windows, KD + VD, rows), BF),
            jax.ShapeDtypeStruct((2, KD, 1), F32),
            jax.ShapeDtypeStruct((KD, RPF), F32),
        ),
        in_specs=[
            pl.BlockSpec(memory_space=pltpu.SMEM),
            whole(*rates.shape),
            whole(1, 128),
            whole(*bias.shape),
            whole(*rel.shape),
            per_window(groups, 1, 2 * KD + VD, rows),
            per_window(parts - 1, groups, 1, KD + VD, rows),
            per_window(groups, 1, VD, rows),
            per_window(groups, 1, VD, rows),
            per_window(groups, 1, 8, rows),
        ],
        out_specs=(
            per_window(groups, 1, KD, rows),
            per_window(groups, 1, KD + VD, rows),
            per_window(parts - 1, groups, 1, KD + VD, rows),
            whole(2, KD, 1),
            whole(KD, RPF),
        ),
        scratch_shapes=[
            pltpu.VMEM((total, 128), BF),
            pltpu.VMEM((KD, total), BF),
            pltpu.VMEM((total, VD), BF),
            pltpu.VMEM((rows * per, 128), F32),
            pltpu.VMEM((RPF, rows * per), F32),
            pltpu.VMEM((2, rows * per, rows), F32),
            pltpu.VMEM((2, rows * per, rows), F32),
            pltpu.VMEM((total, KD), F32),
            pltpu.VMEM((total, VD), F32),
            pltpu.VMEM((KD + RPF, rows), F32),
            pltpu.VMEM((2, KD, rows), F32),
        ],
        compiler_params=pltpu.CompilerParams(vmem_limit_bytes=56 * 2**20),
        cost_estimate=attention_cost(windows, groups, rows, parts, 3 * 256 + 2 * 256),
        name="attention_backward",
    )(info, rates, lanes_of(rates), bias, rel, mine, other, grad, wide, lse)

MESH = pl.DeviceIdType.MESH


def links_kernel(pairs, counts, parts, early, *refs):
    n_in, n_out = counts
    refs = list(refs)

    def take(count):
        out, refs[:count] = refs[:count], []
        return out

    refs_in = take(n_in)
    if early:
        values, spread_gain, pick_gain, spread_bias, pick_bias = take(5)
    elif parts:
        (blocks,) = take(1)
    refs_out = take(n_out)
    if parts:
        mine, other = take(2)
    if early:
        (normed,) = take(1)
    local_sem, send_hi, recv_hi, send_y, recv_y, send_dp, recv_dp, send_c, recv_c = take(9)
    dp, seq = lax.axis_index("dp"), lax.axis_index("seq")
    ndp, nhi = refs_out[0].shape[:2]
    hi, low = lax.div(seq, 4), lax.rem(seq, 4)
    y, c = lax.div(low, 2), lax.rem(low, 2)

    def place(dp_to, hi_to, y_to, c_to):
        return (dp_to, hi_to * 4 + y_to * 2 + c_to)

    hi_peers = [place(dp, lax.rem(hi + k, nhi), y, c) for k in range(1, nhi)]
    y_peers = [place(dp, hi, 1 - y, c)]
    dp_peers = [place(lax.rem(dp + k, ndp), hi, y, c) for k in range(1, ndp)]
    c_peers = [place(dp, hi, y, 1 - c)]
    everyone = hi_peers + y_peers + dp_peers + c_peers
    if parts:
        head, part = lax.div(seq, parts), lax.rem(seq, parts)
        head_of = [lax.rem(head + k, H) for k in range(1, H)]
        head_peers = [(dp, h * parts + part) for h in head_of]
        part_peers = [(dp, head * parts + slot_part(part, k, parts)) for k in range(1, parts)]
        everyone = everyone + head_peers + part_peers

    barrier = pltpu.get_barrier_semaphore()
    for peer in everyone:
        pl.semaphore_signal(barrier, inc=1, device_id=peer, device_id_type=MESH)
    pl.semaphore_wait(barrier, len(everyone))

    def remote(source, target, ss, rs, peer):
        return pltpu.make_async_remote_copy(
            src_ref=source,
            dst_ref=target,
            send_sem=ss,
            recv_sem=rs,
            device_id=peer,
            device_id_type=MESH,
        )

    step_chunks, serial = [], 0
    for pair in pairs:
        step_chunks.append([])
        for side in (0, 1):
            for chunk in pair[side]:
                step_chunks[-1].append((serial, side) + chunk)
                serial += 1

    def copies(chunk, stage):
        n, side, array, row, rows, first, columns = chunk
        out = refs_out[array]
        piece = (pl.ds(row, rows), pl.ds(first, columns))
        which = (("hi", "y", "dp", "c"), ("hi", "dp", "y", "c"))[side][stage]
        if which == "hi":
            target = out.at[(dp, hi, y, c) + piece]
            source = refs_in[array].at[piece]
            peers, ss, rs = hi_peers, send_hi, recv_hi
        else:
            every = slice(None)
            if which == "c":
                target = out.at[(every, every, every, c) + piece]
                peers, ss, rs = c_peers, send_c, recv_c
            elif which == "y":
                there = (dp, every, y, c) if stage == 1 else (every, every, y, c)
                target = out.at[there + piece]
                peers, ss, rs = y_peers, send_y, recv_y
            else:
                there = (dp, every, y, c) if stage == 1 else (dp, every, every, c)
                target = out.at[there + piece]
                peers, ss, rs = dp_peers, send_dp, recv_dp
            source = target
        return [remote(source, target, ss.at[n, k], rs.at[n, k], p) for k, p in enumerate(peers)]

    def own(array):
        return pltpu.make_async_copy(
            refs_in[array], refs_out[array].at[dp, hi, y, c], local_sem.at[array]
        )

    everything = [chunk for group in step_chunks for chunk in group]
    head_copies, head_own = [], None
    if parts:
        head_local, head_send, head_recv, part_send, part_recv = take(5)
        if early:
            blocks = take(1)[0]
        head_copies = [
            remote(blocks.at[:, h], mine.at[head], head_send.at[k], head_recv.at[k], p)
            for k, (h, p) in enumerate(zip(head_of, head_peers, strict=True))
        ]
        head_own = pltpu.make_async_copy(blocks.at[:, head], mine.at[head], head_local.at[0])
        keys = mine.at[:, :, pl.ds(KD, KD + VD)]
        part_copies = [
            remote(keys, other.at[k], part_send.at[k], part_recv.at[k], p)
            for k, p in enumerate(part_peers)
        ]
        if not early:
            head_own.start()
    if early:
        small_v, query_v, key_v, values_v, inputs_v, gain_v, bias_v, load_sem = take(8)
        inputs_load = pltpu.make_async_copy(values, inputs_v, load_sem.at[0])
        inputs_load.start()

    def make_blocks():
        loads = [
            pltpu.make_async_copy(source, target, load_sem.at[k + 1])
            for k, (source, target) in enumerate(
                zip(refs_out[:4], (small_v, query_v, key_v, values_v), strict=True)
            )
        ]
        for load in loads:
            load.start()
        inputs_load.wait()
        for load in loads:
            load.wait()

        @pl.loop(0, ndp * nhi * 4)
        def _(k):
            rows = small_v[
                lax.div(k, nhi * 4),
                lax.rem(lax.div(k, 4), nhi),
                lax.rem(lax.div(k, 2), 2),
                lax.rem(k, 2),
            ].astype(F32)
            gain_v[pl.ds(k, 1), :] = rows[0:1, :]
            bias_v[pl.ds(k, 1), :] = rows[1:2, :]

        def line_up(table, spread, pick):
            return jnp.sum(dot(table[...].astype(BF), spread[...]) * pick[...], axis=0, keepdims=True)

        gain = line_up(gain_v, spread_gain, pick_gain)
        bias = line_up(bias_v, spread_bias, pick_bias)
        windows, rows = inputs_v.shape[:2]
        for w in range(windows):
            normed[w * rows : (w + 1) * rows, :] = layer_norm(
                inputs_v[w].astype(F32), gain
            ).astype(BF)
        low = normed[...]
        width = low.shape[1]

        def weight(table, first, columns):
            return table[:, :, :, :, :, first : first + columns].reshape(width, columns)

        for pair in range(H // 2):
            spot, wide = pair * 2 * KD, pair * 2 * VD
            content = dot(low, weight(query_v, spot, 2 * KD)) + bias[:, spot : spot + 2 * KD]
            content = (content * (KD**-0.5)).astype(BF).T
            key = dot(low, weight(key_v, spot, 2 * KD)).astype(BF).T
            value = dot(low, weight(values_v, wide, 2 * VD)).astype(BF).T
            for h in range(2):
                for w in range(windows):
                    span = slice(w * rows, (w + 1) * rows)
                    blocks[w, 2 * pair + h, :KD, :] = content[h * KD : (h + 1) * KD, span]
                    blocks[w, 2 * pair + h, KD : 2 * KD, :] = key[h * KD : (h + 1) * KD, span]
                    blocks[w, 2 * pair + h, 2 * KD :, :] = value[h * VD : (h + 1) * VD, span]
        head_own.start()

    ahead, lag = 3, 2

    def launch(step):
        for chunk in step_chunks[step]:
            for copy in copies(chunk, 0):
                copy.start()

    events = {}
    for spot in range(len(pairs)):
        gap = 1 if spot < early else lag
        for stage in (3, 2, 1):
            events.setdefault(spot + gap * (stage - 1), []).append((stage, spot))
    made_at = early + 2 if early else 0
    heads_at = [made_at + k for k in range(len(head_copies))]
    for step in range(min(ahead, len(pairs))):
        launch(step)
    for array in range(n_out):
        own(array).start()
    for array in range(n_out):
        own(array).wait()
    for step in range(max(list(events) + heads_at) + 1):
        for stage, spot in sorted(events.get(step, []), reverse=True):
            for chunk in step_chunks[spot]:
                for copy in copies(chunk, stage - 1):
                    copy.wait_recv()
                for copy in copies(chunk, stage):
                    copy.start()
        if step + ahead < len(pairs):
            launch(step + ahead)
        if early and step == made_at:
            for group in step_chunks[:early]:
                for chunk in group:
                    for copy in copies(chunk, 3):
                        copy.wait_recv()
            make_blocks()
        if step in heads_at:
            head_copies[heads_at.index(step)].start()
    if parts:
        head_own.wait()
        for copy in head_copies:
            copy.wait_recv()
        for copy in part_copies:
            copy.start()
    for group in step_chunks[early:]:
        for chunk in group:
            for copy in copies(chunk, 3):
                copy.wait_recv()
    if parts:
        for copy in part_copies:
            copy.wait_recv()
        for copy in head_copies + part_copies:
            copy.wait_send()
    for chunk in everything:
        for stage in range(4):
            for copy in copies(chunk, stage):
                copy.wait_send()


def spread_tables(length, share):
    column = jnp.arange(length, dtype=jnp.int32)
    lane = jnp.arange(128, dtype=jnp.int32)
    device = jnp.arange(length // share, dtype=jnp.int32)
    spread = (column[None, :] % share == lane[:, None]).astype(BF)
    pick = (column[None, :] // share == device[:, None]).astype(F32)
    return spread, pick


def use_links(name, collective, shards, pairs, blocks=None, values=None, early=0):
    ndp, nseq = lax.axis_size("dp"), lax.axis_size("seq")
    nhi, devices = nseq // 4, ndp * nseq
    parts = nseq // H if blocks is not None or early else 0
    chunks = sum(len(side) for pair in pairs for side in pair)
    arrays = [shard.shape for shard in shards]
    out_shape = [jax.ShapeDtypeStruct((ndp, nhi, 2, 2) + shape, BF) for shape in arrays]
    operands = list(shards)
    in_specs = [pl.BlockSpec(memory_space=pl.ANY)] * len(operands)
    sizes = [(len(arrays),)] + [
        (chunks, size) for size in (nhi - 1, nhi - 1, 1, 1, ndp - 1, ndp - 1, 1, 1)
    ]
    scratch = []
    if early:
        windows, rows, width = values.shape
        operands += [values]
        operands += [
            *spread_tables(width, width // devices),
            *spread_tables(H * KD, H * KD // devices),
        ]
        in_specs += [pl.BlockSpec(memory_space=pl.ANY)] + [
            pl.BlockSpec(memory_space=pltpu.VMEM)
        ] * 4
        scratch = [
            pltpu.VMEM((windows, H, 2 * KD + VD, rows), BF),
            pltpu.VMEM(out_shape[0].shape, BF),
            pltpu.VMEM(out_shape[1].shape, BF),
            pltpu.VMEM(out_shape[2].shape, BF),
            pltpu.VMEM(out_shape[3].shape, BF),
            pltpu.VMEM(values.shape, BF),
            pltpu.VMEM((devices, 128), F32),
            pltpu.VMEM((devices, 128), F32),
            pltpu.SemaphoreType.DMA((5,)),
        ]
    elif parts:
        windows, _, _, rows = blocks.shape
        operands.append(blocks)
        in_specs.append(pl.BlockSpec(memory_space=pl.ANY))
    out_specs = [pl.BlockSpec(memory_space=pl.ANY)] * len(out_shape)
    if parts:
        out_shape += [
            jax.ShapeDtypeStruct((H, windows, 2 * KD + VD, rows), BF),
            jax.ShapeDtypeStruct((parts - 1, H, windows, KD + VD, rows), BF),
        ]
        out_specs += [pl.BlockSpec(memory_space=pl.ANY)] * 2
        sizes += [(1,), (H - 1,), (H - 1,), (parts - 1,), (parts - 1,)]
    if early:
        out_shape.append(jax.ShapeDtypeStruct((windows * rows, width), BF))
        out_specs.append(pl.BlockSpec(memory_space=pltpu.VMEM))
    outs = pl.pallas_call(
        functools.partial(links_kernel, pairs, (len(shards), len(arrays)), parts, early),
        out_shape=out_shape,
        in_specs=in_specs,
        out_specs=out_specs,
        scratch_shapes=[pltpu.SemaphoreType.DMA(size) for size in sizes] + scratch,
        compiler_params=pltpu.CompilerParams(
            collective_id=collective, has_side_effects=True, vmem_limit_bytes=60 * 2**20
        ),
        name=name,
    )(*operands)
    flat = [out.reshape(-1, out.shape[-1]) for out in outs[: len(arrays)]]
    return flat + list(outs[len(arrays) :])


def tie(*values):
    return lax.optimization_barrier(values)


def project_kernel(values, gain, content_bias, w_query, w_key, w_value, normed, sent, scratch):
    windows, rows, _ = values.shape

    @pl.when(pl.program_id(0) == 0)
    def _():
        for w in range(windows):
            low = layer_norm(values[w].astype(F32), gain[...]).astype(BF)
            scratch[w * rows : (w + 1) * rows, :] = low
            normed[w * rows : (w + 1) * rows, :] = low

    low = scratch[...]
    content = ((dot(low, w_query[...]) + content_bias[0]) * (KD**-0.5)).astype(BF).T
    keys = dot(low, w_key[...]).astype(BF).T
    mixable = dot(low, w_value[...]).astype(BF).T
    for h in range(2):
        for w in range(windows):
            span = slice(w * rows, (w + 1) * rows)
            sent[w, h, :KD, :] = content[h * KD : (h + 1) * KD, span]
            sent[w, h, KD : 2 * KD, :] = keys[h * KD : (h + 1) * KD, span]
            sent[w, h, 2 * KD :, :] = mixable[h * VD : (h + 1) * VD, span]


def project(values, gain, content_bias, weight_query, weight_key, weight_value):
    windows, rows, width = values.shape
    steps = H // 2
    return pl.pallas_call(
        project_kernel,
        grid=(steps,),
        out_shape=(
            jax.ShapeDtypeStruct((windows * rows, width), BF),
            jax.ShapeDtypeStruct((windows, H, 2 * KD + VD, rows), BF),
        ),
        in_specs=[
            pl.BlockSpec((windows, rows, width), lambda i: (0, 0, 0)),
            pl.BlockSpec((1, width), lambda i: (0, 0)),
            pl.BlockSpec((1, 1, 2 * KD), lambda i: (i, 0, 0)),
            pl.BlockSpec((width, 2 * KD), lambda i: (0, i)),
            pl.BlockSpec((width, 2 * KD), lambda i: (0, i)),
            pl.BlockSpec((width, 2 * VD), lambda i: (0, i)),
        ],
        out_specs=(
            pl.BlockSpec((windows * rows, width), lambda i: (0, 0)),
            pl.BlockSpec((windows, 2, 2 * KD + VD, rows), lambda i: (0, i, 0, 0)),
        ),
        scratch_shapes=[pltpu.VMEM((windows * rows, width), BF)],
        compiler_params=pltpu.CompilerParams(vmem_limit_bytes=48 * 2**20),
        name="project",
    )(
        values,
        gain.reshape(1, width),
        content_bias.reshape(steps, 1, 2 * KD),
        weight_query,
        weight_key,
        weight_value,
    )


def sums_kernel(plan, refs_spec, *refs):
    groups, n_terms, mode, parts, n_small, made_here = plan
    refs = list(refs)

    def take(count):
        out, refs[:count] = refs[:count], []
        return out

    terms = take(n_terms * (2 if made_here else 1))
    head_in = take({None: 0, "in": 1, "out": 3}[mode])
    small_in = take(1 if n_small else 0)
    outs = take(n_terms)
    head_out = take(1 if mode else 0)
    small_out = take(1 if n_small else 0)
    own, arrived, result, back, hop1, hop2, line = [], [], [], [], [], [], []
    flat = [(side, unit) for group in groups for side in (0, 1) for unit in group[side]]
    count = len(flat)
    own = take(count)
    arrived = take(count)
    hop1 = take(count)
    hop2 = take(count)
    line = take(count)
    result = take(count)
    back = take(count)
    if made_here:
        slots = min(2, n_terms)
        lefts, rights, turned = take(slots), take(slots), take(slots)
        going, left_sem, right_sem = take(3)
    load_sem, c_send, c_recv, s1, r1, s2, r2, s3, r3, s4, r4 = take(11)
    dp, seq = lax.axis_index("dp"), lax.axis_index("seq")
    ndp, nhi = own[0].shape[:2]
    nseq = nhi * 4
    hi, low = lax.div(seq, 4), lax.rem(seq, 4)
    y, c = lax.div(low, 2), lax.rem(low, 2)

    def place(dp_to, hi_to, y_to, c_to):
        return (dp_to, hi_to * 4 + y_to * 2 + c_to)

    hi_index = [lax.rem(hi + k, nhi) for k in range(1, nhi)]
    dp_index = [lax.rem(dp + k, ndp) for k in range(1, ndp)]
    hi_peers = [place(dp, h, y, c) for h in hi_index]
    dp_peers = [place(d, hi, y, c) for d in dp_index]
    y_peer, c_peer = place(dp, hi, 1 - y, c), place(dp, hi, y, 1 - c)
    everyone = hi_peers + dp_peers + [y_peer, c_peer]
    if mode:
        head, part = lax.div(seq, parts), lax.rem(seq, parts)
        head_of = [lax.rem(head + k, H) for k in range(1, H)]
        head_peers = [(dp, h * parts + part) for h in head_of]
        part_peers = [(dp, head * parts + slot_part(part, k, parts)) for k in range(1, parts)]
        everyone = everyone + head_peers + part_peers

    barrier = pltpu.get_barrier_semaphore()
    for peer in everyone:
        pl.semaphore_signal(barrier, inc=1, device_id=peer, device_id_type=MESH)
    expected = len(everyone)
    me = dp * nseq + seq
    if n_small:

        def other_device(k):
            there = lax.rem(me + k, n_small)
            return (lax.div(there, nseq), lax.rem(there, nseq))

        @pl.loop(1, n_small)
        def _(k):
            pl.semaphore_signal(barrier, inc=1, device_id=other_device(k), device_id_type=MESH)

        expected += n_small - 1
    pl.semaphore_wait(barrier, expected)

    def remote(source, target, ss, rs, peer):
        return pltpu.make_async_remote_copy(
            src_ref=source,
            dst_ref=target,
            send_sem=ss,
            recv_sem=rs,
            device_id=peer,
            device_id_type=MESH,
        )

    def half_of(array):
        return outs[array].shape[1] // 2

    def columns_of(unit, core):
        array, row, rows, column, columns = unit
        half = half_of(array)
        spot = pl.multiple_of(core * half + column, 128)
        return terms[array].at[:, :, :, :, pl.ds(row, rows), pl.ds(spot, columns)]

    def load(n):
        return pltpu.make_async_copy(columns_of(flat[n][1], c), own[n], load_sem.at[n])

    def over_core(n):
        source = going_of(n) if made_here else columns_of(flat[n][1], 1 - c)
        return [remote(source, arrived[n], c_send.at[n], c_recv.at[n], c_peer)]

    def first_hop(n):
        if flat[n][0] == 0:
            return [
                remote(own[n].at[d], hop1[n].at[k], s1.at[n, k], r1.at[n, k], p)
                for k, (d, p) in enumerate(zip(dp_index, dp_peers, strict=True))
            ]
        return [remote(own[n].at[:, :, 1 - y], hop1[n], s1.at[n, 0], r1.at[n, 0], y_peer)]

    def second_hop(n):
        if flat[n][0] == 0:
            return [remote(own[n].at[dp, :, 1 - y], hop2[n], s2.at[n, 0], r2.at[n, 0], y_peer)]
        return [
            remote(own[n].at[d, :, y], hop2[n].at[k], s2.at[n, k], r2.at[n, k], p)
            for k, (d, p) in enumerate(zip(dp_index, dp_peers, strict=True))
        ]

    def along_line(n):
        return [
            remote(own[n].at[dp, h, y], line[n].at[k], s3.at[n, k], r3.at[n, k], p)
            for k, (h, p) in enumerate(zip(hi_index, hi_peers, strict=True))
        ]

    def back_home(n):
        return [remote(result[n].at[1 - c], back[n], s4.at[n], r4.at[n], c_peer)]

    hops = (over_core, first_hop, second_hop, along_line, back_home)

    def add(a, b):
        return (a.astype(F32) + b.astype(F32)).astype(BF)

    def absorb(n, stage):
        mine = own[n]
        if stage == 1:

            @pl.loop(0, ndp * nhi)
            def _(k):
                d, h = lax.div(k, nhi), lax.rem(k, nhi)
                mine[d, h] = add(mine[d, h], arrived[n][d, h])

        elif stage == 2 and flat[n][0] == 0:

            @pl.loop(0, nhi)
            def _(h):
                total = mine[dp, h].astype(F32)
                for k in range(ndp - 1):
                    total = total + hop1[n][k, h].astype(F32)
                mine[dp, h] = total.astype(BF)

        elif stage == 2:

            @pl.loop(0, ndp * nhi)
            def _(k):
                d, h = lax.div(k, nhi), lax.rem(k, nhi)
                mine[d, h, y] = add(mine[d, h, y], hop1[n][d, h])

        elif stage == 3 and flat[n][0] == 0:

            @pl.loop(0, nhi)
            def _(h):
                mine[dp, h, y] = add(mine[dp, h, y], hop2[n][h])

        elif stage == 3:

            @pl.loop(0, nhi)
            def _(h):
                total = mine[dp, h, y].astype(F32)
                for k in range(ndp - 1):
                    total = total + hop2[n][k, h].astype(F32)
                mine[dp, h, y] = total.astype(BF)

        elif stage == 4:
            total = mine[dp, hi, y].astype(F32)
            for k in range(nhi - 1):
                total = total + line[n][k].astype(F32)
            result[n][...] = total
        else:
            array, row, rows, column, columns = flat[n][1]
            half = half_of(array)
            here, there = result[n][c], back[n][...]
            outs[array][row : row + rows, column : column + columns] = jnp.where(
                c == 0, here, there
            )
            outs[array][row : row + rows, half + column : half + column + columns] = jnp.where(
                c == 0, there, here
            )

    numbers, serial = [], 0
    for group in groups:
        size = len(group[0]) + len(group[1])
        numbers.append(range(serial, serial + size))
        serial += size

    def going_of(n):
        step = next(k for k, some in enumerate(numbers) if n in some)
        unit = flat[n][1]
        side = numbers[step].index(n)
        return going.at[step % 2, side, :, :, :, :, pl.ds(0, unit[2]), pl.ds(0, unit[4])]

    def fetch(array):
        left, right = terms[2 * array], terms[2 * array + 1]
        tokens, slot = left.shape[0], array % 2
        return [
            pltpu.make_async_copy(
                left,
                lefts[slot].at[pl.ds(0, tokens), pl.ds(0, left.shape[1])],
                left_sem.at[array],
            ),
            pltpu.make_async_copy(
                right,
                rights[slot].at[pl.ds(0, tokens), pl.ds(0, right.shape[1])],
                right_sem.at[array],
            ),
        ]

    def make(step):
        units = [flat[n][1] for n in numbers[step]]
        array, rows = units[0][0], units[0][2]
        first, size = units[0][3], sum(u[4] for u in units)
        left = terms[2 * array]
        tokens, slot = left.shape[0], array % 2
        if step == 0 or flat[numbers[step - 1][0]][1][0] != array:
            for copy in fetch(array):
                copy.wait()
            if array >= 1 and array + 1 < n_terms:
                for copy in fetch(array + 1):
                    copy.start()

            @pl.loop(0, left.shape[1] // 256)
            def _(k):
                spot = pl.multiple_of(k * 256, 256)
                turned[slot][pl.ds(spot, 256), pl.ds(0, tokens)] = lefts[slot][
                    pl.ds(0, tokens), pl.ds(spot, 256)
                ].T

        if step >= 2:
            for n in numbers[step - 2]:
                for copy in over_core(n):
                    copy.wait_send()
        span = nhi * 4 * rows
        for whose in (1 - c, c):
            spot = pl.multiple_of(whose * half_of(array) + first, 128)
            part_right = rights[slot][pl.ds(0, tokens), pl.ds(spot, size)]
            for d in range(ndp):
                made = dot(turned[slot][pl.ds(d * span, span), pl.ds(0, tokens)], part_right)
                made = made.astype(BF).reshape(nhi, 2, 2, rows, size)
                at = 0
                for k, n in enumerate(numbers[step]):
                    piece = made[..., at : at + units[k][4]]
                    if whose is c:
                        own[n][d] = piece
                    else:
                        going[step % 2, k, d, :, :, :, pl.ds(0, rows), pl.ds(0, units[k][4])] = piece
                    at += units[k][4]
            if whose is not c:
                for n in numbers[step]:
                    for copy in over_core(n):
                        copy.start()

    def launch(step):
        if made_here:
            make(step)
        else:
            for n in numbers[step]:
                load(n).start()
                for copy in over_core(n):
                    copy.start()

    if made_here:
        for array in range(min(2, n_terms)):
            for copy in fetch(array):
                copy.start()

    if mode == "in":
        head_send, head_recv, head_local = take(3)
        blocks, gathered = head_in[0], head_out[0]
        head_copies = [
            remote(blocks.at[:, h], gathered.at[head], head_send.at[k], head_recv.at[k], p)
            for k, (h, p) in enumerate(zip(head_of, head_peers, strict=True))
        ]
        head_own = [
            pltpu.make_async_copy(blocks.at[:, head], gathered.at[head], head_local.at[0])
        ]
        for copy in head_copies + head_own:
            copy.start()
    if mode == "out":
        head_send, head_recv, head_local, part_send, part_recv, mine_kv, arrived_kv = take(7)
        query, pair_mine, pair_other = head_in
        gathered = head_out[0]
        part_copies = [
            remote(pair_other.at[k], arrived_kv.at[k], part_send.at[k], part_recv.at[k], p)
            for k, p in enumerate(part_peers)
        ]
        kv_load = pltpu.make_async_copy(pair_mine, mine_kv, head_local.at[0])
        for copy in part_copies + [kv_load]:
            copy.start()
    if n_small:
        small_send, small_recv, small_sc = take(3)
        small = small_in[0]

        def small_copy(k):
            there = lax.rem(me + k, n_small)
            return remote(
                small.at[there],
                small_sc.at[k - 1],
                small_send.at[k - 1],
                small_recv.at[k - 1],
                other_device(k),
            )

        @pl.loop(1, n_small)
        def _(k):
            small_copy(k).start()

    ahead = 3
    for step in range(min(ahead, len(groups))):
        launch(step)
    if mode == "out":
        for copy in part_copies:
            copy.wait_recv()
        kv_load.wait()

        @pl.loop(0, H)
        def _(g):
            total = mine_kv[g].astype(F32)
            for k in range(parts - 1):
                total = total + arrived_kv[k, g].astype(F32)
            mine_kv[g] = total.astype(BF)

        q_target = gathered.at[head, :, pl.ds(0, KD)]
        kv_target = gathered.at[head, :, pl.ds(KD, KD + VD)]
        head_copies = [
            remote(source.at[h], target, head_send.at[i, k], head_recv.at[i, k], p)
            for k, (h, p) in enumerate(zip(head_of, head_peers, strict=True))
            for i, (source, target) in enumerate(((query, q_target), (mine_kv, kv_target)))
        ]
        head_own = [
            pltpu.make_async_copy(query.at[head], q_target, head_local.at[1]),
            pltpu.make_async_copy(mine_kv.at[head], kv_target, head_local.at[2]),
        ]
        for copy in head_copies + head_own:
            copy.start()
    lag = 2
    for step in range(len(groups) + 4 * lag):
        for stage in (5, 4, 3, 2, 1):
            spot = step - lag * (stage - 1)
            if 0 <= spot < len(groups):
                for n in numbers[spot]:
                    if stage == 1 and not made_here:
                        load(n).wait()
                    for copy in hops[stage - 1](n):
                        copy.wait_recv()
                    absorb(n, stage)
                    if stage < 5:
                        for copy in hops[stage](n):
                            copy.start()
        if step + ahead < len(groups):
            launch(step + ahead)
    if n_small:

        @pl.loop(1, n_small)
        def _(k):
            small_copy(k).wait_recv()

        small_out[0][...] = small[me] + jnp.sum(small_sc[...], axis=0)

        @pl.loop(1, n_small)
        def _(k):
            small_copy(k).wait_send()

    if mode:
        for copy in head_own:
            copy.wait()
        for copy in head_copies:
            copy.wait_recv()
        for copy in head_copies:
            copy.wait_send()
    if mode == "out":
        for copy in part_copies:
            copy.wait_send()
    for n in range(count):
        for hop in hops:
            if hop is not over_core or not made_here or n in tuple(numbers[-1]) + tuple(numbers[-2]):
                for copy in hop(n):
                    copy.wait_send()


def sum_terms(name, collective, pairs, groups, mode=None, heads=(), small=None):
    ndp, nseq = lax.axis_size("dp"), lax.axis_size("seq")
    nhi, parts, devices = nseq // 4, nseq // H, ndp * nseq
    shares = [(left.shape[1] // devices, right.shape[1]) for left, right in pairs]
    made_here = all(rows % 16 == 0 for rows, _ in shares)
    if made_here:
        operands = [x for pair in pairs for x in pair]
    else:
        operands = [
            transposed_times(left, right).astype(BF).reshape((ndp, nhi, 2, 2) + share)
            for (left, right), share in zip(pairs, shares, strict=True)
        ]
    in_specs = [pl.BlockSpec(memory_space=pl.ANY)] * len(operands)
    out_shape = [jax.ShapeDtypeStruct(share, F32) for share in shares]
    out_specs = [pl.BlockSpec(memory_space=pltpu.VMEM)] * len(out_shape)
    flat = [(side, unit) for group in groups for side in (0, 1) for unit in group[side]]
    count = len(flat)
    shapes = [(unit[2], unit[4]) for _, unit in flat]
    sides = [side for side, _ in flat]
    scratch = [pltpu.VMEM((ndp, nhi, 2, 2) + s, BF) for s in shapes] * 2
    scratch += [
        pltpu.VMEM(((ndp, nhi, 2) if side else (ndp - 1, nhi, 2, 2)) + s, BF)
        if not side
        else pltpu.VMEM((ndp, nhi, 2) + s, BF)
        for side, s in zip(sides, shapes, strict=True)
    ]
    scratch += [
        pltpu.VMEM((ndp - 1, nhi, 2) + s if side else (nhi, 2) + s, BF)
        for side, s in zip(sides, shapes, strict=True)
    ]
    scratch += [pltpu.VMEM((nhi - 1, 2) + s, BF) for s in shapes]
    scratch += [pltpu.VMEM((2,) + s, F32) for s in shapes]
    scratch += [pltpu.VMEM(s, F32) for s in shapes]
    if made_here:
        slots = [pairs[k::2] for k in range(min(2, len(pairs)))]
        tokens = [max(left.shape[0] for left, _ in slot) for slot in slots]
        tall = [max(left.shape[1] for left, _ in slot) for slot in slots]
        wide = [max(right.shape[1] for _, right in slot) for slot in slots]
        unit_rows = max(rows for rows, _ in shapes)
        unit_columns = max(columns for _, columns in shapes)
        scratch += [
            *[pltpu.VMEM(s, BF) for s in zip(tokens, tall, strict=True)],
            *[pltpu.VMEM(s, BF) for s in zip(tokens, wide, strict=True)],
            *[pltpu.VMEM(s, BF) for s in zip(tall, tokens, strict=True)],
            pltpu.VMEM((2, 2, ndp, nhi, 2, 2, unit_rows, unit_columns), BF),
            pltpu.SemaphoreType.DMA((len(pairs),)),
            pltpu.SemaphoreType.DMA((len(pairs),)),
        ]
    hop = max(ndp - 1, 1)
    sizes = [(count,)] * 3 + [(count, hop)] * 4 + [(count, nhi - 1)] * 2 + [(count,)] * 2
    scratch += [pltpu.SemaphoreType.DMA(size) for size in sizes]
    if mode == "in":
        windows, _, size, rows = heads[0].shape
        operands.append(heads[0])
        in_specs.append(pl.BlockSpec(memory_space=pl.ANY))
        out_shape.append(jax.ShapeDtypeStruct((H, windows, size, rows), BF))
        out_specs.append(pl.BlockSpec(memory_space=pl.ANY))
        scratch += [pltpu.SemaphoreType.DMA((n,)) for n in (H - 1, H - 1, 1)]
    if mode == "out":
        _, windows, _, rows = heads[0].shape
        operands += list(heads)
        in_specs += [pl.BlockSpec(memory_space=pl.ANY)] * 3
        out_shape.append(jax.ShapeDtypeStruct((H, windows, 2 * KD + VD, rows), BF))
        out_specs.append(pl.BlockSpec(memory_space=pl.ANY))
        scratch += [
            pltpu.SemaphoreType.DMA(size)
            for size in ((2, H - 1), (2, H - 1), (3,), (parts - 1,), (parts - 1,))
        ]
        scratch += [pltpu.VMEM(heads[1].shape, BF), pltpu.VMEM(heads[2].shape, BF)]
    n_small = 0
    if small is not None:
        n_small = devices
        operands.append(small)
        in_specs.append(pl.BlockSpec(memory_space=pltpu.VMEM))
        out_shape.append(jax.ShapeDtypeStruct(small.shape[1:], F32))
        out_specs.append(pl.BlockSpec(memory_space=pltpu.VMEM))
        scratch += [
            pltpu.SemaphoreType.DMA((devices - 1,)),
            pltpu.SemaphoreType.DMA((devices - 1,)),
            pltpu.VMEM((devices - 1,) + small.shape[1:], F32),
        ]
    plan = (groups, len(pairs), mode, parts, n_small, made_here)
    return pl.pallas_call(
        functools.partial(sums_kernel, plan, None),
        out_shape=out_shape,
        in_specs=in_specs,
        out_specs=out_specs,
        scratch_shapes=scratch,
        compiler_params=pltpu.CompilerParams(
            collective_id=collective, has_side_effects=True, vmem_limit_bytes=60 * 2**20
        ),
        name=name,
    )(*operands)


def halves(array, rows, columns, size=128):
    out, spot = [], 0
    while spot < columns:
        size = min(size, (columns - spot) // 2)
        out.append((((array, 0, rows, spot, size),), ((array, 0, rows, spot + size, size),)))
        spot += 2 * size
    return tuple(out)


def full(array, shards):
    rows, columns = shards[array].shape
    return (array, 0, rows, 0, columns)


def columns_of_rows(array, rows, first, columns):
    return (array, 0, rows, first, columns)


def weight_pairs(shapes, offset):
    def pieces(n, parts):
        rows, columns = shapes[n]
        if rows % (16 * parts):
            return [(offset + n, 0, rows, 0, columns)]
        size = rows // parts
        return [(offset + n, k * size, size, 0, columns) for k in range(parts)]

    first = pieces(0, 3) + pieces(2, 3) + pieces(4, 3) + pieces(5, 3)
    second = pieces(1, 3) + pieces(3, 6)
    steps = max(len(second), 1)
    spare = len(first) - steps
    pairs, spot = [], 0
    for k in range(steps):
        take = 2 if k >= steps - spare else 1
        pairs.append((tuple(first[spot : spot + take]), (second[k],)))
        spot += take
    if spot < len(first):
        pairs.append((tuple(first[spot:]), ()))
    return tuple(pairs)


def on_device(
    inputs,
    skip_input,
    lengths,
    cotangent,
    first_gain,
    query_weight,
    key_weight,
    value_weight,
    content_bias,
    position_bias,
    relative_weight,
    mixing_weight,
    second_gain,
    inner_weight,
    inner_bias,
    outer_weight,
    outer_bias,
    third_gain,
    upsample_weight,
    skip_weight,
    skip_bias,
    depth_weight,
    point_weight,
):
    windows, rows, width = inputs.shape
    scale = float(KD) ** (-0.5)
    nseq, ndp = lax.axis_size("seq"), lax.axis_size("dp")
    devices = nseq * ndp
    parts = nseq // H
    keys_total = rows * nseq
    seq = lax.axis_index("seq")
    head, part = lax.div(seq, parts), lax.rem(seq, parts)
    first = seq * rows
    hidden_width = inner_weight.shape[1]

    r = shard_rows = query_weight.shape[0]
    vectors = (
        first_gain,
        content_bias,
        position_bias,
        second_gain,
        inner_bias,
        outer_bias,
        third_gain,
        skip_bias,
    )
    small_rows = [v.reshape(1, -1) for v in vectors] + [depth_weight.T]
    small_rows = [jnp.pad(v, ((0, 0), (0, 128 - v.shape[1]))) for v in small_rows]
    small_rows.append(jnp.zeros((16 - len(vectors) - 3, 128), BF))
    relative_rows = relative_weight.shape[0]
    small_rows.append(
        jnp.pad(relative_weight, ((0, -relative_rows % 16), (0, 128 - relative_weight.shape[1])))
    )
    small_shard = jnp.concatenate(small_rows, axis=0)
    keys_width, values_width = 2 * H * KD, H * VD
    half_hidden, half_width = hidden_width // 2, width // 2
    head_shards = [small_shard, query_weight, key_weight, value_weight]
    head_pairs = (
        ((full(0, head_shards), full(1, head_shards)), (full(2, head_shards),)),
        ((columns_of_rows(3, r, 0, values_width // 2),), (columns_of_rows(3, r, values_width // 2, values_width // 2),)),
    )
    shards = [
        skip_weight,
        mixing_weight,
        inner_weight,
        outer_weight,
        upsample_weight,
        point_weight,
    ]
    if r % 16 == 0:
        (
            small_full,
            weight_query,
            weight_key,
            weight_value,
            weight_skip,
            weight_mixing,
            weight_inner,
            weight_outer,
            weight_upsample,
            weight_point,
            mine,
            other,
            normed_low,
        ) = use_links(
            "gather_weights",
            1,
            head_shards + shards,
            head_pairs + weight_pairs([w.shape for w in shards], len(head_shards)),
            values=inputs,
            early=len(head_pairs),
        )
    else:
        small_full, weight_query, weight_key, weight_value = use_links(
            "gather_heads", 1, head_shards, head_pairs
        )
    small_full = small_full.reshape((devices,) + small_shard.shape).astype(jnp.float32)

    def vector(k):
        return small_full[:, k, : vectors[k].shape[0]].reshape(-1)

    (
        gain_first,
        bias_content,
        bias_position,
        gain_second,
        bias_inner,
        bias_outer,
        gain_third,
        bias_skip,
    ) = map(vector, range(len(vectors)))
    taken = len(vectors)
    weight_depth = (
        small_full[:, taken : taken + 3, :r].transpose(0, 2, 1).reshape(width, 3)
    )
    weight_relative = small_full[:, 16 : 16 + relative_rows, :RPF].reshape(H * KD, RPF)

    lives = jnp.exp(
        jnp.linspace(math.log(3.0), math.log(keys_total), RPF // 2, dtype=jnp.float32)
    )
    rates = (math.log(2.0) / lives)[:, None]
    bias_gap = ((bias_position - bias_content) * scale).reshape(H, KD, 1)
    bias_gap = lax.dynamic_index_in_dim(bias_gap, head, 0, keepdims=False)
    relative = lax.dynamic_index_in_dim(
        weight_relative.reshape(H, KD, RPF), head, 0, keepdims=False
    ).T
    info = jnp.concatenate([lengths, part[None].astype(jnp.int32)])
    groups = [[p + parts * g for g in range(H)] for p in range(parts)]

    def exchange(array):
        return lax.all_to_all(array, "seq", 0, 0, axis_index_groups=groups, tiled=True)

    def swap_part(array, slot):
        return lax.ppermute(array, "seq", [(i, i ^ slot) for i in range(nseq)])

    flat = inputs.reshape(windows * rows, width).astype(jnp.float32)
    _, first_norm_back = jax.vjp(layer_norm, flat, gain_first)
    if r % 16:
        normed_low, sent = project(
            inputs, gain_first, bias_content, weight_query, weight_key, weight_value
        )
        (
            weight_skip,
            weight_mixing,
            weight_inner,
            weight_outer,
            weight_upsample,
            weight_point,
            mine,
            other,
        ) = use_links(
            "gather_weights", 2, shards, weight_pairs([w.shape for w in shards], 0), sent
        )

    def by_row(array):
        (array,) = tie(array.transpose(1, 3, 0, 2).reshape(windows * rows, -1))
        return array

    mixed_own, mixed_wide, log_total = attention_forward(
        info, rates, bias_gap, relative, mine, other, parts
    )
    mixed_low = by_row(exchange(mixed_own))
    middle = flat + matmul(mixed_low, weight_mixing)
    second, second_norm_back = jax.vjp(layer_norm, middle, gain_second)
    second_low = second.astype(jnp.bfloat16)
    before = matmul(second_low, weight_inner) + bias_inner
    hidden, gelu_back = jax.vjp(smooth_gelu, before)
    hidden_low = hidden.astype(jnp.bfloat16)
    block_out = middle + matmul(hidden_low, weight_outer) + bias_outer
    third, third_back = jax.vjp(norm_gelu, block_out, gain_third)
    third_low = third.astype(jnp.bfloat16)
    fine = jnp.arange(2 * rows, dtype=jnp.int32)[:, None] // 2
    twice = (fine == jnp.arange(rows, dtype=jnp.int32)[None, :]).astype(jnp.bfloat16)
    third_twice = (
        jnp.einsum(
            "ts,wsd->wtd",
            twice,
            third_low.reshape(windows, rows, width),
            preferred_element_type=jnp.float32,
        )
        .astype(jnp.bfloat16)
        .reshape(windows * 2 * rows, width)
    )
    skip_flat = skip_input.reshape(windows * 2 * rows, width)
    skip_part = matmul(skip_flat, weight_skip) + bias_skip
    joined_low = (
        (matmul(third_twice, weight_upsample) + skip_part)
        .astype(jnp.bfloat16)
        .reshape(windows, 2 * rows, width)
    )
    joined_rim = extended_2(joined_low, (("seq", 1),), 1)
    taps = weight_depth
    joined_wide = joined_rim.astype(jnp.float32)
    conv_low = depth_apply(joined_wide, taps).astype(jnp.bfloat16)
    conv_flat = conv_low.reshape(windows * 2 * rows, width)
    bins = 2 * first + jnp.arange(2 * rows, dtype=jnp.int32)
    keep = (bins // 2)[None, :] < lengths[:, None]
    keep_wide = keep.astype(jnp.float32)[:, :, None]
    outputs = (
        matmul(conv_flat, weight_point).reshape(windows, 2 * rows, width) * keep_wide
    ).astype(jnp.bfloat16)

    out_grad = (cotangent * keep.astype(jnp.bfloat16)[:, :, None]).reshape(
        windows * 2 * rows, width
    )
    conv_grad = (
        times_transposed(out_grad, weight_point)
        .astype(jnp.bfloat16)
        .reshape(windows, 2 * rows, width)
    )
    grad_rim = extended_2(conv_grad, (("seq", 1),), 1).astype(jnp.float32)
    joined_grad = (
        grad_rim[:, 2:] * taps[:, 0]
        + grad_rim[:, 1:-1] * taps[:, 1]
        + grad_rim[:, :-2] * taps[:, 2]
    )
    conv_wide = conv_grad.astype(jnp.float32)
    grad_depth = jnp.stack(
        [
            jnp.sum(conv_wide * joined_wide[:, :-2], axis=(0, 1)),
            jnp.sum(conv_wide * joined_wide[:, 1:-1], axis=(0, 1)),
            jnp.sum(conv_wide * joined_wide[:, 2:], axis=(0, 1)),
        ],
        axis=1,
    )
    grad_skip_bias = jnp.sum(joined_grad, axis=(0, 1))
    joined_back = joined_grad.astype(jnp.bfloat16)
    joined_flat = joined_back.reshape(windows * 2 * rows, width)
    lifted_grad = (
        jnp.einsum("ts,wtd->wsd", twice, joined_back, preferred_element_type=jnp.float32)
        .astype(jnp.bfloat16)
        .reshape(windows * rows, width)
    )
    third_grad = times_transposed(lifted_grad, weight_upsample)
    skip_grad = (
        times_transposed(joined_flat, weight_skip)
        .astype(jnp.bfloat16)
        .reshape(windows, 2 * rows, width)
    )
    block_grad, grad_third = third_back(third_grad)
    block_low = block_grad.astype(jnp.bfloat16)
    grad_outer_bias = jnp.sum(block_grad, axis=0)
    (before_grad,) = gelu_back(times_transposed(block_low, weight_outer))
    before_low = before_grad.astype(jnp.bfloat16)
    grad_inner_bias = jnp.sum(before_low.astype(jnp.float32), axis=0)
    middle_part, grad_second = second_norm_back(times_transposed(before_low, weight_inner))
    middle_grad = block_grad + middle_part
    middle_low = middle_grad.astype(jnp.bfloat16)
    middle_rows = middle_low.reshape(windows, rows, width)
    mixed_grad = (
        jnp.einsum("vd,wrd->wvr", weight_mixing, middle_rows, preferred_element_type=jnp.float32)
        .astype(jnp.bfloat16)
        .reshape(windows, H, VD, rows)
    )
    own_point, own_outer, own_skip, own_upsample, arrived_grad = sum_terms(
        "sum_upper",
        3,
        [
            (conv_flat, out_grad),
            (hidden_low, block_low),
            (skip_flat, joined_flat),
            (third_low, lifted_grad),
        ],
        halves(0, r, half_width)
        + halves(1, outer_weight.shape[0], half_width)
        + halves(2, r, half_width)
        + halves(3, r, half_width),
        "in",
        (mixed_grad,),
    )
    query_own, own_side, other_side, bias_sums, relative_sum = attention_backward(
        info, rates, bias_gap, relative, mine, other, arrived_grad, mixed_wide, log_total, parts
    )
    own_inner, own_mixing, heads_grad = sum_terms(
        "sum_lower",
        4,
        [(second_low, before_low), (mixed_low, middle_low)],
        halves(0, r, half_hidden) + halves(1, r, half_width),
        "out",
        (query_own, own_side, other_side),
    )
    packed_grad = jnp.concatenate(
        [
            by_row(heads_grad[:, :, :KD]),
            by_row(heads_grad[:, :, KD : 2 * KD]),
            by_row(heads_grad[:, :, 2 * KD :]),
        ],
        axis=1,
    )
    (packed_grad,) = tie(packed_grad)
    normed_grad = (
        times_transposed(packed_grad[:, : H * KD], weight_query)
        + times_transposed(packed_grad[:, H * KD : keys_width], weight_key)
        + times_transposed(packed_grad[:, keys_width:], weight_value)
    )
    input_part, grad_first = first_norm_back(normed_grad)
    input_grad = (middle_grad + input_part).astype(jnp.bfloat16).reshape(windows, rows, width)

    def at_head(value):
        full = jnp.zeros((H,) + value.shape, jnp.float32)
        return lax.dynamic_update_index_in_dim(full, value, head, 0)

    pieces = [
        grad_first,
        at_head(bias_sums[0, :, 0]).reshape(-1),
        at_head(bias_sums[1, :, 0]).reshape(-1),
        at_head(relative_sum).reshape(H * KD, RPF),
        grad_second,
        grad_inner_bias,
        grad_outer_bias,
        grad_third,
        grad_skip_bias,
        grad_depth,
    ]
    packed = jnp.concatenate([p.reshape(devices, -1) for p in pieces], axis=1)
    packed = jnp.pad(packed, ((0, 0), (0, -packed.shape[1] % 1024))).reshape(devices, -1, 128)
    own_heads, small_total = sum_terms(
        "sum_heads",
        5,
        [(normed_low, packed_grad)],
        halves(0, r, packed_grad.shape[1] // 2),
        small=packed,
    )
    small_total, spot, small_grads = small_total.reshape(-1), 0, []
    for p in pieces:
        size = p.size // devices
        small_grads.append(
            small_total[spot : spot + size].reshape((p.shape[0] // devices,) + p.shape[1:])
        )
        spot += size
    (
        own_first,
        own_content,
        own_position,
        own_relative,
        own_second,
        own_inner_bias,
        own_outer_bias,
        own_third,
        own_skip_bias,
        own_depth,
    ) = small_grads
    return (
        outputs,
        input_grad,
        skip_grad,
        own_first,
        own_heads[:, : H * KD],
        own_heads[:, H * KD : keys_width],
        own_heads[:, keys_width:],
        own_content,
        own_position,
        own_relative,
        own_mixing,
        own_second,
        own_inner,
        own_inner_bias,
        own_outer,
        own_outer_bias,
        own_third,
        own_upsample,
        own_skip,
        own_skip_bias,
        own_depth,
        own_point,
    )


def solution(mesh):
    in_specs = (
        P("dp", "seq", None),
        P("dp", "seq", None),
        P("dp"),
        P("dp", "seq", None),
        P(("dp", "seq")),
        P(("dp", "seq"), None),
        P(("dp", "seq"), None),
        P(("dp", "seq"), None),
        P(("dp", "seq")),
        P(("dp", "seq")),
        P(("dp", "seq"), None),
        P(("dp", "seq"), None),
        P(("dp", "seq")),
        P(("dp", "seq"), None),
        P(("dp", "seq")),
        P(("dp", "seq"), None),
        P(("dp", "seq")),
        P(("dp", "seq")),
        P(("dp", "seq"), None),
        P(("dp", "seq"), None),
        P(("dp", "seq")),
        P(("dp", "seq"), None),
        P(("dp", "seq"), None),
    )
    out_specs = (
        P("dp", "seq", None),
        P("dp", "seq", None),
        P("dp", "seq", None),
        P(("dp", "seq")),
        P(("dp", "seq"), None),
        P(("dp", "seq"), None),
        P(("dp", "seq"), None),
        P(("dp", "seq")),
        P(("dp", "seq")),
        P(("dp", "seq"), None),
        P(("dp", "seq"), None),
        P(("dp", "seq")),
        P(("dp", "seq"), None),
        P(("dp", "seq")),
        P(("dp", "seq"), None),
        P(("dp", "seq")),
        P(("dp", "seq")),
        P(("dp", "seq"), None),
        P(("dp", "seq"), None),
        P(("dp", "seq")),
        P(("dp", "seq"), None),
        P(("dp", "seq"), None),
    )
    return jax.shard_map(
        on_device, mesh=mesh, in_specs=in_specs, out_specs=out_specs, check_vma=False
    )
```

```python
import functools
import math

import jax
import jax.numpy as jnp
from jax import lax
from jax.experimental import pallas as pl
from jax.experimental.pallas import tpu as pltpu
from jax.sharding import PartitionSpec as P

H = 8
KD = 64
VD = 192
RPF = 32
NEG = -1e30
BF = jnp.bfloat16
F32 = jnp.float32
epsilon = 1e-05


def extended_2(array, sides, width):
    for axis, dim in sides:
        peers, length = (lax.axis_size(axis), array.shape[dim])
        up = [(i, (i + 1) % peers) for i in range(peers - 1)]
        down = [(j, i) for i, j in up]
        last = lax.slice_in_dim(array, length - width, length, axis=dim)
        initial = lax.slice_in_dim(array, 0, width, axis=dim)
        before = lax.ppermute(last, axis, up)
        after = lax.ppermute(initial, axis, down)
        array = jnp.concatenate([before, array, after], axis=dim)
    return array


def layer_norm(values, gain):
    mean = jnp.mean(values, axis=-1, keepdims=True)
    centered = values - mean
    spread = jnp.mean(centered * centered, axis=-1, keepdims=True)
    return centered * lax.rsqrt(spread + epsilon) * gain


def smooth_gelu(values):
    return jax.nn.gelu(values, approximate=False)


def norm_gelu(values, gain):
    return smooth_gelu(layer_norm(values, gain))


def matmul(left, right):
    return jnp.dot(left, right, preferred_element_type=jnp.float32)


def times_transposed(left, right):
    return lax.dot_general(
        left, right, (((1,), (1,)), ((), ())), preferred_element_type=jnp.float32
    )


def transposed_times(left, right):
    return lax.dot_general(
        left, right, (((0,), (0,)), ((), ())), preferred_element_type=jnp.float32
    )


def depth_apply(extended, taps):
    return (
        extended[:, :-2] * taps[:, 0]
        + extended[:, 1:-1] * taps[:, 1]
        + extended[:, 2:] * taps[:, 2]
    )


def dot(a, b):
    return lax.dot_general(a, b, (((1,), (0,)), ((), ())), preferred_element_type=F32)


def dot32(a, b, dims=((1,), (0,))):
    return lax.dot_general(
        a, b, (dims, ((), ())), precision=lax.Precision.HIGHEST, preferred_element_type=F32
    )


def key_side(parts, part, groups, mine, other, store):
    for slot in range(parts):
        theirs = slot_part(part, slot, parts)
        for g in range(groups):
            if slot == 0:
                kt, vt = mine[g, 0, KD : 2 * KD, :], mine[g, 0, 2 * KD :, :]
            else:
                kt, vt = other[slot - 1, g, 0, :KD, :], other[slot - 1, g, 0, KD:, :]
            store(g * parts + theirs, kt, vt)


def slot_part(part, slot, parts):
    out, bit = part, 1
    while bit < parts:
        if slot & bit:
            has = lax.rem(lax.div(part, bit), 2)
            out = out + bit - 2 * bit * has
        bit *= 2
    return out


def query_side(content, bias, relative, half):
    positional = content.astype(F32) + bias
    projected = dot32(relative, positional).astype(BF).astype(F32)
    return positional, projected[:half] + projected[half:], projected[:half] - projected[half:]


def query_block(content, plus, minus, rates):
    spot = lax.broadcasted_iota(jnp.int32, plus.shape, 1).astype(F32)
    last = plus.shape[1] - 1
    from_first, to_last = jnp.exp(-rates * spot), jnp.exp(-rates * (last - spot))
    rest = jnp.zeros((128 - KD - RPF, content.shape[1]), BF)
    block = jnp.concatenate(
        [content, (plus * from_first).astype(BF), (minus * to_last).astype(BF), rest], axis=0
    )
    return block, from_first, to_last


def lane_rates(rates_row):
    lane = lax.broadcasted_iota(jnp.int32, (1, 128), 1)
    half = RPF // 2
    below = (lane >= KD) & (lane < KD + half)
    above = (lane >= KD + half) & (lane < KD + RPF)
    return rates_row, below, above


def decay_table(rates_row, span):
    rates_row, below, above = lane_rates(rates_row)
    spot = lax.broadcasted_iota(jnp.int32, (span, 128), 0).astype(F32)
    table = jnp.where(below, jnp.exp(-rates_row * (span - 1 - spot)), 0.0)
    return jnp.where(above, jnp.exp(-rates_row * spot), table)


def key_decays(table, rates_row, first_query, last_query, first_key, span, kind):
    rates_row, below, above = lane_rates(rates_row)
    if kind == "plain":
        before = first_key < first_query
        gap = jnp.where(before, first_query - (first_key + span - 1), first_key - last_query)
        used = (below & before) | (above & jnp.logical_not(before))
        return (table * jnp.where(used, jnp.exp(-rates_row * gap.astype(F32)), 0.0)).astype(BF)
    key = first_key + lax.broadcasted_iota(jnp.int32, (span, 128), 0)
    down = jnp.exp(jnp.minimum(-rates_row * (first_query - key).astype(F32), 60.0))
    up = jnp.exp(jnp.minimum(-rates_row * (key - last_query).astype(F32), 60.0))
    return jnp.where(below, down, 0.0).astype(BF), jnp.where(above, up, 0.0).astype(BF)


def order_of(first_query, first_key, span, rows):
    i = first_query + lax.broadcasted_iota(jnp.int32, (span, rows), 1)
    j = first_key + lax.broadcasted_iota(jnp.int32, (span, rows), 0)
    return i, j


def tile_scores(keys, decays, query, first_query, first_key, length, kind):
    if kind != "both":
        return dot(keys + decays, query)
    s_below, s_above = dot(keys + decays[0], query), dot(keys + decays[1], query)
    i, j = order_of(first_query, first_key, *s_below.shape)
    scores = jnp.where(i > j, s_below, jnp.where(i < j, s_above, 0.5 * (s_below + s_above)))
    return jnp.where(j < length, scores, NEG)


def visit_tiles(scores_into, use, slots, whole_tile, q_block, length, rows, per):
    span = rows * per
    count = lax.div(length + span - 1, span)
    full = lax.div(length, span)
    own = lax.div(q_block, per)
    plain = full - jnp.where(own < full, 1, 0)

    def tile_of(k):
        return k + jnp.where(k >= own, 1, 0)

    @pl.when(plain > 0)
    def _():
        scores_into(slots[0], tile_of(0), own)

    @pl.loop(0, lax.div(plain, 2))
    def _(k):
        first = 2 * k
        scores_into(slots[1], tile_of(first + 1), own)
        use(slots[0], tile_of(first), own)
        scores_into(slots[0], tile_of(jnp.minimum(first + 2, plain - 1)), own)
        use(slots[1], tile_of(first + 1), own)

    @pl.when(lax.rem(plain, 2) == 1)
    def _():
        use(slots[0], tile_of(plain - 1), own)

    @pl.loop(0, 2)
    def _(k):
        t = jnp.where(k == 0, own, full)
        go = (t < count) & ((k == 0) | (full != own))

        @pl.when(go)
        def _():
            whole_tile(t)


def forward_kernel(
    parts, per, info, rates_ref, lanes_ref, bias_ref, rel_ref, mine, other, mixed, wide, lse, k_sc, v_sc, table_sc, s0_sc, s1_sc, m_sc, l_sc, acc
):
    groups, rows = mine.shape[0], mine.shape[3]
    half = RPF // 2
    length = info[pl.program_id(0)]
    part = info[pl.num_programs(0)]
    rates = rates_ref[...]

    def store(block, kt, vt):
        spot = pl.multiple_of(block * rows, rows)
        k_sc[pl.ds(spot, rows), :] = jnp.concatenate([kt, jnp.zeros_like(kt)], axis=0).T
        v_sc[:, pl.ds(spot, rows)] = vt

    key_side(parts, part, groups, mine, other, store)
    span = rows * per
    table_sc[...] = decay_table(lanes_ref[...], span)

    @pl.loop(0, groups)
    def _(g):
        q_block = g * parts + part

        @pl.when(q_block * rows > length)
        def _():
            mixed[g, 0] = jnp.zeros(mixed.shape[2:], mixed.dtype)
            wide[g, 0] = jnp.zeros(wide.shape[2:], wide.dtype)
            lse[g, 0] = jnp.zeros(lse.shape[2:], lse.dtype)

        @pl.when(q_block * rows <= length)
        def _():
            content = mine[g, 0, :KD, :]
            _, plus, minus = query_side(content, bias_ref[...], rel_ref[...], half)
            query, _, _ = query_block(content, plus, minus, rates)
            first_query = q_block * rows
            m_sc[...] = jnp.full(m_sc.shape, NEG, F32)
            l_sc[...] = jnp.zeros(l_sc.shape, F32)
            acc[...] = jnp.zeros(acc.shape, F32)

            def scores_of(t, kind):
                first_key = pl.multiple_of(t * span, span)
                decays = key_decays(
                    table_sc[...], lanes_ref[...], first_query, first_query + rows - 1, first_key, span, kind
                )
                keys = k_sc[pl.ds(first_key, span), :]
                return tile_scores(keys, decays, query, first_query, first_key, length, kind)

            def scores_into(slot, t, own):
                slot[...] = scores_of(t, "plain")

            def use(slot, t, own):
                scores = slot[...]
                old = m_sc[...]
                new = jnp.maximum(old, jnp.max(scores, axis=0, keepdims=True))
                alpha = jnp.exp(old - new)
                probs = jnp.exp(scores - new)
                m_sc[...] = new
                l_sc[...] = l_sc[...] * alpha + jnp.sum(probs, axis=0, keepdims=True)
                values = v_sc[:, pl.ds(pl.multiple_of(t * span, span), span)]
                acc[...] = acc[...] * alpha + dot(values, probs.astype(BF))

            def whole_tile(t):
                s0_sc[...] = scores_of(t, "both")
                use(s0_sc, t, None)

            visit_tiles(scores_into, use, (s0_sc, s1_sc), whole_tile, q_block, length, rows, per)
            total = l_sc[...]
            out = acc[...] / total
            mixed[g, 0] = out.astype(BF)
            wide[g, 0] = out
            lse[g, 0] = jnp.broadcast_to(m_sc[...] + jnp.log(total), lse.shape[2:])


def backward_kernel(
    parts, per, info, rates_ref, lanes_ref, bias_ref, rel_ref, mine, other, grad, wide, lse,
    dq, dkv_mine, dkv_other, sums, rel_grad,
    k_sc, kt_sc, v_sc, table_sc, turned_sc, s0_sc, s1_sc, dk_sc, dv_sc, dq_sc, bias_sc,
):
    groups, rows = mine.shape[0], mine.shape[3]
    half = RPF // 2
    step = pl.program_id(0)
    length = info[step]
    part = info[pl.num_programs(0)]
    rates = rates_ref[...]
    scale = KD**-0.5

    def store(block, kt, vt):
        spot = pl.multiple_of(block * rows, rows)
        k_sc[pl.ds(spot, rows), :] = jnp.concatenate([kt, jnp.zeros_like(kt)], axis=0).T
        kt_sc[:, pl.ds(spot, rows)] = kt
        v_sc[pl.ds(spot, rows), :] = vt.T

    key_side(parts, part, groups, mine, other, store)
    span = rows * per
    table_sc[...] = decay_table(lanes_ref[...], span)
    turned_sc[...] = table_sc[...].T[KD : KD + RPF]
    dk_sc[...] = jnp.zeros(dk_sc.shape, F32)
    dv_sc[...] = jnp.zeros(dv_sc.shape, F32)

    @pl.when(step == 0)
    def _():
        bias_sc[...] = jnp.zeros(bias_sc.shape, F32)
        rel_grad[...] = jnp.zeros(rel_grad.shape, F32)

    @pl.loop(0, groups)
    def _(g):
        q_block = g * parts + part

        @pl.when(q_block * rows > length)
        def _():
            dq[g, 0] = jnp.zeros(dq.shape[2:], dq.dtype)

        @pl.when(q_block * rows <= length)
        def _():
            content = mine[g, 0, :KD, :]
            content_rows = content.T
            positional, plus, minus = query_side(content, bias_ref[...], rel_ref[...], half)
            query, from_first, to_last = query_block(content, plus, minus, rates)
            first_query = q_block * rows
            last_query = first_query + rows - 1
            grad_t = grad[g, 0]
            grad_rows = grad_t.T
            log_total = lse[g, 0, :1, :]
            row_sum = jnp.sum(grad_t.astype(F32) * wide[g, 0], axis=0, keepdims=True)
            dq_sc[...] = jnp.zeros(dq_sc.shape, F32)

            def decays_of(first_key, kind):
                return key_decays(
                    table_sc[...], lanes_ref[...], first_query, last_query, first_key, span, kind
                )

            def scores_of(t, decays, kind):
                first_key = pl.multiple_of(t * span, span)
                keys = k_sc[pl.ds(first_key, span), :]
                return tile_scores(keys, decays, query, first_query, first_key, length, kind)

            def scores_into(slot, t, own):
                first_key = pl.multiple_of(t * span, span)
                slot[0] = scores_of(t, decays_of(first_key, "plain"), "plain")
                slot[1] = dot(v_sc[pl.ds(first_key, span), :], grad_t)

            def use(slot, t, own):
                absorb(slot, t, "plain", None)

            def whole_tile(t):
                first_key = pl.multiple_of(t * span, span)
                decays = decays_of(first_key, "both")
                s0_sc[0] = scores_of(t, decays, "both")
                s0_sc[1] = dot(v_sc[pl.ds(first_key, span), :], grad_t)
                absorb(s0_sc, t, "both", decays)

            def absorb(slot, t, kind, decays):
                first_key = spot = pl.multiple_of(t * span, span)
                scores, prob_grad = slot[0], slot[1]
                exact = jnp.exp(scores - log_total)
                score_grad = exact * (prob_grad - row_sum)
                low = score_grad.astype(BF)
                dv_sc[pl.ds(spot, span), :] += dot(exact.astype(BF), grad_rows)
                dk_sc[pl.ds(spot, span), :] += dot(low, content_rows)
                keys_turned = kt_sc[:, pl.ds(spot, span)]
                if kind == "both":
                    i, j = order_of(first_query, first_key, span, rows)
                    equal = 0.5 * score_grad
                    lower = jnp.where(i > j, score_grad, jnp.where(i < j, 0.0, equal)).astype(BF)
                    upper = jnp.where(i < j, score_grad, jnp.where(i > j, 0.0, equal)).astype(BF)
                    dq_sc[:KD] += dot(keys_turned, low)
                    below, above = decays
                    dq_sc[KD : KD + half] += dot(below.T[KD : KD + half], lower)
                    dq_sc[KD + half : KD + RPF] += dot(above.T[KD + half : KD + RPF], upper)
                else:
                    before = first_key < first_query
                    gap = jnp.where(before, first_query - (first_key + span - 1), first_key - last_query)
                    faded = jnp.exp(-rates * gap.astype(F32))
                    down = turned_sc[:half] * jnp.where(before, faded, 0.0)
                    up = turned_sc[half:] * jnp.where(before, 0.0, faded)
                    pos = jnp.concatenate([down, up], axis=0).astype(BF)
                    dq_sc[...] += dot(jnp.concatenate([keys_turned, pos], axis=0), low)

            visit_tiles(scores_into, use, (s0_sc, s1_sc), whole_tile, q_block, length, rows, per)
            content_grad = dq_sc[:KD]
            down, up = dq_sc[KD : KD + half] * from_first, dq_sc[KD + half :] * to_last
            projected_grad = jnp.concatenate([down + up, down - up], axis=0)
            positional_grad = dot32(rel_ref[...], projected_grad, ((0,), (0,)))
            dq[g, 0] = (scale * (content_grad + positional_grad)).astype(BF)
            bias_sc[0] += content_grad
            bias_sc[1] += positional_grad
            rel_grad[...] += dot32(positional, projected_grad, ((1,), (1,)))

    for slot in range(parts):
        theirs = slot_part(part, slot, parts)
        for g in range(groups):
            spot = pl.multiple_of((g * parts + theirs) * rows, rows)
            dkt = dk_sc[pl.ds(spot, rows), :].astype(BF).T
            dvt = dv_sc[pl.ds(spot, rows), :].astype(BF).T
            both = jnp.concatenate([dkt, dvt], axis=0)
            if slot == 0:
                dkv_mine[g, 0] = both
            else:
                dkv_other[slot - 1, g, 0] = both

    @pl.when(step == pl.num_programs(0) - 1)
    def _():
        sums[...] = scale * jnp.sum(bias_sc[...], axis=-1, keepdims=True)


def attention_cost(windows, groups, rows, parts, wide):
    pairs = windows * groups * rows * groups * parts * rows
    return pl.CostEstimate(
        flops=int(pairs * 2 * wide * 0.75), bytes_accessed=20_000_000, transcendentals=int(pairs)
    )


def whole(*shape):
    return pl.BlockSpec(shape, lambda w: (0,) * len(shape))


def per_window(*shape):
    lead = len(shape) - 3
    return pl.BlockSpec(shape, lambda w: (0,) * lead + (w, 0, 0))


def tile_blocks(rows, groups, parts, target):
    per = max(1, target // rows)
    while (groups * parts) % per:
        per -= 1
    return per


def lanes_of(rates):
    line = rates.reshape(1, -1)
    return jnp.pad(jnp.concatenate([line, line], axis=1), ((0, 0), (KD, 128 - KD - RPF)))


def attention_forward(info, rates, bias, rel, mine, other, parts):
    groups, windows, _, rows = mine.shape
    per = tile_blocks(rows, groups, parts, 1024)
    total = groups * parts * rows
    return pl.pallas_call(
        functools.partial(forward_kernel, parts, per),
        grid=(windows,),
        out_shape=(
            jax.ShapeDtypeStruct((groups, windows, VD, rows), BF),
            jax.ShapeDtypeStruct((groups, windows, VD, rows), F32),
            jax.ShapeDtypeStruct((groups, windows, 8, rows), F32),
        ),
        in_specs=[
            pl.BlockSpec(memory_space=pltpu.SMEM),
            whole(*rates.shape),
            whole(1, 128),
            whole(*bias.shape),
            whole(*rel.shape),
            per_window(groups, 1, 2 * KD + VD, rows),
            per_window(parts - 1, groups, 1, KD + VD, rows),
        ],
        out_specs=(
            per_window(groups, 1, VD, rows),
            per_window(groups, 1, VD, rows),
            per_window(groups, 1, 8, rows),
        ),
        scratch_shapes=[
            pltpu.VMEM((total, 128), BF),
            pltpu.VMEM((VD, total), BF),
            pltpu.VMEM((rows * per, 128), F32),
            pltpu.VMEM((rows * per, rows), F32),
            pltpu.VMEM((rows * per, rows), F32),
            pltpu.VMEM((1, rows), F32),
            pltpu.VMEM((1, rows), F32),
            pltpu.VMEM((VD, rows), F32),
        ],
        compiler_params=pltpu.CompilerParams(vmem_limit_bytes=56 * 2**20),
        cost_estimate=attention_cost(windows, groups, rows, parts, 128 + 256),
        name="attention_forward",
    )(info, rates, lanes_of(rates), bias, rel, mine, other)


def attention_backward(info, rates, bias, rel, mine, other, grad, wide, lse, parts):
    groups, windows, _, rows = mine.shape
    per = tile_blocks(rows, groups, parts, 1024)
    total = groups * parts * rows
    return pl.pallas_call(
        functools.partial(backward_kernel, parts, per),
        grid=(windows,),
        out_shape=(
            jax.ShapeDtypeStruct((groups, windows, KD, rows), BF),
            jax.ShapeDtypeStruct((groups, windows, KD + VD, rows), BF),
            jax.ShapeDtypeStruct((parts - 1, groups, windows, KD + VD, rows), BF),
            jax.ShapeDtypeStruct((2, KD, 1), F32),
            jax.ShapeDtypeStruct((KD, RPF), F32),
        ),
        in_specs=[
            pl.BlockSpec(memory_space=pltpu.SMEM),
            whole(*rates.shape),
            whole(1, 128),
            whole(*bias.shape),
            whole(*rel.shape),
            per_window(groups, 1, 2 * KD + VD, rows),
            per_window(parts - 1, groups, 1, KD + VD, rows),
            per_window(groups, 1, VD, rows),
            per_window(groups, 1, VD, rows),
            per_window(groups, 1, 8, rows),
        ],
        out_specs=(
            per_window(groups, 1, KD, rows),
            per_window(groups, 1, KD + VD, rows),
            per_window(parts - 1, groups, 1, KD + VD, rows),
            whole(2, KD, 1),
            whole(KD, RPF),
        ),
        scratch_shapes=[
            pltpu.VMEM((total, 128), BF),
            pltpu.VMEM((KD, total), BF),
            pltpu.VMEM((total, VD), BF),
            pltpu.VMEM((rows * per, 128), F32),
            pltpu.VMEM((RPF, rows * per), F32),
            pltpu.VMEM((2, rows * per, rows), F32),
            pltpu.VMEM((2, rows * per, rows), F32),
            pltpu.VMEM((total, KD), F32),
            pltpu.VMEM((total, VD), F32),
            pltpu.VMEM((KD + RPF, rows), F32),
            pltpu.VMEM((2, KD, rows), F32),
        ],
        compiler_params=pltpu.CompilerParams(vmem_limit_bytes=56 * 2**20),
        cost_estimate=attention_cost(windows, groups, rows, parts, 3 * 256 + 2 * 256),
        name="attention_backward",
    )(info, rates, lanes_of(rates), bias, rel, mine, other, grad, wide, lse)

MESH = pl.DeviceIdType.MESH


def upper_work(here, lengths, cotangent, skip_input, outs, gathered, scratch, remote, neighbours):
    out_grad_o, conv_o, joined_o, lifted_o, third_o, skip_grad_o, skip_part_o, bias_o = outs
    (
        table_rows,
        lines,
        w_point,
        w_skip,
        w_upsample,
        grad_v,
        skip_v,
        conv_v,
        joined_v,
        lifted_v,
        part_v,
        halo_before,
        halo_after,
        sem,
        halo_sem,
    ) = scratch
    dp, seq = here
    windows, fine, width = grad_v.shape
    rows = fine // 2
    before, after = neighbours

    def load(source, target, n):
        return pltpu.make_async_copy(source, target, sem.at[n])

    point_load = load(gathered[9], w_point, 0)
    skip_load = load(gathered[4], w_skip, 1)
    upsample_load = load(gathered[8], w_upsample, 2)
    grad_load = load(cotangent, grad_v, 3)
    input_load = load(skip_input, skip_v, 4)
    grad_load.start()
    input_load.start()
    stores = {
        "out_grad": load(grad_v, out_grad_o, 5),
        "conv": load(conv_v, conv_o, 6),
        "joined": load(joined_v, joined_o, 7),
        "lifted": load(lifted_v, lifted_o, 8),
        "skip": load(skip_v, skip_grad_o, 9),
    }

    def against(x, table):
        return lax.dot_general(
            x, table[...].reshape(width, width), (((1,), (1,)), ((), ())), preferred_element_type=F32
        )

    def halo_copies():
        out = []
        for w in range(windows):
            out.append(
                remote(
                    conv_v.at[w, pl.ds(fine - 16, 16)],
                    halo_before.at[w],
                    halo_sem.at[0, w],
                    halo_sem.at[1, w],
                    after,
                )
            )
            out.append(
                remote(
                    conv_v.at[w, pl.ds(0, 16)],
                    halo_after.at[w],
                    halo_sem.at[2, w],
                    halo_sem.at[3, w],
                    before,
                )
            )
        return out

    def conv_grad(w):
        if w == 0:
            point_load.start()
            grad_load.wait()
            point_load.wait()
        length = lengths[w]

        @pl.loop(0, fine // 256)
        def _(k):
            at = pl.ds(pl.multiple_of(k * 256, 256), 256)
            bin_ = seq * rows + lax.div(
                k * 256 + lax.broadcasted_iota(jnp.int32, (256, width), 0), 2
            )
            grad = jnp.where(bin_ < length, grad_v[w, at, :].astype(F32), 0.0).astype(BF)
            grad_v[w, at, :] = grad
            conv_v[w, at, :] = against(grad, w_point).astype(BF)

        if w == windows - 1:
            stores["out_grad"].start()
            stores["conv"].start()
            for copy in halo_copies():
                copy.start()

    def skip_part(w):
        if w == 0:
            skip_load.start()
            input_load.wait()
            skip_load.wait()

        @pl.loop(0, fine // 256)
        def _(k):
            at = pl.ds(pl.multiple_of(k * 256, 256), 256)
            made = dot(skip_v[w, at, :], w_skip[...].reshape(width, width)) + lines[0:1, :]
            part_v[...] = made
            store = load(part_v, skip_part_o.at[w, at], 10)
            store.start()
            store.wait()

    def joined_grad():
        for copy in halo_copies():
            copy.wait_recv()
        total = jnp.zeros((1, width), F32)
        tap = [lines[n : n + 1, :] for n in (1, 2, 3)]
        tile = 64
        for w in range(windows):
            first = halo_before[w].astype(F32)[15:16, :]
            first = jnp.where(seq == 0, 0.0, first)
            last = halo_after[w].astype(F32)[0:1, :]
            last = jnp.where(seq == lax.axis_size("seq") - 1, 0.0, last)
            for k in range(fine // tile):
                at = slice(k * tile, (k + 1) * tile)
                here_rows = conv_v[w, at, :].astype(F32)
                up = first if k == 0 else conv_v[w, k * tile - 16 : k * tile, :].astype(F32)[15:16, :]
                down = (
                    last
                    if k == fine // tile - 1
                    else conv_v[w, (k + 1) * tile : (k + 1) * tile + 16, :].astype(F32)[0:1, :]
                )
                index = lax.broadcasted_iota(jnp.int32, here_rows.shape, 0)
                earlier = jnp.where(index == 0, up, pltpu.roll(here_rows, 1, 0))
                later = jnp.where(index == tile - 1, down, pltpu.roll(here_rows, tile - 1, 0))
                made = later * tap[0] + here_rows * tap[1] + earlier * tap[2]
                total = total + jnp.sum(made, axis=0, keepdims=True)
                joined_v[w, at, :] = made.astype(BF)
        bias_o[...] = total
        stores["joined"].start()
        pair = lax.div(lax.broadcasted_iota(jnp.int32, (rows, fine), 1), 2)
        twice = (pair == lax.broadcasted_iota(jnp.int32, (rows, fine), 0)).astype(F32).astype(BF)
        for w in range(windows):
            lifted_v[w * rows : (w + 1) * rows, :] = dot(twice, joined_v[w]).astype(BF)
        stores["lifted"].start()

    def skip_grad(w):
        @pl.loop(0, fine // 256)
        def _(k):
            at = pl.ds(pl.multiple_of(k * 256, 256), 256)
            skip_v[w, at, :] = against(joined_v[w, at, :], w_skip).astype(BF)

        if w == windows - 1:
            stores["skip"].start()

    def third_grad():
        upsample_load.start()
        upsample_load.wait()

        @pl.loop(0, windows * rows // 256)
        def _(k):
            at = pl.ds(pl.multiple_of(k * 256, 256), 256)
            part_v[...] = against(lifted_v[at, :], w_upsample)
            store = load(part_v, third_o.at[at], 10)
            store.start()
            store.wait()

    def finish():
        for store in stores.values():
            store.wait()
        for copy in halo_copies():
            copy.wait_send()

    jobs = {
        9: [(9, functools.partial(conv_grad, 0))],
        10: [(None, functools.partial(conv_grad, 1))],
        11: [(4, functools.partial(skip_part, 0)), (None, functools.partial(skip_part, 1))],
        12: [(None, joined_grad)],
        13: [(None, functools.partial(skip_grad, 0)), (None, functools.partial(skip_grad, 1))],
        14: [(8, third_grad)],
    }
    return {"rows": table_rows, "lines": lines, "jobs": jobs, "finish": finish}


def links_kernel(pairs, counts, parts, early, *refs):
    n_in, n_out = counts
    refs = list(refs)

    def take(count):
        out, refs[:count] = refs[:count], []
        return out

    refs_in = take(n_in)
    if early:
        values, spread_gain, pick_gain, spread_bias, pick_bias = take(5)
        lengths, cotangent, skip_input = take(3)
    elif parts:
        (blocks,) = take(1)
    refs_out = take(n_out)
    if parts:
        mine, other = take(2)
    if early:
        (normed,) = take(1)
        upper_out = take(8)
    local_sem, send_hi, recv_hi, send_y, recv_y, send_dp, recv_dp, send_c, recv_c = take(9)
    dp, seq = lax.axis_index("dp"), lax.axis_index("seq")
    ndp, nhi = refs_out[0].shape[:2]
    hi, low = lax.div(seq, 4), lax.rem(seq, 4)
    y, c = lax.div(low, 2), lax.rem(low, 2)

    def place(dp_to, hi_to, y_to, c_to):
        return (dp_to, hi_to * 4 + y_to * 2 + c_to)

    hi_peers = [place(dp, lax.rem(hi + k, nhi), y, c) for k in range(1, nhi)]
    y_peers = [place(dp, hi, 1 - y, c)]
    dp_peers = [place(lax.rem(dp + k, ndp), hi, y, c) for k in range(1, ndp)]
    c_peers = [place(dp, hi, y, 1 - c)]
    everyone = hi_peers + y_peers + dp_peers + c_peers
    if parts:
        head, part = lax.div(seq, parts), lax.rem(seq, parts)
        head_of = [lax.rem(head + k, H) for k in range(1, H)]
        head_peers = [(dp, h * parts + part) for h in head_of]
        part_peers = [(dp, head * parts + slot_part(part, k, parts)) for k in range(1, parts)]
        everyone = everyone + head_peers + part_peers
    if early:
        nseq = nhi * 4
        after = (dp, lax.rem(seq + 1, nseq))
        before = (dp, lax.rem(seq + nseq - 1, nseq))
        everyone = everyone + [after, before]

    barrier = pltpu.get_barrier_semaphore()
    for peer in everyone:
        pl.semaphore_signal(barrier, inc=1, device_id=peer, device_id_type=MESH)
    pl.semaphore_wait(barrier, len(everyone))

    def remote(source, target, ss, rs, peer):
        return pltpu.make_async_remote_copy(
            src_ref=source,
            dst_ref=target,
            send_sem=ss,
            recv_sem=rs,
            device_id=peer,
            device_id_type=MESH,
        )

    step_chunks, serial = [], 0
    for pair in pairs:
        step_chunks.append([])
        for side in (0, 1):
            for chunk in pair[side]:
                step_chunks[-1].append((serial, side) + chunk)
                serial += 1

    def copies(chunk, stage):
        n, side, array, row, rows, first, columns = chunk
        out = refs_out[array]
        piece = (pl.ds(row, rows), pl.ds(first, columns))
        which = (("hi", "y", "dp", "c"), ("hi", "dp", "y", "c"))[side][stage]
        if which == "hi":
            target = out.at[(dp, hi, y, c) + piece]
            source = refs_in[array].at[piece]
            peers, ss, rs = hi_peers, send_hi, recv_hi
        else:
            every = slice(None)
            if which == "c":
                target = out.at[(every, every, every, c) + piece]
                peers, ss, rs = c_peers, send_c, recv_c
            elif which == "y":
                there = (dp, every, y, c) if stage == 1 else (every, every, y, c)
                target = out.at[there + piece]
                peers, ss, rs = y_peers, send_y, recv_y
            else:
                there = (dp, every, y, c) if stage == 1 else (dp, every, every, c)
                target = out.at[there + piece]
                peers, ss, rs = dp_peers, send_dp, recv_dp
            source = target
        return [remote(source, target, ss.at[n, k], rs.at[n, k], p) for k, p in enumerate(peers)]

    def own(array):
        return pltpu.make_async_copy(
            refs_in[array], refs_out[array].at[dp, hi, y, c], local_sem.at[array]
        )

    everything = [chunk for group in step_chunks for chunk in group]
    head_copies, head_own = [], None
    if parts:
        head_local, head_send, head_recv, part_send, part_recv = take(5)
        if early:
            blocks = take(1)[0]
        head_copies = [
            remote(blocks.at[:, h], mine.at[head], head_send.at[k], head_recv.at[k], p)
            for k, (h, p) in enumerate(zip(head_of, head_peers, strict=True))
        ]
        head_own = pltpu.make_async_copy(blocks.at[:, head], mine.at[head], head_local.at[0])
        keys = mine.at[:, :, pl.ds(KD, KD + VD)]
        part_copies = [
            remote(keys, other.at[k], part_send.at[k], part_recv.at[k], p)
            for k, p in enumerate(part_peers)
        ]
        if not early:
            head_own.start()
    if early:
        small_v, query_v, key_v, values_v, inputs_v, gain_v, bias_v, load_sem = take(8)
        inputs_load = pltpu.make_async_copy(values, inputs_v, load_sem.at[0])
        inputs_load.start()
        upper = upper_work(
            (dp, seq), lengths, cotangent, skip_input, upper_out, refs_out, take(15), remote, (before, after)
        )

    def make_blocks():
        loads = [
            pltpu.make_async_copy(source, target, load_sem.at[k + 1])
            for k, (source, target) in enumerate(
                zip(refs_out[:4], (small_v, query_v, key_v, values_v), strict=True)
            )
        ]
        for load in loads:
            load.start()
        inputs_load.wait()
        for load in loads:
            load.wait()

        @pl.loop(0, ndp * nhi * 4)
        def _(k):
            rows = small_v[
                lax.div(k, nhi * 4),
                lax.rem(lax.div(k, 4), nhi),
                lax.rem(lax.div(k, 2), 2),
                lax.rem(k, 2),
            ].astype(F32)
            gain_v[pl.ds(k, 1), :] = rows[0:1, :]
            bias_v[pl.ds(k, 1), :] = rows[1:2, :]
            for n in range(4):
                upper["rows"][n, pl.ds(k, 1), :] = rows[7 + n : 8 + n, :]

        def line_up(table, spread, pick):
            return jnp.sum(dot(table[...].astype(BF), spread[...]) * pick[...], axis=0, keepdims=True)

        gain = line_up(gain_v, spread_gain, pick_gain)
        for n in range(4):
            upper["lines"][n : n + 1, :] = line_up(upper["rows"].at[n], spread_gain, pick_gain)
        bias = line_up(bias_v, spread_bias, pick_bias)
        windows, rows = inputs_v.shape[:2]
        for w in range(windows):
            normed[w * rows : (w + 1) * rows, :] = layer_norm(
                inputs_v[w].astype(F32), gain
            ).astype(BF)
        low = normed[...]
        width = low.shape[1]

        def weight(table, first, columns):
            return table[:, :, :, :, :, first : first + columns].reshape(width, columns)

        for pair in range(H // 2):
            spot, wide = pair * 2 * KD, pair * 2 * VD
            content = dot(low, weight(query_v, spot, 2 * KD)) + bias[:, spot : spot + 2 * KD]
            content = (content * (KD**-0.5)).astype(BF).T
            key = dot(low, weight(key_v, spot, 2 * KD)).astype(BF).T
            value = dot(low, weight(values_v, wide, 2 * VD)).astype(BF).T
            for h in range(2):
                for w in range(windows):
                    span = slice(w * rows, (w + 1) * rows)
                    blocks[w, 2 * pair + h, :KD, :] = content[h * KD : (h + 1) * KD, span]
                    blocks[w, 2 * pair + h, KD : 2 * KD, :] = key[h * KD : (h + 1) * KD, span]
                    blocks[w, 2 * pair + h, 2 * KD :, :] = value[h * VD : (h + 1) * VD, span]
        head_own.start()

    ahead, lag = 3, 2

    def launch(step):
        for chunk in step_chunks[step]:
            for copy in copies(chunk, 0):
                copy.start()

    events = {}
    for spot in range(len(pairs)):
        gap = 1 if spot < early else lag
        for stage in (3, 2, 1):
            events.setdefault(spot + gap * (stage - 1), []).append((stage, spot))
    made_at = early + 2 if early else 0
    waited = []
    heads_at = [made_at + k for k in range(len(head_copies))]
    for step in range(min(ahead, len(pairs))):
        launch(step)
    for array in range(n_out):
        own(array).start()
    for array in range(n_out):
        own(array).wait()
    for step in range(max(list(events) + heads_at) + 1):
        for stage, spot in sorted(events.get(step, []), reverse=True):
            for chunk in step_chunks[spot]:
                for copy in copies(chunk, stage - 1):
                    copy.wait_recv()
                for copy in copies(chunk, stage):
                    copy.start()
        if step + ahead < len(pairs):
            launch(step + ahead)
        if early and step == made_at:
            for group in step_chunks[:early]:
                for chunk in group:
                    for copy in copies(chunk, 3):
                        copy.wait_recv()
            make_blocks()
        if step in heads_at:
            head_copies[heads_at.index(step)].start()
        if early:
            for need, job in upper["jobs"].get(step, []):
                for chunk in everything:
                    if chunk[2] == need:
                        for copy in copies(chunk, 3):
                            copy.wait_recv()
                        waited.append(chunk)
                job()
    if parts:
        head_own.wait()
        for copy in head_copies:
            copy.wait_recv()
        for copy in part_copies:
            copy.start()
    for group in step_chunks[early:]:
        for chunk in group:
            if chunk not in waited:
                for copy in copies(chunk, 3):
                    copy.wait_recv()
    if early:
        upper["finish"]()
    if parts:
        for copy in part_copies:
            copy.wait_recv()
        for copy in head_copies + part_copies:
            copy.wait_send()
    for chunk in everything:
        for stage in range(4):
            for copy in copies(chunk, stage):
                copy.wait_send()


def spread_tables(length, share):
    column = jnp.arange(length, dtype=jnp.int32)
    lane = jnp.arange(128, dtype=jnp.int32)
    device = jnp.arange(length // share, dtype=jnp.int32)
    spread = (column[None, :] % share == lane[:, None]).astype(BF)
    pick = (column[None, :] // share == device[:, None]).astype(F32)
    return spread, pick


def use_links(name, collective, shards, pairs, blocks=None, values=None, early=0, upper=()):
    ndp, nseq = lax.axis_size("dp"), lax.axis_size("seq")
    nhi, devices = nseq // 4, ndp * nseq
    parts = nseq // H if blocks is not None or early else 0
    chunks = sum(len(side) for pair in pairs for side in pair)
    arrays = [shard.shape for shard in shards]
    out_shape = [jax.ShapeDtypeStruct((ndp, nhi, 2, 2) + shape, BF) for shape in arrays]
    operands = list(shards)
    in_specs = [pl.BlockSpec(memory_space=pl.ANY)] * len(operands)
    sizes = [(len(arrays),)] + [
        (chunks, size) for size in (nhi - 1, nhi - 1, 1, 1, ndp - 1, ndp - 1, 1, 1)
    ]
    scratch = []
    if early:
        windows, rows, width = values.shape
        operands += [values]
        operands += [
            *spread_tables(width, width // devices),
            *spread_tables(H * KD, H * KD // devices),
        ]
        in_specs += [pl.BlockSpec(memory_space=pl.ANY)] + [
            pl.BlockSpec(memory_space=pltpu.VMEM)
        ] * 4
        operands += list(upper)
        in_specs += [pl.BlockSpec(memory_space=pltpu.SMEM)] + [
            pl.BlockSpec(memory_space=pl.ANY)
        ] * 2
        scratch = [
            pltpu.VMEM((windows, H, 2 * KD + VD, rows), BF),
            pltpu.VMEM(out_shape[0].shape, BF),
            pltpu.VMEM(out_shape[1].shape, BF),
            pltpu.VMEM(out_shape[2].shape, BF),
            pltpu.VMEM(out_shape[3].shape, BF),
            pltpu.VMEM(values.shape, BF),
            pltpu.VMEM((devices, 128), F32),
            pltpu.VMEM((devices, 128), F32),
            pltpu.SemaphoreType.DMA((5,)),
            pltpu.VMEM((4, devices, 128), F32),
            pltpu.VMEM((8, width), F32),
            *[pltpu.VMEM((ndp, nhi, 2, 2, width // devices, width), BF)] * 3,
            *[pltpu.VMEM((windows, 2 * rows, width), BF)] * 4,
            pltpu.VMEM((windows * rows, width), BF),
            pltpu.VMEM((256, width), F32),
            pltpu.VMEM((windows, 16, width), BF),
            pltpu.VMEM((windows, 16, width), BF),
            pltpu.SemaphoreType.DMA((11,)),
            pltpu.SemaphoreType.DMA((4, windows)),
        ]
    elif parts:
        windows, _, _, rows = blocks.shape
        operands.append(blocks)
        in_specs.append(pl.BlockSpec(memory_space=pl.ANY))
    out_specs = [pl.BlockSpec(memory_space=pl.ANY)] * len(out_shape)
    if parts:
        out_shape += [
            jax.ShapeDtypeStruct((H, windows, 2 * KD + VD, rows), BF),
            jax.ShapeDtypeStruct((parts - 1, H, windows, KD + VD, rows), BF),
        ]
        out_specs += [pl.BlockSpec(memory_space=pl.ANY)] * 2
        sizes += [(1,), (H - 1,), (H - 1,), (parts - 1,), (parts - 1,)]
    if early:
        out_shape.append(jax.ShapeDtypeStruct((windows * rows, width), BF))
        out_specs.append(pl.BlockSpec(memory_space=pltpu.VMEM))
        fine, coarse = (windows, 2 * rows, width), (windows * rows, width)
        out_shape += [
            jax.ShapeDtypeStruct(*s)
            for s in (
                (fine, BF),
                (fine, BF),
                (fine, BF),
                (coarse, BF),
                (coarse, F32),
                (fine, BF),
                (fine, F32),
                ((1, width), F32),
            )
        ]
        out_specs += [pl.BlockSpec(memory_space=pl.ANY)] * 7
        out_specs.append(pl.BlockSpec(memory_space=pltpu.VMEM))
    outs = pl.pallas_call(
        functools.partial(links_kernel, pairs, (len(shards), len(arrays)), parts, early),
        out_shape=out_shape,
        in_specs=in_specs,
        out_specs=out_specs,
        scratch_shapes=[pltpu.SemaphoreType.DMA(size) for size in sizes] + scratch,
        compiler_params=pltpu.CompilerParams(
            collective_id=collective, has_side_effects=True, vmem_limit_bytes=60 * 2**20
        ),
        name=name,
    )(*operands)
    flat = [out.reshape(-1, out.shape[-1]) for out in outs[: len(arrays)]]
    return flat + list(outs[len(arrays) :])


def tie(*values):
    return lax.optimization_barrier(values)


def project_kernel(values, gain, content_bias, w_query, w_key, w_value, normed, sent, scratch):
    windows, rows, _ = values.shape

    @pl.when(pl.program_id(0) == 0)
    def _():
        for w in range(windows):
            low = layer_norm(values[w].astype(F32), gain[...]).astype(BF)
            scratch[w * rows : (w + 1) * rows, :] = low
            normed[w * rows : (w + 1) * rows, :] = low

    low = scratch[...]
    content = ((dot(low, w_query[...]) + content_bias[0]) * (KD**-0.5)).astype(BF).T
    keys = dot(low, w_key[...]).astype(BF).T
    mixable = dot(low, w_value[...]).astype(BF).T
    for h in range(2):
        for w in range(windows):
            span = slice(w * rows, (w + 1) * rows)
            sent[w, h, :KD, :] = content[h * KD : (h + 1) * KD, span]
            sent[w, h, KD : 2 * KD, :] = keys[h * KD : (h + 1) * KD, span]
            sent[w, h, 2 * KD :, :] = mixable[h * VD : (h + 1) * VD, span]


def project(values, gain, content_bias, weight_query, weight_key, weight_value):
    windows, rows, width = values.shape
    steps = H // 2
    return pl.pallas_call(
        project_kernel,
        grid=(steps,),
        out_shape=(
            jax.ShapeDtypeStruct((windows * rows, width), BF),
            jax.ShapeDtypeStruct((windows, H, 2 * KD + VD, rows), BF),
        ),
        in_specs=[
            pl.BlockSpec((windows, rows, width), lambda i: (0, 0, 0)),
            pl.BlockSpec((1, width), lambda i: (0, 0)),
            pl.BlockSpec((1, 1, 2 * KD), lambda i: (i, 0, 0)),
            pl.BlockSpec((width, 2 * KD), lambda i: (0, i)),
            pl.BlockSpec((width, 2 * KD), lambda i: (0, i)),
            pl.BlockSpec((width, 2 * VD), lambda i: (0, i)),
        ],
        out_specs=(
            pl.BlockSpec((windows * rows, width), lambda i: (0, 0)),
            pl.BlockSpec((windows, 2, 2 * KD + VD, rows), lambda i: (0, i, 0, 0)),
        ),
        scratch_shapes=[pltpu.VMEM((windows * rows, width), BF)],
        compiler_params=pltpu.CompilerParams(vmem_limit_bytes=48 * 2**20),
        name="project",
    )(
        values,
        gain.reshape(1, width),
        content_bias.reshape(steps, 1, 2 * KD),
        weight_query,
        weight_key,
        weight_value,
    )


def sums_kernel(plan, refs_spec, *refs):
    groups, n_terms, mode, parts, n_small, made_here, late, masked = plan
    refs = list(refs)

    def take(count):
        out, refs[:count] = refs[:count], []
        return out

    terms = take(n_terms * (2 if made_here else 1) - (1 if late else 0))
    head_in = take({None: 0, "in": 1, "back": 1, "out": 3}[mode])
    small_in = take(1 if n_small else 0)
    if late:
        w_query, w_key, w_value, values, middle_grad, gain, spread, pick = take(8)
    if masked:
        lengths, w_masked = take(2)
    outs = take(n_terms)
    head_out = take(0 if late or not mode else 1)
    small_out = take(1 if n_small else 0)
    if late:
        (input_grad,) = take(1)
    if masked:
        (masked_o,) = take(1)
    own, arrived, result, back, hop1, hop2, line = [], [], [], [], [], [], []
    flat = [(side, unit) for group in groups for side in (0, 1) for unit in group[side]]
    count = len(flat)
    own = take(count)
    arrived = take(count)
    hop1 = take(count)
    hop2 = take(count)
    line = take(count)
    result = take(count)
    back = take(count)
    if made_here:
        slots = min(2, n_terms)
        lefts, rights, turned = take(1), take(slots), take(slots)
        going, left_sem, right_sem = take(3)
    load_sem, c_send, c_recv, s1, r1, s2, r2, s3, r3, s4, r4 = take(11)
    dp, seq = lax.axis_index("dp"), lax.axis_index("seq")
    ndp, nhi = own[0].shape[:2]
    nseq = nhi * 4
    hi, low = lax.div(seq, 4), lax.rem(seq, 4)
    y, c = lax.div(low, 2), lax.rem(low, 2)

    def place(dp_to, hi_to, y_to, c_to):
        return (dp_to, hi_to * 4 + y_to * 2 + c_to)

    hi_index = [lax.rem(hi + k, nhi) for k in range(1, nhi)]
    dp_index = [lax.rem(dp + k, ndp) for k in range(1, ndp)]
    hi_peers = [place(dp, h, y, c) for h in hi_index]
    dp_peers = [place(d, hi, y, c) for d in dp_index]
    y_peer, c_peer = place(dp, hi, 1 - y, c), place(dp, hi, y, 1 - c)
    everyone = hi_peers + dp_peers + [y_peer, c_peer]
    if mode:
        head, part = lax.div(seq, parts), lax.rem(seq, parts)
        head_of = [lax.rem(head + k, H) for k in range(1, H)]
        head_peers = [(dp, h * parts + part) for h in head_of]
        part_peers = [(dp, head * parts + slot_part(part, k, parts)) for k in range(1, parts)]
        everyone = everyone + head_peers + part_peers

    barrier = pltpu.get_barrier_semaphore()
    for peer in everyone:
        pl.semaphore_signal(barrier, inc=1, device_id=peer, device_id_type=MESH)
    expected = len(everyone)
    me = dp * nseq + seq
    if n_small:

        def other_device(k):
            there = lax.rem(me + k, n_small)
            return (lax.div(there, nseq), lax.rem(there, nseq))

        @pl.loop(1, n_small)
        def _(k):
            pl.semaphore_signal(barrier, inc=1, device_id=other_device(k), device_id_type=MESH)

        expected += n_small - 1
    pl.semaphore_wait(barrier, expected)

    def remote(source, target, ss, rs, peer):
        return pltpu.make_async_remote_copy(
            src_ref=source,
            dst_ref=target,
            send_sem=ss,
            recv_sem=rs,
            device_id=peer,
            device_id_type=MESH,
        )

    def half_of(array):
        return outs[array].shape[1] // 2

    def columns_of(unit, core):
        array, row, rows, column, columns = unit
        half = half_of(array)
        spot = pl.multiple_of(core * half + column, 128)
        return terms[array].at[:, :, :, :, pl.ds(row, rows), pl.ds(spot, columns)]

    def load(n):
        return pltpu.make_async_copy(columns_of(flat[n][1], c), own[n], load_sem.at[n])

    def over_core(n):
        source = going_of(n) if made_here else columns_of(flat[n][1], 1 - c)
        return [remote(source, arrived[n], c_send.at[n], c_recv.at[n], c_peer)]

    def first_hop(n):
        if flat[n][0] == 0:
            return [
                remote(own[n].at[d], hop1[n].at[k], s1.at[n, k], r1.at[n, k], p)
                for k, (d, p) in enumerate(zip(dp_index, dp_peers, strict=True))
            ]
        return [remote(own[n].at[:, :, 1 - y], hop1[n], s1.at[n, 0], r1.at[n, 0], y_peer)]

    def second_hop(n):
        if flat[n][0] == 0:
            return [remote(own[n].at[dp, :, 1 - y], hop2[n], s2.at[n, 0], r2.at[n, 0], y_peer)]
        return [
            remote(own[n].at[d, :, y], hop2[n].at[k], s2.at[n, k], r2.at[n, k], p)
            for k, (d, p) in enumerate(zip(dp_index, dp_peers, strict=True))
        ]

    def along_line(n):
        return [
            remote(own[n].at[dp, h, y], line[n].at[k], s3.at[n, k], r3.at[n, k], p)
            for k, (h, p) in enumerate(zip(hi_index, hi_peers, strict=True))
        ]

    def back_home(n):
        return [remote(result[n].at[1 - c], back[n], s4.at[n], r4.at[n], c_peer)]

    hops = (over_core, first_hop, second_hop, along_line, back_home)

    def add(a, b):
        return (a.astype(F32) + b.astype(F32)).astype(BF)

    def absorb(n, stage):
        mine = own[n]
        if stage == 1:

            @pl.loop(0, ndp * nhi)
            def _(k):
                d, h = lax.div(k, nhi), lax.rem(k, nhi)
                mine[d, h] = add(mine[d, h], arrived[n][d, h])

        elif stage == 2 and flat[n][0] == 0:

            @pl.loop(0, nhi)
            def _(h):
                total = mine[dp, h].astype(F32)
                for k in range(ndp - 1):
                    total = total + hop1[n][k, h].astype(F32)
                mine[dp, h] = total.astype(BF)

        elif stage == 2:

            @pl.loop(0, ndp * nhi)
            def _(k):
                d, h = lax.div(k, nhi), lax.rem(k, nhi)
                mine[d, h, y] = add(mine[d, h, y], hop1[n][d, h])

        elif stage == 3 and flat[n][0] == 0:

            @pl.loop(0, nhi)
            def _(h):
                mine[dp, h, y] = add(mine[dp, h, y], hop2[n][h])

        elif stage == 3:

            @pl.loop(0, nhi)
            def _(h):
                total = mine[dp, h, y].astype(F32)
                for k in range(ndp - 1):
                    total = total + hop2[n][k, h].astype(F32)
                mine[dp, h, y] = total.astype(BF)

        elif stage == 4:
            total = mine[dp, hi, y].astype(F32)
            for k in range(nhi - 1):
                total = total + line[n][k].astype(F32)
            result[n][...] = total
        else:
            array, row, rows, column, columns = flat[n][1]
            half = half_of(array)
            here, there = result[n][c], back[n][...]
            outs[array][row : row + rows, column : column + columns] = jnp.where(
                c == 0, here, there
            )
            outs[array][row : row + rows, half + column : half + column + columns] = jnp.where(
                c == 0, there, here
            )

    numbers, serial = [], 0
    for group in groups:
        size = len(group[0]) + len(group[1])
        numbers.append(range(serial, serial + size))
        serial += size

    def going_of(n):
        step = next(k for k, some in enumerate(numbers) if n in some)
        unit = flat[n][1]
        side = numbers[step].index(n)
        return going.at[step % 2, side, :, :, :, :, pl.ds(0, unit[2]), pl.ds(0, unit[4])]

    def fetch_left(array):
        left = terms[2 * array]
        return pltpu.make_async_copy(
            left,
            lefts[0].at[pl.ds(0, left.shape[0]), pl.ds(0, left.shape[1])],
            left_sem.at[array],
        )

    def fetch_right(array):
        right = terms[2 * array + 1]
        return pltpu.make_async_copy(
            right,
            rights[array % 2].at[pl.ds(0, right.shape[0]), pl.ds(0, right.shape[1])],
            right_sem.at[array],
        )

    def arrive():
        for copy in head_own:
            copy.wait()
        for copy in head_copies:
            copy.wait_recv()
        packed = rights[(n_terms - 1) % 2]
        windows, rows = gathered.shape[1], gathered.shape[3]
        for w in range(windows):
            for pair in range(H // 2):
                for first, size, start in ((0, KD, 0), (KD, KD, H * KD), (2 * KD, VD, 2 * H * KD)):
                    both = jnp.concatenate(
                        [gathered[2 * pair + h, w, first : first + size, :] for h in range(2)], axis=0
                    )
                    at = start + pair * 2 * size
                    packed[w * rows : (w + 1) * rows, at : at + 2 * size] = both.T

    def make(step):
        units = [flat[n][1] for n in numbers[step]]
        array, rows = units[0][0], units[0][2]
        first, size = units[0][3], sum(u[4] for u in units)
        left = terms[2 * array]
        tokens, slot = left.shape[0], array % 2
        if step == 0 or flat[numbers[step - 1][0]][1][0] != array:
            fetch_left(array).wait()

            @pl.loop(0, left.shape[1] // 256)
            def _(k):
                spot = pl.multiple_of(k * 256, 256)
                turned[slot][pl.ds(spot, 256), pl.ds(0, tokens)] = lefts[0][
                    pl.ds(0, tokens), pl.ds(spot, 256)
                ].T

            if array + 1 < n_terms:
                fetch_left(array + 1).start()
                if array >= 1 and not (late and array + 1 == n_terms - 1):
                    fetch_right(array + 1).start()
            if late and array == n_terms - 1:
                arrive()
            else:
                fetch_right(array).wait()

        if step >= 2:
            for n in numbers[step - 2]:
                for copy in over_core(n):
                    copy.wait_send()
        span = nhi * 4 * rows
        for whose in (1 - c, c):
            spot = pl.multiple_of(whose * half_of(array) + first, 128)
            part_right = rights[slot][pl.ds(0, tokens), pl.ds(spot, size)]
            for d in range(ndp):
                made = dot(turned[slot][pl.ds(d * span, span), pl.ds(0, tokens)], part_right)
                made = made.astype(BF).reshape(nhi, 2, 2, rows, size)
                at = 0
                for k, n in enumerate(numbers[step]):
                    piece = made[..., at : at + units[k][4]]
                    if whose is c:
                        own[n][d] = piece
                    else:
                        going[step % 2, k, d, :, :, :, pl.ds(0, rows), pl.ds(0, units[k][4])] = piece
                    at += units[k][4]
            if whose is not c:
                for n in numbers[step]:
                    for copy in over_core(n):
                        copy.start()

    def launch(step):
        if made_here:
            make(step)
        else:
            for n in numbers[step]:
                load(n).start()
                for copy in over_core(n):
                    copy.start()

    if made_here:
        fetch_left(0).start()
        for array in range(min(2, n_terms)):
            if not (late and array == n_terms - 1):
                fetch_right(array).start()

    if mode in ("in", "back"):
        head_send, head_recv, head_local = take(3)
        blocks, gathered = head_in[0], head_out[0]

        def block_of(h):
            return blocks.at[:, h] if mode == "in" else blocks.at[h]

        head_copies = [
            remote(block_of(h), gathered.at[head], head_send.at[k], head_recv.at[k], p)
            for k, (h, p) in enumerate(zip(head_of, head_peers, strict=True))
        ]
        head_own = [
            pltpu.make_async_copy(block_of(head), gathered.at[head], head_local.at[0])
        ]
        for copy in head_copies + head_own:
            copy.start()
    if mode == "out":
        head_send, head_recv, head_local, part_send, part_recv, mine_kv, arrived_kv = take(7)
        query, pair_mine, pair_other = head_in
        gathered = take(1)[0] if late else head_out[0]
        part_copies = [
            remote(pair_other.at[k], arrived_kv.at[k], part_send.at[k], part_recv.at[k], p)
            for k, p in enumerate(part_peers)
        ]
        kv_load = pltpu.make_async_copy(pair_mine, mine_kv, head_local.at[0])
        for copy in part_copies + [kv_load]:
            copy.start()
    if n_small:
        small_send, small_recv, small_sc = take(3)
        small = small_in[0]
    if masked:
        w_v, x_v, y_v, masked_sem = take(4)
        w_masked_load = pltpu.make_async_copy(w_masked, w_v, masked_sem.at[0])
        w_masked_load.start()
        windows, fine = masked_o.shape[:2]
        tile = x_v.shape[0]

        def masked_product(k):
            w, at = divmod(k * tile, fine)
            load = pltpu.make_async_copy(terms[0].at[pl.ds(k * tile, tile)], x_v, masked_sem.at[1])
            load.start()
            load.wait()
            if k == 0:
                w_masked_load.wait()
            made = dot(x_v[...], w_v[...])
            bin_ = seq * (fine // 2) + lax.div(
                at + lax.broadcasted_iota(jnp.int32, made.shape, 0), 2
            )
            y_v[...] = jnp.where(bin_ < lengths[w], made, 0.0).astype(BF)
            store = pltpu.make_async_copy(
                y_v, masked_o.at[w, pl.ds(at, tile)], masked_sem.at[2]
            )
            store.start()
            store.wait()

    if late:
        small, w_buffer, acc, flat_v, middle_v, out_v, gain_sum, late_sem = take(8)
        w_loads = [
            pltpu.make_async_copy(w_query, w_buffer.at[:, pl.ds(0, H * KD)], late_sem.at[0]),
            pltpu.make_async_copy(w_key, w_buffer.at[:, pl.ds(H * KD, H * KD)], late_sem.at[1]),
        ]
        for copy in w_loads:
            copy.start()

        def window_loads(w):
            span = pl.ds(w * flat_v.shape[0], flat_v.shape[0])
            return [
                pltpu.make_async_copy(values.at[w], flat_v, late_sem.at[2]),
                pltpu.make_async_copy(middle_grad.at[span], middle_v, late_sem.at[3]),
            ]

        def store_window(w):
            span = pl.ds(w * flat_v.shape[0], flat_v.shape[0])
            return pltpu.make_async_copy(out_v, input_grad.at[span], late_sem.at[4])

        for copy in window_loads(0):
            copy.start()

        def back_through(w_ref, first, columns, into_first):
            packed = rights[(n_terms - 1) % 2]

            @pl.loop(0, acc.shape[0] // 128)
            def _(k):
                rows = pl.ds(pl.multiple_of(k * 128, 128), 128)
                made = lax.dot_general(
                    packed[rows, first : first + columns],
                    w_ref[:, 0:columns],
                    (((1,), (1,)), ((), ())),
                    preferred_element_type=F32,
                )
                acc[rows, :] = made if into_first else acc[rows, :] + made

        def value_load(k):
            half = H * VD // 2
            return pltpu.make_async_copy(
                w_value.at[:, pl.ds(k * half, half)],
                w_buffer.at[:, pl.ds(0, half)],
                late_sem.at[5 + k],
            )

        def products(stage):
            half = H * VD // 2
            if stage == 0:
                for copy in w_loads:
                    copy.wait()
                back_through(w_buffer, 0, 2 * H * KD, True)
                value_load(0).start()
            else:
                value_load(0).wait()
                back_through(w_buffer, 2 * H * KD, half, False)
                value_load(1).start()
                value_load(1).wait()
                back_through(w_buffer, 2 * H * KD + half, half, False)

        def norm_back(w):
            for copy in window_loads(w):
                copy.wait()
            if w:
                store_window(w - 1).wait()
            else:
                gain_sum[...] = jnp.zeros(gain_sum.shape, F32)
            size = flat_v.shape[0]

            @pl.loop(0, size // 32)
            def _(k):
                rows = pl.ds(pl.multiple_of(k * 32, 32), 32)
                value = flat_v[rows, :].astype(F32)
                centered = value - jnp.mean(value, axis=-1, keepdims=True)
                scale = lax.rsqrt(jnp.mean(centered * centered, axis=-1, keepdims=True) + epsilon)
                unit = centered * scale
                grad = acc[pl.ds(pl.multiple_of(w * size + k * 32, 32), 32), :]
                gain_sum[...] += jnp.sum(grad * unit, axis=0, keepdims=True)
                grad = grad * gain[...]
                along = jnp.mean(grad * unit, axis=-1, keepdims=True)
                back = scale * (grad - jnp.mean(grad, axis=-1, keepdims=True) - unit * along)
                out_v[rows, :] = (middle_v[rows, :] + back).astype(BF)

            store_window(w).start()
            if w + 1 < values.shape[0]:
                for copy in window_loads(w + 1):
                    copy.start()
            else:
                rows = dot32(pick[...] * gain_sum[...], spread[...].astype(F32), ((1,), (1,)))
                wide = small_in[0].shape[1]
                small[:, :wide, :] = small_in[0][...]
                small[:, wide:, :] = jnp.broadcast_to(
                    rows[:, None, :], (rows.shape[0], 8, rows.shape[1])
                )

    if n_small:

        def small_copy(k):
            there = lax.rem(me + k, n_small)
            return remote(
                small.at[there],
                small_sc.at[k - 1],
                small_send.at[k - 1],
                small_recv.at[k - 1],
                other_device(k),
            )

        def start_small():
            @pl.loop(1, n_small)
            def _(k):
                small_copy(k).start()

        if not late:
            start_small()

    ahead = 3
    for step in range(min(ahead, len(groups))):
        launch(step)
    if mode == "out":
        for copy in part_copies:
            copy.wait_recv()
        kv_load.wait()

        @pl.loop(0, H)
        def _(g):
            total = mine_kv[g].astype(F32)
            for k in range(parts - 1):
                total = total + arrived_kv[k, g].astype(F32)
            mine_kv[g] = total.astype(BF)

        q_target = gathered.at[head, :, pl.ds(0, KD)]
        kv_target = gathered.at[head, :, pl.ds(KD, KD + VD)]
        head_copies = [
            remote(source.at[h], target, head_send.at[i, k], head_recv.at[i, k], p)
            for k, (h, p) in enumerate(zip(head_of, head_peers, strict=True))
            for i, (source, target) in enumerate(((query, q_target), (mine_kv, kv_target)))
        ]
        head_own = [
            pltpu.make_async_copy(query.at[head], q_target, head_local.at[1]),
            pltpu.make_async_copy(mine_kv.at[head], kv_target, head_local.at[2]),
        ]
        for copy in head_copies + head_own:
            copy.start()
    lag = 2
    for step in range(len(groups) + 4 * lag):
        for stage in (5, 4, 3, 2, 1):
            spot = step - lag * (stage - 1)
            if 0 <= spot < len(groups):
                for n in numbers[spot]:
                    if stage == 1 and not made_here:
                        load(n).wait()
                    for copy in hops[stage - 1](n):
                        copy.wait_recv()
                    absorb(n, stage)
                    if stage < 5:
                        for copy in hops[stage](n):
                            copy.start()
        if step + ahead < len(groups):
            launch(step + ahead)
        if masked and 0 <= step - (len(groups) - ahead) < terms[0].shape[0] // tile:
            masked_product(step - (len(groups) - ahead))
        if late and step >= len(groups) - ahead:
            turn = step - (len(groups) - ahead)
            if turn < 2:
                products(turn)
            elif turn < 2 + values.shape[0]:
                norm_back(turn - 2)
                if turn == 1 + values.shape[0]:
                    start_small()
    if n_small:

        @pl.loop(1, n_small)
        def _(k):
            small_copy(k).wait_recv()

        small_out[0][...] = small[me] + jnp.sum(small_sc[...], axis=0)

        @pl.loop(1, n_small)
        def _(k):
            small_copy(k).wait_send()

    if late:
        store_window(values.shape[0] - 1).wait()
    if mode:
        if not late:
            for copy in head_own:
                copy.wait()
            for copy in head_copies:
                copy.wait_recv()
        for copy in head_copies:
            copy.wait_send()
    if mode == "out":
        for copy in part_copies:
            copy.wait_send()
    for n in range(count):
        for hop in hops:
            if hop is not over_core or not made_here or n in tuple(numbers[-1]) + tuple(numbers[-2]):
                for copy in hop(n):
                    copy.wait_send()


def sum_terms(name, collective, pairs, groups, mode=None, heads=(), small=None, late=None, masked=None):
    ndp, nseq = lax.axis_size("dp"), lax.axis_size("seq")
    nhi, parts, devices = nseq // 4, nseq // H, ndp * nseq
    shares = [(left.shape[1] // devices, right.shape[1]) for left, right in pairs]
    made_here = all(rows % 16 == 0 for rows, _ in shares)
    if made_here:
        operands = [x for pair in pairs for x in pair][: -1 if late else None]
    else:
        operands = [
            transposed_times(left, right).astype(BF).reshape((ndp, nhi, 2, 2) + share)
            for (left, right), share in zip(pairs, shares, strict=True)
        ]
    in_specs = [pl.BlockSpec(memory_space=pl.ANY)] * len(operands)
    out_shape = [jax.ShapeDtypeStruct(share, F32) for share in shares]
    out_specs = [pl.BlockSpec(memory_space=pltpu.VMEM)] * len(out_shape)
    flat = [(side, unit) for group in groups for side in (0, 1) for unit in group[side]]
    count = len(flat)
    shapes = [(unit[2], unit[4]) for _, unit in flat]
    sides = [side for side, _ in flat]
    scratch = [pltpu.VMEM((ndp, nhi, 2, 2) + s, BF) for s in shapes] * 2
    scratch += [
        pltpu.VMEM(((ndp, nhi, 2) if side else (ndp - 1, nhi, 2, 2)) + s, BF)
        if not side
        else pltpu.VMEM((ndp, nhi, 2) + s, BF)
        for side, s in zip(sides, shapes, strict=True)
    ]
    scratch += [
        pltpu.VMEM((ndp - 1, nhi, 2) + s if side else (nhi, 2) + s, BF)
        for side, s in zip(sides, shapes, strict=True)
    ]
    scratch += [pltpu.VMEM((nhi - 1, 2) + s, BF) for s in shapes]
    scratch += [pltpu.VMEM((2,) + s, F32) for s in shapes]
    scratch += [pltpu.VMEM(s, F32) for s in shapes]
    if made_here:
        slots = [pairs[k::2] for k in range(min(2, len(pairs)))]
        tokens = [max(left.shape[0] for left, _ in slot) for slot in slots]
        tall = [max(left.shape[1] for left, _ in slot) for slot in slots]
        wide = [max(right.shape[1] for _, right in slot) for slot in slots]
        unit_rows = max(rows for rows, _ in shapes)
        unit_columns = max(columns for _, columns in shapes)
        scratch += [
            pltpu.VMEM((max(tokens), max(tall)), BF),
            *[pltpu.VMEM(s, BF) for s in zip(tokens, wide, strict=True)],
            *[pltpu.VMEM(s, BF) for s in zip(tall, tokens, strict=True)],
            pltpu.VMEM((2, 2, ndp, nhi, 2, 2, unit_rows, unit_columns), BF),
            pltpu.SemaphoreType.DMA((len(pairs),)),
            pltpu.SemaphoreType.DMA((len(pairs),)),
        ]
    hop = max(ndp - 1, 1)
    sizes = [(count,)] * 3 + [(count, hop)] * 4 + [(count, nhi - 1)] * 2 + [(count,)] * 2
    scratch += [pltpu.SemaphoreType.DMA(size) for size in sizes]
    if mode in ("in", "back"):
        windows = heads[0].shape[0 if mode == "in" else 1]
        size, rows = heads[0].shape[2:]
        operands.append(heads[0])
        in_specs.append(pl.BlockSpec(memory_space=pl.ANY))
        out_shape.append(jax.ShapeDtypeStruct((H, windows, size, rows), BF))
        out_specs.append(pl.BlockSpec(memory_space=pl.ANY))
        scratch += [pltpu.SemaphoreType.DMA((n,)) for n in (H - 1, H - 1, 1)]
    if mode == "out":
        _, windows, _, rows = heads[0].shape
        operands += list(heads)
        in_specs += [pl.BlockSpec(memory_space=pl.ANY)] * 3
        if not late:
            out_shape.append(jax.ShapeDtypeStruct((H, windows, 2 * KD + VD, rows), BF))
            out_specs.append(pl.BlockSpec(memory_space=pl.ANY))
        scratch += [
            pltpu.SemaphoreType.DMA(size)
            for size in ((2, H - 1), (2, H - 1), (3,), (parts - 1,), (parts - 1,))
        ]
        scratch += [pltpu.VMEM(heads[1].shape, BF), pltpu.VMEM(heads[2].shape, BF)]
        if late:
            scratch.append(pltpu.VMEM((H, windows, 2 * KD + VD, rows), BF))
    n_small = 0
    if small is not None:
        n_small = devices
        operands.append(small)
        in_specs.append(pl.BlockSpec(memory_space=pltpu.VMEM))
        message = (small.shape[1] + (8 if late else 0), small.shape[2])
        out_shape.append(jax.ShapeDtypeStruct(message, F32))
        out_specs.append(pl.BlockSpec(memory_space=pltpu.VMEM))
        scratch += [
            pltpu.SemaphoreType.DMA((devices - 1,)),
            pltpu.SemaphoreType.DMA((devices - 1,)),
            pltpu.VMEM((devices - 1,) + message, F32),
        ]
    if late:
        windows, rows, width = late[3].shape
        operands += list(late) + list(spread_tables(width, width // devices))
        in_specs += [pl.BlockSpec(memory_space=pl.ANY)] * 5
        in_specs += [pl.BlockSpec(memory_space=pltpu.VMEM)] * 3
        out_shape.append(jax.ShapeDtypeStruct((windows * rows, width), BF))
        out_specs.append(pl.BlockSpec(memory_space=pl.ANY))
        scratch += [
            pltpu.VMEM((devices,) + message, F32),
            pltpu.VMEM((width, 2 * H * KD), BF),
            pltpu.VMEM((windows * rows, width), F32),
            pltpu.VMEM((rows, width), BF),
            pltpu.VMEM((rows, width), F32),
            pltpu.VMEM((rows, width), BF),
            pltpu.VMEM((1, width), F32),
            pltpu.SemaphoreType.DMA((7,)),
        ]
    if masked:
        lengths, weight, shape = masked
        operands += [lengths, weight]
        in_specs += [pl.BlockSpec(memory_space=pltpu.SMEM), pl.BlockSpec(memory_space=pl.ANY)]
        out_shape.append(jax.ShapeDtypeStruct(shape, BF))
        out_specs.append(pl.BlockSpec(memory_space=pl.ANY))
        scratch += [
            pltpu.VMEM(weight.shape, BF),
            pltpu.VMEM((256, shape[2]), BF),
            pltpu.VMEM((256, shape[2]), BF),
            pltpu.SemaphoreType.DMA((3,)),
        ]
    plan = (
        groups, len(pairs), mode, parts, n_small, made_here, late is not None, masked is not None
    )
    return pl.pallas_call(
        functools.partial(sums_kernel, plan, None),
        out_shape=out_shape,
        in_specs=in_specs,
        out_specs=out_specs,
        scratch_shapes=scratch,
        compiler_params=pltpu.CompilerParams(
            collective_id=collective, has_side_effects=True, vmem_limit_bytes=63 * 2**20
        ),
        name=name,
    )(*operands)


def halves(array, rows, columns, size=128):
    out, spot = [], 0
    while spot < columns:
        size = min(size, (columns - spot) // 2)
        out.append((((array, 0, rows, spot, size),), ((array, 0, rows, spot + size, size),)))
        spot += 2 * size
    return tuple(out)


def full(array, shards):
    rows, columns = shards[array].shape
    return (array, 0, rows, 0, columns)


def columns_of_rows(array, rows, first, columns):
    return (array, 0, rows, first, columns)


def gelu_parts(x):
    below = 0.5 * (1.0 + lax.erf(x * (0.5**0.5)))
    density = jnp.exp(-0.5 * x * x) * (1.0 / math.sqrt(2.0 * math.pi))
    return x * below, below + x * density


def norm_parts(value):
    centered = value - jnp.mean(value, axis=-1, keepdims=True)
    scale = lax.rsqrt(jnp.mean(centered * centered, axis=-1, keepdims=True) + epsilon)
    return centered * scale, scale


def norm_backward(unit, scale, grad, gain):
    grad = grad * gain
    along = jnp.mean(grad * unit, axis=-1, keepdims=True)
    return scale * (grad - jnp.mean(grad, axis=-1, keepdims=True) - unit * along)


def times_rows(x, table):
    return lax.dot_general(x, table, (((1,), (1,)), ((), ())), preferred_element_type=F32)


def block_kernel(
    values, arrived, third_grad, w_mixing, w_inner, w_outer,
    second_gain, third_gain, inner_bias, outer_bias,
    mixed_o, second_o, hidden_o, third_o, block_o, before_o, middle_o, middle_grad_o, mixed_grad_o,
    second_sum, third_sum, inner_sum, outer_sum,
    mixing_v, inner_v, outer_v, middle_v, block_v, slope_v, sem,
):
    first = pl.program_id(0) == 0
    rows, width = middle_v.shape
    wide = slope_v.shape[1]
    tile = 512
    loads = [
        pltpu.make_async_copy(source, target, sem.at[k])
        for k, (source, target) in enumerate(
            ((w_mixing, mixing_v), (w_inner, inner_v), (w_outer, outer_v))
        )
    ]

    @pl.when(first)
    def _():
        for load in loads:
            load.start()
        for total in (second_sum, third_sum, inner_sum, outer_sum):
            total[...] = jnp.zeros(total.shape, F32)

    def ready(k):
        @pl.when(first)
        def _():
            loads[k].wait()

    for pair in range(H // 2):
        both = jnp.concatenate([arrived[2 * pair + h, 0] for h in range(2)], axis=0)
        mixed_o[:, pair * 2 * VD : (pair + 1) * 2 * VD] = both.T
    ready(0)
    for k in range(0, width, tile):
        cols = slice(k, k + tile)
        middle_v[:, cols] = values[0][:, cols].astype(F32) + dot(mixed_o[...], mixing_v[:, cols])

    chunk = 32

    @pl.loop(0, rows // chunk)
    def _(k):
        at = pl.ds(pl.multiple_of(k * chunk, chunk), chunk)
        unit, _ = norm_parts(middle_v[at, :])
        second_o[at, :] = (unit * second_gain[...]).astype(BF)

    ready(1)
    for k in range(0, wide, tile):
        cols = slice(k, k + tile)
        before = dot(second_o[...], inner_v[:, cols]) + inner_bias[:, cols]
        hidden, slope = gelu_parts(before)
        hidden_o[:, cols] = hidden.astype(BF)
        slope_v[:, cols] = slope.astype(BF)
    ready(2)
    for k in range(0, width, tile):
        cols = slice(k, k + tile)
        block_v[:, cols] = (
            middle_v[:, cols] + dot(hidden_o[...], outer_v[:, cols]) + outer_bias[:, cols]
        )

    @pl.loop(0, rows // chunk)
    def _(k):
        at = pl.ds(pl.multiple_of(k * chunk, chunk), chunk)
        unit, scale = norm_parts(block_v[at, :])
        third, slope = gelu_parts(unit * third_gain[...])
        third_o[at, :] = third.astype(BF)
        grad = third_grad[at, :] * slope
        third_sum[...] += jnp.sum(grad * unit, axis=0, keepdims=True)
        back = norm_backward(unit, scale, grad, third_gain[...])
        outer_sum[...] += jnp.sum(back, axis=0, keepdims=True)
        block_v[at, :] = back
        block_o[at, :] = back.astype(BF)

    for k in range(0, wide, tile):
        cols = slice(k, k + tile)
        grad = times_rows(block_o[...], outer_v[cols, :]) * slope_v[:, cols].astype(F32)
        low = grad.astype(BF)
        before_o[:, cols] = low
        inner_sum[:, cols] += jnp.sum(low.astype(F32), axis=0, keepdims=True)
    for k in range(0, width, tile):
        cols = slice(k, k + tile)
        middle_grad_o[:, cols] = times_rows(before_o[...], inner_v[cols, :])

    @pl.loop(0, rows // chunk)
    def _(k):
        at = pl.ds(pl.multiple_of(k * chunk, chunk), chunk)
        unit, scale = norm_parts(middle_v[at, :])
        grad = middle_grad_o[at, :]
        second_sum[...] += jnp.sum(grad * unit, axis=0, keepdims=True)
        back = block_v[at, :] + norm_backward(unit, scale, grad, second_gain[...])
        middle_grad_o[at, :] = back
        middle_o[at, :] = back.astype(BF)

    for pair in range(H // 2):
        cols = slice(pair * 2 * VD, (pair + 1) * 2 * VD)
        turned = times_rows(middle_o[...], mixing_v[cols, :]).astype(BF).T
        for h in range(2):
            mixed_grad_o[0, 2 * pair + h] = turned[h * VD : (h + 1) * VD]


def block_pass(values, arrived, third_grad, weights, gains, biases):
    windows, rows, width = values.shape
    wide = weights[1].shape[1]

    def by_rows(columns):
        return pl.BlockSpec((rows, columns), lambda w: (w, 0))

    def line(columns):
        return pl.BlockSpec((1, columns), lambda w: (0, 0))

    narrow = jax.ShapeDtypeStruct((windows * rows, width), BF)
    broad = jax.ShapeDtypeStruct((windows * rows, wide), BF)
    sums = [jax.ShapeDtypeStruct((1, n), F32) for n in (width, width, wide, width)]
    any_space = pl.BlockSpec(memory_space=pl.ANY)
    return pl.pallas_call(
        block_kernel,
        grid=(windows,),
        out_shape=[
            narrow, narrow, broad, narrow, narrow, broad, narrow,
            jax.ShapeDtypeStruct((windows * rows, width), F32),
            jax.ShapeDtypeStruct((windows, H, VD, rows), BF),
            *sums,
        ],
        in_specs=[
            pl.BlockSpec((1, rows, width), lambda w: (w, 0, 0)),
            pl.BlockSpec((H, 1, VD, rows), lambda w: (0, w, 0, 0)),
            by_rows(width),
            any_space, any_space, any_space,
            line(width), line(width), line(wide), line(width),
        ],
        out_specs=[
            by_rows(width), by_rows(width), by_rows(wide), by_rows(width), by_rows(width),
            by_rows(wide), by_rows(width), by_rows(width),
            pl.BlockSpec((1, H, VD, rows), lambda w: (w, 0, 0, 0)),
            line(width), line(width), line(wide), line(width),
        ],
        scratch_shapes=[
            *[pltpu.VMEM(w.shape, BF) for w in weights],
            pltpu.VMEM((rows, width), F32),
            pltpu.VMEM((rows, width), F32),
            pltpu.VMEM((rows, wide), BF),
            pltpu.SemaphoreType.DMA((3,)),
        ],
        compiler_params=pltpu.CompilerParams(vmem_limit_bytes=62 * 2**20),
        name="block_pass",
    )(values, arrived, third_grad, *weights, *gains, *biases)


def weight_pairs(shapes, offset):
    def pieces(n, parts):
        rows, columns = shapes[n]
        if rows % (16 * parts):
            return [(offset + n, 0, rows, 0, columns)]
        size = rows // parts
        return [(offset + n, k * size, size, 0, columns) for k in range(parts)]

    first = pieces(5, 3) + pieces(0, 3) + pieces(4, 3) + pieces(2, 3)
    second = pieces(1, 3) + pieces(3, 6)
    steps = max(len(second), 1)
    spare = len(first) - steps
    pairs, spot = [], 0
    for k in range(steps):
        take = 2 if 3 <= k < 3 + spare else 1
        pairs.append((tuple(first[spot : spot + take]), (second[k],)))
        spot += take
    if spot < len(first):
        pairs.append((tuple(first[spot:]), ()))
    return tuple(pairs)


def on_device(
    inputs,
    skip_input,
    lengths,
    cotangent,
    first_gain,
    query_weight,
    key_weight,
    value_weight,
    content_bias,
    position_bias,
    relative_weight,
    mixing_weight,
    second_gain,
    inner_weight,
    inner_bias,
    outer_weight,
    outer_bias,
    third_gain,
    upsample_weight,
    skip_weight,
    skip_bias,
    depth_weight,
    point_weight,
):
    windows, rows, width = inputs.shape
    scale = float(KD) ** (-0.5)
    nseq, ndp = lax.axis_size("seq"), lax.axis_size("dp")
    devices = nseq * ndp
    parts = nseq // H
    keys_total = rows * nseq
    seq = lax.axis_index("seq")
    head, part = lax.div(seq, parts), lax.rem(seq, parts)
    first = seq * rows
    hidden_width = inner_weight.shape[1]

    r = shard_rows = query_weight.shape[0]
    vectors = (
        first_gain,
        content_bias,
        position_bias,
        second_gain,
        inner_bias,
        outer_bias,
        third_gain,
        skip_bias,
    )
    small_rows = [v.reshape(1, -1) for v in vectors] + [depth_weight.T]
    small_rows = [jnp.pad(v, ((0, 0), (0, 128 - v.shape[1]))) for v in small_rows]
    small_rows.append(jnp.zeros((16 - len(vectors) - 3, 128), BF))
    relative_rows = relative_weight.shape[0]
    small_rows.append(
        jnp.pad(relative_weight, ((0, -relative_rows % 16), (0, 128 - relative_weight.shape[1])))
    )
    small_shard = jnp.concatenate(small_rows, axis=0)
    keys_width, values_width = 2 * H * KD, H * VD
    half_hidden, half_width = hidden_width // 2, width // 2
    head_shards = [small_shard, query_weight, key_weight, value_weight]
    head_pairs = (
        ((full(0, head_shards), full(1, head_shards)), (full(2, head_shards),)),
        ((columns_of_rows(3, r, 0, values_width // 2),), (columns_of_rows(3, r, values_width // 2, values_width // 2),)),
    )
    shards = [
        skip_weight,
        mixing_weight,
        inner_weight,
        outer_weight,
        upsample_weight,
        point_weight,
    ]
    if r % 16 == 0:
        (
            small_full,
            weight_query,
            weight_key,
            weight_value,
            weight_skip,
            weight_mixing,
            weight_inner,
            weight_outer,
            weight_upsample,
            weight_point,
            mine,
            other,
            normed_low,
            out_grad,
            conv_grad,
            joined_flat,
            lifted_grad,
            third_grad,
            skip_grad,
            skip_part,
            grad_skip_bias,
        ) = use_links(
            "gather_weights",
            1,
            head_shards + shards,
            head_pairs + weight_pairs([w.shape for w in shards], len(head_shards)),
            values=inputs,
            early=len(head_pairs),
            upper=(lengths, cotangent, skip_input),
        )
        out_grad, joined_flat, skip_part = (
            x.reshape(-1, width) for x in (out_grad, joined_flat, skip_part)
        )
        grad_skip_bias = grad_skip_bias[0]
    else:
        small_full, weight_query, weight_key, weight_value = use_links(
            "gather_heads", 1, head_shards, head_pairs
        )
    small_full = small_full.reshape((devices,) + small_shard.shape).astype(jnp.float32)

    def vector(k):
        return small_full[:, k, : vectors[k].shape[0]].reshape(-1)

    (
        gain_first,
        bias_content,
        bias_position,
        gain_second,
        bias_inner,
        bias_outer,
        gain_third,
        bias_skip,
    ) = map(vector, range(len(vectors)))
    taken = len(vectors)
    weight_depth = (
        small_full[:, taken : taken + 3, :r].transpose(0, 2, 1).reshape(width, 3)
    )
    weight_relative = small_full[:, 16 : 16 + relative_rows, :RPF].reshape(H * KD, RPF)

    lives = jnp.exp(
        jnp.linspace(math.log(3.0), math.log(keys_total), RPF // 2, dtype=jnp.float32)
    )
    rates = (math.log(2.0) / lives)[:, None]
    bias_gap = ((bias_position - bias_content) * scale).reshape(H, KD, 1)
    bias_gap = lax.dynamic_index_in_dim(bias_gap, head, 0, keepdims=False)
    relative = lax.dynamic_index_in_dim(
        weight_relative.reshape(H, KD, RPF), head, 0, keepdims=False
    ).T
    info = jnp.concatenate([lengths, part[None].astype(jnp.int32)])
    groups = [[p + parts * g for g in range(H)] for p in range(parts)]

    def exchange(array):
        return lax.all_to_all(array, "seq", 0, 0, axis_index_groups=groups, tiled=True)

    def swap_part(array, slot):
        return lax.ppermute(array, "seq", [(i, i ^ slot) for i in range(nseq)])

    flat = inputs.reshape(windows * rows, width).astype(jnp.float32)
    if r % 16:
        normed_low, sent = project(
            inputs, gain_first, bias_content, weight_query, weight_key, weight_value
        )
        (
            weight_skip,
            weight_mixing,
            weight_inner,
            weight_outer,
            weight_upsample,
            weight_point,
            mine,
            other,
        ) = use_links(
            "gather_weights", 2, shards, weight_pairs([w.shape for w in shards], 0), sent
        )

    def by_row(array):
        (array,) = tie(array.transpose(1, 3, 0, 2).reshape(windows * rows, -1))
        return array

    mixed_own, mixed_wide, log_total = attention_forward(
        info, rates, bias_gap, relative, mine, other, parts
    )
    if r % 16 == 0:
        skip_flat = skip_input.reshape(windows * 2 * rows, width)
        own_skip, mixed_arrived = sum_terms(
            "sum_skip",
            6,
            [(skip_flat, joined_flat)],
            halves(0, r, half_width),
            "back",
            (mixed_own,),
        )
    else:
        mixed_arrived = exchange(mixed_own)
    if r % 16 == 0:
        (
            mixed_low,
            second_low,
            hidden_low,
            third_low,
            block_low,
            before_low,
            middle_low,
            middle_grad,
            mixed_grad,
            *block_sums,
        ) = block_pass(
            inputs,
            mixed_arrived,
            third_grad,
            (weight_mixing, weight_inner, weight_outer),
            (gain_second[None, :], gain_third[None, :]),
            (bias_inner[None, :], bias_outer[None, :]),
        )
        grad_second, grad_third, grad_inner_bias, grad_outer_bias = (s[0] for s in block_sums)
    else:
        mixed_low = by_row(mixed_arrived)
        middle = flat + matmul(mixed_low, weight_mixing)
        second, second_norm_back = jax.vjp(layer_norm, middle, gain_second)
        second_low = second.astype(jnp.bfloat16)
        before = matmul(second_low, weight_inner) + bias_inner
        hidden, gelu_back = jax.vjp(smooth_gelu, before)
        hidden_low = hidden.astype(jnp.bfloat16)
        block_out = middle + matmul(hidden_low, weight_outer) + bias_outer
        third, third_back = jax.vjp(norm_gelu, block_out, gain_third)
        third_low = third.astype(jnp.bfloat16)
    fine = jnp.arange(2 * rows, dtype=jnp.int32)[:, None] // 2
    twice = (fine == jnp.arange(rows, dtype=jnp.int32)[None, :]).astype(jnp.bfloat16)
    third_twice = (
        jnp.einsum(
            "ts,wsd->wtd",
            twice,
            third_low.reshape(windows, rows, width),
            preferred_element_type=jnp.float32,
        )
        .astype(jnp.bfloat16)
        .reshape(windows * 2 * rows, width)
    )
    skip_flat = skip_input.reshape(windows * 2 * rows, width)
    if r % 16:
        skip_part = matmul(skip_flat, weight_skip) + bias_skip
    joined_low = (
        (matmul(third_twice, weight_upsample) + skip_part)
        .astype(jnp.bfloat16)
        .reshape(windows, 2 * rows, width)
    )
    joined_rim = extended_2(joined_low, (("seq", 1),), 1)
    taps = weight_depth
    joined_wide = joined_rim.astype(jnp.float32)
    conv_low = depth_apply(joined_wide, taps).astype(jnp.bfloat16)
    conv_flat = conv_low.reshape(windows * 2 * rows, width)
    bins = 2 * first + jnp.arange(2 * rows, dtype=jnp.int32)
    keep = (bins // 2)[None, :] < lengths[:, None]
    keep_wide = keep.astype(jnp.float32)[:, :, None]
    if r % 16:
        outputs = (
            matmul(conv_flat, weight_point).reshape(windows, 2 * rows, width) * keep_wide
        ).astype(jnp.bfloat16)
    if r % 16:
        out_grad = (cotangent * keep.astype(jnp.bfloat16)[:, :, None]).reshape(
            windows * 2 * rows, width
        )
        conv_grad = (
            times_transposed(out_grad, weight_point)
            .astype(jnp.bfloat16)
            .reshape(windows, 2 * rows, width)
        )
        grad_rim = extended_2(conv_grad, (("seq", 1),), 1).astype(jnp.float32)
        joined_grad = (
            grad_rim[:, 2:] * taps[:, 0]
            + grad_rim[:, 1:-1] * taps[:, 1]
            + grad_rim[:, :-2] * taps[:, 2]
        )
        grad_skip_bias = jnp.sum(joined_grad, axis=(0, 1))
        joined_back = joined_grad.astype(jnp.bfloat16)
        joined_flat = joined_back.reshape(windows * 2 * rows, width)
        lifted_grad = (
            jnp.einsum("ts,wtd->wsd", twice, joined_back, preferred_element_type=jnp.float32)
            .astype(jnp.bfloat16)
            .reshape(windows * rows, width)
        )
        third_grad = times_transposed(lifted_grad, weight_upsample)
        skip_grad = (
            times_transposed(joined_flat, weight_skip)
            .astype(jnp.bfloat16)
            .reshape(windows, 2 * rows, width)
        )
    conv_wide = conv_grad.astype(jnp.float32)
    grad_depth = jnp.stack(
        [
            jnp.sum(conv_wide * joined_wide[:, :-2], axis=(0, 1)),
            jnp.sum(conv_wide * joined_wide[:, 1:-1], axis=(0, 1)),
            jnp.sum(conv_wide * joined_wide[:, 2:], axis=(0, 1)),
        ],
        axis=1,
    )
    if r % 16:
        block_grad, grad_third = third_back(third_grad)
        block_low = block_grad.astype(jnp.bfloat16)
        grad_outer_bias = jnp.sum(block_grad, axis=0)
        (before_grad,) = gelu_back(times_transposed(block_low, weight_outer))
        before_low = before_grad.astype(jnp.bfloat16)
        grad_inner_bias = jnp.sum(before_low.astype(jnp.float32), axis=0)
        middle_part, grad_second = second_norm_back(times_transposed(before_low, weight_inner))
        middle_grad = block_grad + middle_part
        middle_low = middle_grad.astype(jnp.bfloat16)
        middle_rows = middle_low.reshape(windows, rows, width)
        mixed_grad = (
            jnp.einsum("vd,wrd->wvr", weight_mixing, middle_rows, preferred_element_type=jnp.float32)
            .astype(jnp.bfloat16)
            .reshape(windows, H, VD, rows)
        )
    if r % 16 == 0:
        own_point, own_outer, own_upsample, arrived_grad, outputs = sum_terms(
            "sum_upper",
            3,
            [(conv_flat, out_grad), (hidden_low, block_low), (third_low, lifted_grad)],
            halves(0, r, half_width)
            + halves(1, outer_weight.shape[0], half_width)
            + halves(2, r, half_width),
            "in",
            (mixed_grad,),
            masked=(lengths, weight_point, skip_input.shape),
        )
    else:
        own_point, own_outer, own_skip, own_upsample, arrived_grad = sum_terms(
            "sum_upper",
            3,
            [
                (conv_flat, out_grad),
                (hidden_low, block_low),
                (skip_flat, joined_flat),
                (third_low, lifted_grad),
            ],
            halves(0, r, half_width)
            + halves(1, outer_weight.shape[0], half_width)
            + halves(2, r, half_width)
            + halves(3, r, half_width),
            "in",
            (mixed_grad,),
        )
    query_own, own_side, other_side, bias_sums, relative_sum = attention_backward(
        info, rates, bias_gap, relative, mine, other, arrived_grad, mixed_wide, log_total, parts
    )

    def at_head(value):
        full = jnp.zeros((H,) + value.shape, jnp.float32)
        return lax.dynamic_update_index_in_dim(full, value, head, 0)

    pieces = [
        at_head(bias_sums[0, :, 0]).reshape(-1),
        at_head(bias_sums[1, :, 0]).reshape(-1),
        at_head(relative_sum).reshape(H * KD, RPF),
        grad_second,
        grad_inner_bias,
        grad_outer_bias,
        grad_third,
        grad_skip_bias,
        grad_depth,
    ]

    def pack(pieces):
        packed = jnp.concatenate([p.reshape(devices, -1) for p in pieces], axis=1)
        return jnp.pad(packed, ((0, 0), (0, -packed.shape[1] % 1024))).reshape(devices, -1, 128)

    lower = [(second_low, before_low), (mixed_low, middle_low)]
    lower_groups = halves(0, r, half_hidden) + halves(1, r, half_width)
    lower_heads = (query_own, own_side, other_side)
    packed_width = keys_width + values_width
    if r % 16 == 0:
        right = jax.ShapeDtypeStruct((windows * rows, packed_width), BF)
        own_inner, own_mixing, own_heads, small_total, input_grad = sum_terms(
            "sum_lower",
            4,
            lower + [(normed_low, right)],
            lower_groups + halves(2, r, packed_width // 2),
            "out",
            lower_heads,
            pack(pieces),
            (weight_query, weight_key, weight_value, inputs, middle_grad, gain_first[None, :]),
        )
        own_first = small_total[-8, : width // devices]
        input_grad = input_grad.reshape(windows, rows, width)
        names = pieces
    else:
        own_inner, own_mixing, heads_grad = sum_terms(
            "sum_lower", 4, lower, lower_groups, "out", lower_heads
        )
        packed_grad = jnp.concatenate(
            [
                by_row(heads_grad[:, :, :KD]),
                by_row(heads_grad[:, :, KD : 2 * KD]),
                by_row(heads_grad[:, :, 2 * KD :]),
            ],
            axis=1,
        )
        (packed_grad,) = tie(packed_grad)
        normed_grad = (
            times_transposed(packed_grad[:, : H * KD], weight_query)
            + times_transposed(packed_grad[:, H * KD : keys_width], weight_key)
            + times_transposed(packed_grad[:, keys_width:], weight_value)
        )
        _, first_norm_back = jax.vjp(layer_norm, flat, gain_first)
        input_part, grad_first = first_norm_back(normed_grad)
        input_grad = (middle_grad + input_part).astype(jnp.bfloat16).reshape(windows, rows, width)
        names = [grad_first] + pieces
        own_heads, small_total = sum_terms(
            "sum_heads",
            5,
            [(normed_low, packed_grad)],
            halves(0, r, packed_width // 2),
            small=pack(names),
        )
    small_total, spot, small_grads = small_total.reshape(-1), 0, []
    for p in names:
        size = p.size // devices
        small_grads.append(
            small_total[spot : spot + size].reshape((p.shape[0] // devices,) + p.shape[1:])
        )
        spot += size
    if len(names) > len(pieces):
        own_first = small_grads.pop(0)
    (
        own_content,
        own_position,
        own_relative,
        own_second,
        own_inner_bias,
        own_outer_bias,
        own_third,
        own_skip_bias,
        own_depth,
    ) = small_grads
    return (
        outputs,
        input_grad,
        skip_grad,
        own_first,
        own_heads[:, : H * KD],
        own_heads[:, H * KD : keys_width],
        own_heads[:, keys_width:],
        own_content,
        own_position,
        own_relative,
        own_mixing,
        own_second,
        own_inner,
        own_inner_bias,
        own_outer,
        own_outer_bias,
        own_third,
        own_upsample,
        own_skip,
        own_skip_bias,
        own_depth,
        own_point,
    )


def solution(mesh):
    in_specs = (
        P("dp", "seq", None),
        P("dp", "seq", None),
        P("dp"),
        P("dp", "seq", None),
        P(("dp", "seq")),
        P(("dp", "seq"), None),
        P(("dp", "seq"), None),
        P(("dp", "seq"), None),
        P(("dp", "seq")),
        P(("dp", "seq")),
        P(("dp", "seq"), None),
        P(("dp", "seq"), None),
        P(("dp", "seq")),
        P(("dp", "seq"), None),
        P(("dp", "seq")),
        P(("dp", "seq"), None),
        P(("dp", "seq")),
        P(("dp", "seq")),
        P(("dp", "seq"), None),
        P(("dp", "seq"), None),
        P(("dp", "seq")),
        P(("dp", "seq"), None),
        P(("dp", "seq"), None),
    )
    out_specs = (
        P("dp", "seq", None),
        P("dp", "seq", None),
        P("dp", "seq", None),
        P(("dp", "seq")),
        P(("dp", "seq"), None),
        P(("dp", "seq"), None),
        P(("dp", "seq"), None),
        P(("dp", "seq")),
        P(("dp", "seq")),
        P(("dp", "seq"), None),
        P(("dp", "seq"), None),
        P(("dp", "seq")),
        P(("dp", "seq"), None),
        P(("dp", "seq")),
        P(("dp", "seq"), None),
        P(("dp", "seq")),
        P(("dp", "seq")),
        P(("dp", "seq"), None),
        P(("dp", "seq"), None),
        P(("dp", "seq")),
        P(("dp", "seq"), None),
        P(("dp", "seq"), None),
    )
    return jax.shard_map(
        on_device, mesh=mesh, in_specs=in_specs, out_specs=out_specs, check_vma=False
    )
```

```python
import functools
import math

import jax
import jax.numpy as jnp
from jax import lax
from jax.experimental import pallas as pl
from jax.experimental.pallas import tpu as pltpu
from jax.sharding import PartitionSpec as P

H = 8
KD = 64
VD = 192
RPF = 32
NEG = -1e30
BF = jnp.bfloat16
F32 = jnp.float32
epsilon = 1e-05


def extended_2(array, sides, width):
    for axis, dim in sides:
        peers, length = (lax.axis_size(axis), array.shape[dim])
        up = [(i, (i + 1) % peers) for i in range(peers - 1)]
        down = [(j, i) for i, j in up]
        last = lax.slice_in_dim(array, length - width, length, axis=dim)
        initial = lax.slice_in_dim(array, 0, width, axis=dim)
        before = lax.ppermute(last, axis, up)
        after = lax.ppermute(initial, axis, down)
        array = jnp.concatenate([before, array, after], axis=dim)
    return array


def layer_norm(values, gain):
    mean = jnp.mean(values, axis=-1, keepdims=True)
    centered = values - mean
    spread = jnp.mean(centered * centered, axis=-1, keepdims=True)
    return centered * lax.rsqrt(spread + epsilon) * gain


def smooth_gelu(values):
    return jax.nn.gelu(values, approximate=False)


def norm_gelu(values, gain):
    return smooth_gelu(layer_norm(values, gain))


def matmul(left, right):
    return jnp.dot(left, right, preferred_element_type=jnp.float32)


def times_transposed(left, right):
    return lax.dot_general(
        left, right, (((1,), (1,)), ((), ())), preferred_element_type=jnp.float32
    )


def transposed_times(left, right):
    return lax.dot_general(
        left, right, (((0,), (0,)), ((), ())), preferred_element_type=jnp.float32
    )


def depth_apply(extended, taps):
    return (
        extended[:, :-2] * taps[:, 0]
        + extended[:, 1:-1] * taps[:, 1]
        + extended[:, 2:] * taps[:, 2]
    )


def dot(a, b):
    return lax.dot_general(a, b, (((1,), (0,)), ((), ())), preferred_element_type=F32)


def dot32(a, b, dims=((1,), (0,))):
    return lax.dot_general(
        a, b, (dims, ((), ())), precision=lax.Precision.HIGHEST, preferred_element_type=F32
    )


def key_side(parts, part, groups, mine, other, store):
    for slot in range(parts):
        theirs = slot_part(part, slot, parts)
        for g in range(groups):
            if slot == 0:
                kt, vt = mine[g, 0, KD : 2 * KD, :], mine[g, 0, 2 * KD :, :]
            else:
                kt, vt = other[slot - 1, g, 0, :KD, :], other[slot - 1, g, 0, KD:, :]
            store(g * parts + theirs, kt, vt)


def slot_part(part, slot, parts):
    out, bit = part, 1
    while bit < parts:
        if slot & bit:
            has = lax.rem(lax.div(part, bit), 2)
            out = out + bit - 2 * bit * has
        bit *= 2
    return out


def query_side(content, bias, relative, half):
    positional = content.astype(F32) + bias
    projected = dot32(relative, positional).astype(BF).astype(F32)
    return positional, projected[:half] + projected[half:], projected[:half] - projected[half:]


def query_block(content, plus, minus, rates):
    spot = lax.broadcasted_iota(jnp.int32, plus.shape, 1).astype(F32)
    last = plus.shape[1] - 1
    from_first, to_last = jnp.exp(-rates * spot), jnp.exp(-rates * (last - spot))
    rest = jnp.zeros((128 - KD - RPF, content.shape[1]), BF)
    block = jnp.concatenate(
        [content, (plus * from_first).astype(BF), (minus * to_last).astype(BF), rest], axis=0
    )
    return block, from_first, to_last


def lane_rates(rates_row):
    lane = lax.broadcasted_iota(jnp.int32, (1, 128), 1)
    half = RPF // 2
    below = (lane >= KD) & (lane < KD + half)
    above = (lane >= KD + half) & (lane < KD + RPF)
    return rates_row, below, above


def decay_table(rates_row, span):
    rates_row, below, above = lane_rates(rates_row)
    spot = lax.broadcasted_iota(jnp.int32, (span, 128), 0).astype(F32)
    table = jnp.where(below, jnp.exp(-rates_row * (span - 1 - spot)), 0.0)
    return jnp.where(above, jnp.exp(-rates_row * spot), table)


def key_decays(table, rates_row, first_query, last_query, first_key, span, kind):
    rates_row, below, above = lane_rates(rates_row)
    if kind == "plain":
        before = first_key < first_query
        gap = jnp.where(before, first_query - (first_key + span - 1), first_key - last_query)
        used = (below & before) | (above & jnp.logical_not(before))
        return (table * jnp.where(used, jnp.exp(-rates_row * gap.astype(F32)), 0.0)).astype(BF)
    key = first_key + lax.broadcasted_iota(jnp.int32, (span, 128), 0)
    down = jnp.exp(jnp.minimum(-rates_row * (first_query - key).astype(F32), 60.0))
    up = jnp.exp(jnp.minimum(-rates_row * (key - last_query).astype(F32), 60.0))
    return jnp.where(below, down, 0.0).astype(BF), jnp.where(above, up, 0.0).astype(BF)


def order_of(first_query, first_key, span, rows):
    i = first_query + lax.broadcasted_iota(jnp.int32, (span, rows), 1)
    j = first_key + lax.broadcasted_iota(jnp.int32, (span, rows), 0)
    return i, j


def tile_scores(keys, decays, query, first_query, first_key, length, kind):
    if kind != "both":
        return dot(keys + decays, query)
    s_below, s_above = dot(keys + decays[0], query), dot(keys + decays[1], query)
    i, j = order_of(first_query, first_key, *s_below.shape)
    scores = jnp.where(i > j, s_below, jnp.where(i < j, s_above, 0.5 * (s_below + s_above)))
    return jnp.where(j < length, scores, NEG)


def visit_tiles(scores_into, use, slots, whole_tile, q_block, length, rows, per):
    span = rows * per
    count = lax.div(length + span - 1, span)
    full = lax.div(length, span)
    own = lax.div(q_block, per)
    plain = full - jnp.where(own < full, 1, 0)

    def tile_of(k):
        return k + jnp.where(k >= own, 1, 0)

    @pl.when(plain > 0)
    def _():
        scores_into(slots[0], tile_of(0), own)

    @pl.loop(0, lax.div(plain, 2))
    def _(k):
        first = 2 * k
        scores_into(slots[1], tile_of(first + 1), own)
        use(slots[0], tile_of(first), own)
        scores_into(slots[0], tile_of(jnp.minimum(first + 2, plain - 1)), own)
        use(slots[1], tile_of(first + 1), own)

    @pl.when(lax.rem(plain, 2) == 1)
    def _():
        use(slots[0], tile_of(plain - 1), own)

    @pl.loop(0, 2)
    def _(k):
        t = jnp.where(k == 0, own, full)
        go = (t < count) & ((k == 0) | (full != own))

        @pl.when(go)
        def _():
            whole_tile(t)


def forward_kernel(
    parts, per, info, rates_ref, lanes_ref, bias_ref, rel_ref, mine, other, mixed, wide, lse, k_sc, v_sc, table_sc, s0_sc, s1_sc, m_sc, l_sc, acc
):
    groups, rows = mine.shape[0], mine.shape[3]
    half = RPF // 2
    length = info[pl.program_id(0)]
    part = info[pl.num_programs(0)]
    rates = rates_ref[...]

    def store(block, kt, vt):
        spot = pl.multiple_of(block * rows, rows)
        k_sc[pl.ds(spot, rows), :] = jnp.concatenate([kt, jnp.zeros_like(kt)], axis=0).T
        v_sc[:, pl.ds(spot, rows)] = vt

    key_side(parts, part, groups, mine, other, store)
    span = rows * per
    table_sc[...] = decay_table(lanes_ref[...], span)

    @pl.loop(0, groups)
    def _(g):
        q_block = g * parts + part

        @pl.when(q_block * rows > length)
        def _():
            mixed[g, 0] = jnp.zeros(mixed.shape[2:], mixed.dtype)
            wide[g, 0] = jnp.zeros(wide.shape[2:], wide.dtype)
            lse[g, 0] = jnp.zeros(lse.shape[2:], lse.dtype)

        @pl.when(q_block * rows <= length)
        def _():
            content = mine[g, 0, :KD, :]
            _, plus, minus = query_side(content, bias_ref[...], rel_ref[...], half)
            query, _, _ = query_block(content, plus, minus, rates)
            first_query = q_block * rows
            m_sc[...] = jnp.full(m_sc.shape, NEG, F32)
            l_sc[...] = jnp.zeros(l_sc.shape, F32)
            acc[...] = jnp.zeros(acc.shape, F32)

            def scores_of(t, kind):
                first_key = pl.multiple_of(t * span, span)
                decays = key_decays(
                    table_sc[...], lanes_ref[...], first_query, first_query + rows - 1, first_key, span, kind
                )
                keys = k_sc[pl.ds(first_key, span), :]
                return tile_scores(keys, decays, query, first_query, first_key, length, kind)

            def scores_into(slot, t, own):
                slot[...] = scores_of(t, "plain")

            def use(slot, t, own):
                scores = slot[...]
                old = m_sc[...]
                new = jnp.maximum(old, jnp.max(scores, axis=0, keepdims=True))
                alpha = jnp.exp(old - new)
                probs = jnp.exp(scores - new)
                m_sc[...] = new
                l_sc[...] = l_sc[...] * alpha + jnp.sum(probs, axis=0, keepdims=True)
                values = v_sc[:, pl.ds(pl.multiple_of(t * span, span), span)]
                acc[...] = acc[...] * alpha + dot(values, probs.astype(BF))

            def whole_tile(t):
                s0_sc[...] = scores_of(t, "both")
                use(s0_sc, t, None)

            visit_tiles(scores_into, use, (s0_sc, s1_sc), whole_tile, q_block, length, rows, per)
            total = l_sc[...]
            out = acc[...] / total
            mixed[g, 0] = out.astype(BF)
            wide[g, 0] = out
            lse[g, 0] = jnp.broadcast_to(m_sc[...] + jnp.log(total), lse.shape[2:])


def backward_kernel(
    parts, per, info, rates_ref, lanes_ref, bias_ref, rel_ref, mine, other, grad, wide, lse,
    dq, dkv_mine, dkv_other, sums, rel_grad,
    k_sc, kt_sc, v_sc, table_sc, turned_sc, s0_sc, s1_sc, dk_sc, dv_sc, dq_sc, bias_sc,
):
    groups, rows = mine.shape[0], mine.shape[3]
    half = RPF // 2
    step = pl.program_id(0)
    length = info[step]
    part = info[pl.num_programs(0)]
    rates = rates_ref[...]
    scale = KD**-0.5

    def store(block, kt, vt):
        spot = pl.multiple_of(block * rows, rows)
        k_sc[pl.ds(spot, rows), :] = jnp.concatenate([kt, jnp.zeros_like(kt)], axis=0).T
        kt_sc[:, pl.ds(spot, rows)] = kt
        v_sc[pl.ds(spot, rows), :] = vt.T

    key_side(parts, part, groups, mine, other, store)
    span = rows * per
    table_sc[...] = decay_table(lanes_ref[...], span)
    turned_sc[...] = table_sc[...].T[KD : KD + RPF]
    dk_sc[...] = jnp.zeros(dk_sc.shape, F32)
    dv_sc[...] = jnp.zeros(dv_sc.shape, F32)

    @pl.when(step == 0)
    def _():
        bias_sc[...] = jnp.zeros(bias_sc.shape, F32)
        rel_grad[...] = jnp.zeros(rel_grad.shape, F32)

    @pl.loop(0, groups)
    def _(g):
        q_block = g * parts + part

        @pl.when(q_block * rows > length)
        def _():
            dq[g, 0] = jnp.zeros(dq.shape[2:], dq.dtype)

        @pl.when(q_block * rows <= length)
        def _():
            content = mine[g, 0, :KD, :]
            content_rows = content.T
            positional, plus, minus = query_side(content, bias_ref[...], rel_ref[...], half)
            query, from_first, to_last = query_block(content, plus, minus, rates)
            first_query = q_block * rows
            last_query = first_query + rows - 1
            grad_t = grad[g, 0]
            grad_rows = grad_t.T
            log_total = lse[g, 0, :1, :]
            row_sum = jnp.sum(grad_t.astype(F32) * wide[g, 0], axis=0, keepdims=True)
            dq_sc[...] = jnp.zeros(dq_sc.shape, F32)

            def decays_of(first_key, kind):
                return key_decays(
                    table_sc[...], lanes_ref[...], first_query, last_query, first_key, span, kind
                )

            def scores_of(t, decays, kind):
                first_key = pl.multiple_of(t * span, span)
                keys = k_sc[pl.ds(first_key, span), :]
                return tile_scores(keys, decays, query, first_query, first_key, length, kind)

            def scores_into(slot, t, own):
                first_key = pl.multiple_of(t * span, span)
                slot[0] = scores_of(t, decays_of(first_key, "plain"), "plain")
                slot[1] = dot(v_sc[pl.ds(first_key, span), :], grad_t)

            def use(slot, t, own):
                absorb(slot, t, "plain", None)

            def whole_tile(t):
                first_key = pl.multiple_of(t * span, span)
                decays = decays_of(first_key, "both")
                s0_sc[0] = scores_of(t, decays, "both")
                s0_sc[1] = dot(v_sc[pl.ds(first_key, span), :], grad_t)
                absorb(s0_sc, t, "both", decays)

            def absorb(slot, t, kind, decays):
                first_key = spot = pl.multiple_of(t * span, span)
                scores, prob_grad = slot[0], slot[1]
                exact = jnp.exp(scores - log_total)
                score_grad = exact * (prob_grad - row_sum)
                low = score_grad.astype(BF)
                dv_sc[pl.ds(spot, span), :] += dot(exact.astype(BF), grad_rows)
                dk_sc[pl.ds(spot, span), :] += dot(low, content_rows)
                keys_turned = kt_sc[:, pl.ds(spot, span)]
                if kind == "both":
                    i, j = order_of(first_query, first_key, span, rows)
                    equal = 0.5 * score_grad
                    lower = jnp.where(i > j, score_grad, jnp.where(i < j, 0.0, equal)).astype(BF)
                    upper = jnp.where(i < j, score_grad, jnp.where(i > j, 0.0, equal)).astype(BF)
                    dq_sc[:KD] += dot(keys_turned, low)
                    below, above = decays
                    dq_sc[KD : KD + half] += dot(below.T[KD : KD + half], lower)
                    dq_sc[KD + half : KD + RPF] += dot(above.T[KD + half : KD + RPF], upper)
                else:
                    before = first_key < first_query
                    gap = jnp.where(before, first_query - (first_key + span - 1), first_key - last_query)
                    faded = jnp.exp(-rates * gap.astype(F32))
                    down = turned_sc[:half] * jnp.where(before, faded, 0.0)
                    up = turned_sc[half:] * jnp.where(before, 0.0, faded)
                    pos = jnp.concatenate([down, up], axis=0).astype(BF)
                    dq_sc[...] += dot(jnp.concatenate([keys_turned, pos], axis=0), low)

            visit_tiles(scores_into, use, (s0_sc, s1_sc), whole_tile, q_block, length, rows, per)
            content_grad = dq_sc[:KD]
            down, up = dq_sc[KD : KD + half] * from_first, dq_sc[KD + half :] * to_last
            projected_grad = jnp.concatenate([down + up, down - up], axis=0)
            positional_grad = dot32(rel_ref[...], projected_grad, ((0,), (0,)))
            dq[g, 0] = (scale * (content_grad + positional_grad)).astype(BF)
            bias_sc[0] += content_grad
            bias_sc[1] += positional_grad
            rel_grad[...] += dot32(positional, projected_grad, ((1,), (1,)))

    for slot in range(parts):
        theirs = slot_part(part, slot, parts)
        for g in range(groups):
            spot = pl.multiple_of((g * parts + theirs) * rows, rows)
            dkt = dk_sc[pl.ds(spot, rows), :].astype(BF).T
            dvt = dv_sc[pl.ds(spot, rows), :].astype(BF).T
            both = jnp.concatenate([dkt, dvt], axis=0)
            if slot == 0:
                dkv_mine[g, 0] = both
            else:
                dkv_other[slot - 1, g, 0] = both

    @pl.when(step == pl.num_programs(0) - 1)
    def _():
        sums[...] = scale * jnp.sum(bias_sc[...], axis=-1, keepdims=True)


def attention_cost(windows, groups, rows, parts, wide):
    pairs = windows * groups * rows * groups * parts * rows
    return pl.CostEstimate(
        flops=int(pairs * 2 * wide * 0.75), bytes_accessed=20_000_000, transcendentals=int(pairs)
    )


def whole(*shape):
    return pl.BlockSpec(shape, lambda w: (0,) * len(shape))


def per_window(*shape):
    lead = len(shape) - 3
    return pl.BlockSpec(shape, lambda w: (0,) * lead + (w, 0, 0))


def tile_blocks(rows, groups, parts, target):
    per = max(1, target // rows)
    while (groups * parts) % per:
        per -= 1
    return per


def lanes_of(rates):
    line = rates.reshape(1, -1)
    return jnp.pad(jnp.concatenate([line, line], axis=1), ((0, 0), (KD, 128 - KD - RPF)))


def attention_forward(info, rates, bias, rel, mine, other, parts):
    groups, windows, _, rows = mine.shape
    per = tile_blocks(rows, groups, parts, 1024)
    total = groups * parts * rows
    return pl.pallas_call(
        functools.partial(forward_kernel, parts, per),
        grid=(windows,),
        out_shape=(
            jax.ShapeDtypeStruct((groups, windows, VD, rows), BF),
            jax.ShapeDtypeStruct((groups, windows, VD, rows), F32),
            jax.ShapeDtypeStruct((groups, windows, 8, rows), F32),
        ),
        in_specs=[
            pl.BlockSpec(memory_space=pltpu.SMEM),
            whole(*rates.shape),
            whole(1, 128),
            whole(*bias.shape),
            whole(*rel.shape),
            per_window(groups, 1, 2 * KD + VD, rows),
            per_window(parts - 1, groups, 1, KD + VD, rows),
        ],
        out_specs=(
            per_window(groups, 1, VD, rows),
            per_window(groups, 1, VD, rows),
            per_window(groups, 1, 8, rows),
        ),
        scratch_shapes=[
            pltpu.VMEM((total, 128), BF),
            pltpu.VMEM((VD, total), BF),
            pltpu.VMEM((rows * per, 128), F32),
            pltpu.VMEM((rows * per, rows), F32),
            pltpu.VMEM((rows * per, rows), F32),
            pltpu.VMEM((1, rows), F32),
            pltpu.VMEM((1, rows), F32),
            pltpu.VMEM((VD, rows), F32),
        ],
        compiler_params=pltpu.CompilerParams(vmem_limit_bytes=56 * 2**20),
        cost_estimate=attention_cost(windows, groups, rows, parts, 128 + 256),
        name="attention_forward",
    )(info, rates, lanes_of(rates), bias, rel, mine, other)


def attention_backward(info, rates, bias, rel, mine, other, grad, wide, lse, parts):
    groups, windows, _, rows = mine.shape
    per = tile_blocks(rows, groups, parts, 1024)
    total = groups * parts * rows
    return pl.pallas_call(
        functools.partial(backward_kernel, parts, per),
        grid=(windows,),
        out_shape=(
            jax.ShapeDtypeStruct((groups, windows, KD, rows), BF),
            jax.ShapeDtypeStruct((groups, windows, KD + VD, rows), BF),
            jax.ShapeDtypeStruct((parts - 1, groups, windows, KD + VD, rows), BF),
            jax.ShapeDtypeStruct((2, KD, 1), F32),
            jax.ShapeDtypeStruct((KD, RPF), F32),
        ),
        in_specs=[
            pl.BlockSpec(memory_space=pltpu.SMEM),
            whole(*rates.shape),
            whole(1, 128),
            whole(*bias.shape),
            whole(*rel.shape),
            per_window(groups, 1, 2 * KD + VD, rows),
            per_window(parts - 1, groups, 1, KD + VD, rows),
            per_window(groups, 1, VD, rows),
            per_window(groups, 1, VD, rows),
            per_window(groups, 1, 8, rows),
        ],
        out_specs=(
            per_window(groups, 1, KD, rows),
            per_window(groups, 1, KD + VD, rows),
            per_window(parts - 1, groups, 1, KD + VD, rows),
            whole(2, KD, 1),
            whole(KD, RPF),
        ),
        scratch_shapes=[
            pltpu.VMEM((total, 128), BF),
            pltpu.VMEM((KD, total), BF),
            pltpu.VMEM((total, VD), BF),
            pltpu.VMEM((rows * per, 128), F32),
            pltpu.VMEM((RPF, rows * per), F32),
            pltpu.VMEM((2, rows * per, rows), F32),
            pltpu.VMEM((2, rows * per, rows), F32),
            pltpu.VMEM((total, KD), F32),
            pltpu.VMEM((total, VD), F32),
            pltpu.VMEM((KD + RPF, rows), F32),
            pltpu.VMEM((2, KD, rows), F32),
        ],
        compiler_params=pltpu.CompilerParams(vmem_limit_bytes=56 * 2**20),
        cost_estimate=attention_cost(windows, groups, rows, parts, 3 * 256 + 2 * 256),
        name="attention_backward",
    )(info, rates, lanes_of(rates), bias, rel, mine, other, grad, wide, lse)

MESH = pl.DeviceIdType.MESH


def upper_work(here, lengths, cotangent, skip_input, outs, gathered, scratch, remote, neighbours):
    out_grad_o, conv_o, joined_o, lifted_o, third_o, skip_grad_o, skip_part_o, bias_o = outs
    (
        table_rows,
        lines,
        w_point,
        w_skip,
        w_upsample,
        grad_v,
        skip_v,
        conv_v,
        joined_v,
        lifted_v,
        part_v,
        halo_before,
        halo_after,
        sem,
        halo_sem,
    ) = scratch
    dp, seq = here
    windows, fine, width = grad_v.shape
    rows = fine // 2
    before, after = neighbours

    def load(source, target, n):
        return pltpu.make_async_copy(source, target, sem.at[n])

    point_load = load(gathered[9], w_point, 0)
    skip_load = load(gathered[4], w_skip, 1)
    upsample_load = load(gathered[8], w_upsample, 2)
    grad_load = load(cotangent, grad_v, 3)
    input_load = load(skip_input, skip_v, 4)
    grad_load.start()
    input_load.start()
    stores = {
        "out_grad": load(grad_v, out_grad_o, 5),
        "conv": load(conv_v, conv_o, 6),
        "joined": load(joined_v, joined_o, 7),
        "lifted": load(lifted_v, lifted_o, 8),
        "skip": load(skip_v, skip_grad_o, 9),
    }

    def against(x, table):
        return lax.dot_general(
            x, table[...].reshape(width, width), (((1,), (1,)), ((), ())), preferred_element_type=F32
        )

    def halo_copies():
        out = []
        for w in range(windows):
            out.append(
                remote(
                    conv_v.at[w, pl.ds(fine - 16, 16)],
                    halo_before.at[w],
                    halo_sem.at[0, w],
                    halo_sem.at[1, w],
                    after,
                )
            )
            out.append(
                remote(
                    conv_v.at[w, pl.ds(0, 16)],
                    halo_after.at[w],
                    halo_sem.at[2, w],
                    halo_sem.at[3, w],
                    before,
                )
            )
        return out

    def conv_grad(w):
        if w == 0:
            point_load.start()
            grad_load.wait()
            point_load.wait()
        length = lengths[w]

        @pl.loop(0, fine // 256)
        def _(k):
            at = pl.ds(pl.multiple_of(k * 256, 256), 256)
            bin_ = seq * rows + lax.div(
                k * 256 + lax.broadcasted_iota(jnp.int32, (256, width), 0), 2
            )
            grad = jnp.where(bin_ < length, grad_v[w, at, :].astype(F32), 0.0).astype(BF)
            grad_v[w, at, :] = grad
            conv_v[w, at, :] = against(grad, w_point).astype(BF)

        if w == windows - 1:
            stores["out_grad"].start()
            stores["conv"].start()
            for copy in halo_copies():
                copy.start()

    def skip_part(w):
        if w == 0:
            skip_load.start()
            input_load.wait()
            skip_load.wait()

        @pl.loop(0, fine // 256)
        def _(k):
            at = pl.ds(pl.multiple_of(k * 256, 256), 256)
            made = dot(skip_v[w, at, :], w_skip[...].reshape(width, width)) + lines[0:1, :]
            part_v[...] = made
            store = load(part_v, skip_part_o.at[w, at], 10)
            store.start()
            store.wait()

    def joined_grad():
        for copy in halo_copies():
            copy.wait_recv()
        total = jnp.zeros((1, width), F32)
        tap = [lines[n : n + 1, :] for n in (1, 2, 3)]
        tile = 64
        for w in range(windows):
            first = halo_before[w].astype(F32)[15:16, :]
            first = jnp.where(seq == 0, 0.0, first)
            last = halo_after[w].astype(F32)[0:1, :]
            last = jnp.where(seq == lax.axis_size("seq") - 1, 0.0, last)
            for k in range(fine // tile):
                at = slice(k * tile, (k + 1) * tile)
                here_rows = conv_v[w, at, :].astype(F32)
                up = first if k == 0 else conv_v[w, k * tile - 16 : k * tile, :].astype(F32)[15:16, :]
                down = (
                    last
                    if k == fine // tile - 1
                    else conv_v[w, (k + 1) * tile : (k + 1) * tile + 16, :].astype(F32)[0:1, :]
                )
                index = lax.broadcasted_iota(jnp.int32, here_rows.shape, 0)
                earlier = jnp.where(index == 0, up, pltpu.roll(here_rows, 1, 0))
                later = jnp.where(index == tile - 1, down, pltpu.roll(here_rows, tile - 1, 0))
                made = later * tap[0] + here_rows * tap[1] + earlier * tap[2]
                total = total + jnp.sum(made, axis=0, keepdims=True)
                joined_v[w, at, :] = made.astype(BF)
        bias_o[...] = total
        stores["joined"].start()
        pair = lax.div(lax.broadcasted_iota(jnp.int32, (rows, fine), 1), 2)
        twice = (pair == lax.broadcasted_iota(jnp.int32, (rows, fine), 0)).astype(F32).astype(BF)
        for w in range(windows):
            lifted_v[w * rows : (w + 1) * rows, :] = dot(twice, joined_v[w]).astype(BF)
        stores["lifted"].start()

    def skip_grad(w):
        @pl.loop(0, fine // 256)
        def _(k):
            at = pl.ds(pl.multiple_of(k * 256, 256), 256)
            skip_v[w, at, :] = against(joined_v[w, at, :], w_skip).astype(BF)

        if w == windows - 1:
            stores["skip"].start()

    def third_grad():
        upsample_load.start()
        upsample_load.wait()

        @pl.loop(0, windows * rows // 256)
        def _(k):
            at = pl.ds(pl.multiple_of(k * 256, 256), 256)
            part_v[...] = against(lifted_v[at, :], w_upsample)
            store = load(part_v, third_o.at[at], 10)
            store.start()
            store.wait()

    def finish():
        for store in stores.values():
            store.wait()
        for copy in halo_copies():
            copy.wait_send()

    jobs = {
        9: [(9, functools.partial(conv_grad, 0))],
        10: [(None, functools.partial(conv_grad, 1))],
        11: [(4, functools.partial(skip_part, 0)), (None, functools.partial(skip_part, 1))],
        12: [(None, joined_grad)],
        13: [(None, functools.partial(skip_grad, 0)), (None, functools.partial(skip_grad, 1))],
        14: [(8, third_grad)],
    }
    return {"rows": table_rows, "lines": lines, "jobs": jobs, "finish": finish}


def links_kernel(pairs, counts, parts, early, *refs):
    n_in, n_out = counts
    refs = list(refs)

    def take(count):
        out, refs[:count] = refs[:count], []
        return out

    refs_in = take(n_in)
    if early:
        values, spread_gain, pick_gain, spread_bias, pick_bias = take(5)
        lengths, cotangent, skip_input = take(3)
    elif parts:
        (blocks,) = take(1)
    refs_out = take(n_out)
    if parts:
        mine, other = take(2)
    if early:
        (normed,) = take(1)
        upper_out = take(8)
    local_sem, send_hi, recv_hi, send_y, recv_y, send_dp, recv_dp, send_c, recv_c = take(9)
    dp, seq = lax.axis_index("dp"), lax.axis_index("seq")
    ndp, nhi = refs_out[0].shape[:2]
    hi, low = lax.div(seq, 4), lax.rem(seq, 4)
    y, c = lax.div(low, 2), lax.rem(low, 2)

    def place(dp_to, hi_to, y_to, c_to):
        return (dp_to, hi_to * 4 + y_to * 2 + c_to)

    hi_peers = [place(dp, lax.rem(hi + k, nhi), y, c) for k in range(1, nhi)]
    y_peers = [place(dp, hi, 1 - y, c)]
    dp_peers = [place(lax.rem(dp + k, ndp), hi, y, c) for k in range(1, ndp)]
    c_peers = [place(dp, hi, y, 1 - c)]
    everyone = hi_peers + y_peers + dp_peers + c_peers
    if parts:
        head, part = lax.div(seq, parts), lax.rem(seq, parts)
        head_of = [lax.rem(head + k, H) for k in range(1, H)]
        head_peers = [(dp, h * parts + part) for h in head_of]
        part_peers = [(dp, head * parts + slot_part(part, k, parts)) for k in range(1, parts)]
        everyone = everyone + head_peers + part_peers
    if early:
        nseq = nhi * 4
        after = (dp, lax.rem(seq + 1, nseq))
        before = (dp, lax.rem(seq + nseq - 1, nseq))
        everyone = everyone + [after, before]

    barrier = pltpu.get_barrier_semaphore()
    for peer in everyone:
        pl.semaphore_signal(barrier, inc=1, device_id=peer, device_id_type=MESH)
    pl.semaphore_wait(barrier, len(everyone))

    def remote(source, target, ss, rs, peer):
        return pltpu.make_async_remote_copy(
            src_ref=source,
            dst_ref=target,
            send_sem=ss,
            recv_sem=rs,
            device_id=peer,
            device_id_type=MESH,
        )

    step_chunks, serial = [], 0
    for pair in pairs:
        step_chunks.append([])
        for side in (0, 1):
            for chunk in pair[side]:
                step_chunks[-1].append((serial, side) + chunk)
                serial += 1

    def copies(chunk, stage):
        n, side, array, row, rows, first, columns = chunk
        out = refs_out[array]
        piece = (pl.ds(row, rows), pl.ds(first, columns))
        which = (("hi", "y", "dp", "c"), ("hi", "dp", "y", "c"))[side][stage]
        if which == "hi":
            target = out.at[(dp, hi, y, c) + piece]
            source = refs_in[array].at[piece]
            peers, ss, rs = hi_peers, send_hi, recv_hi
        else:
            every = slice(None)
            if which == "c":
                target = out.at[(every, every, every, c) + piece]
                peers, ss, rs = c_peers, send_c, recv_c
            elif which == "y":
                there = (dp, every, y, c) if stage == 1 else (every, every, y, c)
                target = out.at[there + piece]
                peers, ss, rs = y_peers, send_y, recv_y
            else:
                there = (dp, every, y, c) if stage == 1 else (dp, every, every, c)
                target = out.at[there + piece]
                peers, ss, rs = dp_peers, send_dp, recv_dp
            source = target
        return [remote(source, target, ss.at[n, k], rs.at[n, k], p) for k, p in enumerate(peers)]

    def own(array):
        return pltpu.make_async_copy(
            refs_in[array], refs_out[array].at[dp, hi, y, c], local_sem.at[array]
        )

    everything = [chunk for group in step_chunks for chunk in group]
    head_copies, head_own = [], None
    if parts:
        head_local, head_send, head_recv, part_send, part_recv = take(5)
        if early:
            blocks = take(1)[0]
        head_copies = [
            remote(blocks.at[:, h], mine.at[head], head_send.at[k], head_recv.at[k], p)
            for k, (h, p) in enumerate(zip(head_of, head_peers, strict=True))
        ]
        head_own = pltpu.make_async_copy(blocks.at[:, head], mine.at[head], head_local.at[0])
        keys = mine.at[:, :, pl.ds(KD, KD + VD)]
        part_copies = [
            remote(keys, other.at[k], part_send.at[k], part_recv.at[k], p)
            for k, p in enumerate(part_peers)
        ]
        if not early:
            head_own.start()
    if early:
        small_v, query_v, key_v, values_v, inputs_v, gain_v, bias_v, load_sem = take(8)
        inputs_load = pltpu.make_async_copy(values, inputs_v, load_sem.at[0])
        inputs_load.start()
        upper = upper_work(
            (dp, seq), lengths, cotangent, skip_input, upper_out, refs_out, take(15), remote, (before, after)
        )

    def make_blocks():
        loads = [
            pltpu.make_async_copy(source, target, load_sem.at[k + 1])
            for k, (source, target) in enumerate(
                zip(refs_out[:4], (small_v, query_v, key_v, values_v), strict=True)
            )
        ]
        for load in loads:
            load.start()
        inputs_load.wait()
        for load in loads:
            load.wait()

        @pl.loop(0, ndp * nhi * 4)
        def _(k):
            rows = small_v[
                lax.div(k, nhi * 4),
                lax.rem(lax.div(k, 4), nhi),
                lax.rem(lax.div(k, 2), 2),
                lax.rem(k, 2),
            ].astype(F32)
            gain_v[pl.ds(k, 1), :] = rows[0:1, :]
            bias_v[pl.ds(k, 1), :] = rows[1:2, :]
            for n in range(4):
                upper["rows"][n, pl.ds(k, 1), :] = rows[7 + n : 8 + n, :]

        def line_up(table, spread, pick):
            return jnp.sum(dot(table[...].astype(BF), spread[...]) * pick[...], axis=0, keepdims=True)

        gain = line_up(gain_v, spread_gain, pick_gain)
        for n in range(4):
            upper["lines"][n : n + 1, :] = line_up(upper["rows"].at[n], spread_gain, pick_gain)
        bias = line_up(bias_v, spread_bias, pick_bias)
        windows, rows = inputs_v.shape[:2]
        for w in range(windows):
            normed[w * rows : (w + 1) * rows, :] = layer_norm(
                inputs_v[w].astype(F32), gain
            ).astype(BF)
        low = normed[...]
        width = low.shape[1]

        def weight(table, first, columns):
            return table[:, :, :, :, :, first : first + columns].reshape(width, columns)

        for pair in range(H // 2):
            spot, wide = pair * 2 * KD, pair * 2 * VD
            content = dot(low, weight(query_v, spot, 2 * KD)) + bias[:, spot : spot + 2 * KD]
            content = (content * (KD**-0.5)).astype(BF).T
            key = dot(low, weight(key_v, spot, 2 * KD)).astype(BF).T
            value = dot(low, weight(values_v, wide, 2 * VD)).astype(BF).T
            for h in range(2):
                for w in range(windows):
                    span = slice(w * rows, (w + 1) * rows)
                    blocks[w, 2 * pair + h, :KD, :] = content[h * KD : (h + 1) * KD, span]
                    blocks[w, 2 * pair + h, KD : 2 * KD, :] = key[h * KD : (h + 1) * KD, span]
                    blocks[w, 2 * pair + h, 2 * KD :, :] = value[h * VD : (h + 1) * VD, span]
        head_own.start()

    ahead, lag = 3, 2

    def launch(step):
        for chunk in step_chunks[step]:
            for copy in copies(chunk, 0):
                copy.start()

    events = {}
    for spot in range(len(pairs)):
        gap = 1 if spot < early else lag
        for stage in (3, 2, 1):
            events.setdefault(spot + gap * (stage - 1), []).append((stage, spot))
    made_at = early + 2 if early else 0
    waited = []
    heads_at = [made_at + k for k in range(len(head_copies))]
    for step in range(min(ahead, len(pairs))):
        launch(step)
    for array in range(n_out):
        own(array).start()
    for array in range(n_out):
        own(array).wait()
    for step in range(max(list(events) + heads_at) + 1):
        for stage, spot in sorted(events.get(step, []), reverse=True):
            for chunk in step_chunks[spot]:
                for copy in copies(chunk, stage - 1):
                    copy.wait_recv()
                for copy in copies(chunk, stage):
                    copy.start()
        if step + ahead < len(pairs):
            launch(step + ahead)
        if early and step == made_at:
            for group in step_chunks[:early]:
                for chunk in group:
                    for copy in copies(chunk, 3):
                        copy.wait_recv()
            make_blocks()
        if step in heads_at:
            head_copies[heads_at.index(step)].start()
        if early:
            for need, job in upper["jobs"].get(step, []):
                for chunk in everything:
                    if chunk[2] == need:
                        for copy in copies(chunk, 3):
                            copy.wait_recv()
                        waited.append(chunk)
                job()
    if parts:
        head_own.wait()
        for copy in head_copies:
            copy.wait_recv()
        for copy in part_copies:
            copy.start()
    for group in step_chunks[early:]:
        for chunk in group:
            if chunk not in waited:
                for copy in copies(chunk, 3):
                    copy.wait_recv()
    if early:
        upper["finish"]()
    if parts:
        for copy in part_copies:
            copy.wait_recv()
        for copy in head_copies + part_copies:
            copy.wait_send()
    for chunk in everything:
        for stage in range(4):
            for copy in copies(chunk, stage):
                copy.wait_send()


def spread_tables(length, share):
    column = jnp.arange(length, dtype=jnp.int32)
    lane = jnp.arange(128, dtype=jnp.int32)
    device = jnp.arange(length // share, dtype=jnp.int32)
    spread = (column[None, :] % share == lane[:, None]).astype(BF)
    pick = (column[None, :] // share == device[:, None]).astype(F32)
    return spread, pick


def use_links(name, collective, shards, pairs, blocks=None, values=None, early=0, upper=()):
    ndp, nseq = lax.axis_size("dp"), lax.axis_size("seq")
    nhi, devices = nseq // 4, ndp * nseq
    parts = nseq // H if blocks is not None or early else 0
    chunks = sum(len(side) for pair in pairs for side in pair)
    arrays = [shard.shape for shard in shards]
    out_shape = [jax.ShapeDtypeStruct((ndp, nhi, 2, 2) + shape, BF) for shape in arrays]
    operands = list(shards)
    in_specs = [pl.BlockSpec(memory_space=pl.ANY)] * len(operands)
    sizes = [(len(arrays),)] + [
        (chunks, size) for size in (nhi - 1, nhi - 1, 1, 1, ndp - 1, ndp - 1, 1, 1)
    ]
    scratch = []
    if early:
        windows, rows, width = values.shape
        operands += [values]
        operands += [
            *spread_tables(width, width // devices),
            *spread_tables(H * KD, H * KD // devices),
        ]
        in_specs += [pl.BlockSpec(memory_space=pl.ANY)] + [
            pl.BlockSpec(memory_space=pltpu.VMEM)
        ] * 4
        operands += list(upper)
        in_specs += [pl.BlockSpec(memory_space=pltpu.SMEM)] + [
            pl.BlockSpec(memory_space=pl.ANY)
        ] * 2
        scratch = [
            pltpu.VMEM((windows, H, 2 * KD + VD, rows), BF),
            pltpu.VMEM(out_shape[0].shape, BF),
            pltpu.VMEM(out_shape[1].shape, BF),
            pltpu.VMEM(out_shape[2].shape, BF),
            pltpu.VMEM(out_shape[3].shape, BF),
            pltpu.VMEM(values.shape, BF),
            pltpu.VMEM((devices, 128), F32),
            pltpu.VMEM((devices, 128), F32),
            pltpu.SemaphoreType.DMA((5,)),
            pltpu.VMEM((4, devices, 128), F32),
            pltpu.VMEM((8, width), F32),
            *[pltpu.VMEM((ndp, nhi, 2, 2, width // devices, width), BF)] * 3,
            *[pltpu.VMEM((windows, 2 * rows, width), BF)] * 4,
            pltpu.VMEM((windows * rows, width), BF),
            pltpu.VMEM((256, width), F32),
            pltpu.VMEM((windows, 16, width), BF),
            pltpu.VMEM((windows, 16, width), BF),
            pltpu.SemaphoreType.DMA((11,)),
            pltpu.SemaphoreType.DMA((4, windows)),
        ]
    elif parts:
        windows, _, _, rows = blocks.shape
        operands.append(blocks)
        in_specs.append(pl.BlockSpec(memory_space=pl.ANY))
    out_specs = [pl.BlockSpec(memory_space=pl.ANY)] * len(out_shape)
    if parts:
        out_shape += [
            jax.ShapeDtypeStruct((H, windows, 2 * KD + VD, rows), BF),
            jax.ShapeDtypeStruct((parts - 1, H, windows, KD + VD, rows), BF),
        ]
        out_specs += [pl.BlockSpec(memory_space=pl.ANY)] * 2
        sizes += [(1,), (H - 1,), (H - 1,), (parts - 1,), (parts - 1,)]
    if early:
        out_shape.append(jax.ShapeDtypeStruct((windows * rows, width), BF))
        out_specs.append(pl.BlockSpec(memory_space=pltpu.VMEM))
        fine, coarse = (windows, 2 * rows, width), (windows * rows, width)
        out_shape += [
            jax.ShapeDtypeStruct(*s)
            for s in (
                (fine, BF),
                (fine, BF),
                (fine, BF),
                (coarse, BF),
                (coarse, F32),
                (fine, BF),
                (fine, F32),
                ((1, width), F32),
            )
        ]
        out_specs += [pl.BlockSpec(memory_space=pl.ANY)] * 7
        out_specs.append(pl.BlockSpec(memory_space=pltpu.VMEM))
    outs = pl.pallas_call(
        functools.partial(links_kernel, pairs, (len(shards), len(arrays)), parts, early),
        out_shape=out_shape,
        in_specs=in_specs,
        out_specs=out_specs,
        scratch_shapes=[pltpu.SemaphoreType.DMA(size) for size in sizes] + scratch,
        compiler_params=pltpu.CompilerParams(
            collective_id=collective, has_side_effects=True, vmem_limit_bytes=60 * 2**20
        ),
        name=name,
    )(*operands)
    flat = [out.reshape(-1, out.shape[-1]) for out in outs[: len(arrays)]]
    return flat + list(outs[len(arrays) :])


def tie(*values):
    return lax.optimization_barrier(values)


def project_kernel(values, gain, content_bias, w_query, w_key, w_value, normed, sent, scratch):
    windows, rows, _ = values.shape

    @pl.when(pl.program_id(0) == 0)
    def _():
        for w in range(windows):
            low = layer_norm(values[w].astype(F32), gain[...]).astype(BF)
            scratch[w * rows : (w + 1) * rows, :] = low
            normed[w * rows : (w + 1) * rows, :] = low

    low = scratch[...]
    content = ((dot(low, w_query[...]) + content_bias[0]) * (KD**-0.5)).astype(BF).T
    keys = dot(low, w_key[...]).astype(BF).T
    mixable = dot(low, w_value[...]).astype(BF).T
    for h in range(2):
        for w in range(windows):
            span = slice(w * rows, (w + 1) * rows)
            sent[w, h, :KD, :] = content[h * KD : (h + 1) * KD, span]
            sent[w, h, KD : 2 * KD, :] = keys[h * KD : (h + 1) * KD, span]
            sent[w, h, 2 * KD :, :] = mixable[h * VD : (h + 1) * VD, span]


def project(values, gain, content_bias, weight_query, weight_key, weight_value):
    windows, rows, width = values.shape
    steps = H // 2
    return pl.pallas_call(
        project_kernel,
        grid=(steps,),
        out_shape=(
            jax.ShapeDtypeStruct((windows * rows, width), BF),
            jax.ShapeDtypeStruct((windows, H, 2 * KD + VD, rows), BF),
        ),
        in_specs=[
            pl.BlockSpec((windows, rows, width), lambda i: (0, 0, 0)),
            pl.BlockSpec((1, width), lambda i: (0, 0)),
            pl.BlockSpec((1, 1, 2 * KD), lambda i: (i, 0, 0)),
            pl.BlockSpec((width, 2 * KD), lambda i: (0, i)),
            pl.BlockSpec((width, 2 * KD), lambda i: (0, i)),
            pl.BlockSpec((width, 2 * VD), lambda i: (0, i)),
        ],
        out_specs=(
            pl.BlockSpec((windows * rows, width), lambda i: (0, 0)),
            pl.BlockSpec((windows, 2, 2 * KD + VD, rows), lambda i: (0, i, 0, 0)),
        ),
        scratch_shapes=[pltpu.VMEM((windows * rows, width), BF)],
        compiler_params=pltpu.CompilerParams(vmem_limit_bytes=48 * 2**20),
        name="project",
    )(
        values,
        gain.reshape(1, width),
        content_bias.reshape(steps, 1, 2 * KD),
        weight_query,
        weight_key,
        weight_value,
    )


def block_work(operands, outs, scratch, arrived, wait_heads):
    values, third_grad, w_mixing, w_inner, w_outer = operands[:5]
    second_gain, third_gain, inner_bias, outer_bias = operands[5:]
    second_sum, third_sum, inner_sum, outer_sum = outs[9:]
    mixing_v, inner_v, outer_v, values_v, third_grad_v, middle_v, block_v, slope_v = scratch[:8]
    mixed_b, second_b, hidden_b, third_b, block_b, before_b, middle_b, back_b, heads_b = scratch[8:17]
    weight_sem, load_sem, store_sem = scratch[17:]
    windows, rows, width = values.shape
    wide = slope_v.shape[1]
    tile, chunk = 512, 32
    weight_loads = [
        pltpu.make_async_copy(source, target, weight_sem.at[k])
        for k, (source, target) in enumerate(
            ((w_mixing, mixing_v), (w_inner, inner_v), (w_outer, outer_v))
        )
    ]

    def loads(w):
        return [
            pltpu.make_async_copy(values.at[w], values_v, load_sem.at[0]),
            pltpu.make_async_copy(third_grad.at[pl.ds(w * rows, rows)], third_grad_v, load_sem.at[1]),
        ]

    buffers = (mixed_b, second_b, hidden_b, third_b, block_b, before_b, middle_b, back_b, heads_b)

    def store(k, w):
        target = outs[k].at[w] if k == 8 else outs[k].at[pl.ds(w * rows, rows)]
        return pltpu.make_async_copy(buffers[k], target, store_sem.at[k])

    def free(w, *numbers):
        if w:
            for k in numbers:
                store(k, w - 1).wait()

    def begin():
        for load in weight_loads + loads(0):
            load.start()
        for total in (second_sum, third_sum, inner_sum, outer_sum):
            total[...] = jnp.zeros(total.shape, F32)

    def mix(w):
        wait_heads(w)
        free(w, 0)
        for pair in range(H // 2):
            both = jnp.concatenate([arrived[2 * pair + h, w] for h in range(2)], axis=0)
            mixed_b[:, pair * 2 * VD : (pair + 1) * 2 * VD] = both.T
        store(0, w).start()
        if w == 0:
            weight_loads[0].wait()
        loads(w)[0].wait()
        for k in range(0, width, tile):
            cols = slice(k, k + tile)
            middle_v[:, cols] = values_v[:, cols].astype(F32) + dot(mixed_b[...], mixing_v[:, cols])

    def inner(w, part):
        if part == 0:
            free(w, 1, 2)

            @pl.loop(0, rows // chunk)
            def _(k):
                at = pl.ds(pl.multiple_of(k * chunk, chunk), chunk)
                unit, _ = norm_parts(middle_v[at, :])
                second_b[at, :] = (unit * second_gain[...]).astype(BF)

            store(1, w).start()
            if w == 0:
                weight_loads[1].wait()
        for k in range(part * wide // 2, (part + 1) * wide // 2, tile):
            cols = slice(k, k + tile)
            before = dot(second_b[...], inner_v[:, cols]) + inner_bias[:, cols]
            hidden, slope = gelu_parts(before)
            hidden_b[:, cols] = hidden.astype(BF)
            slope_v[:, cols] = slope.astype(BF)
        if part == 1:
            store(2, w).start()

    def outer(w):
        if w == 0:
            weight_loads[2].wait()
        for k in range(0, width, tile):
            cols = slice(k, k + tile)
            block_v[:, cols] = (
                middle_v[:, cols] + dot(hidden_b[...], outer_v[:, cols]) + outer_bias[:, cols]
            )

    def turn(w):
        free(w, 3, 4)
        loads(w)[1].wait()

        @pl.loop(0, rows // chunk)
        def _(k):
            at = pl.ds(pl.multiple_of(k * chunk, chunk), chunk)
            unit, scale = norm_parts(block_v[at, :])
            third, slope = gelu_parts(unit * third_gain[...])
            third_b[at, :] = third.astype(BF)
            grad = third_grad_v[at, :] * slope
            third_sum[...] += jnp.sum(grad * unit, axis=0, keepdims=True)
            back = norm_backward(unit, scale, grad, third_gain[...])
            outer_sum[...] += jnp.sum(back, axis=0, keepdims=True)
            block_v[at, :] = back
            block_b[at, :] = back.astype(BF)

        store(3, w).start()
        store(4, w).start()
        if w + 1 < windows:
            for load in loads(w + 1):
                load.start()

    def before_grad(w):
        free(w, 5)
        for k in range(0, wide, tile):
            cols = slice(k, k + tile)
            grad = times_rows(block_b[...], outer_v[cols, :]) * slope_v[:, cols].astype(F32)
            low = grad.astype(BF)
            before_b[:, cols] = low
            inner_sum[:, cols] += jnp.sum(low.astype(F32), axis=0, keepdims=True)
        store(5, w).start()

    def second_grad(w):
        free(w, 7)
        for k in range(0, width, tile):
            cols = slice(k, k + tile)
            back_b[:, cols] = times_rows(before_b[...], inner_v[cols, :])

    def middle_grad(w):
        free(w, 6, 8)

        @pl.loop(0, rows // chunk)
        def _(k):
            at = pl.ds(pl.multiple_of(k * chunk, chunk), chunk)
            unit, scale = norm_parts(middle_v[at, :])
            grad = back_b[at, :]
            second_sum[...] += jnp.sum(grad * unit, axis=0, keepdims=True)
            back = block_v[at, :] + norm_backward(unit, scale, grad, second_gain[...])
            back_b[at, :] = back
            middle_b[at, :] = back.astype(BF)

        store(6, w).start()
        store(7, w).start()
        for pair in range(H // 2):
            cols = slice(pair * 2 * VD, (pair + 1) * 2 * VD)
            turned = times_rows(middle_b[...], mixing_v[cols, :]).astype(BF).T
            for h in range(2):
                heads_b[2 * pair + h] = turned[h * VD : (h + 1) * VD]
        store(8, w).start()

    def finish():
        for k in range(len(buffers)):
            store(k, windows - 1).wait()

    jobs = []
    for w in range(windows):
        jobs += [
            functools.partial(mix, w),
            functools.partial(inner, w, 0),
            functools.partial(inner, w, 1),
            functools.partial(outer, w),
            functools.partial(turn, w),
            functools.partial(before_grad, w),
            functools.partial(second_grad, w),
            functools.partial(middle_grad, w),
        ]
    return begin, jobs, finish


def sums_kernel(plan, refs_spec, *refs):
    groups, n_terms, mode, parts, n_small, made_here, late, masked = plan
    refs = list(refs)

    def take(count):
        out, refs[:count] = refs[:count], []
        return out

    terms = take(n_terms * (2 if made_here else 1) - (1 if late else 0))
    head_in = take({None: 0, "in": 1, "block": 1, "out": 3}[mode])
    small_in = take(1 if n_small else 0)
    if late:
        w_query, w_key, w_value, values, middle_grad, gain, spread, pick = take(8)
    if masked:
        lengths, w_masked = take(2)
    if mode == "block":
        block_in = take(9)
    outs = take(n_terms)
    head_out = take(0 if late or not mode or mode == "block" else 1)
    small_out = take(1 if n_small else 0)
    if late:
        (input_grad,) = take(1)
    if masked:
        (masked_o,) = take(1)
    if mode == "block":
        block_out = take(13)
    own, arrived, result, back, hop1, hop2, line = [], [], [], [], [], [], []
    flat = [(side, unit) for group in groups for side in (0, 1) for unit in group[side]]
    count = len(flat)
    own = take(count)
    arrived = take(count)
    hop1 = take(count)
    hop2 = take(count)
    line = take(count)
    result = take(count)
    back = take(count)
    if made_here:
        slots = min(2, n_terms)
        lefts, rights, turned = take(1), take(slots), take(slots)
        going, left_sem, right_sem = take(3)
    load_sem, c_send, c_recv, s1, r1, s2, r2, s3, r3, s4, r4 = take(11)
    dp, seq = lax.axis_index("dp"), lax.axis_index("seq")
    ndp, nhi = own[0].shape[:2]
    nseq = nhi * 4
    hi, low = lax.div(seq, 4), lax.rem(seq, 4)
    y, c = lax.div(low, 2), lax.rem(low, 2)

    def place(dp_to, hi_to, y_to, c_to):
        return (dp_to, hi_to * 4 + y_to * 2 + c_to)

    hi_index = [lax.rem(hi + k, nhi) for k in range(1, nhi)]
    dp_index = [lax.rem(dp + k, ndp) for k in range(1, ndp)]
    hi_peers = [place(dp, h, y, c) for h in hi_index]
    dp_peers = [place(d, hi, y, c) for d in dp_index]
    y_peer, c_peer = place(dp, hi, 1 - y, c), place(dp, hi, y, 1 - c)
    everyone = hi_peers + dp_peers + [y_peer, c_peer]
    if mode:
        head, part = lax.div(seq, parts), lax.rem(seq, parts)
        head_of = [lax.rem(head + k, H) for k in range(1, H)]
        head_peers = [(dp, h * parts + part) for h in head_of]
        part_peers = [(dp, head * parts + slot_part(part, k, parts)) for k in range(1, parts)]
        everyone = everyone + head_peers + part_peers

    barrier = pltpu.get_barrier_semaphore()
    for peer in everyone:
        pl.semaphore_signal(barrier, inc=1, device_id=peer, device_id_type=MESH)
    expected = len(everyone)
    me = dp * nseq + seq
    if n_small:

        def other_device(k):
            there = lax.rem(me + k, n_small)
            return (lax.div(there, nseq), lax.rem(there, nseq))

        @pl.loop(1, n_small)
        def _(k):
            pl.semaphore_signal(barrier, inc=1, device_id=other_device(k), device_id_type=MESH)

        expected += n_small - 1
    pl.semaphore_wait(barrier, expected)

    def remote(source, target, ss, rs, peer):
        return pltpu.make_async_remote_copy(
            src_ref=source,
            dst_ref=target,
            send_sem=ss,
            recv_sem=rs,
            device_id=peer,
            device_id_type=MESH,
        )

    def half_of(array):
        return outs[array].shape[1] // 2

    def columns_of(unit, core):
        array, row, rows, column, columns = unit
        half = half_of(array)
        spot = pl.multiple_of(core * half + column, 128)
        return terms[array].at[:, :, :, :, pl.ds(row, rows), pl.ds(spot, columns)]

    def load(n):
        return pltpu.make_async_copy(columns_of(flat[n][1], c), own[n], load_sem.at[n])

    def over_core(n):
        source = going_of(n) if made_here else columns_of(flat[n][1], 1 - c)
        return [remote(source, arrived[n], c_send.at[n], c_recv.at[n], c_peer)]

    def first_hop(n):
        if flat[n][0] == 0:
            return [
                remote(own[n].at[d], hop1[n].at[k], s1.at[n, k], r1.at[n, k], p)
                for k, (d, p) in enumerate(zip(dp_index, dp_peers, strict=True))
            ]
        return [remote(own[n].at[:, :, 1 - y], hop1[n], s1.at[n, 0], r1.at[n, 0], y_peer)]

    def second_hop(n):
        if flat[n][0] == 0:
            return [remote(own[n].at[dp, :, 1 - y], hop2[n], s2.at[n, 0], r2.at[n, 0], y_peer)]
        return [
            remote(own[n].at[d, :, y], hop2[n].at[k], s2.at[n, k], r2.at[n, k], p)
            for k, (d, p) in enumerate(zip(dp_index, dp_peers, strict=True))
        ]

    def along_line(n):
        return [
            remote(own[n].at[dp, h, y], line[n].at[k], s3.at[n, k], r3.at[n, k], p)
            for k, (h, p) in enumerate(zip(hi_index, hi_peers, strict=True))
        ]

    def back_home(n):
        return [remote(result[n].at[1 - c], back[n], s4.at[n], r4.at[n], c_peer)]

    hops = (over_core, first_hop, second_hop, along_line, back_home)

    def add(a, b):
        return (a.astype(F32) + b.astype(F32)).astype(BF)

    def absorb(n, stage):
        mine = own[n]
        if stage == 1:

            @pl.loop(0, ndp * nhi)
            def _(k):
                d, h = lax.div(k, nhi), lax.rem(k, nhi)
                mine[d, h] = add(mine[d, h], arrived[n][d, h])

        elif stage == 2 and flat[n][0] == 0:

            @pl.loop(0, nhi)
            def _(h):
                total = mine[dp, h].astype(F32)
                for k in range(ndp - 1):
                    total = total + hop1[n][k, h].astype(F32)
                mine[dp, h] = total.astype(BF)

        elif stage == 2:

            @pl.loop(0, ndp * nhi)
            def _(k):
                d, h = lax.div(k, nhi), lax.rem(k, nhi)
                mine[d, h, y] = add(mine[d, h, y], hop1[n][d, h])

        elif stage == 3 and flat[n][0] == 0:

            @pl.loop(0, nhi)
            def _(h):
                mine[dp, h, y] = add(mine[dp, h, y], hop2[n][h])

        elif stage == 3:

            @pl.loop(0, nhi)
            def _(h):
                total = mine[dp, h, y].astype(F32)
                for k in range(ndp - 1):
                    total = total + hop2[n][k, h].astype(F32)
                mine[dp, h, y] = total.astype(BF)

        elif stage == 4:
            total = mine[dp, hi, y].astype(F32)
            for k in range(nhi - 1):
                total = total + line[n][k].astype(F32)
            result[n][...] = total
        else:
            array, row, rows, column, columns = flat[n][1]
            half = half_of(array)
            here, there = result[n][c], back[n][...]
            outs[array][row : row + rows, column : column + columns] = jnp.where(
                c == 0, here, there
            )
            outs[array][row : row + rows, half + column : half + column + columns] = jnp.where(
                c == 0, there, here
            )

    numbers, serial = [], 0
    for group in groups:
        size = len(group[0]) + len(group[1])
        numbers.append(range(serial, serial + size))
        serial += size

    def going_of(n):
        step = next(k for k, some in enumerate(numbers) if n in some)
        unit = flat[n][1]
        side = numbers[step].index(n)
        return going.at[step % 2, side, :, :, :, :, pl.ds(0, unit[2]), pl.ds(0, unit[4])]

    def fetch_left(array):
        left = terms[2 * array]
        return pltpu.make_async_copy(
            left,
            lefts[0].at[pl.ds(0, left.shape[0]), pl.ds(0, left.shape[1])],
            left_sem.at[array],
        )

    def fetch_right(array):
        right = terms[2 * array + 1]
        return pltpu.make_async_copy(
            right,
            rights[array % 2].at[pl.ds(0, right.shape[0]), pl.ds(0, right.shape[1])],
            right_sem.at[array],
        )

    def arrive():
        for copy in head_own:
            copy.wait()
        for copy in head_copies:
            copy.wait_recv()
        packed = rights[(n_terms - 1) % 2]
        windows, rows = gathered.shape[1], gathered.shape[3]
        for w in range(windows):
            for pair in range(H // 2):
                for first, size, start in ((0, KD, 0), (KD, KD, H * KD), (2 * KD, VD, 2 * H * KD)):
                    both = jnp.concatenate(
                        [gathered[2 * pair + h, w, first : first + size, :] for h in range(2)], axis=0
                    )
                    at = start + pair * 2 * size
                    packed[w * rows : (w + 1) * rows, at : at + 2 * size] = both.T

    def make(step):
        units = [flat[n][1] for n in numbers[step]]
        array, rows = units[0][0], units[0][2]
        first, size = units[0][3], sum(u[4] for u in units)
        left = terms[2 * array]
        tokens, slot = left.shape[0], array % 2
        if step == 0 or flat[numbers[step - 1][0]][1][0] != array:
            fetch_left(array).wait()

            @pl.loop(0, left.shape[1] // 256)
            def _(k):
                spot = pl.multiple_of(k * 256, 256)
                turned[slot][pl.ds(spot, 256), pl.ds(0, tokens)] = lefts[0][
                    pl.ds(0, tokens), pl.ds(spot, 256)
                ].T

            if array + 1 < n_terms:
                fetch_left(array + 1).start()
                if array >= 1 and not (late and array + 1 == n_terms - 1):
                    fetch_right(array + 1).start()
            if late and array == n_terms - 1:
                arrive()
            else:
                fetch_right(array).wait()

        if step >= 2:
            for n in numbers[step - 2]:
                for copy in over_core(n):
                    copy.wait_send()
        span = nhi * 4 * rows
        for whose in (1 - c, c):
            spot = pl.multiple_of(whose * half_of(array) + first, 128)
            part_right = rights[slot][pl.ds(0, tokens), pl.ds(spot, size)]
            for d in range(ndp):
                made = dot(turned[slot][pl.ds(d * span, span), pl.ds(0, tokens)], part_right)
                made = made.astype(BF).reshape(nhi, 2, 2, rows, size)
                at = 0
                for k, n in enumerate(numbers[step]):
                    piece = made[..., at : at + units[k][4]]
                    if whose is c:
                        own[n][d] = piece
                    else:
                        going[step % 2, k, d, :, :, :, pl.ds(0, rows), pl.ds(0, units[k][4])] = piece
                    at += units[k][4]
            if whose is not c:
                for n in numbers[step]:
                    for copy in over_core(n):
                        copy.start()

    def launch(step):
        if made_here:
            make(step)
        else:
            for n in numbers[step]:
                load(n).start()
                for copy in over_core(n):
                    copy.start()

    if made_here:
        fetch_left(0).start()
        for array in range(min(2, n_terms)):
            if not (late and array == n_terms - 1):
                fetch_right(array).start()

    if mode == "in":
        head_send, head_recv, head_local = take(3)
        blocks, gathered = head_in[0], head_out[0]
        head_copies = [
            remote(blocks.at[:, h], gathered.at[head], head_send.at[k], head_recv.at[k], p)
            for k, (h, p) in enumerate(zip(head_of, head_peers, strict=True))
        ]
        head_own = [
            pltpu.make_async_copy(blocks.at[:, head], gathered.at[head], head_local.at[0])
        ]
        for copy in head_copies + head_own:
            copy.start()
    if mode == "block":
        head_send, head_recv, head_local, gathered = take(4)
        blocks = head_in[0]
        windows = blocks.shape[1]
        by_window = [
            [
                remote(
                    blocks.at[h, w],
                    gathered.at[head, w],
                    head_send.at[w, k],
                    head_recv.at[w, k],
                    p,
                )
                for k, (h, p) in enumerate(zip(head_of, head_peers, strict=True))
            ]
            for w in range(windows)
        ]
        head_copies = [copy for some in by_window for copy in some]
        head_own = [
            pltpu.make_async_copy(blocks.at[head, w], gathered.at[head, w], head_local.at[w])
            for w in range(windows)
        ]
        for copy in by_window[0] + head_own:
            copy.start()

        def wait_heads(w):
            head_own[w].wait()
            for copy in by_window[w]:
                copy.wait_recv()

        begin_block, block_jobs, finish_block = block_work(
            block_in, block_out, take(20), gathered, wait_heads
        )
        begin_block()
    if mode == "out":
        head_send, head_recv, head_local, part_send, part_recv, mine_kv, arrived_kv = take(7)
        query, pair_mine, pair_other = head_in
        gathered = take(1)[0] if late else head_out[0]
        part_copies = [
            remote(pair_other.at[k], arrived_kv.at[k], part_send.at[k], part_recv.at[k], p)
            for k, p in enumerate(part_peers)
        ]
        kv_load = pltpu.make_async_copy(pair_mine, mine_kv, head_local.at[0])
        for copy in part_copies + [kv_load]:
            copy.start()
    if n_small:
        small_send, small_recv, small_sc = take(3)
        small = small_in[0]
    if masked:
        w_v, x_v, y_v, masked_sem = take(4)
        w_masked_load = pltpu.make_async_copy(w_masked, w_v, masked_sem.at[0])
        w_masked_load.start()
        windows, fine = masked_o.shape[:2]
        tile = x_v.shape[0]

        def masked_product(k):
            w, at = divmod(k * tile, fine)
            load = pltpu.make_async_copy(terms[0].at[pl.ds(k * tile, tile)], x_v, masked_sem.at[1])
            load.start()
            load.wait()
            if k == 0:
                w_masked_load.wait()
            made = dot(x_v[...], w_v[...])
            bin_ = seq * (fine // 2) + lax.div(
                at + lax.broadcasted_iota(jnp.int32, made.shape, 0), 2
            )
            y_v[...] = jnp.where(bin_ < lengths[w], made, 0.0).astype(BF)
            store = pltpu.make_async_copy(
                y_v, masked_o.at[w, pl.ds(at, tile)], masked_sem.at[2]
            )
            store.start()
            store.wait()

    if late:
        small, w_buffer, acc, flat_v, middle_v, out_v, gain_sum, late_sem = take(8)
        w_loads = [
            pltpu.make_async_copy(w_query, w_buffer.at[:, pl.ds(0, H * KD)], late_sem.at[0]),
            pltpu.make_async_copy(w_key, w_buffer.at[:, pl.ds(H * KD, H * KD)], late_sem.at[1]),
        ]
        for copy in w_loads:
            copy.start()

        def window_loads(w):
            span = pl.ds(w * flat_v.shape[0], flat_v.shape[0])
            return [
                pltpu.make_async_copy(values.at[w], flat_v, late_sem.at[2]),
                pltpu.make_async_copy(middle_grad.at[span], middle_v, late_sem.at[3]),
            ]

        def store_window(w):
            span = pl.ds(w * flat_v.shape[0], flat_v.shape[0])
            return pltpu.make_async_copy(out_v, input_grad.at[span], late_sem.at[4])

        for copy in window_loads(0):
            copy.start()

        def back_through(w_ref, first, columns, into_first):
            packed = rights[(n_terms - 1) % 2]

            @pl.loop(0, acc.shape[0] // 128)
            def _(k):
                rows = pl.ds(pl.multiple_of(k * 128, 128), 128)
                made = lax.dot_general(
                    packed[rows, first : first + columns],
                    w_ref[:, 0:columns],
                    (((1,), (1,)), ((), ())),
                    preferred_element_type=F32,
                )
                acc[rows, :] = made if into_first else acc[rows, :] + made

        def value_load(k):
            half = H * VD // 2
            return pltpu.make_async_copy(
                w_value.at[:, pl.ds(k * half, half)],
                w_buffer.at[:, pl.ds(0, half)],
                late_sem.at[5 + k],
            )

        def products(stage):
            half = H * VD // 2
            if stage == 0:
                for copy in w_loads:
                    copy.wait()
                back_through(w_buffer, 0, 2 * H * KD, True)
                value_load(0).start()
            else:
                value_load(0).wait()
                back_through(w_buffer, 2 * H * KD, half, False)
                value_load(1).start()
                value_load(1).wait()
                back_through(w_buffer, 2 * H * KD + half, half, False)

        def norm_back(w):
            for copy in window_loads(w):
                copy.wait()
            if w:
                store_window(w - 1).wait()
            else:
                gain_sum[...] = jnp.zeros(gain_sum.shape, F32)
            size = flat_v.shape[0]

            @pl.loop(0, size // 32)
            def _(k):
                rows = pl.ds(pl.multiple_of(k * 32, 32), 32)
                value = flat_v[rows, :].astype(F32)
                centered = value - jnp.mean(value, axis=-1, keepdims=True)
                scale = lax.rsqrt(jnp.mean(centered * centered, axis=-1, keepdims=True) + epsilon)
                unit = centered * scale
                grad = acc[pl.ds(pl.multiple_of(w * size + k * 32, 32), 32), :]
                gain_sum[...] += jnp.sum(grad * unit, axis=0, keepdims=True)
                grad = grad * gain[...]
                along = jnp.mean(grad * unit, axis=-1, keepdims=True)
                back = scale * (grad - jnp.mean(grad, axis=-1, keepdims=True) - unit * along)
                out_v[rows, :] = (middle_v[rows, :] + back).astype(BF)

            store_window(w).start()
            if w + 1 < values.shape[0]:
                for copy in window_loads(w + 1):
                    copy.start()
            else:
                rows = dot32(pick[...] * gain_sum[...], spread[...].astype(F32), ((1,), (1,)))
                wide = small_in[0].shape[1]
                small[:, :wide, :] = small_in[0][...]
                small[:, wide:, :] = jnp.broadcast_to(
                    rows[:, None, :], (rows.shape[0], 8, rows.shape[1])
                )

    if n_small:

        def small_copy(k):
            there = lax.rem(me + k, n_small)
            return remote(
                small.at[there],
                small_sc.at[k - 1],
                small_send.at[k - 1],
                small_recv.at[k - 1],
                other_device(k),
            )

        def start_small():
            @pl.loop(1, n_small)
            def _(k):
                small_copy(k).start()

        if not late:
            start_small()

    ahead = 3
    for step in range(min(ahead, len(groups))):
        launch(step)
    if mode == "block":
        for some in by_window[1:]:
            for copy in some:
                copy.start()
    if mode == "out":
        for copy in part_copies:
            copy.wait_recv()
        kv_load.wait()

        @pl.loop(0, H)
        def _(g):
            total = mine_kv[g].astype(F32)
            for k in range(parts - 1):
                total = total + arrived_kv[k, g].astype(F32)
            mine_kv[g] = total.astype(BF)

        q_target = gathered.at[head, :, pl.ds(0, KD)]
        kv_target = gathered.at[head, :, pl.ds(KD, KD + VD)]
        head_copies = [
            remote(source.at[h], target, head_send.at[i, k], head_recv.at[i, k], p)
            for k, (h, p) in enumerate(zip(head_of, head_peers, strict=True))
            for i, (source, target) in enumerate(((query, q_target), (mine_kv, kv_target)))
        ]
        head_own = [
            pltpu.make_async_copy(query.at[head], q_target, head_local.at[1]),
            pltpu.make_async_copy(mine_kv.at[head], kv_target, head_local.at[2]),
        ]
        for copy in head_copies + head_own:
            copy.start()
    lag = 2
    for step in range(len(groups) + 4 * lag):
        for stage in (5, 4, 3, 2, 1):
            spot = step - lag * (stage - 1)
            if 0 <= spot < len(groups):
                for n in numbers[spot]:
                    if stage == 1 and not made_here:
                        load(n).wait()
                    for copy in hops[stage - 1](n):
                        copy.wait_recv()
                    absorb(n, stage)
                    if stage < 5:
                        for copy in hops[stage](n):
                            copy.start()
        if step + ahead < len(groups):
            launch(step + ahead)
        if mode == "block":
            steps = len(groups) + 4 * lag
            for job in block_jobs[
                step * len(block_jobs) // steps : (step + 1) * len(block_jobs) // steps
            ]:
                job()
        if masked and 0 <= step - (len(groups) - ahead) < terms[0].shape[0] // tile:
            masked_product(step - (len(groups) - ahead))
        if late and step >= len(groups) - ahead:
            turn = step - (len(groups) - ahead)
            if turn < 2:
                products(turn)
            elif turn < 2 + values.shape[0]:
                norm_back(turn - 2)
                if turn == 1 + values.shape[0]:
                    start_small()
    if n_small:

        @pl.loop(1, n_small)
        def _(k):
            small_copy(k).wait_recv()

        small_out[0][...] = small[me] + jnp.sum(small_sc[...], axis=0)

        @pl.loop(1, n_small)
        def _(k):
            small_copy(k).wait_send()

    if late:
        store_window(values.shape[0] - 1).wait()
    if mode == "block":
        finish_block()
    if mode:
        if not late and mode != "block":
            for copy in head_own:
                copy.wait()
            for copy in head_copies:
                copy.wait_recv()
        for copy in head_copies:
            copy.wait_send()
    if mode == "out":
        for copy in part_copies:
            copy.wait_send()
    for n in range(count):
        for hop in hops:
            if hop is not over_core or not made_here or n in tuple(numbers[-1]) + tuple(numbers[-2]):
                for copy in hop(n):
                    copy.wait_send()


def sum_terms(name, collective, pairs, groups, mode=None, heads=(), small=None, late=None, masked=None, block=None):
    ndp, nseq = lax.axis_size("dp"), lax.axis_size("seq")
    nhi, parts, devices = nseq // 4, nseq // H, ndp * nseq
    shares = [(left.shape[1] // devices, right.shape[1]) for left, right in pairs]
    made_here = all(rows % 16 == 0 for rows, _ in shares)
    if made_here:
        operands = [x for pair in pairs for x in pair][: -1 if late else None]
    else:
        operands = [
            transposed_times(left, right).astype(BF).reshape((ndp, nhi, 2, 2) + share)
            for (left, right), share in zip(pairs, shares, strict=True)
        ]
    in_specs = [pl.BlockSpec(memory_space=pl.ANY)] * len(operands)
    out_shape = [jax.ShapeDtypeStruct(share, F32) for share in shares]
    out_specs = [pl.BlockSpec(memory_space=pltpu.VMEM)] * len(out_shape)
    flat = [(side, unit) for group in groups for side in (0, 1) for unit in group[side]]
    count = len(flat)
    shapes = [(unit[2], unit[4]) for _, unit in flat]
    sides = [side for side, _ in flat]
    scratch = [pltpu.VMEM((ndp, nhi, 2, 2) + s, BF) for s in shapes] * 2
    scratch += [
        pltpu.VMEM(((ndp, nhi, 2) if side else (ndp - 1, nhi, 2, 2)) + s, BF)
        if not side
        else pltpu.VMEM((ndp, nhi, 2) + s, BF)
        for side, s in zip(sides, shapes, strict=True)
    ]
    scratch += [
        pltpu.VMEM((ndp - 1, nhi, 2) + s if side else (nhi, 2) + s, BF)
        for side, s in zip(sides, shapes, strict=True)
    ]
    scratch += [pltpu.VMEM((nhi - 1, 2) + s, BF) for s in shapes]
    scratch += [pltpu.VMEM((2,) + s, F32) for s in shapes]
    scratch += [pltpu.VMEM(s, F32) for s in shapes]
    if made_here:
        slots = [pairs[k::2] for k in range(min(2, len(pairs)))]
        tokens = [max(left.shape[0] for left, _ in slot) for slot in slots]
        tall = [max(left.shape[1] for left, _ in slot) for slot in slots]
        wide = [max(right.shape[1] for _, right in slot) for slot in slots]
        unit_rows = max(rows for rows, _ in shapes)
        unit_columns = max(columns for _, columns in shapes)
        scratch += [
            pltpu.VMEM((max(tokens), max(tall)), BF),
            *[pltpu.VMEM(s, BF) for s in zip(tokens, wide, strict=True)],
            *[pltpu.VMEM(s, BF) for s in zip(tall, tokens, strict=True)],
            pltpu.VMEM((2, 2, ndp, nhi, 2, 2, unit_rows, unit_columns), BF),
            pltpu.SemaphoreType.DMA((len(pairs),)),
            pltpu.SemaphoreType.DMA((len(pairs),)),
        ]
    hop = max(ndp - 1, 1)
    sizes = [(count,)] * 3 + [(count, hop)] * 4 + [(count, nhi - 1)] * 2 + [(count,)] * 2
    scratch += [pltpu.SemaphoreType.DMA(size) for size in sizes]
    if mode == "in":
        windows, _, size, rows = heads[0].shape
        operands.append(heads[0])
        in_specs.append(pl.BlockSpec(memory_space=pl.ANY))
        out_shape.append(jax.ShapeDtypeStruct((H, windows, size, rows), BF))
        out_specs.append(pl.BlockSpec(memory_space=pl.ANY))
        scratch += [pltpu.SemaphoreType.DMA((n,)) for n in (H - 1, H - 1, 1)]
    if mode == "block":
        operands += [heads[0], *block]
        in_specs += [pl.BlockSpec(memory_space=pl.ANY)] * 6
        in_specs += [pl.BlockSpec(memory_space=pltpu.VMEM)] * 4
        windows, rows, width = block[0].shape
        wide = block[3].shape[1]
        coarse, broad = (windows * rows, width), (windows * rows, wide)
        out_shape += [
            jax.ShapeDtypeStruct(s, BF)
            for s in (coarse, coarse, broad, coarse, coarse, broad, coarse)
        ]
        out_shape.append(jax.ShapeDtypeStruct(coarse, F32))
        out_shape.append(jax.ShapeDtypeStruct((windows, H, VD, rows), BF))
        out_shape += [jax.ShapeDtypeStruct((1, n), F32) for n in (width, width, wide, width)]
        out_specs += [pl.BlockSpec(memory_space=pl.ANY)] * 9
        out_specs += [pl.BlockSpec(memory_space=pltpu.VMEM)] * 4
        narrow, long = pltpu.VMEM((rows, width), BF), pltpu.VMEM((rows, wide), BF)
        full_rows = pltpu.VMEM((rows, width), F32)
        scratch += [
            pltpu.SemaphoreType.DMA((windows, H - 1)),
            pltpu.SemaphoreType.DMA((windows, H - 1)),
            pltpu.SemaphoreType.DMA((windows,)),
            pltpu.VMEM(heads[0].shape, BF),
            *[pltpu.VMEM(w.shape, BF) for w in block[2:5]],
            narrow,
            full_rows,
            full_rows,
            full_rows,
            long,
            narrow,
            narrow,
            long,
            narrow,
            narrow,
            long,
            narrow,
            full_rows,
            pltpu.VMEM((H, VD, rows), BF),
            pltpu.SemaphoreType.DMA((3,)),
            pltpu.SemaphoreType.DMA((2,)),
            pltpu.SemaphoreType.DMA((9,)),
        ]
    if mode == "out":
        _, windows, _, rows = heads[0].shape
        operands += list(heads)
        in_specs += [pl.BlockSpec(memory_space=pl.ANY)] * 3
        if not late:
            out_shape.append(jax.ShapeDtypeStruct((H, windows, 2 * KD + VD, rows), BF))
            out_specs.append(pl.BlockSpec(memory_space=pl.ANY))
        scratch += [
            pltpu.SemaphoreType.DMA(size)
            for size in ((2, H - 1), (2, H - 1), (3,), (parts - 1,), (parts - 1,))
        ]
        scratch += [pltpu.VMEM(heads[1].shape, BF), pltpu.VMEM(heads[2].shape, BF)]
        if late:
            scratch.append(pltpu.VMEM((H, windows, 2 * KD + VD, rows), BF))
    n_small = 0
    if small is not None:
        n_small = devices
        operands.append(small)
        in_specs.append(pl.BlockSpec(memory_space=pltpu.VMEM))
        message = (small.shape[1] + (8 if late else 0), small.shape[2])
        out_shape.append(jax.ShapeDtypeStruct(message, F32))
        out_specs.append(pl.BlockSpec(memory_space=pltpu.VMEM))
        scratch += [
            pltpu.SemaphoreType.DMA((devices - 1,)),
            pltpu.SemaphoreType.DMA((devices - 1,)),
            pltpu.VMEM((devices - 1,) + message, F32),
        ]
    if late:
        windows, rows, width = late[3].shape
        operands += list(late) + list(spread_tables(width, width // devices))
        in_specs += [pl.BlockSpec(memory_space=pl.ANY)] * 5
        in_specs += [pl.BlockSpec(memory_space=pltpu.VMEM)] * 3
        out_shape.append(jax.ShapeDtypeStruct((windows * rows, width), BF))
        out_specs.append(pl.BlockSpec(memory_space=pl.ANY))
        scratch += [
            pltpu.VMEM((devices,) + message, F32),
            pltpu.VMEM((width, 2 * H * KD), BF),
            pltpu.VMEM((windows * rows, width), F32),
            pltpu.VMEM((rows, width), BF),
            pltpu.VMEM((rows, width), F32),
            pltpu.VMEM((rows, width), BF),
            pltpu.VMEM((1, width), F32),
            pltpu.SemaphoreType.DMA((7,)),
        ]
    if masked:
        lengths, weight, shape = masked
        operands += [lengths, weight]
        in_specs += [pl.BlockSpec(memory_space=pltpu.SMEM), pl.BlockSpec(memory_space=pl.ANY)]
        out_shape.append(jax.ShapeDtypeStruct(shape, BF))
        out_specs.append(pl.BlockSpec(memory_space=pl.ANY))
        scratch += [
            pltpu.VMEM(weight.shape, BF),
            pltpu.VMEM((256, shape[2]), BF),
            pltpu.VMEM((256, shape[2]), BF),
            pltpu.SemaphoreType.DMA((3,)),
        ]
    plan = (
        groups, len(pairs), mode, parts, n_small, made_here, late is not None, masked is not None
    )
    return pl.pallas_call(
        functools.partial(sums_kernel, plan, None),
        out_shape=out_shape,
        in_specs=in_specs,
        out_specs=out_specs,
        scratch_shapes=scratch,
        compiler_params=pltpu.CompilerParams(
            collective_id=collective, has_side_effects=True, vmem_limit_bytes=63 * 2**20
        ),
        name=name,
    )(*operands)


def halves(array, rows, columns, size=128):
    out, spot = [], 0
    while spot < columns:
        size = min(size, (columns - spot) // 2)
        out.append((((array, 0, rows, spot, size),), ((array, 0, rows, spot + size, size),)))
        spot += 2 * size
    return tuple(out)


def full(array, shards):
    rows, columns = shards[array].shape
    return (array, 0, rows, 0, columns)


def columns_of_rows(array, rows, first, columns):
    return (array, 0, rows, first, columns)


def gelu_parts(x):
    below = 0.5 * (1.0 + lax.erf(x * (0.5**0.5)))
    density = jnp.exp(-0.5 * x * x) * (1.0 / math.sqrt(2.0 * math.pi))
    return x * below, below + x * density


def norm_parts(value):
    centered = value - jnp.mean(value, axis=-1, keepdims=True)
    scale = lax.rsqrt(jnp.mean(centered * centered, axis=-1, keepdims=True) + epsilon)
    return centered * scale, scale


def norm_backward(unit, scale, grad, gain):
    grad = grad * gain
    along = jnp.mean(grad * unit, axis=-1, keepdims=True)
    return scale * (grad - jnp.mean(grad, axis=-1, keepdims=True) - unit * along)


def times_rows(x, table):
    return lax.dot_general(x, table, (((1,), (1,)), ((), ())), preferred_element_type=F32)


def weight_pairs(shapes, offset):
    def pieces(n, parts):
        rows, columns = shapes[n]
        if rows % (16 * parts):
            return [(offset + n, 0, rows, 0, columns)]
        size = rows // parts
        return [(offset + n, k * size, size, 0, columns) for k in range(parts)]

    first = pieces(5, 3) + pieces(0, 3) + pieces(4, 3) + pieces(2, 3)
    second = pieces(1, 3) + pieces(3, 6)
    steps = max(len(second), 1)
    spare = len(first) - steps
    pairs, spot = [], 0
    for k in range(steps):
        take = 2 if 3 <= k < 3 + spare else 1
        pairs.append((tuple(first[spot : spot + take]), (second[k],)))
        spot += take
    if spot < len(first):
        pairs.append((tuple(first[spot:]), ()))
    return tuple(pairs)


def on_device(
    inputs,
    skip_input,
    lengths,
    cotangent,
    first_gain,
    query_weight,
    key_weight,
    value_weight,
    content_bias,
    position_bias,
    relative_weight,
    mixing_weight,
    second_gain,
    inner_weight,
    inner_bias,
    outer_weight,
    outer_bias,
    third_gain,
    upsample_weight,
    skip_weight,
    skip_bias,
    depth_weight,
    point_weight,
):
    windows, rows, width = inputs.shape
    scale = float(KD) ** (-0.5)
    nseq, ndp = lax.axis_size("seq"), lax.axis_size("dp")
    devices = nseq * ndp
    parts = nseq // H
    keys_total = rows * nseq
    seq = lax.axis_index("seq")
    head, part = lax.div(seq, parts), lax.rem(seq, parts)
    first = seq * rows
    hidden_width = inner_weight.shape[1]

    r = shard_rows = query_weight.shape[0]
    vectors = (
        first_gain,
        content_bias,
        position_bias,
        second_gain,
        inner_bias,
        outer_bias,
        third_gain,
        skip_bias,
    )
    small_rows = [v.reshape(1, -1) for v in vectors] + [depth_weight.T]
    small_rows = [jnp.pad(v, ((0, 0), (0, 128 - v.shape[1]))) for v in small_rows]
    small_rows.append(jnp.zeros((16 - len(vectors) - 3, 128), BF))
    relative_rows = relative_weight.shape[0]
    small_rows.append(
        jnp.pad(relative_weight, ((0, -relative_rows % 16), (0, 128 - relative_weight.shape[1])))
    )
    small_shard = jnp.concatenate(small_rows, axis=0)
    keys_width, values_width = 2 * H * KD, H * VD
    half_hidden, half_width = hidden_width // 2, width // 2
    head_shards = [small_shard, query_weight, key_weight, value_weight]
    head_pairs = (
        ((full(0, head_shards), full(1, head_shards)), (full(2, head_shards),)),
        ((columns_of_rows(3, r, 0, values_width // 2),), (columns_of_rows(3, r, values_width // 2, values_width // 2),)),
    )
    shards = [
        skip_weight,
        mixing_weight,
        inner_weight,
        outer_weight,
        upsample_weight,
        point_weight,
    ]
    if r % 16 == 0:
        (
            small_full,
            weight_query,
            weight_key,
            weight_value,
            weight_skip,
            weight_mixing,
            weight_inner,
            weight_outer,
            weight_upsample,
            weight_point,
            mine,
            other,
            normed_low,
            out_grad,
            conv_grad,
            joined_flat,
            lifted_grad,
            third_grad,
            skip_grad,
            skip_part,
            grad_skip_bias,
        ) = use_links(
            "gather_weights",
            1,
            head_shards + shards,
            head_pairs + weight_pairs([w.shape for w in shards], len(head_shards)),
            values=inputs,
            early=len(head_pairs),
            upper=(lengths, cotangent, skip_input),
        )
        out_grad, joined_flat, skip_part = (
            x.reshape(-1, width) for x in (out_grad, joined_flat, skip_part)
        )
        grad_skip_bias = grad_skip_bias[0]
    else:
        small_full, weight_query, weight_key, weight_value = use_links(
            "gather_heads", 1, head_shards, head_pairs
        )
    small_full = small_full.reshape((devices,) + small_shard.shape).astype(jnp.float32)

    def vector(k):
        return small_full[:, k, : vectors[k].shape[0]].reshape(-1)

    (
        gain_first,
        bias_content,
        bias_position,
        gain_second,
        bias_inner,
        bias_outer,
        gain_third,
        bias_skip,
    ) = map(vector, range(len(vectors)))
    taken = len(vectors)
    weight_depth = (
        small_full[:, taken : taken + 3, :r].transpose(0, 2, 1).reshape(width, 3)
    )
    weight_relative = small_full[:, 16 : 16 + relative_rows, :RPF].reshape(H * KD, RPF)

    lives = jnp.exp(
        jnp.linspace(math.log(3.0), math.log(keys_total), RPF // 2, dtype=jnp.float32)
    )
    rates = (math.log(2.0) / lives)[:, None]
    bias_gap = ((bias_position - bias_content) * scale).reshape(H, KD, 1)
    bias_gap = lax.dynamic_index_in_dim(bias_gap, head, 0, keepdims=False)
    relative = lax.dynamic_index_in_dim(
        weight_relative.reshape(H, KD, RPF), head, 0, keepdims=False
    ).T
    info = jnp.concatenate([lengths, part[None].astype(jnp.int32)])
    groups = [[p + parts * g for g in range(H)] for p in range(parts)]

    def exchange(array):
        return lax.all_to_all(array, "seq", 0, 0, axis_index_groups=groups, tiled=True)

    def swap_part(array, slot):
        return lax.ppermute(array, "seq", [(i, i ^ slot) for i in range(nseq)])

    flat = inputs.reshape(windows * rows, width).astype(jnp.float32)
    if r % 16:
        normed_low, sent = project(
            inputs, gain_first, bias_content, weight_query, weight_key, weight_value
        )
        (
            weight_skip,
            weight_mixing,
            weight_inner,
            weight_outer,
            weight_upsample,
            weight_point,
            mine,
            other,
        ) = use_links(
            "gather_weights", 2, shards, weight_pairs([w.shape for w in shards], 0), sent
        )

    def by_row(array):
        (array,) = tie(array.transpose(1, 3, 0, 2).reshape(windows * rows, -1))
        return array

    mixed_own, mixed_wide, log_total = attention_forward(
        info, rates, bias_gap, relative, mine, other, parts
    )
    if r % 16 == 0:
        skip_flat = skip_input.reshape(windows * 2 * rows, width)
        (
            own_skip,
            mixed_low,
            second_low,
            hidden_low,
            third_low,
            block_low,
            before_low,
            middle_low,
            middle_grad,
            mixed_grad,
            *block_sums,
        ) = sum_terms(
            "block_and_skip",
            6,
            [(skip_flat, joined_flat)],
            halves(0, r, half_width),
            "block",
            (mixed_own,),
            block=(
                inputs,
                third_grad,
                weight_mixing,
                weight_inner,
                weight_outer,
                gain_second[None, :],
                gain_third[None, :],
                bias_inner[None, :],
                bias_outer[None, :],
            ),
        )
        grad_second, grad_third, grad_inner_bias, grad_outer_bias = (s[0] for s in block_sums)
    else:
        mixed_low = by_row(exchange(mixed_own))
        middle = flat + matmul(mixed_low, weight_mixing)
        second, second_norm_back = jax.vjp(layer_norm, middle, gain_second)
        second_low = second.astype(jnp.bfloat16)
        before = matmul(second_low, weight_inner) + bias_inner
        hidden, gelu_back = jax.vjp(smooth_gelu, before)
        hidden_low = hidden.astype(jnp.bfloat16)
        block_out = middle + matmul(hidden_low, weight_outer) + bias_outer
        third, third_back = jax.vjp(norm_gelu, block_out, gain_third)
        third_low = third.astype(jnp.bfloat16)
    fine = jnp.arange(2 * rows, dtype=jnp.int32)[:, None] // 2
    twice = (fine == jnp.arange(rows, dtype=jnp.int32)[None, :]).astype(jnp.bfloat16)
    third_twice = (
        jnp.einsum(
            "ts,wsd->wtd",
            twice,
            third_low.reshape(windows, rows, width),
            preferred_element_type=jnp.float32,
        )
        .astype(jnp.bfloat16)
        .reshape(windows * 2 * rows, width)
    )
    skip_flat = skip_input.reshape(windows * 2 * rows, width)
    if r % 16:
        skip_part = matmul(skip_flat, weight_skip) + bias_skip
    joined_low = (
        (matmul(third_twice, weight_upsample) + skip_part)
        .astype(jnp.bfloat16)
        .reshape(windows, 2 * rows, width)
    )
    joined_rim = extended_2(joined_low, (("seq", 1),), 1)
    taps = weight_depth
    joined_wide = joined_rim.astype(jnp.float32)
    conv_low = depth_apply(joined_wide, taps).astype(jnp.bfloat16)
    conv_flat = conv_low.reshape(windows * 2 * rows, width)
    bins = 2 * first + jnp.arange(2 * rows, dtype=jnp.int32)
    keep = (bins // 2)[None, :] < lengths[:, None]
    keep_wide = keep.astype(jnp.float32)[:, :, None]
    if r % 16:
        outputs = (
            matmul(conv_flat, weight_point).reshape(windows, 2 * rows, width) * keep_wide
        ).astype(jnp.bfloat16)
    if r % 16:
        out_grad = (cotangent * keep.astype(jnp.bfloat16)[:, :, None]).reshape(
            windows * 2 * rows, width
        )
        conv_grad = (
            times_transposed(out_grad, weight_point)
            .astype(jnp.bfloat16)
            .reshape(windows, 2 * rows, width)
        )
        grad_rim = extended_2(conv_grad, (("seq", 1),), 1).astype(jnp.float32)
        joined_grad = (
            grad_rim[:, 2:] * taps[:, 0]
            + grad_rim[:, 1:-1] * taps[:, 1]
            + grad_rim[:, :-2] * taps[:, 2]
        )
        grad_skip_bias = jnp.sum(joined_grad, axis=(0, 1))
        joined_back = joined_grad.astype(jnp.bfloat16)
        joined_flat = joined_back.reshape(windows * 2 * rows, width)
        lifted_grad = (
            jnp.einsum("ts,wtd->wsd", twice, joined_back, preferred_element_type=jnp.float32)
            .astype(jnp.bfloat16)
            .reshape(windows * rows, width)
        )
        third_grad = times_transposed(lifted_grad, weight_upsample)
        skip_grad = (
            times_transposed(joined_flat, weight_skip)
            .astype(jnp.bfloat16)
            .reshape(windows, 2 * rows, width)
        )
    conv_wide = conv_grad.astype(jnp.float32)
    grad_depth = jnp.stack(
        [
            jnp.sum(conv_wide * joined_wide[:, :-2], axis=(0, 1)),
            jnp.sum(conv_wide * joined_wide[:, 1:-1], axis=(0, 1)),
            jnp.sum(conv_wide * joined_wide[:, 2:], axis=(0, 1)),
        ],
        axis=1,
    )
    if r % 16:
        block_grad, grad_third = third_back(third_grad)
        block_low = block_grad.astype(jnp.bfloat16)
        grad_outer_bias = jnp.sum(block_grad, axis=0)
        (before_grad,) = gelu_back(times_transposed(block_low, weight_outer))
        before_low = before_grad.astype(jnp.bfloat16)
        grad_inner_bias = jnp.sum(before_low.astype(jnp.float32), axis=0)
        middle_part, grad_second = second_norm_back(times_transposed(before_low, weight_inner))
        middle_grad = block_grad + middle_part
        middle_low = middle_grad.astype(jnp.bfloat16)
        middle_rows = middle_low.reshape(windows, rows, width)
        mixed_grad = (
            jnp.einsum("vd,wrd->wvr", weight_mixing, middle_rows, preferred_element_type=jnp.float32)
            .astype(jnp.bfloat16)
            .reshape(windows, H, VD, rows)
        )
    if r % 16 == 0:
        own_point, own_outer, own_upsample, arrived_grad, outputs = sum_terms(
            "sum_upper",
            3,
            [(conv_flat, out_grad), (hidden_low, block_low), (third_low, lifted_grad)],
            halves(0, r, half_width)
            + halves(1, outer_weight.shape[0], half_width)
            + halves(2, r, half_width),
            "in",
            (mixed_grad,),
            masked=(lengths, weight_point, skip_input.shape),
        )
    else:
        own_point, own_outer, own_skip, own_upsample, arrived_grad = sum_terms(
            "sum_upper",
            3,
            [
                (conv_flat, out_grad),
                (hidden_low, block_low),
                (skip_flat, joined_flat),
                (third_low, lifted_grad),
            ],
            halves(0, r, half_width)
            + halves(1, outer_weight.shape[0], half_width)
            + halves(2, r, half_width)
            + halves(3, r, half_width),
            "in",
            (mixed_grad,),
        )
    query_own, own_side, other_side, bias_sums, relative_sum = attention_backward(
        info, rates, bias_gap, relative, mine, other, arrived_grad, mixed_wide, log_total, parts
    )

    def at_head(value):
        full = jnp.zeros((H,) + value.shape, jnp.float32)
        return lax.dynamic_update_index_in_dim(full, value, head, 0)

    pieces = [
        at_head(bias_sums[0, :, 0]).reshape(-1),
        at_head(bias_sums[1, :, 0]).reshape(-1),
        at_head(relative_sum).reshape(H * KD, RPF),
        grad_second,
        grad_inner_bias,
        grad_outer_bias,
        grad_third,
        grad_skip_bias,
        grad_depth,
    ]

    def pack(pieces):
        packed = jnp.concatenate([p.reshape(devices, -1) for p in pieces], axis=1)
        return jnp.pad(packed, ((0, 0), (0, -packed.shape[1] % 1024))).reshape(devices, -1, 128)

    lower = [(second_low, before_low), (mixed_low, middle_low)]
    lower_groups = halves(0, r, half_hidden) + halves(1, r, half_width)
    lower_heads = (query_own, own_side, other_side)
    packed_width = keys_width + values_width
    if r % 16 == 0:
        right = jax.ShapeDtypeStruct((windows * rows, packed_width), BF)
        own_inner, own_mixing, own_heads, small_total, input_grad = sum_terms(
            "sum_lower",
            4,
            lower + [(normed_low, right)],
            lower_groups + halves(2, r, packed_width // 2),
            "out",
            lower_heads,
            pack(pieces),
            (weight_query, weight_key, weight_value, inputs, middle_grad, gain_first[None, :]),
        )
        own_first = small_total[-8, : width // devices]
        input_grad = input_grad.reshape(windows, rows, width)
        names = pieces
    else:
        own_inner, own_mixing, heads_grad = sum_terms(
            "sum_lower", 4, lower, lower_groups, "out", lower_heads
        )
        packed_grad = jnp.concatenate(
            [
                by_row(heads_grad[:, :, :KD]),
                by_row(heads_grad[:, :, KD : 2 * KD]),
                by_row(heads_grad[:, :, 2 * KD :]),
            ],
            axis=1,
        )
        (packed_grad,) = tie(packed_grad)
        normed_grad = (
            times_transposed(packed_grad[:, : H * KD], weight_query)
            + times_transposed(packed_grad[:, H * KD : keys_width], weight_key)
            + times_transposed(packed_grad[:, keys_width:], weight_value)
        )
        _, first_norm_back = jax.vjp(layer_norm, flat, gain_first)
        input_part, grad_first = first_norm_back(normed_grad)
        input_grad = (middle_grad + input_part).astype(jnp.bfloat16).reshape(windows, rows, width)
        names = [grad_first] + pieces
        own_heads, small_total = sum_terms(
            "sum_heads",
            5,
            [(normed_low, packed_grad)],
            halves(0, r, packed_width // 2),
            small=pack(names),
        )
    small_total, spot, small_grads = small_total.reshape(-1), 0, []
    for p in names:
        size = p.size // devices
        small_grads.append(
            small_total[spot : spot + size].reshape((p.shape[0] // devices,) + p.shape[1:])
        )
        spot += size
    if len(names) > len(pieces):
        own_first = small_grads.pop(0)
    (
        own_content,
        own_position,
        own_relative,
        own_second,
        own_inner_bias,
        own_outer_bias,
        own_third,
        own_skip_bias,
        own_depth,
    ) = small_grads
    return (
        outputs,
        input_grad,
        skip_grad,
        own_first,
        own_heads[:, : H * KD],
        own_heads[:, H * KD : keys_width],
        own_heads[:, keys_width:],
        own_content,
        own_position,
        own_relative,
        own_mixing,
        own_second,
        own_inner,
        own_inner_bias,
        own_outer,
        own_outer_bias,
        own_third,
        own_upsample,
        own_skip,
        own_skip_bias,
        own_depth,
        own_point,
    )


def solution(mesh):
    in_specs = (
        P("dp", "seq", None),
        P("dp", "seq", None),
        P("dp"),
        P("dp", "seq", None),
        P(("dp", "seq")),
        P(("dp", "seq"), None),
        P(("dp", "seq"), None),
        P(("dp", "seq"), None),
        P(("dp", "seq")),
        P(("dp", "seq")),
        P(("dp", "seq"), None),
        P(("dp", "seq"), None),
        P(("dp", "seq")),
        P(("dp", "seq"), None),
        P(("dp", "seq")),
        P(("dp", "seq"), None),
        P(("dp", "seq")),
        P(("dp", "seq")),
        P(("dp", "seq"), None),
        P(("dp", "seq"), None),
        P(("dp", "seq")),
        P(("dp", "seq"), None),
        P(("dp", "seq"), None),
    )
    out_specs = (
        P("dp", "seq", None),
        P("dp", "seq", None),
        P("dp", "seq", None),
        P(("dp", "seq")),
        P(("dp", "seq"), None),
        P(("dp", "seq"), None),
        P(("dp", "seq"), None),
        P(("dp", "seq")),
        P(("dp", "seq")),
        P(("dp", "seq"), None),
        P(("dp", "seq"), None),
        P(("dp", "seq")),
        P(("dp", "seq"), None),
        P(("dp", "seq")),
        P(("dp", "seq"), None),
        P(("dp", "seq")),
        P(("dp", "seq")),
        P(("dp", "seq"), None),
        P(("dp", "seq"), None),
        P(("dp", "seq")),
        P(("dp", "seq"), None),
        P(("dp", "seq"), None),
    )
    return jax.shard_map(
        on_device, mesh=mesh, in_specs=in_specs, out_specs=out_specs, check_vma=False
    )
```

```python
import functools
import math

import jax
import jax.numpy as jnp
from jax import lax
from jax.experimental import pallas as pl
from jax.experimental.pallas import tpu as pltpu
from jax.sharding import PartitionSpec as P

H = 8
KD = 64
VD = 192
RPF = 32
NEG = -1e30
BF = jnp.bfloat16
F32 = jnp.float32
epsilon = 1e-05


def extended_2(array, sides, width):
    for axis, dim in sides:
        peers, length = (lax.axis_size(axis), array.shape[dim])
        up = [(i, (i + 1) % peers) for i in range(peers - 1)]
        down = [(j, i) for i, j in up]
        last = lax.slice_in_dim(array, length - width, length, axis=dim)
        initial = lax.slice_in_dim(array, 0, width, axis=dim)
        before = lax.ppermute(last, axis, up)
        after = lax.ppermute(initial, axis, down)
        array = jnp.concatenate([before, array, after], axis=dim)
    return array


def layer_norm(values, gain):
    mean = jnp.mean(values, axis=-1, keepdims=True)
    centered = values - mean
    spread = jnp.mean(centered * centered, axis=-1, keepdims=True)
    return centered * lax.rsqrt(spread + epsilon) * gain


def smooth_gelu(values):
    return jax.nn.gelu(values, approximate=False)


def norm_gelu(values, gain):
    return smooth_gelu(layer_norm(values, gain))


def matmul(left, right):
    return jnp.dot(left, right, preferred_element_type=jnp.float32)


def times_transposed(left, right):
    return lax.dot_general(
        left, right, (((1,), (1,)), ((), ())), preferred_element_type=jnp.float32
    )


def transposed_times(left, right):
    return lax.dot_general(
        left, right, (((0,), (0,)), ((), ())), preferred_element_type=jnp.float32
    )


def depth_apply(extended, taps):
    return (
        extended[:, :-2] * taps[:, 0]
        + extended[:, 1:-1] * taps[:, 1]
        + extended[:, 2:] * taps[:, 2]
    )


def dot(a, b):
    return lax.dot_general(a, b, (((1,), (0,)), ((), ())), preferred_element_type=F32)


def dot32(a, b, dims=((1,), (0,))):
    return lax.dot_general(
        a, b, (dims, ((), ())), precision=lax.Precision.HIGHEST, preferred_element_type=F32
    )


def key_side(parts, part, groups, mine, other, store):
    for slot in range(parts):
        theirs = slot_part(part, slot, parts)
        for g in range(groups):
            if slot == 0:
                kt, vt = mine[g, 0, KD : 2 * KD, :], mine[g, 0, 2 * KD :, :]
            else:
                kt, vt = other[slot - 1, g, 0, :KD, :], other[slot - 1, g, 0, KD:, :]
            store(g * parts + theirs, kt, vt)


def slot_part(part, slot, parts):
    out, bit = part, 1
    while bit < parts:
        if slot & bit:
            has = lax.rem(lax.div(part, bit), 2)
            out = out + bit - 2 * bit * has
        bit *= 2
    return out


def query_side(content, bias, relative, half):
    positional = content.astype(F32) + bias
    projected = dot32(relative, positional).astype(BF).astype(F32)
    return positional, projected[:half] + projected[half:], projected[:half] - projected[half:]


def query_block(content, plus, minus, rates):
    spot = lax.broadcasted_iota(jnp.int32, plus.shape, 1).astype(F32)
    last = plus.shape[1] - 1
    from_first, to_last = jnp.exp(-rates * spot), jnp.exp(-rates * (last - spot))
    rest = jnp.zeros((128 - KD - RPF, content.shape[1]), BF)
    block = jnp.concatenate(
        [content, (plus * from_first).astype(BF), (minus * to_last).astype(BF), rest], axis=0
    )
    return block, from_first, to_last


def lane_rates(rates_row):
    lane = lax.broadcasted_iota(jnp.int32, (1, 128), 1)
    half = RPF // 2
    below = (lane >= KD) & (lane < KD + half)
    above = (lane >= KD + half) & (lane < KD + RPF)
    return rates_row, below, above


def decay_table(rates_row, span):
    rates_row, below, above = lane_rates(rates_row)
    spot = lax.broadcasted_iota(jnp.int32, (span, 128), 0).astype(F32)
    table = jnp.where(below, jnp.exp(-rates_row * (span - 1 - spot)), 0.0)
    return jnp.where(above, jnp.exp(-rates_row * spot), table)


def key_decays(table, rates_row, first_query, last_query, first_key, span, kind):
    rates_row, below, above = lane_rates(rates_row)
    if kind == "plain":
        before = first_key < first_query
        gap = jnp.where(before, first_query - (first_key + span - 1), first_key - last_query)
        used = (below & before) | (above & jnp.logical_not(before))
        return (table * jnp.where(used, jnp.exp(-rates_row * gap.astype(F32)), 0.0)).astype(BF)
    key = first_key + lax.broadcasted_iota(jnp.int32, (span, 128), 0)
    down = jnp.exp(jnp.minimum(-rates_row * (first_query - key).astype(F32), 60.0))
    up = jnp.exp(jnp.minimum(-rates_row * (key - last_query).astype(F32), 60.0))
    return jnp.where(below, down, 0.0).astype(BF), jnp.where(above, up, 0.0).astype(BF)


def order_of(first_query, first_key, span, rows):
    i = first_query + lax.broadcasted_iota(jnp.int32, (span, rows), 1)
    j = first_key + lax.broadcasted_iota(jnp.int32, (span, rows), 0)
    return i, j


def tile_scores(keys, decays, query, first_query, first_key, length, kind):
    if kind != "both":
        return dot(keys + decays, query)
    s_below, s_above = dot(keys + decays[0], query), dot(keys + decays[1], query)
    i, j = order_of(first_query, first_key, *s_below.shape)
    scores = jnp.where(i > j, s_below, jnp.where(i < j, s_above, 0.5 * (s_below + s_above)))
    return jnp.where(j < length, scores, NEG)


def visit_tiles(scores_into, use, slots, whole_tile, q_block, length, rows, per):
    span = rows * per
    count = lax.div(length + span - 1, span)
    full = lax.div(length, span)
    own = lax.div(q_block, per)
    plain = full - jnp.where(own < full, 1, 0)

    def tile_of(k):
        return k + jnp.where(k >= own, 1, 0)

    @pl.when(plain > 0)
    def _():
        scores_into(slots[0], tile_of(0), own)

    @pl.loop(0, lax.div(plain, 2))
    def _(k):
        first = 2 * k
        scores_into(slots[1], tile_of(first + 1), own)
        use(slots[0], tile_of(first), own)
        scores_into(slots[0], tile_of(jnp.minimum(first + 2, plain - 1)), own)
        use(slots[1], tile_of(first + 1), own)

    @pl.when(lax.rem(plain, 2) == 1)
    def _():
        use(slots[0], tile_of(plain - 1), own)

    @pl.loop(0, 2)
    def _(k):
        t = jnp.where(k == 0, own, full)
        go = (t < count) & ((k == 0) | (full != own))

        @pl.when(go)
        def _():
            whole_tile(t)


def forward_kernel(
    parts, per, info, rates_ref, lanes_ref, bias_ref, rel_ref, mine, other, mixed, wide, lse, k_sc, v_sc, table_sc, s0_sc, s1_sc, m_sc, l_sc, acc
):
    groups, rows = mine.shape[0], mine.shape[3]
    half = RPF // 2
    length = info[pl.program_id(0)]
    part = info[pl.num_programs(0)]
    rates = rates_ref[...]

    def store(block, kt, vt):
        spot = pl.multiple_of(block * rows, rows)
        k_sc[pl.ds(spot, rows), :] = jnp.concatenate([kt, jnp.zeros_like(kt)], axis=0).T
        v_sc[:, pl.ds(spot, rows)] = vt

    key_side(parts, part, groups, mine, other, store)
    span = rows * per
    table_sc[...] = decay_table(lanes_ref[...], span)

    @pl.loop(0, groups)
    def _(g):
        q_block = g * parts + part

        @pl.when(q_block * rows > length)
        def _():
            mixed[g, 0] = jnp.zeros(mixed.shape[2:], mixed.dtype)
            wide[g, 0] = jnp.zeros(wide.shape[2:], wide.dtype)
            lse[g, 0] = jnp.zeros(lse.shape[2:], lse.dtype)

        @pl.when(q_block * rows <= length)
        def _():
            content = mine[g, 0, :KD, :]
            _, plus, minus = query_side(content, bias_ref[...], rel_ref[...], half)
            query, _, _ = query_block(content, plus, minus, rates)
            first_query = q_block * rows
            m_sc[...] = jnp.full(m_sc.shape, NEG, F32)
            l_sc[...] = jnp.zeros(l_sc.shape, F32)
            acc[...] = jnp.zeros(acc.shape, F32)

            def scores_of(t, kind):
                first_key = pl.multiple_of(t * span, span)
                decays = key_decays(
                    table_sc[...], lanes_ref[...], first_query, first_query + rows - 1, first_key, span, kind
                )
                keys = k_sc[pl.ds(first_key, span), :]
                return tile_scores(keys, decays, query, first_query, first_key, length, kind)

            def scores_into(slot, t, own):
                slot[...] = scores_of(t, "plain")

            def use(slot, t, own):
                scores = slot[...]
                old = m_sc[...]
                new = jnp.maximum(old, jnp.max(scores, axis=0, keepdims=True))
                alpha = jnp.exp(old - new)
                probs = jnp.exp(scores - new)
                m_sc[...] = new
                l_sc[...] = l_sc[...] * alpha + jnp.sum(probs, axis=0, keepdims=True)
                values = v_sc[:, pl.ds(pl.multiple_of(t * span, span), span)]
                acc[...] = acc[...] * alpha + dot(values, probs.astype(BF))

            def whole_tile(t):
                s0_sc[...] = scores_of(t, "both")
                use(s0_sc, t, None)

            visit_tiles(scores_into, use, (s0_sc, s1_sc), whole_tile, q_block, length, rows, per)
            total = l_sc[...]
            out = acc[...] / total
            mixed[g, 0] = out.astype(BF)
            wide[g, 0] = out
            lse[g, 0] = jnp.broadcast_to(m_sc[...] + jnp.log(total), lse.shape[2:])


def backward_kernel(
    parts, per, info, rates_ref, lanes_ref, bias_ref, rel_ref, mine, other, grad, wide, lse,
    dq, dkv_mine, dkv_other, sums, rel_grad,
    k_sc, kt_sc, v_sc, table_sc, turned_sc, s0_sc, s1_sc, dk_sc, dv_sc, dq_sc, bias_sc,
):
    groups, rows = mine.shape[0], mine.shape[3]
    half = RPF // 2
    step = pl.program_id(0)
    length = info[step]
    part = info[pl.num_programs(0)]
    rates = rates_ref[...]
    scale = KD**-0.5

    def store(block, kt, vt):
        spot = pl.multiple_of(block * rows, rows)
        k_sc[pl.ds(spot, rows), :] = jnp.concatenate([kt, jnp.zeros_like(kt)], axis=0).T
        kt_sc[:, pl.ds(spot, rows)] = kt
        v_sc[pl.ds(spot, rows), :] = vt.T

    key_side(parts, part, groups, mine, other, store)
    span = rows * per
    table_sc[...] = decay_table(lanes_ref[...], span)
    turned_sc[...] = table_sc[...].T[KD : KD + RPF]
    dk_sc[...] = jnp.zeros(dk_sc.shape, F32)
    dv_sc[...] = jnp.zeros(dv_sc.shape, F32)

    @pl.when(step == 0)
    def _():
        bias_sc[...] = jnp.zeros(bias_sc.shape, F32)
        rel_grad[...] = jnp.zeros(rel_grad.shape, F32)

    @pl.loop(0, groups)
    def _(g):
        q_block = g * parts + part

        @pl.when(q_block * rows > length)
        def _():
            dq[g, 0] = jnp.zeros(dq.shape[2:], dq.dtype)

        @pl.when(q_block * rows <= length)
        def _():
            content = mine[g, 0, :KD, :]
            content_rows = content.T
            positional, plus, minus = query_side(content, bias_ref[...], rel_ref[...], half)
            query, from_first, to_last = query_block(content, plus, minus, rates)
            first_query = q_block * rows
            last_query = first_query + rows - 1
            grad_t = grad[g, 0]
            grad_rows = grad_t.T
            log_total = lse[g, 0, :1, :]
            row_sum = jnp.sum(grad_t.astype(F32) * wide[g, 0], axis=0, keepdims=True)
            dq_sc[...] = jnp.zeros(dq_sc.shape, F32)

            def decays_of(first_key, kind):
                return key_decays(
                    table_sc[...], lanes_ref[...], first_query, last_query, first_key, span, kind
                )

            def scores_of(t, decays, kind):
                first_key = pl.multiple_of(t * span, span)
                keys = k_sc[pl.ds(first_key, span), :]
                return tile_scores(keys, decays, query, first_query, first_key, length, kind)

            def scores_into(slot, t, own):
                first_key = pl.multiple_of(t * span, span)
                slot[0] = scores_of(t, decays_of(first_key, "plain"), "plain")
                slot[1] = dot(v_sc[pl.ds(first_key, span), :], grad_t)

            def use(slot, t, own):
                absorb(slot, t, "plain", None)

            def whole_tile(t):
                first_key = pl.multiple_of(t * span, span)
                decays = decays_of(first_key, "both")
                s0_sc[0] = scores_of(t, decays, "both")
                s0_sc[1] = dot(v_sc[pl.ds(first_key, span), :], grad_t)
                absorb(s0_sc, t, "both", decays)

            def absorb(slot, t, kind, decays):
                first_key = spot = pl.multiple_of(t * span, span)
                scores, prob_grad = slot[0], slot[1]
                exact = jnp.exp(scores - log_total)
                score_grad = exact * (prob_grad - row_sum)
                low = score_grad.astype(BF)
                dv_sc[pl.ds(spot, span), :] += dot(exact.astype(BF), grad_rows)
                dk_sc[pl.ds(spot, span), :] += dot(low, content_rows)
                keys_turned = kt_sc[:, pl.ds(spot, span)]
                if kind == "both":
                    i, j = order_of(first_query, first_key, span, rows)
                    equal = 0.5 * score_grad
                    lower = jnp.where(i > j, score_grad, jnp.where(i < j, 0.0, equal)).astype(BF)
                    upper = jnp.where(i < j, score_grad, jnp.where(i > j, 0.0, equal)).astype(BF)
                    dq_sc[:KD] += dot(keys_turned, low)
                    below, above = decays
                    dq_sc[KD : KD + half] += dot(below.T[KD : KD + half], lower)
                    dq_sc[KD + half : KD + RPF] += dot(above.T[KD + half : KD + RPF], upper)
                else:
                    before = first_key < first_query
                    gap = jnp.where(before, first_query - (first_key + span - 1), first_key - last_query)
                    faded = jnp.exp(-rates * gap.astype(F32))
                    down = turned_sc[:half] * jnp.where(before, faded, 0.0)
                    up = turned_sc[half:] * jnp.where(before, 0.0, faded)
                    pos = jnp.concatenate([down, up], axis=0).astype(BF)
                    dq_sc[...] += dot(jnp.concatenate([keys_turned, pos], axis=0), low)

            visit_tiles(scores_into, use, (s0_sc, s1_sc), whole_tile, q_block, length, rows, per)
            content_grad = dq_sc[:KD]
            down, up = dq_sc[KD : KD + half] * from_first, dq_sc[KD + half :] * to_last
            projected_grad = jnp.concatenate([down + up, down - up], axis=0)
            positional_grad = dot32(rel_ref[...], projected_grad, ((0,), (0,)))
            dq[g, 0] = (scale * (content_grad + positional_grad)).astype(BF)
            bias_sc[0] += content_grad
            bias_sc[1] += positional_grad
            rel_grad[...] += dot32(positional, projected_grad, ((1,), (1,)))

    for slot in range(parts):
        theirs = slot_part(part, slot, parts)
        for g in range(groups):
            spot = pl.multiple_of((g * parts + theirs) * rows, rows)
            dkt = dk_sc[pl.ds(spot, rows), :].astype(BF).T
            dvt = dv_sc[pl.ds(spot, rows), :].astype(BF).T
            both = jnp.concatenate([dkt, dvt], axis=0)
            if slot == 0:
                dkv_mine[g, 0] = both
            else:
                dkv_other[slot - 1, g, 0] = both

    @pl.when(step == pl.num_programs(0) - 1)
    def _():
        sums[...] = scale * jnp.sum(bias_sc[...], axis=-1, keepdims=True)


def attention_cost(windows, groups, rows, parts, wide):
    pairs = windows * groups * rows * groups * parts * rows
    return pl.CostEstimate(
        flops=int(pairs * 2 * wide * 0.75), bytes_accessed=20_000_000, transcendentals=int(pairs)
    )


def whole(*shape):
    return pl.BlockSpec(shape, lambda w: (0,) * len(shape))


def per_window(*shape):
    lead = len(shape) - 3
    return pl.BlockSpec(shape, lambda w: (0,) * lead + (w, 0, 0))


def tile_blocks(rows, groups, parts, target):
    per = max(1, target // rows)
    while (groups * parts) % per:
        per -= 1
    return per


def lanes_of(rates):
    line = rates.reshape(1, -1)
    return jnp.pad(jnp.concatenate([line, line], axis=1), ((0, 0), (KD, 128 - KD - RPF)))


def attention_forward(info, rates, bias, rel, mine, other, parts):
    groups, windows, _, rows = mine.shape
    per = tile_blocks(rows, groups, parts, 1024)
    total = groups * parts * rows
    return pl.pallas_call(
        functools.partial(forward_kernel, parts, per),
        grid=(windows,),
        out_shape=(
            jax.ShapeDtypeStruct((groups, windows, VD, rows), BF),
            jax.ShapeDtypeStruct((groups, windows, VD, rows), F32),
            jax.ShapeDtypeStruct((groups, windows, 8, rows), F32),
        ),
        in_specs=[
            pl.BlockSpec(memory_space=pltpu.SMEM),
            whole(*rates.shape),
            whole(1, 128),
            whole(*bias.shape),
            whole(*rel.shape),
            per_window(groups, 1, 2 * KD + VD, rows),
            per_window(parts - 1, groups, 1, KD + VD, rows),
        ],
        out_specs=(
            per_window(groups, 1, VD, rows),
            per_window(groups, 1, VD, rows),
            per_window(groups, 1, 8, rows),
        ),
        scratch_shapes=[
            pltpu.VMEM((total, 128), BF),
            pltpu.VMEM((VD, total), BF),
            pltpu.VMEM((rows * per, 128), F32),
            pltpu.VMEM((rows * per, rows), F32),
            pltpu.VMEM((rows * per, rows), F32),
            pltpu.VMEM((1, rows), F32),
            pltpu.VMEM((1, rows), F32),
            pltpu.VMEM((VD, rows), F32),
        ],
        compiler_params=pltpu.CompilerParams(vmem_limit_bytes=56 * 2**20),
        cost_estimate=attention_cost(windows, groups, rows, parts, 128 + 256),
        name="attention_forward",
    )(info, rates, lanes_of(rates), bias, rel, mine, other)


def attention_backward(info, rates, bias, rel, mine, other, grad, wide, lse, parts):
    groups, windows, _, rows = mine.shape
    per = tile_blocks(rows, groups, parts, 1024)
    total = groups * parts * rows
    return pl.pallas_call(
        functools.partial(backward_kernel, parts, per),
        grid=(windows,),
        out_shape=(
            jax.ShapeDtypeStruct((groups, windows, KD, rows), BF),
            jax.ShapeDtypeStruct((groups, windows, KD + VD, rows), BF),
            jax.ShapeDtypeStruct((parts - 1, groups, windows, KD + VD, rows), BF),
            jax.ShapeDtypeStruct((2, KD, 1), F32),
            jax.ShapeDtypeStruct((KD, RPF), F32),
        ),
        in_specs=[
            pl.BlockSpec(memory_space=pltpu.SMEM),
            whole(*rates.shape),
            whole(1, 128),
            whole(*bias.shape),
            whole(*rel.shape),
            per_window(groups, 1, 2 * KD + VD, rows),
            per_window(parts - 1, groups, 1, KD + VD, rows),
            per_window(groups, 1, VD, rows),
            per_window(groups, 1, VD, rows),
            per_window(groups, 1, 8, rows),
        ],
        out_specs=(
            per_window(groups, 1, KD, rows),
            per_window(groups, 1, KD + VD, rows),
            per_window(parts - 1, groups, 1, KD + VD, rows),
            whole(2, KD, 1),
            whole(KD, RPF),
        ),
        scratch_shapes=[
            pltpu.VMEM((total, 128), BF),
            pltpu.VMEM((KD, total), BF),
            pltpu.VMEM((total, VD), BF),
            pltpu.VMEM((rows * per, 128), F32),
            pltpu.VMEM((RPF, rows * per), F32),
            pltpu.VMEM((2, rows * per, rows), F32),
            pltpu.VMEM((2, rows * per, rows), F32),
            pltpu.VMEM((total, KD), F32),
            pltpu.VMEM((total, VD), F32),
            pltpu.VMEM((KD + RPF, rows), F32),
            pltpu.VMEM((2, KD, rows), F32),
        ],
        compiler_params=pltpu.CompilerParams(vmem_limit_bytes=56 * 2**20),
        cost_estimate=attention_cost(windows, groups, rows, parts, 3 * 256 + 2 * 256),
        name="attention_backward",
    )(info, rates, lanes_of(rates), bias, rel, mine, other, grad, wide, lse)

MESH = pl.DeviceIdType.MESH


def upper_work(here, lengths, cotangent, skip_input, outs, gathered, scratch, remote, neighbours):
    out_grad_o, conv_o, joined_o, lifted_o, third_o, skip_grad_o, skip_part_o, bias_o = outs
    (
        table_rows,
        lines,
        w_point,
        w_skip,
        w_upsample,
        grad_v,
        skip_v,
        conv_v,
        joined_v,
        lifted_v,
        part_v,
        halo_before,
        halo_after,
        sem,
        halo_sem,
    ) = scratch
    dp, seq = here
    windows, fine, width = grad_v.shape
    rows = fine // 2
    before, after = neighbours

    def load(source, target, n):
        return pltpu.make_async_copy(source, target, sem.at[n])

    point_load = load(gathered[9], w_point, 0)
    skip_load = load(gathered[4], w_skip, 1)
    upsample_load = load(gathered[8], w_upsample, 2)
    grad_load = load(cotangent, grad_v, 3)
    input_load = load(skip_input, skip_v, 4)
    grad_load.start()
    input_load.start()
    stores = {
        "out_grad": load(grad_v, out_grad_o, 5),
        "conv": load(conv_v, conv_o, 6),
        "joined": load(joined_v, joined_o, 7),
        "lifted": load(lifted_v, lifted_o, 8),
        "skip": load(skip_v, skip_grad_o, 9),
    }

    def against(x, table):
        return lax.dot_general(
            x, table[...].reshape(width, width), (((1,), (1,)), ((), ())), preferred_element_type=F32
        )

    def halo_copies():
        out = []
        for w in range(windows):
            out.append(
                remote(
                    conv_v.at[w, pl.ds(fine - 16, 16)],
                    halo_before.at[w],
                    halo_sem.at[0, w],
                    halo_sem.at[1, w],
                    after,
                )
            )
            out.append(
                remote(
                    conv_v.at[w, pl.ds(0, 16)],
                    halo_after.at[w],
                    halo_sem.at[2, w],
                    halo_sem.at[3, w],
                    before,
                )
            )
        return out

    def conv_grad(w):
        if w == 0:
            point_load.start()
            grad_load.wait()
            point_load.wait()
        length = lengths[w]

        @pl.loop(0, fine // 256)
        def _(k):
            at = pl.ds(pl.multiple_of(k * 256, 256), 256)
            bin_ = seq * rows + lax.div(
                k * 256 + lax.broadcasted_iota(jnp.int32, (256, width), 0), 2
            )
            grad = jnp.where(bin_ < length, grad_v[w, at, :].astype(F32), 0.0).astype(BF)
            grad_v[w, at, :] = grad
            conv_v[w, at, :] = against(grad, w_point).astype(BF)

        if w == windows - 1:
            stores["out_grad"].start()
            stores["conv"].start()
            for copy in halo_copies():
                copy.start()

    def skip_part(w):
        if w == 0:
            skip_load.start()
            input_load.wait()
            skip_load.wait()

        @pl.loop(0, fine // 256)
        def _(k):
            at = pl.ds(pl.multiple_of(k * 256, 256), 256)
            made = dot(skip_v[w, at, :], w_skip[...].reshape(width, width)) + lines[0:1, :]
            part_v[...] = made
            store = load(part_v, skip_part_o.at[w, at], 10)
            store.start()
            store.wait()

    def joined_grad():
        for copy in halo_copies():
            copy.wait_recv()
        total = jnp.zeros((1, width), F32)
        tap = [lines[n : n + 1, :] for n in (1, 2, 3)]
        tile = 64
        for w in range(windows):
            first = halo_before[w].astype(F32)[15:16, :]
            first = jnp.where(seq == 0, 0.0, first)
            last = halo_after[w].astype(F32)[0:1, :]
            last = jnp.where(seq == lax.axis_size("seq") - 1, 0.0, last)
            for k in range(fine // tile):
                at = slice(k * tile, (k + 1) * tile)
                here_rows = conv_v[w, at, :].astype(F32)
                up = first if k == 0 else conv_v[w, k * tile - 16 : k * tile, :].astype(F32)[15:16, :]
                down = (
                    last
                    if k == fine // tile - 1
                    else conv_v[w, (k + 1) * tile : (k + 1) * tile + 16, :].astype(F32)[0:1, :]
                )
                index = lax.broadcasted_iota(jnp.int32, here_rows.shape, 0)
                earlier = jnp.where(index == 0, up, pltpu.roll(here_rows, 1, 0))
                later = jnp.where(index == tile - 1, down, pltpu.roll(here_rows, tile - 1, 0))
                made = later * tap[0] + here_rows * tap[1] + earlier * tap[2]
                total = total + jnp.sum(made, axis=0, keepdims=True)
                joined_v[w, at, :] = made.astype(BF)
        bias_o[...] = total
        stores["joined"].start()
        pair = lax.div(lax.broadcasted_iota(jnp.int32, (rows, fine), 1), 2)
        twice = (pair == lax.broadcasted_iota(jnp.int32, (rows, fine), 0)).astype(F32).astype(BF)
        for w in range(windows):
            lifted_v[w * rows : (w + 1) * rows, :] = dot(twice, joined_v[w]).astype(BF)
        stores["lifted"].start()

    def skip_grad(w):
        @pl.loop(0, fine // 256)
        def _(k):
            at = pl.ds(pl.multiple_of(k * 256, 256), 256)
            skip_v[w, at, :] = against(joined_v[w, at, :], w_skip).astype(BF)

        if w == windows - 1:
            stores["skip"].start()

    def third_grad():
        upsample_load.start()
        upsample_load.wait()

        @pl.loop(0, windows * rows // 256)
        def _(k):
            at = pl.ds(pl.multiple_of(k * 256, 256), 256)
            part_v[...] = against(lifted_v[at, :], w_upsample)
            store = load(part_v, third_o.at[at], 10)
            store.start()
            store.wait()

    def finish():
        for store in stores.values():
            store.wait()
        for copy in halo_copies():
            copy.wait_send()

    jobs = {
        9: [(9, functools.partial(conv_grad, 0))],
        10: [(None, functools.partial(conv_grad, 1))],
        11: [(4, functools.partial(skip_part, 0)), (None, functools.partial(skip_part, 1))],
        12: [(None, joined_grad)],
        13: [(None, functools.partial(skip_grad, 0)), (None, functools.partial(skip_grad, 1))],
        14: [(8, third_grad)],
    }
    return {"rows": table_rows, "lines": lines, "jobs": jobs, "finish": finish}


def links_kernel(pairs, counts, parts, early, *refs):
    n_in, n_out = counts
    refs = list(refs)

    def take(count):
        out, refs[:count] = refs[:count], []
        return out

    refs_in = take(n_in)
    if early:
        values, spread_gain, pick_gain, spread_bias, pick_bias = take(5)
        lengths, cotangent, skip_input = take(3)
    elif parts:
        (blocks,) = take(1)
    refs_out = take(n_out)
    if parts:
        mine, other = take(2)
    if early:
        (normed,) = take(1)
        upper_out = take(8)
    local_sem, send_hi, recv_hi, send_y, recv_y, send_dp, recv_dp, send_c, recv_c = take(9)
    dp, seq = lax.axis_index("dp"), lax.axis_index("seq")
    ndp, nhi = refs_out[0].shape[:2]
    hi, low = lax.div(seq, 4), lax.rem(seq, 4)
    y, c = lax.div(low, 2), lax.rem(low, 2)

    def place(dp_to, hi_to, y_to, c_to):
        return (dp_to, hi_to * 4 + y_to * 2 + c_to)

    hi_peers = [place(dp, lax.rem(hi + k, nhi), y, c) for k in range(1, nhi)]
    y_peers = [place(dp, hi, 1 - y, c)]
    dp_peers = [place(lax.rem(dp + k, ndp), hi, y, c) for k in range(1, ndp)]
    c_peers = [place(dp, hi, y, 1 - c)]
    everyone = hi_peers + y_peers + dp_peers + c_peers
    if parts:
        head, part = lax.div(seq, parts), lax.rem(seq, parts)
        head_of = [lax.rem(head + k, H) for k in range(1, H)]
        head_peers = [(dp, h * parts + part) for h in head_of]
        part_peers = [(dp, head * parts + slot_part(part, k, parts)) for k in range(1, parts)]
        everyone = everyone + head_peers + part_peers
    if early:
        nseq = nhi * 4
        after = (dp, lax.rem(seq + 1, nseq))
        before = (dp, lax.rem(seq + nseq - 1, nseq))
        everyone = everyone + [after, before]

    barrier = pltpu.get_barrier_semaphore()
    for peer in everyone:
        pl.semaphore_signal(barrier, inc=1, device_id=peer, device_id_type=MESH)
    pl.semaphore_wait(barrier, len(everyone))

    def remote(source, target, ss, rs, peer):
        return pltpu.make_async_remote_copy(
            src_ref=source,
            dst_ref=target,
            send_sem=ss,
            recv_sem=rs,
            device_id=peer,
            device_id_type=MESH,
        )

    step_chunks, serial = [], 0
    for pair in pairs:
        step_chunks.append([])
        for side in (0, 1):
            for chunk in pair[side]:
                step_chunks[-1].append((serial, side) + chunk)
                serial += 1

    def copies(chunk, stage):
        n, side, array, row, rows, first, columns = chunk
        out = refs_out[array]
        piece = (pl.ds(row, rows), pl.ds(first, columns))
        which = (("hi", "y", "dp", "c"), ("hi", "dp", "y", "c"))[side][stage]
        if which == "hi":
            target = out.at[(dp, hi, y, c) + piece]
            source = refs_in[array].at[piece]
            peers, ss, rs = hi_peers, send_hi, recv_hi
        else:
            every = slice(None)
            if which == "c":
                target = out.at[(every, every, every, c) + piece]
                peers, ss, rs = c_peers, send_c, recv_c
            elif which == "y":
                there = (dp, every, y, c) if stage == 1 else (every, every, y, c)
                target = out.at[there + piece]
                peers, ss, rs = y_peers, send_y, recv_y
            else:
                there = (dp, every, y, c) if stage == 1 else (dp, every, every, c)
                target = out.at[there + piece]
                peers, ss, rs = dp_peers, send_dp, recv_dp
            source = target
        return [remote(source, target, ss.at[n, k], rs.at[n, k], p) for k, p in enumerate(peers)]

    def own(array):
        return pltpu.make_async_copy(
            refs_in[array], refs_out[array].at[dp, hi, y, c], local_sem.at[array]
        )

    everything = [chunk for group in step_chunks for chunk in group]
    head_copies, head_own = [], None
    if parts:
        head_local, head_send, head_recv, part_send, part_recv = take(5)
        if early:
            blocks = take(1)[0]
        head_copies = [
            remote(blocks.at[:, h], mine.at[head], head_send.at[k], head_recv.at[k], p)
            for k, (h, p) in enumerate(zip(head_of, head_peers, strict=True))
        ]
        head_own = pltpu.make_async_copy(blocks.at[:, head], mine.at[head], head_local.at[0])
        keys = mine.at[:, :, pl.ds(KD, KD + VD)]
        part_copies = [
            remote(keys, other.at[k], part_send.at[k], part_recv.at[k], p)
            for k, p in enumerate(part_peers)
        ]
        if not early:
            head_own.start()
    if early:
        small_v, query_v, key_v, values_v, inputs_v, gain_v, bias_v, load_sem = take(8)
        inputs_load = pltpu.make_async_copy(values, inputs_v, load_sem.at[0])
        inputs_load.start()
        upper = upper_work(
            (dp, seq), lengths, cotangent, skip_input, upper_out, refs_out, take(15), remote, (before, after)
        )

    def make_blocks():
        loads = [
            pltpu.make_async_copy(source, target, load_sem.at[k + 1])
            for k, (source, target) in enumerate(
                zip(refs_out[:4], (small_v, query_v, key_v, values_v), strict=True)
            )
        ]
        for load in loads:
            load.start()
        inputs_load.wait()
        for load in loads:
            load.wait()

        @pl.loop(0, ndp * nhi * 4)
        def _(k):
            rows = small_v[
                lax.div(k, nhi * 4),
                lax.rem(lax.div(k, 4), nhi),
                lax.rem(lax.div(k, 2), 2),
                lax.rem(k, 2),
            ].astype(F32)
            gain_v[pl.ds(k, 1), :] = rows[0:1, :]
            bias_v[pl.ds(k, 1), :] = rows[1:2, :]
            for n in range(4):
                upper["rows"][n, pl.ds(k, 1), :] = rows[7 + n : 8 + n, :]

        def line_up(table, spread, pick):
            return jnp.sum(dot(table[...].astype(BF), spread[...]) * pick[...], axis=0, keepdims=True)

        gain = line_up(gain_v, spread_gain, pick_gain)
        for n in range(4):
            upper["lines"][n : n + 1, :] = line_up(upper["rows"].at[n], spread_gain, pick_gain)
        bias = line_up(bias_v, spread_bias, pick_bias)
        windows, rows = inputs_v.shape[:2]
        for w in range(windows):
            normed[w * rows : (w + 1) * rows, :] = layer_norm(
                inputs_v[w].astype(F32), gain
            ).astype(BF)
        low = normed[...]
        width = low.shape[1]

        def weight(table, first, columns):
            return table[:, :, :, :, :, first : first + columns].reshape(width, columns)

        for pair in range(H // 2):
            spot, wide = pair * 2 * KD, pair * 2 * VD
            content = dot(low, weight(query_v, spot, 2 * KD)) + bias[:, spot : spot + 2 * KD]
            content = (content * (KD**-0.5)).astype(BF).T
            key = dot(low, weight(key_v, spot, 2 * KD)).astype(BF).T
            value = dot(low, weight(values_v, wide, 2 * VD)).astype(BF).T
            for h in range(2):
                for w in range(windows):
                    span = slice(w * rows, (w + 1) * rows)
                    blocks[w, 2 * pair + h, :KD, :] = content[h * KD : (h + 1) * KD, span]
                    blocks[w, 2 * pair + h, KD : 2 * KD, :] = key[h * KD : (h + 1) * KD, span]
                    blocks[w, 2 * pair + h, 2 * KD :, :] = value[h * VD : (h + 1) * VD, span]
        head_own.start()

    ahead, lag = 3, 2

    def launch(step):
        for chunk in step_chunks[step]:
            for copy in copies(chunk, 0):
                copy.start()

    events = {}
    for spot in range(len(pairs)):
        gap = 1 if spot < early else lag
        for stage in (3, 2, 1):
            events.setdefault(spot + gap * (stage - 1), []).append((stage, spot))
    made_at = early + 2 if early else 0
    waited = []
    exchange_at = made_at + len(head_copies) + 1

    def exchange_parts():
        head_own.wait()
        for copy in head_copies:
            copy.wait_recv()
        for copy in part_copies:
            copy.start()

    heads_at = [made_at + k for k in range(len(head_copies))]
    for step in range(min(ahead, len(pairs))):
        launch(step)
    for array in range(n_out):
        own(array).start()
    for array in range(n_out):
        own(array).wait()
    for step in range(max(list(events) + ([exchange_at] if early else heads_at)) + 1):
        for stage, spot in sorted(events.get(step, []), reverse=True):
            for chunk in step_chunks[spot]:
                for copy in copies(chunk, stage - 1):
                    copy.wait_recv()
                for copy in copies(chunk, stage):
                    copy.start()
        if step + ahead < len(pairs):
            launch(step + ahead)
        if early and step == made_at:
            for group in step_chunks[:early]:
                for chunk in group:
                    for copy in copies(chunk, 3):
                        copy.wait_recv()
            make_blocks()
        if step in heads_at:
            head_copies[heads_at.index(step)].start()
        if early and step == exchange_at:
            exchange_parts()
        if early:
            for need, job in upper["jobs"].get(step, []):
                for chunk in everything:
                    if chunk[2] == need:
                        for copy in copies(chunk, 3):
                            copy.wait_recv()
                        waited.append(chunk)
                job()
    if parts and not early:
        exchange_parts()
    for group in step_chunks[early:]:
        for chunk in group:
            if chunk not in waited:
                for copy in copies(chunk, 3):
                    copy.wait_recv()
    if early:
        upper["finish"]()
    if parts:
        for copy in part_copies:
            copy.wait_recv()
        for copy in head_copies + part_copies:
            copy.wait_send()
    for chunk in everything:
        for stage in range(4):
            for copy in copies(chunk, stage):
                copy.wait_send()


def spread_tables(length, share):
    column = jnp.arange(length, dtype=jnp.int32)
    lane = jnp.arange(128, dtype=jnp.int32)
    device = jnp.arange(length // share, dtype=jnp.int32)
    spread = (column[None, :] % share == lane[:, None]).astype(BF)
    pick = (column[None, :] // share == device[:, None]).astype(F32)
    return spread, pick


def use_links(name, collective, shards, pairs, blocks=None, values=None, early=0, upper=()):
    ndp, nseq = lax.axis_size("dp"), lax.axis_size("seq")
    nhi, devices = nseq // 4, ndp * nseq
    parts = nseq // H if blocks is not None or early else 0
    chunks = sum(len(side) for pair in pairs for side in pair)
    arrays = [shard.shape for shard in shards]
    out_shape = [jax.ShapeDtypeStruct((ndp, nhi, 2, 2) + shape, BF) for shape in arrays]
    operands = list(shards)
    in_specs = [pl.BlockSpec(memory_space=pl.ANY)] * len(operands)
    sizes = [(len(arrays),)] + [
        (chunks, size) for size in (nhi - 1, nhi - 1, 1, 1, ndp - 1, ndp - 1, 1, 1)
    ]
    scratch = []
    if early:
        windows, rows, width = values.shape
        operands += [values]
        operands += [
            *spread_tables(width, width // devices),
            *spread_tables(H * KD, H * KD // devices),
        ]
        in_specs += [pl.BlockSpec(memory_space=pl.ANY)] + [
            pl.BlockSpec(memory_space=pltpu.VMEM)
        ] * 4
        operands += list(upper)
        in_specs += [pl.BlockSpec(memory_space=pltpu.SMEM)] + [
            pl.BlockSpec(memory_space=pl.ANY)
        ] * 2
        scratch = [
            pltpu.VMEM((windows, H, 2 * KD + VD, rows), BF),
            pltpu.VMEM(out_shape[0].shape, BF),
            pltpu.VMEM(out_shape[1].shape, BF),
            pltpu.VMEM(out_shape[2].shape, BF),
            pltpu.VMEM(out_shape[3].shape, BF),
            pltpu.VMEM(values.shape, BF),
            pltpu.VMEM((devices, 128), F32),
            pltpu.VMEM((devices, 128), F32),
            pltpu.SemaphoreType.DMA((5,)),
            pltpu.VMEM((4, devices, 128), F32),
            pltpu.VMEM((8, width), F32),
            *[pltpu.VMEM((ndp, nhi, 2, 2, width // devices, width), BF)] * 3,
            *[pltpu.VMEM((windows, 2 * rows, width), BF)] * 4,
            pltpu.VMEM((windows * rows, width), BF),
            pltpu.VMEM((256, width), F32),
            pltpu.VMEM((windows, 16, width), BF),
            pltpu.VMEM((windows, 16, width), BF),
            pltpu.SemaphoreType.DMA((11,)),
            pltpu.SemaphoreType.DMA((4, windows)),
        ]
    elif parts:
        windows, _, _, rows = blocks.shape
        operands.append(blocks)
        in_specs.append(pl.BlockSpec(memory_space=pl.ANY))
    out_specs = [pl.BlockSpec(memory_space=pl.ANY)] * len(out_shape)
    if parts:
        out_shape += [
            jax.ShapeDtypeStruct((H, windows, 2 * KD + VD, rows), BF),
            jax.ShapeDtypeStruct((parts - 1, H, windows, KD + VD, rows), BF),
        ]
        out_specs += [pl.BlockSpec(memory_space=pl.ANY)] * 2
        sizes += [(1,), (H - 1,), (H - 1,), (parts - 1,), (parts - 1,)]
    if early:
        out_shape.append(jax.ShapeDtypeStruct((windows * rows, width), BF))
        out_specs.append(pl.BlockSpec(memory_space=pltpu.VMEM))
        fine, coarse = (windows, 2 * rows, width), (windows * rows, width)
        out_shape += [
            jax.ShapeDtypeStruct(*s)
            for s in (
                (fine, BF),
                (fine, BF),
                (fine, BF),
                (coarse, BF),
                (coarse, F32),
                (fine, BF),
                (fine, F32),
                ((1, width), F32),
            )
        ]
        out_specs += [pl.BlockSpec(memory_space=pl.ANY)] * 7
        out_specs.append(pl.BlockSpec(memory_space=pltpu.VMEM))
    outs = pl.pallas_call(
        functools.partial(links_kernel, pairs, (len(shards), len(arrays)), parts, early),
        out_shape=out_shape,
        in_specs=in_specs,
        out_specs=out_specs,
        scratch_shapes=[pltpu.SemaphoreType.DMA(size) for size in sizes] + scratch,
        compiler_params=pltpu.CompilerParams(
            collective_id=collective, has_side_effects=True, vmem_limit_bytes=60 * 2**20
        ),
        name=name,
    )(*operands)
    flat = [out.reshape(-1, out.shape[-1]) for out in outs[: len(arrays)]]
    return flat + list(outs[len(arrays) :])


def tie(*values):
    return lax.optimization_barrier(values)


def project_kernel(values, gain, content_bias, w_query, w_key, w_value, normed, sent, scratch):
    windows, rows, _ = values.shape

    @pl.when(pl.program_id(0) == 0)
    def _():
        for w in range(windows):
            low = layer_norm(values[w].astype(F32), gain[...]).astype(BF)
            scratch[w * rows : (w + 1) * rows, :] = low
            normed[w * rows : (w + 1) * rows, :] = low

    low = scratch[...]
    content = ((dot(low, w_query[...]) + content_bias[0]) * (KD**-0.5)).astype(BF).T
    keys = dot(low, w_key[...]).astype(BF).T
    mixable = dot(low, w_value[...]).astype(BF).T
    for h in range(2):
        for w in range(windows):
            span = slice(w * rows, (w + 1) * rows)
            sent[w, h, :KD, :] = content[h * KD : (h + 1) * KD, span]
            sent[w, h, KD : 2 * KD, :] = keys[h * KD : (h + 1) * KD, span]
            sent[w, h, 2 * KD :, :] = mixable[h * VD : (h + 1) * VD, span]


def project(values, gain, content_bias, weight_query, weight_key, weight_value):
    windows, rows, width = values.shape
    steps = H // 2
    return pl.pallas_call(
        project_kernel,
        grid=(steps,),
        out_shape=(
            jax.ShapeDtypeStruct((windows * rows, width), BF),
            jax.ShapeDtypeStruct((windows, H, 2 * KD + VD, rows), BF),
        ),
        in_specs=[
            pl.BlockSpec((windows, rows, width), lambda i: (0, 0, 0)),
            pl.BlockSpec((1, width), lambda i: (0, 0)),
            pl.BlockSpec((1, 1, 2 * KD), lambda i: (i, 0, 0)),
            pl.BlockSpec((width, 2 * KD), lambda i: (0, i)),
            pl.BlockSpec((width, 2 * KD), lambda i: (0, i)),
            pl.BlockSpec((width, 2 * VD), lambda i: (0, i)),
        ],
        out_specs=(
            pl.BlockSpec((windows * rows, width), lambda i: (0, 0)),
            pl.BlockSpec((windows, 2, 2 * KD + VD, rows), lambda i: (0, i, 0, 0)),
        ),
        scratch_shapes=[pltpu.VMEM((windows * rows, width), BF)],
        compiler_params=pltpu.CompilerParams(vmem_limit_bytes=48 * 2**20),
        name="project",
    )(
        values,
        gain.reshape(1, width),
        content_bias.reshape(steps, 1, 2 * KD),
        weight_query,
        weight_key,
        weight_value,
    )


def block_work(operands, outs, scratch, arrived, wait_heads):
    values, third_grad, w_mixing, w_inner, w_outer = operands[:5]
    second_gain, third_gain, inner_bias, outer_bias = operands[5:]
    second_sum, third_sum, inner_sum, outer_sum = outs[9:]
    mixing_v, inner_v, outer_v, values_v, third_grad_v, middle_v, block_v, slope_v = scratch[:8]
    mixed_b, second_b, hidden_b, third_b, block_b, before_b, middle_b, back_b, heads_b = scratch[8:17]
    weight_sem, load_sem, store_sem = scratch[17:]
    windows, rows, width = values.shape
    wide = slope_v.shape[1]
    tile, chunk = 512, 32
    weight_loads = [
        pltpu.make_async_copy(source, target, weight_sem.at[k])
        for k, (source, target) in enumerate(
            ((w_mixing, mixing_v), (w_inner, inner_v), (w_outer, outer_v))
        )
    ]

    def load_values(w):
        return pltpu.make_async_copy(values.at[w], values_v, load_sem.at[0])

    def load_third(w):
        return pltpu.make_async_copy(
            third_grad.at[pl.ds(w * rows, rows)], third_grad_v, load_sem.at[1]
        )

    buffers = (mixed_b, second_b, hidden_b, third_b, block_b, before_b, middle_b, back_b, heads_b)

    def store(k, w):
        target = outs[k].at[w] if k == 8 else outs[k].at[pl.ds(w * rows, rows)]
        return pltpu.make_async_copy(buffers[k], target, store_sem.at[k])

    def free(w, *numbers):
        if w:
            for k in numbers:
                store(k, w - 1).wait()

    def begin():
        for load in weight_loads + [load_values(0), load_third(0)]:
            load.start()
        for total in (second_sum, third_sum, inner_sum, outer_sum):
            total[...] = jnp.zeros(total.shape, F32)

    def mix(w):
        wait_heads(w)
        free(w, 0)
        for pair in range(H // 2):
            both = jnp.concatenate([arrived[2 * pair + h, w] for h in range(2)], axis=0)
            mixed_b[:, pair * 2 * VD : (pair + 1) * 2 * VD] = both.T
        store(0, w).start()
        if w == 0:
            weight_loads[0].wait()
        load_values(w).wait()
        for k in range(0, width, tile):
            cols = slice(k, k + tile)
            middle_v[:, cols] = values_v[:, cols].astype(F32) + dot(mixed_b[...], mixing_v[:, cols])

    def inner(w, part):
        if part == 0:
            free(w, 1, 2)

            @pl.loop(0, rows // chunk)
            def _(k):
                at = pl.ds(pl.multiple_of(k * chunk, chunk), chunk)
                unit, _ = norm_parts(middle_v[at, :])
                second_b[at, :] = (unit * second_gain[...]).astype(BF)

            store(1, w).start()
            if w == 0:
                weight_loads[1].wait()
        for k in range(part * wide // 2, (part + 1) * wide // 2, tile):
            cols = slice(k, k + tile)
            before = dot(second_b[...], inner_v[:, cols]) + inner_bias[:, cols]
            hidden, slope = gelu_parts(before)
            hidden_b[:, cols] = hidden.astype(BF)
            slope_v[:, cols] = slope.astype(BF)
        if part == 1:
            store(2, w).start()

    def outer(w):
        if w == 0:
            weight_loads[2].wait()
        for k in range(0, width, tile):
            cols = slice(k, k + tile)
            block_v[:, cols] = (
                middle_v[:, cols] + dot(hidden_b[...], outer_v[:, cols]) + outer_bias[:, cols]
            )

    def turn(w):
        free(w, 3, 4)
        load_third(w).wait()

        @pl.loop(0, rows // chunk)
        def _(k):
            at = pl.ds(pl.multiple_of(k * chunk, chunk), chunk)
            unit, scale = norm_parts(block_v[at, :])
            third, slope = gelu_parts(unit * third_gain[...])
            third_b[at, :] = third.astype(BF)
            grad = third_grad_v[at, :] * slope
            third_sum[...] += jnp.sum(grad * unit, axis=0, keepdims=True)
            back = norm_backward(unit, scale, grad, third_gain[...])
            outer_sum[...] += jnp.sum(back, axis=0, keepdims=True)
            block_v[at, :] = back
            block_b[at, :] = back.astype(BF)

        store(3, w).start()
        store(4, w).start()
        if w + 1 < windows:
            load_values(w + 1).start()
            load_third(w + 1).start()

    def before_grad(w):
        free(w, 5)
        for k in range(0, wide, tile):
            cols = slice(k, k + tile)
            grad = times_rows(block_b[...], outer_v[cols, :]) * slope_v[:, cols].astype(F32)
            low = grad.astype(BF)
            before_b[:, cols] = low
            inner_sum[:, cols] += jnp.sum(low.astype(F32), axis=0, keepdims=True)
        store(5, w).start()

    def second_grad(w):
        free(w, 7)
        for k in range(0, width, tile):
            cols = slice(k, k + tile)
            back_b[:, cols] = times_rows(before_b[...], inner_v[cols, :])

    def middle_grad(w):
        free(w, 6, 8)

        @pl.loop(0, rows // chunk)
        def _(k):
            at = pl.ds(pl.multiple_of(k * chunk, chunk), chunk)
            unit, scale = norm_parts(middle_v[at, :])
            grad = back_b[at, :]
            second_sum[...] += jnp.sum(grad * unit, axis=0, keepdims=True)
            back = block_v[at, :] + norm_backward(unit, scale, grad, second_gain[...])
            back_b[at, :] = back
            middle_b[at, :] = back.astype(BF)

        store(6, w).start()
        store(7, w).start()
        for pair in range(H // 2):
            cols = slice(pair * 2 * VD, (pair + 1) * 2 * VD)
            turned = times_rows(middle_b[...], mixing_v[cols, :]).astype(BF).T
            for h in range(2):
                heads_b[2 * pair + h] = turned[h * VD : (h + 1) * VD]
        store(8, w).start()

    def finish():
        for k in range(len(buffers)):
            store(k, windows - 1).wait()

    jobs = []
    for w in range(windows):
        jobs += [
            functools.partial(mix, w),
            functools.partial(inner, w, 0),
            functools.partial(inner, w, 1),
            functools.partial(outer, w),
            functools.partial(turn, w),
            functools.partial(before_grad, w),
            functools.partial(second_grad, w),
            functools.partial(middle_grad, w),
        ]
    return begin, jobs, finish


def sums_kernel(plan, refs_spec, *refs):
    groups, n_terms, mode, parts, n_small, made_here, late, masked = plan
    refs = list(refs)

    def take(count):
        out, refs[:count] = refs[:count], []
        return out

    terms = take(n_terms * (2 if made_here else 1) - (1 if late else 0))
    head_in = take({None: 0, "in": 1, "block": 1, "out": 3}[mode])
    small_in = take(1 if n_small else 0)
    if late:
        w_query, w_key, w_value, values, middle_grad, gain, spread, pick = take(8)
    if masked:
        lengths, w_masked = take(2)
    if mode == "block":
        block_in = take(9)
    outs = take(n_terms)
    head_out = take(0 if late or not mode or mode == "block" else 1)
    small_out = take(1 if n_small else 0)
    if late:
        (input_grad,) = take(1)
    if masked:
        (masked_o,) = take(1)
    if mode == "block":
        block_out = take(13)
    own, arrived, result, back, hop1, hop2, line = [], [], [], [], [], [], []
    flat = [(side, unit) for group in groups for side in (0, 1) for unit in group[side]]
    count = len(flat)
    own = take(count)
    arrived = take(count)
    hop1 = take(count)
    hop2 = take(count)
    line = take(count)
    result = take(count)
    back = take(count)
    if made_here:
        slots = min(2, n_terms)
        lefts, rights, turned = take(1), take(slots), take(slots)
        going, left_sem, right_sem = take(3)
    load_sem, c_send, c_recv, s1, r1, s2, r2, s3, r3, s4, r4 = take(11)
    dp, seq = lax.axis_index("dp"), lax.axis_index("seq")
    ndp, nhi = own[0].shape[:2]
    nseq = nhi * 4
    hi, low = lax.div(seq, 4), lax.rem(seq, 4)
    y, c = lax.div(low, 2), lax.rem(low, 2)

    def place(dp_to, hi_to, y_to, c_to):
        return (dp_to, hi_to * 4 + y_to * 2 + c_to)

    hi_index = [lax.rem(hi + k, nhi) for k in range(1, nhi)]
    dp_index = [lax.rem(dp + k, ndp) for k in range(1, ndp)]
    hi_peers = [place(dp, h, y, c) for h in hi_index]
    dp_peers = [place(d, hi, y, c) for d in dp_index]
    y_peer, c_peer = place(dp, hi, 1 - y, c), place(dp, hi, y, 1 - c)
    everyone = hi_peers + dp_peers + [y_peer, c_peer]
    if mode:
        head, part = lax.div(seq, parts), lax.rem(seq, parts)
        head_of = [lax.rem(head + k, H) for k in range(1, H)]
        head_peers = [(dp, h * parts + part) for h in head_of]
        part_peers = [(dp, head * parts + slot_part(part, k, parts)) for k in range(1, parts)]
        everyone = everyone + head_peers + part_peers

    barrier = pltpu.get_barrier_semaphore()
    for peer in everyone:
        pl.semaphore_signal(barrier, inc=1, device_id=peer, device_id_type=MESH)
    expected = len(everyone)
    me = dp * nseq + seq
    if n_small:

        def other_device(k):
            there = lax.rem(me + k, n_small)
            return (lax.div(there, nseq), lax.rem(there, nseq))

        @pl.loop(1, n_small)
        def _(k):
            pl.semaphore_signal(barrier, inc=1, device_id=other_device(k), device_id_type=MESH)

        expected += n_small - 1
    pl.semaphore_wait(barrier, expected)

    def remote(source, target, ss, rs, peer):
        return pltpu.make_async_remote_copy(
            src_ref=source,
            dst_ref=target,
            send_sem=ss,
            recv_sem=rs,
            device_id=peer,
            device_id_type=MESH,
        )

    def half_of(array):
        return outs[array].shape[1] // 2

    def columns_of(unit, core):
        array, row, rows, column, columns = unit
        half = half_of(array)
        spot = pl.multiple_of(core * half + column, 128)
        return terms[array].at[:, :, :, :, pl.ds(row, rows), pl.ds(spot, columns)]

    def load(n):
        return pltpu.make_async_copy(columns_of(flat[n][1], c), own[n], load_sem.at[n])

    def over_core(n):
        source = going_of(n) if made_here else columns_of(flat[n][1], 1 - c)
        return [remote(source, arrived[n], c_send.at[n], c_recv.at[n], c_peer)]

    def first_hop(n):
        if flat[n][0] == 0:
            return [
                remote(own[n].at[d], hop1[n].at[k], s1.at[n, k], r1.at[n, k], p)
                for k, (d, p) in enumerate(zip(dp_index, dp_peers, strict=True))
            ]
        return [remote(own[n].at[:, :, 1 - y], hop1[n], s1.at[n, 0], r1.at[n, 0], y_peer)]

    def second_hop(n):
        if flat[n][0] == 0:
            return [remote(own[n].at[dp, :, 1 - y], hop2[n], s2.at[n, 0], r2.at[n, 0], y_peer)]
        return [
            remote(own[n].at[d, :, y], hop2[n].at[k], s2.at[n, k], r2.at[n, k], p)
            for k, (d, p) in enumerate(zip(dp_index, dp_peers, strict=True))
        ]

    def along_line(n):
        return [
            remote(own[n].at[dp, h, y], line[n].at[k], s3.at[n, k], r3.at[n, k], p)
            for k, (h, p) in enumerate(zip(hi_index, hi_peers, strict=True))
        ]

    def back_home(n):
        return [remote(result[n].at[1 - c], back[n], s4.at[n], r4.at[n], c_peer)]

    hops = (over_core, first_hop, second_hop, along_line, back_home)

    def add(a, b):
        return (a.astype(F32) + b.astype(F32)).astype(BF)

    def absorb(n, stage):
        mine = own[n]
        if stage == 1:

            @pl.loop(0, ndp * nhi)
            def _(k):
                d, h = lax.div(k, nhi), lax.rem(k, nhi)
                mine[d, h] = add(mine[d, h], arrived[n][d, h])

        elif stage == 2 and flat[n][0] == 0:

            @pl.loop(0, nhi)
            def _(h):
                total = mine[dp, h].astype(F32)
                for k in range(ndp - 1):
                    total = total + hop1[n][k, h].astype(F32)
                mine[dp, h] = total.astype(BF)

        elif stage == 2:

            @pl.loop(0, ndp * nhi)
            def _(k):
                d, h = lax.div(k, nhi), lax.rem(k, nhi)
                mine[d, h, y] = add(mine[d, h, y], hop1[n][d, h])

        elif stage == 3 and flat[n][0] == 0:

            @pl.loop(0, nhi)
            def _(h):
                mine[dp, h, y] = add(mine[dp, h, y], hop2[n][h])

        elif stage == 3:

            @pl.loop(0, nhi)
            def _(h):
                total = mine[dp, h, y].astype(F32)
                for k in range(ndp - 1):
                    total = total + hop2[n][k, h].astype(F32)
                mine[dp, h, y] = total.astype(BF)

        elif stage == 4:
            total = mine[dp, hi, y].astype(F32)
            for k in range(nhi - 1):
                total = total + line[n][k].astype(F32)
            result[n][...] = total
        else:
            array, row, rows, column, columns = flat[n][1]
            half = half_of(array)
            here, there = result[n][c], back[n][...]
            outs[array][row : row + rows, column : column + columns] = jnp.where(
                c == 0, here, there
            )
            outs[array][row : row + rows, half + column : half + column + columns] = jnp.where(
                c == 0, there, here
            )

    numbers, serial = [], 0
    for group in groups:
        size = len(group[0]) + len(group[1])
        numbers.append(range(serial, serial + size))
        serial += size

    def going_of(n):
        step = next(k for k, some in enumerate(numbers) if n in some)
        unit = flat[n][1]
        side = numbers[step].index(n)
        return going.at[step % 2, side, :, :, :, :, pl.ds(0, unit[2]), pl.ds(0, unit[4])]

    def fetch_left(array):
        left = terms[2 * array]
        return pltpu.make_async_copy(
            left,
            lefts[0].at[pl.ds(0, left.shape[0]), pl.ds(0, left.shape[1])],
            left_sem.at[array],
        )

    def fetch_right(array):
        right = terms[2 * array + 1]
        return pltpu.make_async_copy(
            right,
            rights[array % 2].at[pl.ds(0, right.shape[0]), pl.ds(0, right.shape[1])],
            right_sem.at[array],
        )

    def arrive():
        for copy in head_own:
            copy.wait()
        for copy in head_copies:
            copy.wait_recv()
        packed = rights[(n_terms - 1) % 2]
        windows, rows = gathered.shape[1], gathered.shape[3]
        for w in range(windows):
            for pair in range(H // 2):
                for first, size, start in ((0, KD, 0), (KD, KD, H * KD), (2 * KD, VD, 2 * H * KD)):
                    both = jnp.concatenate(
                        [gathered[2 * pair + h, w, first : first + size, :] for h in range(2)], axis=0
                    )
                    at = start + pair * 2 * size
                    packed[w * rows : (w + 1) * rows, at : at + 2 * size] = both.T

    def make(step):
        if not numbers[step]:
            return
        units = [flat[n][1] for n in numbers[step]]
        array, rows = units[0][0], units[0][2]
        first, size = units[0][3], sum(u[4] for u in units)
        left = terms[2 * array]
        tokens, slot = left.shape[0], array % 2
        if array not in begun:
            begun.append(array)
            fetch_left(array).wait()

            @pl.loop(0, left.shape[1] // 256)
            def _(k):
                spot = pl.multiple_of(k * 256, 256)
                turned[slot][pl.ds(spot, 256), pl.ds(0, tokens)] = lefts[0][
                    pl.ds(0, tokens), pl.ds(spot, 256)
                ].T

            if array + 1 < n_terms:
                fetch_left(array + 1).start()
                if array >= 1 and not (late and array + 1 == n_terms - 1):
                    fetch_right(array + 1).start()
            if late and array == n_terms - 1:
                arrive()
            else:
                fetch_right(array).wait()

        for n in unsent[step % 2]:
            for copy in over_core(n):
                copy.wait_send()
        unsent[step % 2] = list(numbers[step])
        span = nhi * 4 * rows
        for whose in (1 - c, c):
            spot = pl.multiple_of(whose * half_of(array) + first, 128)
            part_right = rights[slot][pl.ds(0, tokens), pl.ds(spot, size)]
            for d in range(ndp):
                made = dot(turned[slot][pl.ds(d * span, span), pl.ds(0, tokens)], part_right)
                made = made.astype(BF).reshape(nhi, 2, 2, rows, size)
                at = 0
                for k, n in enumerate(numbers[step]):
                    piece = made[..., at : at + units[k][4]]
                    if whose is c:
                        own[n][d] = piece
                    else:
                        going[step % 2, k, d, :, :, :, pl.ds(0, rows), pl.ds(0, units[k][4])] = piece
                    at += units[k][4]
            if whose is not c:
                for n in numbers[step]:
                    for copy in over_core(n):
                        copy.start()

    begun, unsent = [], [[], []]

    def launch(step):
        if made_here:
            make(step)
        else:
            for n in numbers[step]:
                load(n).start()
                for copy in over_core(n):
                    copy.start()

    if made_here:
        fetch_left(0).start()
        for array in range(min(2, n_terms)):
            if not (late and array == n_terms - 1):
                fetch_right(array).start()

    if mode == "in":
        head_send, head_recv, head_local = take(3)
        blocks, gathered = head_in[0], head_out[0]
        head_copies = [
            remote(blocks.at[:, h], gathered.at[head], head_send.at[k], head_recv.at[k], p)
            for k, (h, p) in enumerate(zip(head_of, head_peers, strict=True))
        ]
        head_own = [
            pltpu.make_async_copy(blocks.at[:, head], gathered.at[head], head_local.at[0])
        ]
        for copy in head_copies + head_own:
            copy.start()
    if mode == "block":
        head_send, head_recv, head_local, gathered = take(4)
        blocks = head_in[0]
        windows = blocks.shape[1]
        by_window = [
            [
                remote(
                    blocks.at[h, w],
                    gathered.at[head, w],
                    head_send.at[w, k],
                    head_recv.at[w, k],
                    p,
                )
                for k, (h, p) in enumerate(zip(head_of, head_peers, strict=True))
            ]
            for w in range(windows)
        ]
        head_copies = [copy for some in by_window for copy in some]
        head_own = [
            pltpu.make_async_copy(blocks.at[head, w], gathered.at[head, w], head_local.at[w])
            for w in range(windows)
        ]
        for copy in by_window[0] + head_own:
            copy.start()

        def wait_heads(w):
            head_own[w].wait()
            for copy in by_window[w]:
                copy.wait_recv()

        begin_block, block_jobs, finish_block = block_work(
            block_in, block_out, take(20), gathered, wait_heads
        )
        begin_block()
    if mode == "out":
        head_send, head_recv, head_local, part_send, part_recv, mine_kv, arrived_kv = take(7)
        query, pair_mine, pair_other = head_in
        gathered = take(1)[0] if late else head_out[0]
        part_copies = [
            remote(pair_other.at[k], arrived_kv.at[k], part_send.at[k], part_recv.at[k], p)
            for k, p in enumerate(part_peers)
        ]
        kv_load = pltpu.make_async_copy(pair_mine, mine_kv, head_local.at[0])
        for copy in part_copies + [kv_load]:
            copy.start()
    if n_small:
        small_send, small_recv, small_sc = take(3)
        small = small_in[0]
    if masked:
        w_v, x_v, y_v, masked_sem = take(4)
        w_masked_load = pltpu.make_async_copy(w_masked, w_v, masked_sem.at[0])
        w_masked_load.start()
        windows, fine = masked_o.shape[:2]
        tile = x_v.shape[0]

        def masked_product(k):
            w, at = divmod(k * tile, fine)
            load = pltpu.make_async_copy(terms[0].at[pl.ds(k * tile, tile)], x_v, masked_sem.at[1])
            load.start()
            load.wait()
            if k == 0:
                w_masked_load.wait()
            made = dot(x_v[...], w_v[...])
            bin_ = seq * (fine // 2) + lax.div(
                at + lax.broadcasted_iota(jnp.int32, made.shape, 0), 2
            )
            y_v[...] = jnp.where(bin_ < lengths[w], made, 0.0).astype(BF)
            store = pltpu.make_async_copy(
                y_v, masked_o.at[w, pl.ds(at, tile)], masked_sem.at[2]
            )
            store.start()
            store.wait()

    if late:
        small, w_buffer, acc, flat_v, middle_v, out_v, gain_sum, late_sem = take(8)
        w_loads = [
            pltpu.make_async_copy(w_query, w_buffer.at[:, pl.ds(0, H * KD)], late_sem.at[0]),
            pltpu.make_async_copy(w_key, w_buffer.at[:, pl.ds(H * KD, H * KD)], late_sem.at[1]),
        ]
        for copy in w_loads:
            copy.start()

        def window_loads(w):
            span = pl.ds(w * flat_v.shape[0], flat_v.shape[0])
            return [
                pltpu.make_async_copy(values.at[w], flat_v, late_sem.at[2]),
                pltpu.make_async_copy(middle_grad.at[span], middle_v, late_sem.at[3]),
            ]

        def store_window(w):
            span = pl.ds(w * flat_v.shape[0], flat_v.shape[0])
            return pltpu.make_async_copy(out_v, input_grad.at[span], late_sem.at[4])

        for copy in window_loads(0):
            copy.start()

        def back_through(w_ref, first, columns, into_first):
            packed = rights[(n_terms - 1) % 2]

            @pl.loop(0, acc.shape[0] // 128)
            def _(k):
                rows = pl.ds(pl.multiple_of(k * 128, 128), 128)
                made = lax.dot_general(
                    packed[rows, first : first + columns],
                    w_ref[:, 0:columns],
                    (((1,), (1,)), ((), ())),
                    preferred_element_type=F32,
                )
                acc[rows, :] = made if into_first else acc[rows, :] + made

        def value_load(k):
            half = H * VD // 2
            return pltpu.make_async_copy(
                w_value.at[:, pl.ds(k * half, half)],
                w_buffer.at[:, pl.ds(0, half)],
                late_sem.at[5 + k],
            )

        def products(stage):
            half = H * VD // 2
            if stage == 0:
                for copy in w_loads:
                    copy.wait()
                back_through(w_buffer, 0, 2 * H * KD, True)
                value_load(0).start()
            else:
                value_load(0).wait()
                back_through(w_buffer, 2 * H * KD, half, False)
                value_load(1).start()
                value_load(1).wait()
                back_through(w_buffer, 2 * H * KD + half, half, False)

        def norm_back(w):
            for copy in window_loads(w):
                copy.wait()
            if w:
                store_window(w - 1).wait()
            else:
                gain_sum[...] = jnp.zeros(gain_sum.shape, F32)
            size = flat_v.shape[0]

            @pl.loop(0, size // 32)
            def _(k):
                rows = pl.ds(pl.multiple_of(k * 32, 32), 32)
                value = flat_v[rows, :].astype(F32)
                centered = value - jnp.mean(value, axis=-1, keepdims=True)
                scale = lax.rsqrt(jnp.mean(centered * centered, axis=-1, keepdims=True) + epsilon)
                unit = centered * scale
                grad = acc[pl.ds(pl.multiple_of(w * size + k * 32, 32), 32), :]
                gain_sum[...] += jnp.sum(grad * unit, axis=0, keepdims=True)
                grad = grad * gain[...]
                along = jnp.mean(grad * unit, axis=-1, keepdims=True)
                back = scale * (grad - jnp.mean(grad, axis=-1, keepdims=True) - unit * along)
                out_v[rows, :] = (middle_v[rows, :] + back).astype(BF)

            store_window(w).start()
            if w + 1 < values.shape[0]:
                for copy in window_loads(w + 1):
                    copy.start()
            else:
                rows = dot32(pick[...] * gain_sum[...], spread[...].astype(F32), ((1,), (1,)))
                wide = small_in[0].shape[1]
                small[:, :wide, :] = small_in[0][...]
                small[:, wide:, :] = jnp.broadcast_to(
                    rows[:, None, :], (rows.shape[0], 8, rows.shape[1])
                )

    if n_small:

        def small_copy(k):
            there = lax.rem(me + k, n_small)
            return remote(
                small.at[there],
                small_sc.at[k - 1],
                small_send.at[k - 1],
                small_recv.at[k - 1],
                other_device(k),
            )

        def start_small():
            @pl.loop(1, n_small)
            def _(k):
                small_copy(k).start()

        if not late:
            start_small()

    if mode == "out":
        for copy in part_copies:
            copy.wait_recv()
        kv_load.wait()

        @pl.loop(0, H)
        def _(g):
            total = mine_kv[g].astype(F32)
            for k in range(parts - 1):
                total = total + arrived_kv[k, g].astype(F32)
            mine_kv[g] = total.astype(BF)

        q_target = gathered.at[head, :, pl.ds(0, KD)]
        kv_target = gathered.at[head, :, pl.ds(KD, KD + VD)]
        head_copies = [
            remote(source.at[h], target, head_send.at[i, k], head_recv.at[i, k], p)
            for k, (h, p) in enumerate(zip(head_of, head_peers, strict=True))
            for i, (source, target) in enumerate(((query, q_target), (mine_kv, kv_target)))
        ]
        head_own = [
            pltpu.make_async_copy(query.at[head], q_target, head_local.at[1]),
            pltpu.make_async_copy(mine_kv.at[head], kv_target, head_local.at[2]),
        ]
        for copy in head_copies + head_own:
            copy.start()
    ahead = 3
    for step in range(min(ahead, len(groups))):
        launch(step)
    if mode == "block":
        for some in by_window[1:]:
            for copy in some:
                copy.start()
    lag = 2
    for step in range(len(groups) + 4 * lag):
        for stage in (5, 4, 3, 2, 1):
            spot = step - lag * (stage - 1)
            if 0 <= spot < len(groups):
                for n in numbers[spot]:
                    if stage == 1 and not made_here:
                        load(n).wait()
                    for copy in hops[stage - 1](n):
                        copy.wait_recv()
                    absorb(n, stage)
                    if stage < 5:
                        for copy in hops[stage](n):
                            copy.start()
        if step + ahead < len(groups):
            launch(step + ahead)
        if mode == "block":
            steps = len(groups) + 4 * lag
            for job in block_jobs[
                step * len(block_jobs) // steps : (step + 1) * len(block_jobs) // steps
            ]:
                job()
        if masked and 0 <= step - (len(groups) - ahead) < terms[0].shape[0] // tile:
            masked_product(step - (len(groups) - ahead))
        if late and step >= len(groups) - ahead:
            turn = step - (len(groups) - ahead)
            if turn < 2:
                products(turn)
            elif turn < 2 + values.shape[0]:
                norm_back(turn - 2)
                if turn == 1 + values.shape[0]:
                    start_small()
    if n_small:

        @pl.loop(1, n_small)
        def _(k):
            small_copy(k).wait_recv()

        small_out[0][...] = small[me] + jnp.sum(small_sc[...], axis=0)

        @pl.loop(1, n_small)
        def _(k):
            small_copy(k).wait_send()

    if late:
        store_window(values.shape[0] - 1).wait()
    if mode == "block":
        finish_block()
    if mode:
        if not late and mode != "block":
            for copy in head_own:
                copy.wait()
            for copy in head_copies:
                copy.wait_recv()
        for copy in head_copies:
            copy.wait_send()
    if mode == "out":
        for copy in part_copies:
            copy.wait_send()
    for n in range(count):
        for hop in hops:
            if hop is not over_core or not made_here or n in unsent[0] + unsent[1]:
                for copy in hop(n):
                    copy.wait_send()


def sum_terms(name, collective, pairs, groups, mode=None, heads=(), small=None, late=None, masked=None, block=None):
    ndp, nseq = lax.axis_size("dp"), lax.axis_size("seq")
    nhi, parts, devices = nseq // 4, nseq // H, ndp * nseq
    shares = [(left.shape[1] // devices, right.shape[1]) for left, right in pairs]
    made_here = all(rows % 16 == 0 for rows, _ in shares)
    if made_here:
        operands = [x for pair in pairs for x in pair][: -1 if late else None]
    else:
        operands = [
            transposed_times(left, right).astype(BF).reshape((ndp, nhi, 2, 2) + share)
            for (left, right), share in zip(pairs, shares, strict=True)
        ]
    in_specs = [pl.BlockSpec(memory_space=pl.ANY)] * len(operands)
    out_shape = [jax.ShapeDtypeStruct(share, F32) for share in shares]
    out_specs = [pl.BlockSpec(memory_space=pltpu.VMEM)] * len(out_shape)
    flat = [(side, unit) for group in groups for side in (0, 1) for unit in group[side]]
    count = len(flat)
    shapes = [(unit[2], unit[4]) for _, unit in flat]
    sides = [side for side, _ in flat]
    scratch = [pltpu.VMEM((ndp, nhi, 2, 2) + s, BF) for s in shapes] * 2
    scratch += [
        pltpu.VMEM(((ndp, nhi, 2) if side else (ndp - 1, nhi, 2, 2)) + s, BF)
        if not side
        else pltpu.VMEM((ndp, nhi, 2) + s, BF)
        for side, s in zip(sides, shapes, strict=True)
    ]
    scratch += [
        pltpu.VMEM((ndp - 1, nhi, 2) + s if side else (nhi, 2) + s, BF)
        for side, s in zip(sides, shapes, strict=True)
    ]
    scratch += [pltpu.VMEM((nhi - 1, 2) + s, BF) for s in shapes]
    scratch += [pltpu.VMEM((2,) + s, F32) for s in shapes]
    scratch += [pltpu.VMEM(s, F32) for s in shapes]
    if made_here:
        slots = [pairs[k::2] for k in range(min(2, len(pairs)))]
        tokens = [max(left.shape[0] for left, _ in slot) for slot in slots]
        tall = [max(left.shape[1] for left, _ in slot) for slot in slots]
        wide = [max(right.shape[1] for _, right in slot) for slot in slots]
        unit_rows = max(rows for rows, _ in shapes)
        unit_columns = max(columns for _, columns in shapes)
        scratch += [
            pltpu.VMEM((max(tokens), max(tall)), BF),
            *[pltpu.VMEM(s, BF) for s in zip(tokens, wide, strict=True)],
            *[pltpu.VMEM(s, BF) for s in zip(tall, tokens, strict=True)],
            pltpu.VMEM((2, 2, ndp, nhi, 2, 2, unit_rows, unit_columns), BF),
            pltpu.SemaphoreType.DMA((len(pairs),)),
            pltpu.SemaphoreType.DMA((len(pairs),)),
        ]
    hop = max(ndp - 1, 1)
    sizes = [(count,)] * 3 + [(count, hop)] * 4 + [(count, nhi - 1)] * 2 + [(count,)] * 2
    scratch += [pltpu.SemaphoreType.DMA(size) for size in sizes]
    if mode == "in":
        windows, _, size, rows = heads[0].shape
        operands.append(heads[0])
        in_specs.append(pl.BlockSpec(memory_space=pl.ANY))
        out_shape.append(jax.ShapeDtypeStruct((H, windows, size, rows), BF))
        out_specs.append(pl.BlockSpec(memory_space=pl.ANY))
        scratch += [pltpu.SemaphoreType.DMA((n,)) for n in (H - 1, H - 1, 1)]
    if mode == "block":
        operands += [heads[0], *block]
        in_specs += [pl.BlockSpec(memory_space=pl.ANY)] * 6
        in_specs += [pl.BlockSpec(memory_space=pltpu.VMEM)] * 4
        windows, rows, width = block[0].shape
        wide = block[3].shape[1]
        coarse, broad = (windows * rows, width), (windows * rows, wide)
        out_shape += [
            jax.ShapeDtypeStruct(s, BF)
            for s in (coarse, coarse, broad, coarse, coarse, broad, coarse)
        ]
        out_shape.append(jax.ShapeDtypeStruct(coarse, F32))
        out_shape.append(jax.ShapeDtypeStruct((windows, H, VD, rows), BF))
        out_shape += [jax.ShapeDtypeStruct((1, n), F32) for n in (width, width, wide, width)]
        out_specs += [pl.BlockSpec(memory_space=pl.ANY)] * 9
        out_specs += [pl.BlockSpec(memory_space=pltpu.VMEM)] * 4
        narrow, long = pltpu.VMEM((rows, width), BF), pltpu.VMEM((rows, wide), BF)
        full_rows = pltpu.VMEM((rows, width), F32)
        scratch += [
            pltpu.SemaphoreType.DMA((windows, H - 1)),
            pltpu.SemaphoreType.DMA((windows, H - 1)),
            pltpu.SemaphoreType.DMA((windows,)),
            pltpu.VMEM(heads[0].shape, BF),
            *[pltpu.VMEM(w.shape, BF) for w in block[2:5]],
            narrow,
            full_rows,
            full_rows,
            full_rows,
            long,
            narrow,
            narrow,
            long,
            narrow,
            narrow,
            long,
            narrow,
            full_rows,
            pltpu.VMEM((H, VD, rows), BF),
            pltpu.SemaphoreType.DMA((3,)),
            pltpu.SemaphoreType.DMA((2,)),
            pltpu.SemaphoreType.DMA((9,)),
        ]
    if mode == "out":
        _, windows, _, rows = heads[0].shape
        operands += list(heads)
        in_specs += [pl.BlockSpec(memory_space=pl.ANY)] * 3
        if not late:
            out_shape.append(jax.ShapeDtypeStruct((H, windows, 2 * KD + VD, rows), BF))
            out_specs.append(pl.BlockSpec(memory_space=pl.ANY))
        scratch += [
            pltpu.SemaphoreType.DMA(size)
            for size in ((2, H - 1), (2, H - 1), (3,), (parts - 1,), (parts - 1,))
        ]
        scratch += [pltpu.VMEM(heads[1].shape, BF), pltpu.VMEM(heads[2].shape, BF)]
        if late:
            scratch.append(pltpu.VMEM((H, windows, 2 * KD + VD, rows), BF))
    n_small = 0
    if small is not None:
        n_small = devices
        operands.append(small)
        in_specs.append(pl.BlockSpec(memory_space=pltpu.VMEM))
        message = (small.shape[1] + (8 if late else 0), small.shape[2])
        out_shape.append(jax.ShapeDtypeStruct(message, F32))
        out_specs.append(pl.BlockSpec(memory_space=pltpu.VMEM))
        scratch += [
            pltpu.SemaphoreType.DMA((devices - 1,)),
            pltpu.SemaphoreType.DMA((devices - 1,)),
            pltpu.VMEM((devices - 1,) + message, F32),
        ]
    if late:
        windows, rows, width = late[3].shape
        operands += list(late) + list(spread_tables(width, width // devices))
        in_specs += [pl.BlockSpec(memory_space=pl.ANY)] * 5
        in_specs += [pl.BlockSpec(memory_space=pltpu.VMEM)] * 3
        out_shape.append(jax.ShapeDtypeStruct((windows * rows, width), BF))
        out_specs.append(pl.BlockSpec(memory_space=pl.ANY))
        scratch += [
            pltpu.VMEM((devices,) + message, F32),
            pltpu.VMEM((width, 2 * H * KD), BF),
            pltpu.VMEM((windows * rows, width), F32),
            pltpu.VMEM((rows, width), BF),
            pltpu.VMEM((rows, width), F32),
            pltpu.VMEM((rows, width), BF),
            pltpu.VMEM((1, width), F32),
            pltpu.SemaphoreType.DMA((7,)),
        ]
    if masked:
        lengths, weight, shape = masked
        operands += [lengths, weight]
        in_specs += [pl.BlockSpec(memory_space=pltpu.SMEM), pl.BlockSpec(memory_space=pl.ANY)]
        out_shape.append(jax.ShapeDtypeStruct(shape, BF))
        out_specs.append(pl.BlockSpec(memory_space=pl.ANY))
        scratch += [
            pltpu.VMEM(weight.shape, BF),
            pltpu.VMEM((256, shape[2]), BF),
            pltpu.VMEM((256, shape[2]), BF),
            pltpu.SemaphoreType.DMA((3,)),
        ]
    plan = (
        groups, len(pairs), mode, parts, n_small, made_here, late is not None, masked is not None
    )
    return pl.pallas_call(
        functools.partial(sums_kernel, plan, None),
        out_shape=out_shape,
        in_specs=in_specs,
        out_specs=out_specs,
        scratch_shapes=scratch,
        compiler_params=pltpu.CompilerParams(
            collective_id=collective, has_side_effects=True, vmem_limit_bytes=63 * 2**20
        ),
        name=name,
    )(*operands)


HOLD = 0


def halves(array, rows, columns, size=128):
    out, spot = [], 0
    while spot < columns:
        size = min(size, (columns - spot) // 2)
        out.append((((array, 0, rows, spot, size),), ((array, 0, rows, spot + size, size),)))
        spot += 2 * size
    return tuple(out)


def full(array, shards):
    rows, columns = shards[array].shape
    return (array, 0, rows, 0, columns)


def columns_of_rows(array, rows, first, columns):
    return (array, 0, rows, first, columns)


def gelu_parts(x):
    below = 0.5 * (1.0 + lax.erf(x * (0.5**0.5)))
    density = jnp.exp(-0.5 * x * x) * (1.0 / math.sqrt(2.0 * math.pi))
    return x * below, below + x * density


def norm_parts(value):
    centered = value - jnp.mean(value, axis=-1, keepdims=True)
    scale = lax.rsqrt(jnp.mean(centered * centered, axis=-1, keepdims=True) + epsilon)
    return centered * scale, scale


def norm_backward(unit, scale, grad, gain):
    grad = grad * gain
    along = jnp.mean(grad * unit, axis=-1, keepdims=True)
    return scale * (grad - jnp.mean(grad, axis=-1, keepdims=True) - unit * along)


def times_rows(x, table):
    return lax.dot_general(x, table, (((1,), (1,)), ((), ())), preferred_element_type=F32)


def weight_pairs(shapes, offset):
    def pieces(n, parts):
        rows, columns = shapes[n]
        if rows % (16 * parts):
            return [(offset + n, 0, rows, 0, columns)]
        size = rows // parts
        return [(offset + n, k * size, size, 0, columns) for k in range(parts)]

    first = pieces(5, 3) + pieces(0, 3) + pieces(4, 3) + pieces(2, 3)
    second = pieces(1, 3) + pieces(3, 6)
    steps = max(len(second), 1)
    spare = len(first) - steps
    pairs, spot = [], 0
    for k in range(steps):
        take = 2 if 3 <= k < 3 + spare else 1
        pairs.append((tuple(first[spot : spot + take]), (second[k],)))
        spot += take
    if spot < len(first):
        pairs.append((tuple(first[spot:]), ()))
    return tuple(pairs)


def on_device(
    inputs,
    skip_input,
    lengths,
    cotangent,
    first_gain,
    query_weight,
    key_weight,
    value_weight,
    content_bias,
    position_bias,
    relative_weight,
    mixing_weight,
    second_gain,
    inner_weight,
    inner_bias,
    outer_weight,
    outer_bias,
    third_gain,
    upsample_weight,
    skip_weight,
    skip_bias,
    depth_weight,
    point_weight,
):
    windows, rows, width = inputs.shape
    scale = float(KD) ** (-0.5)
    nseq, ndp = lax.axis_size("seq"), lax.axis_size("dp")
    devices = nseq * ndp
    parts = nseq // H
    keys_total = rows * nseq
    seq = lax.axis_index("seq")
    head, part = lax.div(seq, parts), lax.rem(seq, parts)
    first = seq * rows
    hidden_width = inner_weight.shape[1]

    r = shard_rows = query_weight.shape[0]
    vectors = (
        first_gain,
        content_bias,
        position_bias,
        second_gain,
        inner_bias,
        outer_bias,
        third_gain,
        skip_bias,
    )
    small_rows = [v.reshape(1, -1) for v in vectors] + [depth_weight.T]
    small_rows = [jnp.pad(v, ((0, 0), (0, 128 - v.shape[1]))) for v in small_rows]
    small_rows.append(jnp.zeros((16 - len(vectors) - 3, 128), BF))
    relative_rows = relative_weight.shape[0]
    small_rows.append(
        jnp.pad(relative_weight, ((0, -relative_rows % 16), (0, 128 - relative_weight.shape[1])))
    )
    small_shard = jnp.concatenate(small_rows, axis=0)
    keys_width, values_width = 2 * H * KD, H * VD
    half_hidden, half_width = hidden_width // 2, width // 2
    head_shards = [small_shard, query_weight, key_weight, value_weight]
    head_pairs = (
        ((full(0, head_shards), full(1, head_shards)), (full(2, head_shards),)),
        ((columns_of_rows(3, r, 0, values_width // 2),), (columns_of_rows(3, r, values_width // 2, values_width // 2),)),
    )
    shards = [
        skip_weight,
        mixing_weight,
        inner_weight,
        outer_weight,
        upsample_weight,
        point_weight,
    ]
    if r % 16 == 0:
        (
            small_full,
            weight_query,
            weight_key,
            weight_value,
            weight_skip,
            weight_mixing,
            weight_inner,
            weight_outer,
            weight_upsample,
            weight_point,
            mine,
            other,
            normed_low,
            out_grad,
            conv_grad,
            joined_flat,
            lifted_grad,
            third_grad,
            skip_grad,
            skip_part,
            grad_skip_bias,
        ) = use_links(
            "gather_weights",
            1,
            head_shards + shards,
            head_pairs + weight_pairs([w.shape for w in shards], len(head_shards)),
            values=inputs,
            early=len(head_pairs),
            upper=(lengths, cotangent, skip_input),
        )
        out_grad, joined_flat, skip_part = (
            x.reshape(-1, width) for x in (out_grad, joined_flat, skip_part)
        )
        grad_skip_bias = grad_skip_bias[0]
    else:
        small_full, weight_query, weight_key, weight_value = use_links(
            "gather_heads", 1, head_shards, head_pairs
        )
    small_full = small_full.reshape((devices,) + small_shard.shape).astype(jnp.float32)

    def vector(k):
        return small_full[:, k, : vectors[k].shape[0]].reshape(-1)

    (
        gain_first,
        bias_content,
        bias_position,
        gain_second,
        bias_inner,
        bias_outer,
        gain_third,
        bias_skip,
    ) = map(vector, range(len(vectors)))
    taken = len(vectors)
    weight_depth = (
        small_full[:, taken : taken + 3, :r].transpose(0, 2, 1).reshape(width, 3)
    )
    weight_relative = small_full[:, 16 : 16 + relative_rows, :RPF].reshape(H * KD, RPF)

    lives = jnp.exp(
        jnp.linspace(math.log(3.0), math.log(keys_total), RPF // 2, dtype=jnp.float32)
    )
    rates = (math.log(2.0) / lives)[:, None]
    bias_gap = ((bias_position - bias_content) * scale).reshape(H, KD, 1)
    bias_gap = lax.dynamic_index_in_dim(bias_gap, head, 0, keepdims=False)
    relative = lax.dynamic_index_in_dim(
        weight_relative.reshape(H, KD, RPF), head, 0, keepdims=False
    ).T
    info = jnp.concatenate([lengths, part[None].astype(jnp.int32)])
    groups = [[p + parts * g for g in range(H)] for p in range(parts)]

    def exchange(array):
        return lax.all_to_all(array, "seq", 0, 0, axis_index_groups=groups, tiled=True)

    def swap_part(array, slot):
        return lax.ppermute(array, "seq", [(i, i ^ slot) for i in range(nseq)])

    flat = inputs.reshape(windows * rows, width).astype(jnp.float32)
    if r % 16:
        normed_low, sent = project(
            inputs, gain_first, bias_content, weight_query, weight_key, weight_value
        )
        (
            weight_skip,
            weight_mixing,
            weight_inner,
            weight_outer,
            weight_upsample,
            weight_point,
            mine,
            other,
        ) = use_links(
            "gather_weights", 2, shards, weight_pairs([w.shape for w in shards], 0), sent
        )

    def by_row(array):
        (array,) = tie(array.transpose(1, 3, 0, 2).reshape(windows * rows, -1))
        return array

    mixed_own, mixed_wide, log_total = attention_forward(
        info, rates, bias_gap, relative, mine, other, parts
    )
    if r % 16 == 0:
        skip_flat = skip_input.reshape(windows * 2 * rows, width)
        (
            own_skip,
            mixed_low,
            second_low,
            hidden_low,
            third_low,
            block_low,
            before_low,
            middle_low,
            middle_grad,
            mixed_grad,
            *block_sums,
        ) = sum_terms(
            "block_and_skip",
            6,
            [(skip_flat, joined_flat)],
            halves(0, r, half_width),
            "block",
            (mixed_own,),
            block=(
                inputs,
                third_grad,
                weight_mixing,
                weight_inner,
                weight_outer,
                gain_second[None, :],
                gain_third[None, :],
                bias_inner[None, :],
                bias_outer[None, :],
            ),
        )
        grad_second, grad_third, grad_inner_bias, grad_outer_bias = (s[0] for s in block_sums)
    else:
        mixed_low = by_row(exchange(mixed_own))
        middle = flat + matmul(mixed_low, weight_mixing)
        second, second_norm_back = jax.vjp(layer_norm, middle, gain_second)
        second_low = second.astype(jnp.bfloat16)
        before = matmul(second_low, weight_inner) + bias_inner
        hidden, gelu_back = jax.vjp(smooth_gelu, before)
        hidden_low = hidden.astype(jnp.bfloat16)
        block_out = middle + matmul(hidden_low, weight_outer) + bias_outer
        third, third_back = jax.vjp(norm_gelu, block_out, gain_third)
        third_low = third.astype(jnp.bfloat16)
    fine = jnp.arange(2 * rows, dtype=jnp.int32)[:, None] // 2
    twice = (fine == jnp.arange(rows, dtype=jnp.int32)[None, :]).astype(jnp.bfloat16)
    third_twice = (
        jnp.einsum(
            "ts,wsd->wtd",
            twice,
            third_low.reshape(windows, rows, width),
            preferred_element_type=jnp.float32,
        )
        .astype(jnp.bfloat16)
        .reshape(windows * 2 * rows, width)
    )
    skip_flat = skip_input.reshape(windows * 2 * rows, width)
    if r % 16:
        skip_part = matmul(skip_flat, weight_skip) + bias_skip
    joined_low = (
        (matmul(third_twice, weight_upsample) + skip_part)
        .astype(jnp.bfloat16)
        .reshape(windows, 2 * rows, width)
    )
    joined_rim = extended_2(joined_low, (("seq", 1),), 1)
    taps = weight_depth
    joined_wide = joined_rim.astype(jnp.float32)
    conv_low = depth_apply(joined_wide, taps).astype(jnp.bfloat16)
    conv_flat = conv_low.reshape(windows * 2 * rows, width)
    bins = 2 * first + jnp.arange(2 * rows, dtype=jnp.int32)
    keep = (bins // 2)[None, :] < lengths[:, None]
    keep_wide = keep.astype(jnp.float32)[:, :, None]
    if r % 16:
        outputs = (
            matmul(conv_flat, weight_point).reshape(windows, 2 * rows, width) * keep_wide
        ).astype(jnp.bfloat16)
    if r % 16:
        out_grad = (cotangent * keep.astype(jnp.bfloat16)[:, :, None]).reshape(
            windows * 2 * rows, width
        )
        conv_grad = (
            times_transposed(out_grad, weight_point)
            .astype(jnp.bfloat16)
            .reshape(windows, 2 * rows, width)
        )
        grad_rim = extended_2(conv_grad, (("seq", 1),), 1).astype(jnp.float32)
        joined_grad = (
            grad_rim[:, 2:] * taps[:, 0]
            + grad_rim[:, 1:-1] * taps[:, 1]
            + grad_rim[:, :-2] * taps[:, 2]
        )
        grad_skip_bias = jnp.sum(joined_grad, axis=(0, 1))
        joined_back = joined_grad.astype(jnp.bfloat16)
        joined_flat = joined_back.reshape(windows * 2 * rows, width)
        lifted_grad = (
            jnp.einsum("ts,wtd->wsd", twice, joined_back, preferred_element_type=jnp.float32)
            .astype(jnp.bfloat16)
            .reshape(windows * rows, width)
        )
        third_grad = times_transposed(lifted_grad, weight_upsample)
        skip_grad = (
            times_transposed(joined_flat, weight_skip)
            .astype(jnp.bfloat16)
            .reshape(windows, 2 * rows, width)
        )
    conv_wide = conv_grad.astype(jnp.float32)
    grad_depth = jnp.stack(
        [
            jnp.sum(conv_wide * joined_wide[:, :-2], axis=(0, 1)),
            jnp.sum(conv_wide * joined_wide[:, 1:-1], axis=(0, 1)),
            jnp.sum(conv_wide * joined_wide[:, 2:], axis=(0, 1)),
        ],
        axis=1,
    )
    if r % 16:
        block_grad, grad_third = third_back(third_grad)
        block_low = block_grad.astype(jnp.bfloat16)
        grad_outer_bias = jnp.sum(block_grad, axis=0)
        (before_grad,) = gelu_back(times_transposed(block_low, weight_outer))
        before_low = before_grad.astype(jnp.bfloat16)
        grad_inner_bias = jnp.sum(before_low.astype(jnp.float32), axis=0)
        middle_part, grad_second = second_norm_back(times_transposed(before_low, weight_inner))
        middle_grad = block_grad + middle_part
        middle_low = middle_grad.astype(jnp.bfloat16)
        middle_rows = middle_low.reshape(windows, rows, width)
        mixed_grad = (
            jnp.einsum("vd,wrd->wvr", weight_mixing, middle_rows, preferred_element_type=jnp.float32)
            .astype(jnp.bfloat16)
            .reshape(windows, H, VD, rows)
        )
    if r % 16 == 0:
        own_point, own_outer, own_upsample, arrived_grad, outputs = sum_terms(
            "sum_upper",
            3,
            [(conv_flat, out_grad), (hidden_low, block_low), (third_low, lifted_grad)],
            halves(0, r, half_width)
            + halves(1, outer_weight.shape[0], half_width)
            + halves(2, r, half_width),
            "in",
            (mixed_grad,),
            masked=(lengths, weight_point, skip_input.shape),
        )
    else:
        own_point, own_outer, own_skip, own_upsample, arrived_grad = sum_terms(
            "sum_upper",
            3,
            [
                (conv_flat, out_grad),
                (hidden_low, block_low),
                (skip_flat, joined_flat),
                (third_low, lifted_grad),
            ],
            halves(0, r, half_width)
            + halves(1, outer_weight.shape[0], half_width)
            + halves(2, r, half_width)
            + halves(3, r, half_width),
            "in",
            (mixed_grad,),
        )
    query_own, own_side, other_side, bias_sums, relative_sum = attention_backward(
        info, rates, bias_gap, relative, mine, other, arrived_grad, mixed_wide, log_total, parts
    )

    def at_head(value):
        full = jnp.zeros((H,) + value.shape, jnp.float32)
        return lax.dynamic_update_index_in_dim(full, value, head, 0)

    pieces = [
        at_head(bias_sums[0, :, 0]).reshape(-1),
        at_head(bias_sums[1, :, 0]).reshape(-1),
        at_head(relative_sum).reshape(H * KD, RPF),
        grad_second,
        grad_inner_bias,
        grad_outer_bias,
        grad_third,
        grad_skip_bias,
        grad_depth,
    ]

    def pack(pieces):
        packed = jnp.concatenate([p.reshape(devices, -1) for p in pieces], axis=1)
        return jnp.pad(packed, ((0, 0), (0, -packed.shape[1] % 1024))).reshape(devices, -1, 128)

    lower = [(second_low, before_low), (mixed_low, middle_low)]
    lower_groups = halves(0, r, half_hidden) + halves(1, r, half_width)
    lower_heads = (query_own, own_side, other_side)
    packed_width = keys_width + values_width
    if r % 16 == 0:
        right = jax.ShapeDtypeStruct((windows * rows, packed_width), BF)
        own_inner, own_mixing, own_heads, small_total, input_grad = sum_terms(
            "sum_lower",
            4,
            lower + [(normed_low, right)],
            lower_groups + (((), ()),) * HOLD + halves(2, r, packed_width // 2),
            "out",
            lower_heads,
            pack(pieces),
            (weight_query, weight_key, weight_value, inputs, middle_grad, gain_first[None, :]),
        )
        own_first = small_total[-8, : width // devices]
        input_grad = input_grad.reshape(windows, rows, width)
        names = pieces
    else:
        own_inner, own_mixing, heads_grad = sum_terms(
            "sum_lower", 4, lower, lower_groups, "out", lower_heads
        )
        packed_grad = jnp.concatenate(
            [
                by_row(heads_grad[:, :, :KD]),
                by_row(heads_grad[:, :, KD : 2 * KD]),
                by_row(heads_grad[:, :, 2 * KD :]),
            ],
            axis=1,
        )
        (packed_grad,) = tie(packed_grad)
        normed_grad = (
            times_transposed(packed_grad[:, : H * KD], weight_query)
            + times_transposed(packed_grad[:, H * KD : keys_width], weight_key)
            + times_transposed(packed_grad[:, keys_width:], weight_value)
        )
        _, first_norm_back = jax.vjp(layer_norm, flat, gain_first)
        input_part, grad_first = first_norm_back(normed_grad)
        input_grad = (middle_grad + input_part).astype(jnp.bfloat16).reshape(windows, rows, width)
        names = [grad_first] + pieces
        own_heads, small_total = sum_terms(
            "sum_heads",
            5,
            [(normed_low, packed_grad)],
            halves(0, r, packed_width // 2),
            small=pack(names),
        )
    small_total, spot, small_grads = small_total.reshape(-1), 0, []
    for p in names:
        size = p.size // devices
        small_grads.append(
            small_total[spot : spot + size].reshape((p.shape[0] // devices,) + p.shape[1:])
        )
        spot += size
    if len(names) > len(pieces):
        own_first = small_grads.pop(0)
    (
        own_content,
        own_position,
        own_relative,
        own_second,
        own_inner_bias,
        own_outer_bias,
        own_third,
        own_skip_bias,
        own_depth,
    ) = small_grads
    return (
        outputs,
        input_grad,
        skip_grad,
        own_first,
        own_heads[:, : H * KD],
        own_heads[:, H * KD : keys_width],
        own_heads[:, keys_width:],
        own_content,
        own_position,
        own_relative,
        own_mixing,
        own_second,
        own_inner,
        own_inner_bias,
        own_outer,
        own_outer_bias,
        own_third,
        own_upsample,
        own_skip,
        own_skip_bias,
        own_depth,
        own_point,
    )


def solution(mesh):
    in_specs = (
        P("dp", "seq", None),
        P("dp", "seq", None),
        P("dp"),
        P("dp", "seq", None),
        P(("dp", "seq")),
        P(("dp", "seq"), None),
        P(("dp", "seq"), None),
        P(("dp", "seq"), None),
        P(("dp", "seq")),
        P(("dp", "seq")),
        P(("dp", "seq"), None),
        P(("dp", "seq"), None),
        P(("dp", "seq")),
        P(("dp", "seq"), None),
        P(("dp", "seq")),
        P(("dp", "seq"), None),
        P(("dp", "seq")),
        P(("dp", "seq")),
        P(("dp", "seq"), None),
        P(("dp", "seq"), None),
        P(("dp", "seq")),
        P(("dp", "seq"), None),
        P(("dp", "seq"), None),
    )
    out_specs = (
        P("dp", "seq", None),
        P("dp", "seq", None),
        P("dp", "seq", None),
        P(("dp", "seq")),
        P(("dp", "seq"), None),
        P(("dp", "seq"), None),
        P(("dp", "seq"), None),
        P(("dp", "seq")),
        P(("dp", "seq")),
        P(("dp", "seq"), None),
        P(("dp", "seq"), None),
        P(("dp", "seq")),
        P(("dp", "seq"), None),
        P(("dp", "seq")),
        P(("dp", "seq"), None),
        P(("dp", "seq")),
        P(("dp", "seq")),
        P(("dp", "seq"), None),
        P(("dp", "seq"), None),
        P(("dp", "seq")),
        P(("dp", "seq"), None),
        P(("dp", "seq"), None),
    )
    return jax.shard_map(
        on_device, mesh=mesh, in_specs=in_specs, out_specs=out_specs, check_vma=False
    )
```

```python
import functools
import math

import jax
import jax.numpy as jnp
from jax import lax
from jax.experimental import pallas as pl
from jax.experimental.pallas import tpu as pltpu
from jax.sharding import PartitionSpec as P

H = 8
KD = 64
VD = 192
RPF = 32
NEG = -1e30
BF = jnp.bfloat16
F32 = jnp.float32
epsilon = 1e-05


def extended_2(array, sides, width):
    for axis, dim in sides:
        peers, length = (lax.axis_size(axis), array.shape[dim])
        up = [(i, (i + 1) % peers) for i in range(peers - 1)]
        down = [(j, i) for i, j in up]
        last = lax.slice_in_dim(array, length - width, length, axis=dim)
        initial = lax.slice_in_dim(array, 0, width, axis=dim)
        before = lax.ppermute(last, axis, up)
        after = lax.ppermute(initial, axis, down)
        array = jnp.concatenate([before, array, after], axis=dim)
    return array


def layer_norm(values, gain):
    mean = jnp.mean(values, axis=-1, keepdims=True)
    centered = values - mean
    spread = jnp.mean(centered * centered, axis=-1, keepdims=True)
    return centered * lax.rsqrt(spread + epsilon) * gain


def smooth_gelu(values):
    return jax.nn.gelu(values, approximate=False)


def norm_gelu(values, gain):
    return smooth_gelu(layer_norm(values, gain))


def matmul(left, right):
    return jnp.dot(left, right, preferred_element_type=jnp.float32)


def times_transposed(left, right):
    return lax.dot_general(
        left, right, (((1,), (1,)), ((), ())), preferred_element_type=jnp.float32
    )


def transposed_times(left, right):
    return lax.dot_general(
        left, right, (((0,), (0,)), ((), ())), preferred_element_type=jnp.float32
    )


def depth_apply(extended, taps):
    return (
        extended[:, :-2] * taps[:, 0]
        + extended[:, 1:-1] * taps[:, 1]
        + extended[:, 2:] * taps[:, 2]
    )


def dot(a, b):
    return lax.dot_general(a, b, (((1,), (0,)), ((), ())), preferred_element_type=F32)


def dot32(a, b, dims=((1,), (0,))):
    return lax.dot_general(
        a, b, (dims, ((), ())), precision=lax.Precision.HIGHEST, preferred_element_type=F32
    )


def key_side(parts, part, groups, mine, other, store):
    for slot in range(parts):
        theirs = slot_part(part, slot, parts)
        for g in range(groups):
            if slot == 0:
                kt, vt = mine[g, 0, KD : 2 * KD, :], mine[g, 0, 2 * KD :, :]
            else:
                kt, vt = other[slot - 1, g, 0, :KD, :], other[slot - 1, g, 0, KD:, :]
            store(g * parts + theirs, kt, vt)


def slot_part(part, slot, parts):
    out, bit = part, 1
    while bit < parts:
        if slot & bit:
            has = lax.rem(lax.div(part, bit), 2)
            out = out + bit - 2 * bit * has
        bit *= 2
    return out


def query_side(content, bias, relative, half):
    positional = content.astype(F32) + bias
    projected = dot32(relative, positional).astype(BF).astype(F32)
    return positional, projected[:half] + projected[half:], projected[:half] - projected[half:]


def query_block(content, plus, minus, rates):
    spot = lax.broadcasted_iota(jnp.int32, plus.shape, 1).astype(F32)
    last = plus.shape[1] - 1
    from_first, to_last = jnp.exp(-rates * spot), jnp.exp(-rates * (last - spot))
    rest = jnp.zeros((128 - KD - RPF, content.shape[1]), BF)
    block = jnp.concatenate(
        [content, (plus * from_first).astype(BF), (minus * to_last).astype(BF), rest], axis=0
    )
    return block, from_first, to_last


def lane_rates(rates_row):
    lane = lax.broadcasted_iota(jnp.int32, (1, 128), 1)
    half = RPF // 2
    below = (lane >= KD) & (lane < KD + half)
    above = (lane >= KD + half) & (lane < KD + RPF)
    return rates_row, below, above


def decay_table(rates_row, span):
    rates_row, below, above = lane_rates(rates_row)
    spot = lax.broadcasted_iota(jnp.int32, (span, 128), 0).astype(F32)
    table = jnp.where(below, jnp.exp(-rates_row * (span - 1 - spot)), 0.0)
    return jnp.where(above, jnp.exp(-rates_row * spot), table)


def key_decays(table, rates_row, first_query, last_query, first_key, span, kind):
    rates_row, below, above = lane_rates(rates_row)
    if kind == "plain":
        before = first_key < first_query
        gap = jnp.where(before, first_query - (first_key + span - 1), first_key - last_query)
        used = (below & before) | (above & jnp.logical_not(before))
        return (table * jnp.where(used, jnp.exp(-rates_row * gap.astype(F32)), 0.0)).astype(BF)
    key = first_key + lax.broadcasted_iota(jnp.int32, (span, 128), 0)
    down = jnp.exp(jnp.minimum(-rates_row * (first_query - key).astype(F32), 60.0))
    up = jnp.exp(jnp.minimum(-rates_row * (key - last_query).astype(F32), 60.0))
    return jnp.where(below, down, 0.0).astype(BF), jnp.where(above, up, 0.0).astype(BF)


def order_of(first_query, first_key, span, rows):
    i = first_query + lax.broadcasted_iota(jnp.int32, (span, rows), 1)
    j = first_key + lax.broadcasted_iota(jnp.int32, (span, rows), 0)
    return i, j


def tile_scores(keys, decays, query, first_query, first_key, length, kind):
    if kind != "both":
        return dot(keys + decays, query)
    s_below, s_above = dot(keys + decays[0], query), dot(keys + decays[1], query)
    i, j = order_of(first_query, first_key, *s_below.shape)
    scores = jnp.where(i > j, s_below, jnp.where(i < j, s_above, 0.5 * (s_below + s_above)))
    return jnp.where(j < length, scores, NEG)


def visit_tiles(scores_into, use, slots, whole_tile, q_block, length, rows, per):
    span = rows * per
    count = lax.div(length + span - 1, span)
    full = lax.div(length, span)
    own = lax.div(q_block, per)
    plain = full - jnp.where(own < full, 1, 0)

    def tile_of(k):
        return k + jnp.where(k >= own, 1, 0)

    @pl.when(plain > 0)
    def _():
        scores_into(slots[0], tile_of(0), own)

    @pl.loop(0, lax.div(plain, 2))
    def _(k):
        first = 2 * k
        scores_into(slots[1], tile_of(first + 1), own)
        use(slots[0], tile_of(first), own)
        scores_into(slots[0], tile_of(jnp.minimum(first + 2, plain - 1)), own)
        use(slots[1], tile_of(first + 1), own)

    @pl.when(lax.rem(plain, 2) == 1)
    def _():
        use(slots[0], tile_of(plain - 1), own)

    @pl.loop(0, 2)
    def _(k):
        t = jnp.where(k == 0, own, full)
        go = (t < count) & ((k == 0) | (full != own))

        @pl.when(go)
        def _():
            whole_tile(t)


def forward_kernel(
    parts, per, info, rates_ref, lanes_ref, bias_ref, rel_ref, mine, other, mixed, wide, lse, k_sc, v_sc, table_sc, s0_sc, s1_sc, m_sc, l_sc, acc
):
    groups, rows = mine.shape[0], mine.shape[3]
    half = RPF // 2
    length = info[pl.program_id(0)]
    part = info[pl.num_programs(0)]
    rates = rates_ref[...]

    def store(block, kt, vt):
        spot = pl.multiple_of(block * rows, rows)
        k_sc[pl.ds(spot, rows), :] = jnp.concatenate([kt, jnp.zeros_like(kt)], axis=0).T
        v_sc[:, pl.ds(spot, rows)] = vt

    key_side(parts, part, groups, mine, other, store)
    span = rows * per
    table_sc[...] = decay_table(lanes_ref[...], span)

    @pl.loop(0, groups)
    def _(g):
        q_block = g * parts + part

        @pl.when(q_block * rows > length)
        def _():
            mixed[g, 0] = jnp.zeros(mixed.shape[2:], mixed.dtype)
            wide[g, 0] = jnp.zeros(wide.shape[2:], wide.dtype)
            lse[g, 0] = jnp.zeros(lse.shape[2:], lse.dtype)

        @pl.when(q_block * rows <= length)
        def _():
            content = mine[g, 0, :KD, :]
            _, plus, minus = query_side(content, bias_ref[...], rel_ref[...], half)
            query, _, _ = query_block(content, plus, minus, rates)
            first_query = q_block * rows
            m_sc[...] = jnp.full(m_sc.shape, NEG, F32)
            l_sc[...] = jnp.zeros(l_sc.shape, F32)
            acc[...] = jnp.zeros(acc.shape, F32)

            def scores_of(t, kind):
                first_key = pl.multiple_of(t * span, span)
                decays = key_decays(
                    table_sc[...], lanes_ref[...], first_query, first_query + rows - 1, first_key, span, kind
                )
                keys = k_sc[pl.ds(first_key, span), :]
                return tile_scores(keys, decays, query, first_query, first_key, length, kind)

            def scores_into(slot, t, own):
                slot[...] = scores_of(t, "plain")

            def use(slot, t, own):
                scores = slot[...]
                old = m_sc[...]
                new = jnp.maximum(old, jnp.max(scores, axis=0, keepdims=True))
                alpha = jnp.exp(old - new)
                probs = jnp.exp(scores - new)
                m_sc[...] = new
                l_sc[...] = l_sc[...] * alpha + jnp.sum(probs, axis=0, keepdims=True)
                values = v_sc[:, pl.ds(pl.multiple_of(t * span, span), span)]
                acc[...] = acc[...] * alpha + dot(values, probs.astype(BF))

            def whole_tile(t):
                s0_sc[...] = scores_of(t, "both")
                use(s0_sc, t, None)

            visit_tiles(scores_into, use, (s0_sc, s1_sc), whole_tile, q_block, length, rows, per)
            total = l_sc[...]
            out = acc[...] / total
            mixed[g, 0] = out.astype(BF)
            wide[g, 0] = out
            lse[g, 0] = jnp.broadcast_to(m_sc[...] + jnp.log(total), lse.shape[2:])


def backward_kernel(
    parts, per, info, rates_ref, lanes_ref, bias_ref, rel_ref, mine, other, grad, wide, lse,
    dq, dkv_mine, dkv_other, sums, rel_grad,
    k_sc, kt_sc, v_sc, table_sc, turned_sc, s0_sc, s1_sc, dk_sc, dv_sc, dq_sc, bias_sc,
):
    groups, rows = mine.shape[0], mine.shape[3]
    half = RPF // 2
    step = pl.program_id(0)
    length = info[step]
    part = info[pl.num_programs(0)]
    rates = rates_ref[...]
    scale = KD**-0.5

    def store(block, kt, vt):
        spot = pl.multiple_of(block * rows, rows)
        k_sc[pl.ds(spot, rows), :] = jnp.concatenate([kt, jnp.zeros_like(kt)], axis=0).T
        kt_sc[:, pl.ds(spot, rows)] = kt
        v_sc[pl.ds(spot, rows), :] = vt.T

    key_side(parts, part, groups, mine, other, store)
    span = rows * per
    table_sc[...] = decay_table(lanes_ref[...], span)
    turned_sc[...] = table_sc[...].T[KD : KD + RPF]
    dk_sc[...] = jnp.zeros(dk_sc.shape, F32)
    dv_sc[...] = jnp.zeros(dv_sc.shape, F32)

    @pl.when(step == 0)
    def _():
        bias_sc[...] = jnp.zeros(bias_sc.shape, F32)
        rel_grad[...] = jnp.zeros(rel_grad.shape, F32)

    @pl.loop(0, groups)
    def _(g):
        q_block = g * parts + part

        @pl.when(q_block * rows > length)
        def _():
            dq[g, 0] = jnp.zeros(dq.shape[2:], dq.dtype)

        @pl.when(q_block * rows <= length)
        def _():
            content = mine[g, 0, :KD, :]
            content_rows = content.T
            positional, plus, minus = query_side(content, bias_ref[...], rel_ref[...], half)
            query, from_first, to_last = query_block(content, plus, minus, rates)
            first_query = q_block * rows
            last_query = first_query + rows - 1
            grad_t = grad[g, 0]
            grad_rows = grad_t.T
            log_total = lse[g, 0, :1, :]
            row_sum = jnp.sum(grad_t.astype(F32) * wide[g, 0], axis=0, keepdims=True)
            dq_sc[...] = jnp.zeros(dq_sc.shape, F32)

            def decays_of(first_key, kind):
                return key_decays(
                    table_sc[...], lanes_ref[...], first_query, last_query, first_key, span, kind
                )

            def scores_of(t, decays, kind):
                first_key = pl.multiple_of(t * span, span)
                keys = k_sc[pl.ds(first_key, span), :]
                return tile_scores(keys, decays, query, first_query, first_key, length, kind)

            def scores_into(slot, t, own):
                first_key = pl.multiple_of(t * span, span)
                slot[0] = scores_of(t, decays_of(first_key, "plain"), "plain")
                slot[1] = dot(v_sc[pl.ds(first_key, span), :], grad_t)

            def use(slot, t, own):
                absorb(slot, t, "plain", None)

            def whole_tile(t):
                first_key = pl.multiple_of(t * span, span)
                decays = decays_of(first_key, "both")
                s0_sc[0] = scores_of(t, decays, "both")
                s0_sc[1] = dot(v_sc[pl.ds(first_key, span), :], grad_t)
                absorb(s0_sc, t, "both", decays)

            def absorb(slot, t, kind, decays):
                first_key = spot = pl.multiple_of(t * span, span)
                scores, prob_grad = slot[0], slot[1]
                exact = jnp.exp(scores - log_total)
                score_grad = exact * (prob_grad - row_sum)
                low = score_grad.astype(BF)
                dv_sc[pl.ds(spot, span), :] += dot(exact.astype(BF), grad_rows)
                dk_sc[pl.ds(spot, span), :] += dot(low, content_rows)
                keys_turned = kt_sc[:, pl.ds(spot, span)]
                if kind == "both":
                    i, j = order_of(first_query, first_key, span, rows)
                    equal = 0.5 * score_grad
                    lower = jnp.where(i > j, score_grad, jnp.where(i < j, 0.0, equal)).astype(BF)
                    upper = jnp.where(i < j, score_grad, jnp.where(i > j, 0.0, equal)).astype(BF)
                    dq_sc[:KD] += dot(keys_turned, low)
                    below, above = decays
                    dq_sc[KD : KD + half] += dot(below.T[KD : KD + half], lower)
                    dq_sc[KD + half : KD + RPF] += dot(above.T[KD + half : KD + RPF], upper)
                else:
                    before = first_key < first_query
                    gap = jnp.where(before, first_query - (first_key + span - 1), first_key - last_query)
                    faded = jnp.exp(-rates * gap.astype(F32))
                    down = turned_sc[:half] * jnp.where(before, faded, 0.0)
                    up = turned_sc[half:] * jnp.where(before, 0.0, faded)
                    pos = jnp.concatenate([down, up], axis=0).astype(BF)
                    dq_sc[...] += dot(jnp.concatenate([keys_turned, pos], axis=0), low)

            visit_tiles(scores_into, use, (s0_sc, s1_sc), whole_tile, q_block, length, rows, per)
            content_grad = dq_sc[:KD]
            down, up = dq_sc[KD : KD + half] * from_first, dq_sc[KD + half :] * to_last
            projected_grad = jnp.concatenate([down + up, down - up], axis=0)
            positional_grad = dot32(rel_ref[...], projected_grad, ((0,), (0,)))
            dq[g, 0] = (scale * (content_grad + positional_grad)).astype(BF)
            bias_sc[0] += content_grad
            bias_sc[1] += positional_grad
            rel_grad[...] += dot32(positional, projected_grad, ((1,), (1,)))

    for slot in range(parts):
        theirs = slot_part(part, slot, parts)
        for g in range(groups):
            spot = pl.multiple_of((g * parts + theirs) * rows, rows)
            dkt = dk_sc[pl.ds(spot, rows), :].astype(BF).T
            dvt = dv_sc[pl.ds(spot, rows), :].astype(BF).T
            both = jnp.concatenate([dkt, dvt], axis=0)
            if slot == 0:
                dkv_mine[g, 0] = both
            else:
                dkv_other[slot - 1, g, 0] = both

    @pl.when(step == pl.num_programs(0) - 1)
    def _():
        sums[...] = scale * jnp.sum(bias_sc[...], axis=-1, keepdims=True)


def attention_cost(windows, groups, rows, parts, wide):
    pairs = windows * groups * rows * groups * parts * rows
    return pl.CostEstimate(
        flops=int(pairs * 2 * wide * 0.75), bytes_accessed=20_000_000, transcendentals=int(pairs)
    )


def whole(*shape):
    return pl.BlockSpec(shape, lambda w: (0,) * len(shape))


def per_window(*shape):
    lead = len(shape) - 3
    return pl.BlockSpec(shape, lambda w: (0,) * lead + (w, 0, 0))


def tile_blocks(rows, groups, parts, target):
    per = max(1, target // rows)
    while (groups * parts) % per:
        per -= 1
    return per


def lanes_of(rates):
    line = rates.reshape(1, -1)
    return jnp.pad(jnp.concatenate([line, line], axis=1), ((0, 0), (KD, 128 - KD - RPF)))


def attention_forward(info, rates, bias, rel, mine, other, parts):
    groups, windows, _, rows = mine.shape
    per = tile_blocks(rows, groups, parts, 1024)
    total = groups * parts * rows
    return pl.pallas_call(
        functools.partial(forward_kernel, parts, per),
        grid=(windows,),
        out_shape=(
            jax.ShapeDtypeStruct((groups, windows, VD, rows), BF),
            jax.ShapeDtypeStruct((groups, windows, VD, rows), F32),
            jax.ShapeDtypeStruct((groups, windows, 8, rows), F32),
        ),
        in_specs=[
            pl.BlockSpec(memory_space=pltpu.SMEM),
            whole(*rates.shape),
            whole(1, 128),
            whole(*bias.shape),
            whole(*rel.shape),
            per_window(groups, 1, 2 * KD + VD, rows),
            per_window(parts - 1, groups, 1, KD + VD, rows),
        ],
        out_specs=(
            per_window(groups, 1, VD, rows),
            per_window(groups, 1, VD, rows),
            per_window(groups, 1, 8, rows),
        ),
        scratch_shapes=[
            pltpu.VMEM((total, 128), BF),
            pltpu.VMEM((VD, total), BF),
            pltpu.VMEM((rows * per, 128), F32),
            pltpu.VMEM((rows * per, rows), F32),
            pltpu.VMEM((rows * per, rows), F32),
            pltpu.VMEM((1, rows), F32),
            pltpu.VMEM((1, rows), F32),
            pltpu.VMEM((VD, rows), F32),
        ],
        compiler_params=pltpu.CompilerParams(vmem_limit_bytes=56 * 2**20),
        cost_estimate=attention_cost(windows, groups, rows, parts, 128 + 256),
        name="attention_forward",
    )(info, rates, lanes_of(rates), bias, rel, mine, other)


def attention_backward(info, rates, bias, rel, mine, other, grad, wide, lse, parts):
    groups, windows, _, rows = mine.shape
    per = tile_blocks(rows, groups, parts, 1024)
    total = groups * parts * rows
    return pl.pallas_call(
        functools.partial(backward_kernel, parts, per),
        grid=(windows,),
        out_shape=(
            jax.ShapeDtypeStruct((groups, windows, KD, rows), BF),
            jax.ShapeDtypeStruct((groups, windows, KD + VD, rows), BF),
            jax.ShapeDtypeStruct((parts - 1, groups, windows, KD + VD, rows), BF),
            jax.ShapeDtypeStruct((2, KD, 1), F32),
            jax.ShapeDtypeStruct((KD, RPF), F32),
        ),
        in_specs=[
            pl.BlockSpec(memory_space=pltpu.SMEM),
            whole(*rates.shape),
            whole(1, 128),
            whole(*bias.shape),
            whole(*rel.shape),
            per_window(groups, 1, 2 * KD + VD, rows),
            per_window(parts - 1, groups, 1, KD + VD, rows),
            per_window(groups, 1, VD, rows),
            per_window(groups, 1, VD, rows),
            per_window(groups, 1, 8, rows),
        ],
        out_specs=(
            per_window(groups, 1, KD, rows),
            per_window(groups, 1, KD + VD, rows),
            per_window(parts - 1, groups, 1, KD + VD, rows),
            whole(2, KD, 1),
            whole(KD, RPF),
        ),
        scratch_shapes=[
            pltpu.VMEM((total, 128), BF),
            pltpu.VMEM((KD, total), BF),
            pltpu.VMEM((total, VD), BF),
            pltpu.VMEM((rows * per, 128), F32),
            pltpu.VMEM((RPF, rows * per), F32),
            pltpu.VMEM((2, rows * per, rows), F32),
            pltpu.VMEM((2, rows * per, rows), F32),
            pltpu.VMEM((total, KD), F32),
            pltpu.VMEM((total, VD), F32),
            pltpu.VMEM((KD + RPF, rows), F32),
            pltpu.VMEM((2, KD, rows), F32),
        ],
        compiler_params=pltpu.CompilerParams(vmem_limit_bytes=56 * 2**20),
        cost_estimate=attention_cost(windows, groups, rows, parts, 3 * 256 + 2 * 256),
        name="attention_backward",
    )(info, rates, lanes_of(rates), bias, rel, mine, other, grad, wide, lse)

MESH = pl.DeviceIdType.MESH


def upper_work(here, lengths, cotangent, skip_input, outs, gathered, scratch, remote, neighbours):
    out_grad_o, conv_o, joined_o, lifted_o, third_o, skip_grad_o, skip_part_o, bias_o = outs
    (
        table_rows,
        lines,
        w_point,
        w_skip,
        w_upsample,
        grad_v,
        skip_v,
        conv_v,
        joined_v,
        lifted_v,
        part_v,
        halo_before,
        halo_after,
        sem,
        halo_sem,
    ) = scratch
    dp, seq = here
    windows, fine, width = grad_v.shape
    rows = fine // 2
    before, after = neighbours

    def load(source, target, n):
        return pltpu.make_async_copy(source, target, sem.at[n])

    point_load = load(gathered[9], w_point, 0)
    skip_load = load(gathered[4], w_skip, 1)
    upsample_load = load(gathered[8], w_upsample, 2)
    grad_load = load(cotangent, grad_v, 3)
    input_load = load(skip_input, skip_v, 4)
    grad_load.start()
    input_load.start()
    stores = {
        "out_grad": load(grad_v, out_grad_o, 5),
        "conv": load(conv_v, conv_o, 6),
        "joined": load(joined_v, joined_o, 7),
        "lifted": load(lifted_v, lifted_o, 8),
        "skip": load(skip_v, skip_grad_o, 9),
    }

    def against(x, table):
        return lax.dot_general(
            x, table[...].reshape(width, width), (((1,), (1,)), ((), ())), preferred_element_type=F32
        )

    def halo_copies():
        out = []
        for w in range(windows):
            out.append(
                remote(
                    conv_v.at[w, pl.ds(fine - 16, 16)],
                    halo_before.at[w],
                    halo_sem.at[0, w],
                    halo_sem.at[1, w],
                    after,
                )
            )
            out.append(
                remote(
                    conv_v.at[w, pl.ds(0, 16)],
                    halo_after.at[w],
                    halo_sem.at[2, w],
                    halo_sem.at[3, w],
                    before,
                )
            )
        return out

    def conv_grad(w):
        if w == 0:
            point_load.start()
            grad_load.wait()
            point_load.wait()
        length = lengths[w]

        @pl.loop(0, fine // 256)
        def _(k):
            at = pl.ds(pl.multiple_of(k * 256, 256), 256)
            bin_ = seq * rows + lax.div(
                k * 256 + lax.broadcasted_iota(jnp.int32, (256, width), 0), 2
            )
            grad = jnp.where(bin_ < length, grad_v[w, at, :].astype(F32), 0.0).astype(BF)
            grad_v[w, at, :] = grad
            conv_v[w, at, :] = against(grad, w_point).astype(BF)

        if w == windows - 1:
            stores["out_grad"].start()
            stores["conv"].start()
            for copy in halo_copies():
                copy.start()

    def skip_part(w):
        if w == 0:
            skip_load.start()
            input_load.wait()
            skip_load.wait()

        @pl.loop(0, fine // 256)
        def _(k):
            at = pl.ds(pl.multiple_of(k * 256, 256), 256)
            made = dot(skip_v[w, at, :], w_skip[...].reshape(width, width)) + lines[0:1, :]
            part_v[...] = made
            store = load(part_v, skip_part_o.at[w, at], 10)
            store.start()
            store.wait()

    def joined_grad():
        for copy in halo_copies():
            copy.wait_recv()
        total = jnp.zeros((1, width), F32)
        tap = [lines[n : n + 1, :] for n in (1, 2, 3)]
        tile = 64
        for w in range(windows):
            first = halo_before[w].astype(F32)[15:16, :]
            first = jnp.where(seq == 0, 0.0, first)
            last = halo_after[w].astype(F32)[0:1, :]
            last = jnp.where(seq == lax.axis_size("seq") - 1, 0.0, last)
            for k in range(fine // tile):
                at = slice(k * tile, (k + 1) * tile)
                here_rows = conv_v[w, at, :].astype(F32)
                up = first if k == 0 else conv_v[w, k * tile - 16 : k * tile, :].astype(F32)[15:16, :]
                down = (
                    last
                    if k == fine // tile - 1
                    else conv_v[w, (k + 1) * tile : (k + 1) * tile + 16, :].astype(F32)[0:1, :]
                )
                index = lax.broadcasted_iota(jnp.int32, here_rows.shape, 0)
                earlier = jnp.where(index == 0, up, pltpu.roll(here_rows, 1, 0))
                later = jnp.where(index == tile - 1, down, pltpu.roll(here_rows, tile - 1, 0))
                made = later * tap[0] + here_rows * tap[1] + earlier * tap[2]
                total = total + jnp.sum(made, axis=0, keepdims=True)
                joined_v[w, at, :] = made.astype(BF)
        bias_o[...] = total
        stores["joined"].start()
        pair = lax.div(lax.broadcasted_iota(jnp.int32, (rows, fine), 1), 2)
        twice = (pair == lax.broadcasted_iota(jnp.int32, (rows, fine), 0)).astype(F32).astype(BF)
        for w in range(windows):
            lifted_v[w * rows : (w + 1) * rows, :] = dot(twice, joined_v[w]).astype(BF)
        stores["lifted"].start()

    def skip_grad(w):
        @pl.loop(0, fine // 256)
        def _(k):
            at = pl.ds(pl.multiple_of(k * 256, 256), 256)
            skip_v[w, at, :] = against(joined_v[w, at, :], w_skip).astype(BF)

        if w == windows - 1:
            stores["skip"].start()

    def third_grad():
        upsample_load.start()
        upsample_load.wait()

        @pl.loop(0, windows * rows // 256)
        def _(k):
            at = pl.ds(pl.multiple_of(k * 256, 256), 256)
            part_v[...] = against(lifted_v[at, :], w_upsample)
            store = load(part_v, third_o.at[at], 10)
            store.start()
            store.wait()

    def finish():
        for store in stores.values():
            store.wait()
        for copy in halo_copies():
            copy.wait_send()

    jobs = {
        9: [(9, functools.partial(conv_grad, 0))],
        10: [(None, functools.partial(conv_grad, 1))],
        11: [(4, functools.partial(skip_part, 0)), (None, functools.partial(skip_part, 1))],
        12: [(None, joined_grad)],
        13: [(None, functools.partial(skip_grad, 0)), (None, functools.partial(skip_grad, 1))],
        14: [(8, third_grad)],
    }
    return {"rows": table_rows, "lines": lines, "jobs": jobs, "finish": finish}


def links_kernel(pairs, counts, parts, early, *refs):
    n_in, n_out = counts
    refs = list(refs)

    def take(count):
        out, refs[:count] = refs[:count], []
        return out

    refs_in = take(n_in)
    if early:
        values, spread_gain, pick_gain, spread_bias, pick_bias = take(5)
        lengths, cotangent, skip_input = take(3)
    elif parts:
        (blocks,) = take(1)
    refs_out = take(n_out)
    if parts:
        mine, other = take(2)
    if early:
        (normed,) = take(1)
        upper_out = take(8)
    local_sem, send_hi, recv_hi, send_y, recv_y, send_dp, recv_dp, send_c, recv_c = take(9)
    dp, seq = lax.axis_index("dp"), lax.axis_index("seq")
    ndp, nhi = refs_out[0].shape[:2]
    hi, low = lax.div(seq, 4), lax.rem(seq, 4)
    y, c = lax.div(low, 2), lax.rem(low, 2)

    def place(dp_to, hi_to, y_to, c_to):
        return (dp_to, hi_to * 4 + y_to * 2 + c_to)

    hi_peers = [place(dp, lax.rem(hi + k, nhi), y, c) for k in range(1, nhi)]
    y_peers = [place(dp, hi, 1 - y, c)]
    dp_peers = [place(lax.rem(dp + k, ndp), hi, y, c) for k in range(1, ndp)]
    c_peers = [place(dp, hi, y, 1 - c)]
    everyone = hi_peers + y_peers + dp_peers + c_peers
    if parts:
        head, part = lax.div(seq, parts), lax.rem(seq, parts)
        head_of = [lax.rem(head + k, H) for k in range(1, H)]
        head_peers = [(dp, h * parts + part) for h in head_of]
        part_peers = [(dp, head * parts + slot_part(part, k, parts)) for k in range(1, parts)]
        everyone = everyone + head_peers + part_peers
    if early:
        nseq = nhi * 4
        after = (dp, lax.rem(seq + 1, nseq))
        before = (dp, lax.rem(seq + nseq - 1, nseq))
        everyone = everyone + [after, before]

    barrier = pltpu.get_barrier_semaphore()
    for peer in everyone:
        pl.semaphore_signal(barrier, inc=1, device_id=peer, device_id_type=MESH)
    pl.semaphore_wait(barrier, len(everyone))

    def remote(source, target, ss, rs, peer):
        return pltpu.make_async_remote_copy(
            src_ref=source,
            dst_ref=target,
            send_sem=ss,
            recv_sem=rs,
            device_id=peer,
            device_id_type=MESH,
        )

    step_chunks, serial = [], 0
    for pair in pairs:
        step_chunks.append([])
        for side in (0, 1):
            for chunk in pair[side]:
                step_chunks[-1].append((serial, side) + chunk)
                serial += 1

    def copies(chunk, stage):
        n, side, array, row, rows, first, columns = chunk
        out = refs_out[array]
        piece = (pl.ds(row, rows), pl.ds(first, columns))
        which = (("hi", "y", "dp", "c"), ("hi", "dp", "y", "c"))[side][stage]
        if which == "hi":
            target = out.at[(dp, hi, y, c) + piece]
            source = refs_in[array].at[piece]
            peers, ss, rs = hi_peers, send_hi, recv_hi
        else:
            every = slice(None)
            if which == "c":
                target = out.at[(every, every, every, c) + piece]
                peers, ss, rs = c_peers, send_c, recv_c
            elif which == "y":
                there = (dp, every, y, c) if stage == 1 else (every, every, y, c)
                target = out.at[there + piece]
                peers, ss, rs = y_peers, send_y, recv_y
            else:
                there = (dp, every, y, c) if stage == 1 else (dp, every, every, c)
                target = out.at[there + piece]
                peers, ss, rs = dp_peers, send_dp, recv_dp
            source = target
        return [remote(source, target, ss.at[n, k], rs.at[n, k], p) for k, p in enumerate(peers)]

    def own(array):
        return pltpu.make_async_copy(
            refs_in[array], refs_out[array].at[dp, hi, y, c], local_sem.at[array]
        )

    everything = [chunk for group in step_chunks for chunk in group]
    head_copies, head_own = [], None
    if parts:
        head_local, head_send, head_recv, part_send, part_recv = take(5)
        if early:
            blocks = take(1)[0]
        head_copies = [
            remote(blocks.at[:, h], mine.at[head], head_send.at[k], head_recv.at[k], p)
            for k, (h, p) in enumerate(zip(head_of, head_peers, strict=True))
        ]
        head_own = pltpu.make_async_copy(blocks.at[:, head], mine.at[head], head_local.at[0])
        keys = mine.at[:, :, pl.ds(KD, KD + VD)]
        part_copies = [
            remote(keys, other.at[k], part_send.at[k], part_recv.at[k], p)
            for k, p in enumerate(part_peers)
        ]
        if not early:
            head_own.start()
    if early:
        small_v, query_v, key_v, values_v, inputs_v, gain_v, bias_v, load_sem = take(8)
        inputs_load = pltpu.make_async_copy(values, inputs_v, load_sem.at[0])
        inputs_load.start()
        upper = upper_work(
            (dp, seq), lengths, cotangent, skip_input, upper_out, refs_out, take(15), remote, (before, after)
        )

    def make_blocks():
        loads = [
            pltpu.make_async_copy(source, target, load_sem.at[k + 1])
            for k, (source, target) in enumerate(
                zip(refs_out[:4], (small_v, query_v, key_v, values_v), strict=True)
            )
        ]
        for load in loads:
            load.start()
        inputs_load.wait()
        for load in loads:
            load.wait()

        @pl.loop(0, ndp * nhi * 4)
        def _(k):
            rows = small_v[
                lax.div(k, nhi * 4),
                lax.rem(lax.div(k, 4), nhi),
                lax.rem(lax.div(k, 2), 2),
                lax.rem(k, 2),
            ].astype(F32)
            gain_v[pl.ds(k, 1), :] = rows[0:1, :]
            bias_v[pl.ds(k, 1), :] = rows[1:2, :]
            for n in range(4):
                upper["rows"][n, pl.ds(k, 1), :] = rows[7 + n : 8 + n, :]

        def line_up(table, spread, pick):
            return jnp.sum(dot(table[...].astype(BF), spread[...]) * pick[...], axis=0, keepdims=True)

        gain = line_up(gain_v, spread_gain, pick_gain)
        for n in range(4):
            upper["lines"][n : n + 1, :] = line_up(upper["rows"].at[n], spread_gain, pick_gain)
        bias = line_up(bias_v, spread_bias, pick_bias)
        windows, rows = inputs_v.shape[:2]
        for w in range(windows):
            normed[w * rows : (w + 1) * rows, :] = layer_norm(
                inputs_v[w].astype(F32), gain
            ).astype(BF)
        low = normed[...]
        width = low.shape[1]

        def weight(table, first, columns):
            return table[:, :, :, :, :, first : first + columns].reshape(width, columns)

        for pair in range(H // 2):
            spot, wide = pair * 2 * KD, pair * 2 * VD
            content = dot(low, weight(query_v, spot, 2 * KD)) + bias[:, spot : spot + 2 * KD]
            content = (content * (KD**-0.5)).astype(BF).T
            key = dot(low, weight(key_v, spot, 2 * KD)).astype(BF).T
            value = dot(low, weight(values_v, wide, 2 * VD)).astype(BF).T
            for h in range(2):
                for w in range(windows):
                    span = slice(w * rows, (w + 1) * rows)
                    blocks[w, 2 * pair + h, :KD, :] = content[h * KD : (h + 1) * KD, span]
                    blocks[w, 2 * pair + h, KD : 2 * KD, :] = key[h * KD : (h + 1) * KD, span]
                    blocks[w, 2 * pair + h, 2 * KD :, :] = value[h * VD : (h + 1) * VD, span]
        head_own.start()

    ahead, lag = 3, 2

    def launch(step):
        for chunk in step_chunks[step]:
            for copy in copies(chunk, 0):
                copy.start()

    events = {}
    for spot in range(len(pairs)):
        gap = 1 if spot < early else lag
        for stage in (3, 2, 1):
            events.setdefault(spot + gap * (stage - 1), []).append((stage, spot))
    made_at = early + 2 if early else 0
    waited = []
    exchange_at = made_at + len(head_copies) + 1

    def exchange_parts():
        head_own.wait()
        for copy in head_copies:
            copy.wait_recv()
        for copy in part_copies:
            copy.start()

    heads_at = [made_at + k for k in range(len(head_copies))]
    for step in range(min(ahead, len(pairs))):
        launch(step)
    for array in range(n_out):
        own(array).start()
    for array in range(n_out):
        own(array).wait()
    for step in range(max(list(events) + ([exchange_at] if early else heads_at)) + 1):
        for stage, spot in sorted(events.get(step, []), reverse=True):
            for chunk in step_chunks[spot]:
                for copy in copies(chunk, stage - 1):
                    copy.wait_recv()
                for copy in copies(chunk, stage):
                    copy.start()
        if step + ahead < len(pairs):
            launch(step + ahead)
        if early and step == made_at:
            for group in step_chunks[:early]:
                for chunk in group:
                    for copy in copies(chunk, 3):
                        copy.wait_recv()
            make_blocks()
        if step in heads_at:
            head_copies[heads_at.index(step)].start()
        if early and step == exchange_at:
            exchange_parts()
        if early:
            for need, job in upper["jobs"].get(step, []):
                for chunk in everything:
                    if chunk[2] == need:
                        for copy in copies(chunk, 3):
                            copy.wait_recv()
                        waited.append(chunk)
                job()
    if parts and not early:
        exchange_parts()
    for group in step_chunks[early:]:
        for chunk in group:
            if chunk not in waited:
                for copy in copies(chunk, 3):
                    copy.wait_recv()
    if early:
        upper["finish"]()
    if parts:
        for copy in part_copies:
            copy.wait_recv()
        for copy in head_copies + part_copies:
            copy.wait_send()
    for chunk in everything:
        for stage in range(4):
            for copy in copies(chunk, stage):
                copy.wait_send()


def spread_tables(length, share):
    column = jnp.arange(length, dtype=jnp.int32)
    lane = jnp.arange(128, dtype=jnp.int32)
    device = jnp.arange(length // share, dtype=jnp.int32)
    spread = (column[None, :] % share == lane[:, None]).astype(BF)
    pick = (column[None, :] // share == device[:, None]).astype(F32)
    return spread, pick


def use_links(name, collective, shards, pairs, blocks=None, values=None, early=0, upper=()):
    ndp, nseq = lax.axis_size("dp"), lax.axis_size("seq")
    nhi, devices = nseq // 4, ndp * nseq
    parts = nseq // H if blocks is not None or early else 0
    chunks = sum(len(side) for pair in pairs for side in pair)
    arrays = [shard.shape for shard in shards]
    out_shape = [jax.ShapeDtypeStruct((ndp, nhi, 2, 2) + shape, BF) for shape in arrays]
    operands = list(shards)
    in_specs = [pl.BlockSpec(memory_space=pl.ANY)] * len(operands)
    sizes = [(len(arrays),)] + [
        (chunks, size) for size in (nhi - 1, nhi - 1, 1, 1, ndp - 1, ndp - 1, 1, 1)
    ]
    scratch = []
    if early:
        windows, rows, width = values.shape
        operands += [values]
        operands += [
            *spread_tables(width, width // devices),
            *spread_tables(H * KD, H * KD // devices),
        ]
        in_specs += [pl.BlockSpec(memory_space=pl.ANY)] + [
            pl.BlockSpec(memory_space=pltpu.VMEM)
        ] * 4
        operands += list(upper)
        in_specs += [pl.BlockSpec(memory_space=pltpu.SMEM)] + [
            pl.BlockSpec(memory_space=pl.ANY)
        ] * 2
        scratch = [
            pltpu.VMEM((windows, H, 2 * KD + VD, rows), BF),
            pltpu.VMEM(out_shape[0].shape, BF),
            pltpu.VMEM(out_shape[1].shape, BF),
            pltpu.VMEM(out_shape[2].shape, BF),
            pltpu.VMEM(out_shape[3].shape, BF),
            pltpu.VMEM(values.shape, BF),
            pltpu.VMEM((devices, 128), F32),
            pltpu.VMEM((devices, 128), F32),
            pltpu.SemaphoreType.DMA((5,)),
            pltpu.VMEM((4, devices, 128), F32),
            pltpu.VMEM((8, width), F32),
            *[pltpu.VMEM((ndp, nhi, 2, 2, width // devices, width), BF)] * 3,
            *[pltpu.VMEM((windows, 2 * rows, width), BF)] * 4,
            pltpu.VMEM((windows * rows, width), BF),
            pltpu.VMEM((256, width), F32),
            pltpu.VMEM((windows, 16, width), BF),
            pltpu.VMEM((windows, 16, width), BF),
            pltpu.SemaphoreType.DMA((11,)),
            pltpu.SemaphoreType.DMA((4, windows)),
        ]
    elif parts:
        windows, _, _, rows = blocks.shape
        operands.append(blocks)
        in_specs.append(pl.BlockSpec(memory_space=pl.ANY))
    out_specs = [pl.BlockSpec(memory_space=pl.ANY)] * len(out_shape)
    if parts:
        out_shape += [
            jax.ShapeDtypeStruct((H, windows, 2 * KD + VD, rows), BF),
            jax.ShapeDtypeStruct((parts - 1, H, windows, KD + VD, rows), BF),
        ]
        out_specs += [pl.BlockSpec(memory_space=pl.ANY)] * 2
        sizes += [(1,), (H - 1,), (H - 1,), (parts - 1,), (parts - 1,)]
    if early:
        out_shape.append(jax.ShapeDtypeStruct((windows * rows, width), BF))
        out_specs.append(pl.BlockSpec(memory_space=pltpu.VMEM))
        fine, coarse = (windows, 2 * rows, width), (windows * rows, width)
        out_shape += [
            jax.ShapeDtypeStruct(*s)
            for s in (
                (fine, BF),
                (fine, BF),
                (fine, BF),
                (coarse, BF),
                (coarse, F32),
                (fine, BF),
                (fine, F32),
                ((1, width), F32),
            )
        ]
        out_specs += [pl.BlockSpec(memory_space=pl.ANY)] * 7
        out_specs.append(pl.BlockSpec(memory_space=pltpu.VMEM))
    outs = pl.pallas_call(
        functools.partial(links_kernel, pairs, (len(shards), len(arrays)), parts, early),
        out_shape=out_shape,
        in_specs=in_specs,
        out_specs=out_specs,
        scratch_shapes=[pltpu.SemaphoreType.DMA(size) for size in sizes] + scratch,
        compiler_params=pltpu.CompilerParams(
            collective_id=collective, has_side_effects=True, vmem_limit_bytes=60 * 2**20
        ),
        name=name,
    )(*operands)
    flat = [out.reshape(-1, out.shape[-1]) for out in outs[: len(arrays)]]
    return flat + list(outs[len(arrays) :])


def pack_kernel(*refs):
    out, wide = refs[-2:]
    wide[...] = jnp.zeros(wide.shape, F32)
    spot = 0
    for ref in refs[:-2]:
        rows, columns = ref.shape
        if rows >= 16:
            spot = 16
        wide[spot : spot + rows, :columns] = ref[...].astype(F32)
        spot += rows
    out[...] = wide[...].astype(BF)


def pack_shards(shards):
    rows = 16 + shards[-1].shape[0]
    return pl.pallas_call(
        pack_kernel,
        out_shape=jax.ShapeDtypeStruct((rows, 128), BF),
        scratch_shapes=[pltpu.VMEM((rows, 128), F32)],
        name="pack_shards",
    )(*shards)


def tie(*values):
    return lax.optimization_barrier(values)


def project_kernel(values, gain, content_bias, w_query, w_key, w_value, normed, sent, scratch):
    windows, rows, _ = values.shape

    @pl.when(pl.program_id(0) == 0)
    def _():
        for w in range(windows):
            low = layer_norm(values[w].astype(F32), gain[...]).astype(BF)
            scratch[w * rows : (w + 1) * rows, :] = low
            normed[w * rows : (w + 1) * rows, :] = low

    low = scratch[...]
    content = ((dot(low, w_query[...]) + content_bias[0]) * (KD**-0.5)).astype(BF).T
    keys = dot(low, w_key[...]).astype(BF).T
    mixable = dot(low, w_value[...]).astype(BF).T
    for h in range(2):
        for w in range(windows):
            span = slice(w * rows, (w + 1) * rows)
            sent[w, h, :KD, :] = content[h * KD : (h + 1) * KD, span]
            sent[w, h, KD : 2 * KD, :] = keys[h * KD : (h + 1) * KD, span]
            sent[w, h, 2 * KD :, :] = mixable[h * VD : (h + 1) * VD, span]


def project(values, gain, content_bias, weight_query, weight_key, weight_value):
    windows, rows, width = values.shape
    steps = H // 2
    return pl.pallas_call(
        project_kernel,
        grid=(steps,),
        out_shape=(
            jax.ShapeDtypeStruct((windows * rows, width), BF),
            jax.ShapeDtypeStruct((windows, H, 2 * KD + VD, rows), BF),
        ),
        in_specs=[
            pl.BlockSpec((windows, rows, width), lambda i: (0, 0, 0)),
            pl.BlockSpec((1, width), lambda i: (0, 0)),
            pl.BlockSpec((1, 1, 2 * KD), lambda i: (i, 0, 0)),
            pl.BlockSpec((width, 2 * KD), lambda i: (0, i)),
            pl.BlockSpec((width, 2 * KD), lambda i: (0, i)),
            pl.BlockSpec((width, 2 * VD), lambda i: (0, i)),
        ],
        out_specs=(
            pl.BlockSpec((windows * rows, width), lambda i: (0, 0)),
            pl.BlockSpec((windows, 2, 2 * KD + VD, rows), lambda i: (0, i, 0, 0)),
        ),
        scratch_shapes=[pltpu.VMEM((windows * rows, width), BF)],
        compiler_params=pltpu.CompilerParams(vmem_limit_bytes=48 * 2**20),
        name="project",
    )(
        values,
        gain.reshape(1, width),
        content_bias.reshape(steps, 1, 2 * KD),
        weight_query,
        weight_key,
        weight_value,
    )


def block_work(operands, outs, scratch, arrived, wait_heads):
    values, third_grad, w_mixing, w_inner, w_outer = operands[:5]
    second_gain, third_gain, inner_bias, outer_bias = operands[5:]
    second_sum, third_sum, inner_sum, outer_sum = outs[9:]
    mixing_v, inner_v, outer_v, values_v, third_grad_v, middle_v, block_v, slope_v = scratch[:8]
    mixed_b, second_b, hidden_b, third_b, block_b, before_b, middle_b, back_b, heads_b = scratch[8:17]
    weight_sem, load_sem, store_sem = scratch[17:]
    windows, rows, width = values.shape
    wide = slope_v.shape[1]
    tile, chunk = 512, 32
    weight_loads = [
        pltpu.make_async_copy(source, target, weight_sem.at[k])
        for k, (source, target) in enumerate(
            ((w_mixing, mixing_v), (w_inner, inner_v), (w_outer, outer_v))
        )
    ]

    def load_values(w):
        return pltpu.make_async_copy(values.at[w], values_v, load_sem.at[0])

    def load_third(w):
        return pltpu.make_async_copy(
            third_grad.at[pl.ds(w * rows, rows)], third_grad_v, load_sem.at[1]
        )

    buffers = (mixed_b, second_b, hidden_b, third_b, block_b, before_b, middle_b, back_b, heads_b)

    def store(k, w):
        target = outs[k].at[w] if k == 8 else outs[k].at[pl.ds(w * rows, rows)]
        return pltpu.make_async_copy(buffers[k], target, store_sem.at[k])

    def free(w, *numbers):
        if w:
            for k in numbers:
                store(k, w - 1).wait()

    def begin():
        for load in weight_loads + [load_values(0), load_third(0)]:
            load.start()
        for total in (second_sum, third_sum, inner_sum, outer_sum):
            total[...] = jnp.zeros(total.shape, F32)

    def mix(w):
        wait_heads(w)
        free(w, 0)
        for pair in range(H // 2):
            both = jnp.concatenate([arrived[2 * pair + h, w] for h in range(2)], axis=0)
            mixed_b[:, pair * 2 * VD : (pair + 1) * 2 * VD] = both.T
        store(0, w).start()
        if w == 0:
            weight_loads[0].wait()
        load_values(w).wait()
        for k in range(0, width, tile):
            cols = slice(k, k + tile)
            middle_v[:, cols] = values_v[:, cols].astype(F32) + dot(mixed_b[...], mixing_v[:, cols])

    def inner(w, part):
        if part == 0:
            free(w, 1, 2)

            @pl.loop(0, rows // chunk)
            def _(k):
                at = pl.ds(pl.multiple_of(k * chunk, chunk), chunk)
                unit, _ = norm_parts(middle_v[at, :])
                second_b[at, :] = (unit * second_gain[...]).astype(BF)

            store(1, w).start()
            if w == 0:
                weight_loads[1].wait()
        for k in range(part * wide // 2, (part + 1) * wide // 2, tile):
            cols = slice(k, k + tile)
            before = dot(second_b[...], inner_v[:, cols]) + inner_bias[:, cols]
            hidden, slope = gelu_parts(before)
            hidden_b[:, cols] = hidden.astype(BF)
            slope_v[:, cols] = slope.astype(BF)
        if part == 1:
            store(2, w).start()

    def outer(w):
        if w == 0:
            weight_loads[2].wait()
        for k in range(0, width, tile):
            cols = slice(k, k + tile)
            block_v[:, cols] = (
                middle_v[:, cols] + dot(hidden_b[...], outer_v[:, cols]) + outer_bias[:, cols]
            )

    def turn(w):
        free(w, 3, 4)
        load_third(w).wait()

        @pl.loop(0, rows // chunk)
        def _(k):
            at = pl.ds(pl.multiple_of(k * chunk, chunk), chunk)
            unit, scale = norm_parts(block_v[at, :])
            third, slope = gelu_parts(unit * third_gain[...])
            third_b[at, :] = third.astype(BF)
            grad = third_grad_v[at, :] * slope
            third_sum[...] += jnp.sum(grad * unit, axis=0, keepdims=True)
            back = norm_backward(unit, scale, grad, third_gain[...])
            outer_sum[...] += jnp.sum(back, axis=0, keepdims=True)
            block_v[at, :] = back
            block_b[at, :] = back.astype(BF)

        store(3, w).start()
        store(4, w).start()
        if w + 1 < windows:
            load_values(w + 1).start()
            load_third(w + 1).start()

    def before_grad(w):
        free(w, 5)
        for k in range(0, wide, tile):
            cols = slice(k, k + tile)
            grad = times_rows(block_b[...], outer_v[cols, :]) * slope_v[:, cols].astype(F32)
            low = grad.astype(BF)
            before_b[:, cols] = low
            inner_sum[:, cols] += jnp.sum(low.astype(F32), axis=0, keepdims=True)
        store(5, w).start()

    def second_grad(w):
        free(w, 7)
        for k in range(0, width, tile):
            cols = slice(k, k + tile)
            back_b[:, cols] = times_rows(before_b[...], inner_v[cols, :])

    def middle_grad(w):
        free(w, 6, 8)

        @pl.loop(0, rows // chunk)
        def _(k):
            at = pl.ds(pl.multiple_of(k * chunk, chunk), chunk)
            unit, scale = norm_parts(middle_v[at, :])
            grad = back_b[at, :]
            second_sum[...] += jnp.sum(grad * unit, axis=0, keepdims=True)
            back = block_v[at, :] + norm_backward(unit, scale, grad, second_gain[...])
            back_b[at, :] = back
            middle_b[at, :] = back.astype(BF)

        store(6, w).start()
        store(7, w).start()
        for pair in range(H // 2):
            cols = slice(pair * 2 * VD, (pair + 1) * 2 * VD)
            turned = times_rows(middle_b[...], mixing_v[cols, :]).astype(BF).T
            for h in range(2):
                heads_b[2 * pair + h] = turned[h * VD : (h + 1) * VD]
        store(8, w).start()

    def finish():
        for k in range(len(buffers)):
            store(k, windows - 1).wait()

    jobs = []
    for w in range(windows):
        jobs += [
            functools.partial(mix, w),
            functools.partial(inner, w, 0),
            functools.partial(inner, w, 1),
            functools.partial(outer, w),
            functools.partial(turn, w),
            functools.partial(before_grad, w),
            functools.partial(second_grad, w),
            functools.partial(middle_grad, w),
        ]
    return begin, jobs, finish


def sums_kernel(plan, refs_spec, *refs):
    groups, n_terms, mode, parts, n_small, made_here, late, masked = plan
    refs = list(refs)

    def take(count):
        out, refs[:count] = refs[:count], []
        return out

    terms = take(n_terms * (2 if made_here else 1) - (1 if late else 0))
    head_in = take({None: 0, "in": 1, "block": 1, "out": 3}[mode])
    small_in = take(1 if n_small else 0)
    if late:
        w_query, w_key, w_value, values, middle_grad, gain, spread, pick = take(8)
    if masked:
        lengths, w_masked = take(2)
    if mode == "block":
        block_in = take(9)
    outs = take(n_terms)
    head_out = take(0 if late or not mode or mode == "block" else 1)
    small_out = take(1 if n_small else 0)
    if late:
        (input_grad,) = take(1)
    if masked:
        (masked_o,) = take(1)
    if mode == "block":
        block_out = take(13)
    own, arrived, result, back, hop1, hop2, line = [], [], [], [], [], [], []
    flat = [(side, unit) for group in groups for side in (0, 1) for unit in group[side]]
    count = len(flat)
    own = take(count)
    arrived = take(count)
    hop1 = take(count)
    hop2 = take(count)
    line = take(count)
    result = take(count)
    back = take(count)
    if made_here:
        slots = min(2, n_terms)
        lefts, rights, turned = take(1), take(slots), take(slots)
        going, left_sem, right_sem = take(3)
    load_sem, c_send, c_recv, s1, r1, s2, r2, s3, r3, s4, r4 = take(11)
    dp, seq = lax.axis_index("dp"), lax.axis_index("seq")
    ndp, nhi = own[0].shape[:2]
    nseq = nhi * 4
    hi, low = lax.div(seq, 4), lax.rem(seq, 4)
    y, c = lax.div(low, 2), lax.rem(low, 2)

    def place(dp_to, hi_to, y_to, c_to):
        return (dp_to, hi_to * 4 + y_to * 2 + c_to)

    hi_index = [lax.rem(hi + k, nhi) for k in range(1, nhi)]
    dp_index = [lax.rem(dp + k, ndp) for k in range(1, ndp)]
    hi_peers = [place(dp, h, y, c) for h in hi_index]
    dp_peers = [place(d, hi, y, c) for d in dp_index]
    y_peer, c_peer = place(dp, hi, 1 - y, c), place(dp, hi, y, 1 - c)
    everyone = hi_peers + dp_peers + [y_peer, c_peer]
    if mode:
        head, part = lax.div(seq, parts), lax.rem(seq, parts)
        head_of = [lax.rem(head + k, H) for k in range(1, H)]
        head_peers = [(dp, h * parts + part) for h in head_of]
        part_peers = [(dp, head * parts + slot_part(part, k, parts)) for k in range(1, parts)]
        everyone = everyone + head_peers + part_peers

    barrier = pltpu.get_barrier_semaphore()
    for peer in everyone:
        pl.semaphore_signal(barrier, inc=1, device_id=peer, device_id_type=MESH)
    expected = len(everyone)
    me = dp * nseq + seq
    if n_small:

        def other_device(k):
            there = lax.rem(me + k, n_small)
            return (lax.div(there, nseq), lax.rem(there, nseq))

        @pl.loop(1, n_small)
        def _(k):
            pl.semaphore_signal(barrier, inc=1, device_id=other_device(k), device_id_type=MESH)

        expected += n_small - 1
    pl.semaphore_wait(barrier, expected)

    def remote(source, target, ss, rs, peer):
        return pltpu.make_async_remote_copy(
            src_ref=source,
            dst_ref=target,
            send_sem=ss,
            recv_sem=rs,
            device_id=peer,
            device_id_type=MESH,
        )

    def half_of(array):
        return outs[array].shape[1] // 2

    def columns_of(unit, core):
        array, row, rows, column, columns = unit
        half = half_of(array)
        spot = pl.multiple_of(core * half + column, 128)
        return terms[array].at[:, :, :, :, pl.ds(row, rows), pl.ds(spot, columns)]

    def load(n):
        return pltpu.make_async_copy(columns_of(flat[n][1], c), own[n], load_sem.at[n])

    def over_core(n):
        source = going_of(n) if made_here else columns_of(flat[n][1], 1 - c)
        return [remote(source, arrived[n], c_send.at[n], c_recv.at[n], c_peer)]

    def first_hop(n):
        if flat[n][0] == 0:
            return [
                remote(own[n].at[d], hop1[n].at[k], s1.at[n, k], r1.at[n, k], p)
                for k, (d, p) in enumerate(zip(dp_index, dp_peers, strict=True))
            ]
        return [remote(own[n].at[:, :, 1 - y], hop1[n], s1.at[n, 0], r1.at[n, 0], y_peer)]

    def second_hop(n):
        if flat[n][0] == 0:
            return [remote(own[n].at[dp, :, 1 - y], hop2[n], s2.at[n, 0], r2.at[n, 0], y_peer)]
        return [
            remote(own[n].at[d, :, y], hop2[n].at[k], s2.at[n, k], r2.at[n, k], p)
            for k, (d, p) in enumerate(zip(dp_index, dp_peers, strict=True))
        ]

    def along_line(n):
        return [
            remote(own[n].at[dp, h, y], line[n].at[k], s3.at[n, k], r3.at[n, k], p)
            for k, (h, p) in enumerate(zip(hi_index, hi_peers, strict=True))
        ]

    def back_home(n):
        return [remote(result[n].at[1 - c], back[n], s4.at[n], r4.at[n], c_peer)]

    hops = (over_core, first_hop, second_hop, along_line, back_home)

    def add(a, b):
        return (a.astype(F32) + b.astype(F32)).astype(BF)

    def absorb(n, stage):
        mine = own[n]
        if stage == 1:

            @pl.loop(0, ndp * nhi)
            def _(k):
                d, h = lax.div(k, nhi), lax.rem(k, nhi)
                mine[d, h] = add(mine[d, h], arrived[n][d, h])

        elif stage == 2 and flat[n][0] == 0:

            @pl.loop(0, nhi)
            def _(h):
                total = mine[dp, h].astype(F32)
                for k in range(ndp - 1):
                    total = total + hop1[n][k, h].astype(F32)
                mine[dp, h] = total.astype(BF)

        elif stage == 2:

            @pl.loop(0, ndp * nhi)
            def _(k):
                d, h = lax.div(k, nhi), lax.rem(k, nhi)
                mine[d, h, y] = add(mine[d, h, y], hop1[n][d, h])

        elif stage == 3 and flat[n][0] == 0:

            @pl.loop(0, nhi)
            def _(h):
                mine[dp, h, y] = add(mine[dp, h, y], hop2[n][h])

        elif stage == 3:

            @pl.loop(0, nhi)
            def _(h):
                total = mine[dp, h, y].astype(F32)
                for k in range(ndp - 1):
                    total = total + hop2[n][k, h].astype(F32)
                mine[dp, h, y] = total.astype(BF)

        elif stage == 4:
            total = mine[dp, hi, y].astype(F32)
            for k in range(nhi - 1):
                total = total + line[n][k].astype(F32)
            result[n][...] = total
        else:
            array, row, rows, column, columns = flat[n][1]
            half = half_of(array)
            here, there = result[n][c], back[n][...]
            outs[array][row : row + rows, column : column + columns] = jnp.where(
                c == 0, here, there
            )
            outs[array][row : row + rows, half + column : half + column + columns] = jnp.where(
                c == 0, there, here
            )

    numbers, serial = [], 0
    for group in groups:
        size = len(group[0]) + len(group[1])
        numbers.append(range(serial, serial + size))
        serial += size

    def going_of(n):
        step = next(k for k, some in enumerate(numbers) if n in some)
        unit = flat[n][1]
        side = numbers[step].index(n)
        return going.at[step % 2, side, :, :, :, :, pl.ds(0, unit[2]), pl.ds(0, unit[4])]

    def fetch_left(array):
        left = terms[2 * array]
        return pltpu.make_async_copy(
            left,
            lefts[0].at[pl.ds(0, left.shape[0]), pl.ds(0, left.shape[1])],
            left_sem.at[array],
        )

    def fetch_right(array):
        right = terms[2 * array + 1]
        return pltpu.make_async_copy(
            right,
            rights[array % 2].at[pl.ds(0, right.shape[0]), pl.ds(0, right.shape[1])],
            right_sem.at[array],
        )

    def arrive():
        for copy in head_own:
            copy.wait()
        for copy in head_copies:
            copy.wait_recv()
        packed = rights[(n_terms - 1) % 2]
        windows, rows = gathered.shape[1], gathered.shape[3]
        for w in range(windows):
            for pair in range(H // 2):
                for first, size, start in ((0, KD, 0), (KD, KD, H * KD), (2 * KD, VD, 2 * H * KD)):
                    both = jnp.concatenate(
                        [gathered[2 * pair + h, w, first : first + size, :] for h in range(2)], axis=0
                    )
                    at = start + pair * 2 * size
                    packed[w * rows : (w + 1) * rows, at : at + 2 * size] = both.T

    def make(step):
        if not numbers[step]:
            return
        units = [flat[n][1] for n in numbers[step]]
        array, rows = units[0][0], units[0][2]
        first, size = units[0][3], sum(u[4] for u in units)
        left = terms[2 * array]
        tokens, slot = left.shape[0], array % 2
        if array not in begun:
            begun.append(array)
            fetch_left(array).wait()

            @pl.loop(0, left.shape[1] // 256)
            def _(k):
                spot = pl.multiple_of(k * 256, 256)
                turned[slot][pl.ds(spot, 256), pl.ds(0, tokens)] = lefts[0][
                    pl.ds(0, tokens), pl.ds(spot, 256)
                ].T

            if array + 1 < n_terms:
                fetch_left(array + 1).start()
                if array >= 1 and not (late and array + 1 == n_terms - 1):
                    fetch_right(array + 1).start()
            if late and array == n_terms - 1:
                arrive()
            else:
                fetch_right(array).wait()

        for n in unsent[step % 2]:
            for copy in over_core(n):
                copy.wait_send()
        unsent[step % 2] = list(numbers[step])
        span = nhi * 4 * rows
        for whose in (1 - c, c):
            spot = pl.multiple_of(whose * half_of(array) + first, 128)
            part_right = rights[slot][pl.ds(0, tokens), pl.ds(spot, size)]
            for d in range(ndp):
                made = dot(turned[slot][pl.ds(d * span, span), pl.ds(0, tokens)], part_right)
                made = made.astype(BF).reshape(nhi, 2, 2, rows, size)
                at = 0
                for k, n in enumerate(numbers[step]):
                    piece = made[..., at : at + units[k][4]]
                    if whose is c:
                        own[n][d] = piece
                    else:
                        going[step % 2, k, d, :, :, :, pl.ds(0, rows), pl.ds(0, units[k][4])] = piece
                    at += units[k][4]
            if whose is not c:
                for n in numbers[step]:
                    for copy in over_core(n):
                        copy.start()

    begun, unsent = [], [[], []]

    def launch(step):
        if made_here:
            make(step)
        else:
            for n in numbers[step]:
                load(n).start()
                for copy in over_core(n):
                    copy.start()

    if made_here:
        fetch_left(0).start()
        for array in range(min(2, n_terms)):
            if not (late and array == n_terms - 1):
                fetch_right(array).start()

    if mode == "in":
        head_send, head_recv, head_local = take(3)
        blocks, gathered = head_in[0], head_out[0]
        head_copies = [
            remote(blocks.at[:, h], gathered.at[head], head_send.at[k], head_recv.at[k], p)
            for k, (h, p) in enumerate(zip(head_of, head_peers, strict=True))
        ]
        head_own = [
            pltpu.make_async_copy(blocks.at[:, head], gathered.at[head], head_local.at[0])
        ]
        for copy in head_copies + head_own:
            copy.start()
    if mode == "block":
        head_send, head_recv, head_local, gathered = take(4)
        blocks = head_in[0]
        windows = blocks.shape[1]
        by_window = [
            [
                remote(
                    blocks.at[h, w],
                    gathered.at[head, w],
                    head_send.at[w, k],
                    head_recv.at[w, k],
                    p,
                )
                for k, (h, p) in enumerate(zip(head_of, head_peers, strict=True))
            ]
            for w in range(windows)
        ]
        head_copies = [copy for some in by_window for copy in some]
        head_own = [
            pltpu.make_async_copy(blocks.at[head, w], gathered.at[head, w], head_local.at[w])
            for w in range(windows)
        ]
        for copy in by_window[0] + head_own:
            copy.start()

        def wait_heads(w):
            head_own[w].wait()
            for copy in by_window[w]:
                copy.wait_recv()

        begin_block, block_jobs, finish_block = block_work(
            block_in, block_out, take(20), gathered, wait_heads
        )
        begin_block()
    if mode == "out":
        head_send, head_recv, head_local, part_send, part_recv, mine_kv, arrived_kv = take(7)
        query, pair_mine, pair_other = head_in
        gathered = take(1)[0] if late else head_out[0]
        part_copies = [
            remote(pair_other.at[k], arrived_kv.at[k], part_send.at[k], part_recv.at[k], p)
            for k, p in enumerate(part_peers)
        ]
        kv_load = pltpu.make_async_copy(pair_mine, mine_kv, head_local.at[0])
        for copy in part_copies + [kv_load]:
            copy.start()
    if n_small:
        small_send, small_recv, small_sc = take(3)
        small = small_in[0]
    if masked:
        w_v, x_v, y_v, masked_sem = take(4)
        w_masked_load = pltpu.make_async_copy(w_masked, w_v, masked_sem.at[0])
        w_masked_load.start()
        windows, fine = masked_o.shape[:2]
        tile = x_v.shape[0]

        def masked_product(k):
            w, at = divmod(k * tile, fine)
            load = pltpu.make_async_copy(terms[0].at[pl.ds(k * tile, tile)], x_v, masked_sem.at[1])
            load.start()
            load.wait()
            if k == 0:
                w_masked_load.wait()
            made = dot(x_v[...], w_v[...])
            bin_ = seq * (fine // 2) + lax.div(
                at + lax.broadcasted_iota(jnp.int32, made.shape, 0), 2
            )
            y_v[...] = jnp.where(bin_ < lengths[w], made, 0.0).astype(BF)
            store = pltpu.make_async_copy(
                y_v, masked_o.at[w, pl.ds(at, tile)], masked_sem.at[2]
            )
            store.start()
            store.wait()

    if late:
        small, w_buffer, acc, flat_v, middle_v, out_v, gain_sum, late_sem = take(8)
        w_loads = [
            pltpu.make_async_copy(w_query, w_buffer.at[:, pl.ds(0, H * KD)], late_sem.at[0]),
            pltpu.make_async_copy(w_key, w_buffer.at[:, pl.ds(H * KD, H * KD)], late_sem.at[1]),
        ]
        for copy in w_loads:
            copy.start()

        def window_loads(w):
            span = pl.ds(w * flat_v.shape[0], flat_v.shape[0])
            return [
                pltpu.make_async_copy(values.at[w], flat_v, late_sem.at[2]),
                pltpu.make_async_copy(middle_grad.at[span], middle_v, late_sem.at[3]),
            ]

        def store_window(w):
            span = pl.ds(w * flat_v.shape[0], flat_v.shape[0])
            return pltpu.make_async_copy(out_v, input_grad.at[span], late_sem.at[4])

        for copy in window_loads(0):
            copy.start()

        def back_through(w_ref, first, columns, into_first):
            packed = rights[(n_terms - 1) % 2]

            @pl.loop(0, acc.shape[0] // 128)
            def _(k):
                rows = pl.ds(pl.multiple_of(k * 128, 128), 128)
                made = lax.dot_general(
                    packed[rows, first : first + columns],
                    w_ref[:, 0:columns],
                    (((1,), (1,)), ((), ())),
                    preferred_element_type=F32,
                )
                acc[rows, :] = made if into_first else acc[rows, :] + made

        def value_load(k):
            half = H * VD // 2
            return pltpu.make_async_copy(
                w_value.at[:, pl.ds(k * half, half)],
                w_buffer.at[:, pl.ds(0, half)],
                late_sem.at[5 + k],
            )

        def products(stage):
            half = H * VD // 2
            if stage == 0:
                for copy in w_loads:
                    copy.wait()
                back_through(w_buffer, 0, 2 * H * KD, True)
                value_load(0).start()
            else:
                value_load(0).wait()
                back_through(w_buffer, 2 * H * KD, half, False)
                value_load(1).start()
                value_load(1).wait()
                back_through(w_buffer, 2 * H * KD + half, half, False)

        def norm_back(w):
            for copy in window_loads(w):
                copy.wait()
            if w:
                store_window(w - 1).wait()
            else:
                gain_sum[...] = jnp.zeros(gain_sum.shape, F32)
            size = flat_v.shape[0]

            @pl.loop(0, size // 32)
            def _(k):
                rows = pl.ds(pl.multiple_of(k * 32, 32), 32)
                value = flat_v[rows, :].astype(F32)
                centered = value - jnp.mean(value, axis=-1, keepdims=True)
                scale = lax.rsqrt(jnp.mean(centered * centered, axis=-1, keepdims=True) + epsilon)
                unit = centered * scale
                grad = acc[pl.ds(pl.multiple_of(w * size + k * 32, 32), 32), :]
                gain_sum[...] += jnp.sum(grad * unit, axis=0, keepdims=True)
                grad = grad * gain[...]
                along = jnp.mean(grad * unit, axis=-1, keepdims=True)
                back = scale * (grad - jnp.mean(grad, axis=-1, keepdims=True) - unit * along)
                out_v[rows, :] = (middle_v[rows, :] + back).astype(BF)

            store_window(w).start()
            if w + 1 < values.shape[0]:
                for copy in window_loads(w + 1):
                    copy.start()
            else:
                rows = dot32(pick[...] * gain_sum[...], spread[...].astype(F32), ((1,), (1,)))
                wide = small_in[0].shape[1]
                small[:, :wide, :] = small_in[0][...]
                small[:, wide:, :] = jnp.broadcast_to(
                    rows[:, None, :], (rows.shape[0], 8, rows.shape[1])
                )

    if n_small:

        def small_copy(k):
            there = lax.rem(me + k, n_small)
            return remote(
                small.at[there],
                small_sc.at[k - 1],
                small_send.at[k - 1],
                small_recv.at[k - 1],
                other_device(k),
            )

        def start_small():
            @pl.loop(1, n_small)
            def _(k):
                small_copy(k).start()

        if not late:
            start_small()

    if mode == "out":
        for copy in part_copies:
            copy.wait_recv()
        kv_load.wait()

        @pl.loop(0, H)
        def _(g):
            total = mine_kv[g].astype(F32)
            for k in range(parts - 1):
                total = total + arrived_kv[k, g].astype(F32)
            mine_kv[g] = total.astype(BF)

        q_target = gathered.at[head, :, pl.ds(0, KD)]
        kv_target = gathered.at[head, :, pl.ds(KD, KD + VD)]
        head_copies = [
            remote(source.at[h], target, head_send.at[i, k], head_recv.at[i, k], p)
            for k, (h, p) in enumerate(zip(head_of, head_peers, strict=True))
            for i, (source, target) in enumerate(((query, q_target), (mine_kv, kv_target)))
        ]
        head_own = [
            pltpu.make_async_copy(query.at[head], q_target, head_local.at[1]),
            pltpu.make_async_copy(mine_kv.at[head], kv_target, head_local.at[2]),
        ]
        for copy in head_copies + head_own:
            copy.start()
    ahead = 3
    for step in range(min(ahead, len(groups))):
        launch(step)
    if mode == "block":
        for some in by_window[1:]:
            for copy in some:
                copy.start()
    lag = 2
    for step in range(len(groups) + 4 * lag):
        for stage in (5, 4, 3, 2, 1):
            spot = step - lag * (stage - 1)
            if 0 <= spot < len(groups):
                for n in numbers[spot]:
                    if stage == 1 and not made_here:
                        load(n).wait()
                    for copy in hops[stage - 1](n):
                        copy.wait_recv()
                    absorb(n, stage)
                    if stage < 5:
                        for copy in hops[stage](n):
                            copy.start()
        if step + ahead < len(groups):
            launch(step + ahead)
        if mode == "block":
            steps = len(groups) + 4 * lag
            for job in block_jobs[
                step * len(block_jobs) // steps : (step + 1) * len(block_jobs) // steps
            ]:
                job()
        if masked and 0 <= step - (len(groups) - ahead) < terms[0].shape[0] // tile:
            masked_product(step - (len(groups) - ahead))
        if late and step >= len(groups) - ahead:
            turn = step - (len(groups) - ahead)
            if turn < 2:
                products(turn)
            elif turn < 2 + values.shape[0]:
                norm_back(turn - 2)
                if turn == 1 + values.shape[0]:
                    start_small()
    if n_small:

        @pl.loop(1, n_small)
        def _(k):
            small_copy(k).wait_recv()

        small_out[0][...] = small[me] + jnp.sum(small_sc[...], axis=0)

        @pl.loop(1, n_small)
        def _(k):
            small_copy(k).wait_send()

    if late:
        store_window(values.shape[0] - 1).wait()
    if mode == "block":
        finish_block()
    if mode:
        if not late and mode != "block":
            for copy in head_own:
                copy.wait()
            for copy in head_copies:
                copy.wait_recv()
        for copy in head_copies:
            copy.wait_send()
    if mode == "out":
        for copy in part_copies:
            copy.wait_send()
    for n in range(count):
        for hop in hops:
            if hop is not over_core or not made_here or n in unsent[0] + unsent[1]:
                for copy in hop(n):
                    copy.wait_send()


def sum_terms(name, collective, pairs, groups, mode=None, heads=(), small=None, late=None, masked=None, block=None):
    ndp, nseq = lax.axis_size("dp"), lax.axis_size("seq")
    nhi, parts, devices = nseq // 4, nseq // H, ndp * nseq
    shares = [(left.shape[1] // devices, right.shape[1]) for left, right in pairs]
    made_here = all(rows % 16 == 0 for rows, _ in shares)
    if made_here:
        operands = [x for pair in pairs for x in pair][: -1 if late else None]
    else:
        operands = [
            transposed_times(left, right).astype(BF).reshape((ndp, nhi, 2, 2) + share)
            for (left, right), share in zip(pairs, shares, strict=True)
        ]
    in_specs = [pl.BlockSpec(memory_space=pl.ANY)] * len(operands)
    out_shape = [jax.ShapeDtypeStruct(share, F32) for share in shares]
    out_specs = [pl.BlockSpec(memory_space=pltpu.VMEM)] * len(out_shape)
    flat = [(side, unit) for group in groups for side in (0, 1) for unit in group[side]]
    count = len(flat)
    shapes = [(unit[2], unit[4]) for _, unit in flat]
    sides = [side for side, _ in flat]
    scratch = [pltpu.VMEM((ndp, nhi, 2, 2) + s, BF) for s in shapes] * 2
    scratch += [
        pltpu.VMEM(((ndp, nhi, 2) if side else (ndp - 1, nhi, 2, 2)) + s, BF)
        if not side
        else pltpu.VMEM((ndp, nhi, 2) + s, BF)
        for side, s in zip(sides, shapes, strict=True)
    ]
    scratch += [
        pltpu.VMEM((ndp - 1, nhi, 2) + s if side else (nhi, 2) + s, BF)
        for side, s in zip(sides, shapes, strict=True)
    ]
    scratch += [pltpu.VMEM((nhi - 1, 2) + s, BF) for s in shapes]
    scratch += [pltpu.VMEM((2,) + s, F32) for s in shapes]
    scratch += [pltpu.VMEM(s, F32) for s in shapes]
    if made_here:
        slots = [pairs[k::2] for k in range(min(2, len(pairs)))]
        tokens = [max(left.shape[0] for left, _ in slot) for slot in slots]
        tall = [max(left.shape[1] for left, _ in slot) for slot in slots]
        wide = [max(right.shape[1] for _, right in slot) for slot in slots]
        unit_rows = max(rows for rows, _ in shapes)
        unit_columns = max(columns for _, columns in shapes)
        scratch += [
            pltpu.VMEM((max(tokens), max(tall)), BF),
            *[pltpu.VMEM(s, BF) for s in zip(tokens, wide, strict=True)],
            *[pltpu.VMEM(s, BF) for s in zip(tall, tokens, strict=True)],
            pltpu.VMEM((2, 2, ndp, nhi, 2, 2, unit_rows, unit_columns), BF),
            pltpu.SemaphoreType.DMA((len(pairs),)),
            pltpu.SemaphoreType.DMA((len(pairs),)),
        ]
    hop = max(ndp - 1, 1)
    sizes = [(count,)] * 3 + [(count, hop)] * 4 + [(count, nhi - 1)] * 2 + [(count,)] * 2
    scratch += [pltpu.SemaphoreType.DMA(size) for size in sizes]
    if mode == "in":
        windows, _, size, rows = heads[0].shape
        operands.append(heads[0])
        in_specs.append(pl.BlockSpec(memory_space=pl.ANY))
        out_shape.append(jax.ShapeDtypeStruct((H, windows, size, rows), BF))
        out_specs.append(pl.BlockSpec(memory_space=pl.ANY))
        scratch += [pltpu.SemaphoreType.DMA((n,)) for n in (H - 1, H - 1, 1)]
    if mode == "block":
        operands += [heads[0], *block]
        in_specs += [pl.BlockSpec(memory_space=pl.ANY)] * 6
        in_specs += [pl.BlockSpec(memory_space=pltpu.VMEM)] * 4
        windows, rows, width = block[0].shape
        wide = block[3].shape[1]
        coarse, broad = (windows * rows, width), (windows * rows, wide)
        out_shape += [
            jax.ShapeDtypeStruct(s, BF)
            for s in (coarse, coarse, broad, coarse, coarse, broad, coarse)
        ]
        out_shape.append(jax.ShapeDtypeStruct(coarse, F32))
        out_shape.append(jax.ShapeDtypeStruct((windows, H, VD, rows), BF))
        out_shape += [jax.ShapeDtypeStruct((1, n), F32) for n in (width, width, wide, width)]
        out_specs += [pl.BlockSpec(memory_space=pl.ANY)] * 9
        out_specs += [pl.BlockSpec(memory_space=pltpu.VMEM)] * 4
        narrow, long = pltpu.VMEM((rows, width), BF), pltpu.VMEM((rows, wide), BF)
        full_rows = pltpu.VMEM((rows, width), F32)
        scratch += [
            pltpu.SemaphoreType.DMA((windows, H - 1)),
            pltpu.SemaphoreType.DMA((windows, H - 1)),
            pltpu.SemaphoreType.DMA((windows,)),
            pltpu.VMEM(heads[0].shape, BF),
            *[pltpu.VMEM(w.shape, BF) for w in block[2:5]],
            narrow,
            full_rows,
            full_rows,
            full_rows,
            long,
            narrow,
            narrow,
            long,
            narrow,
            narrow,
            long,
            narrow,
            full_rows,
            pltpu.VMEM((H, VD, rows), BF),
            pltpu.SemaphoreType.DMA((3,)),
            pltpu.SemaphoreType.DMA((2,)),
            pltpu.SemaphoreType.DMA((9,)),
        ]
    if mode == "out":
        _, windows, _, rows = heads[0].shape
        operands += list(heads)
        in_specs += [pl.BlockSpec(memory_space=pl.ANY)] * 3
        if not late:
            out_shape.append(jax.ShapeDtypeStruct((H, windows, 2 * KD + VD, rows), BF))
            out_specs.append(pl.BlockSpec(memory_space=pl.ANY))
        scratch += [
            pltpu.SemaphoreType.DMA(size)
            for size in ((2, H - 1), (2, H - 1), (3,), (parts - 1,), (parts - 1,))
        ]
        scratch += [pltpu.VMEM(heads[1].shape, BF), pltpu.VMEM(heads[2].shape, BF)]
        if late:
            scratch.append(pltpu.VMEM((H, windows, 2 * KD + VD, rows), BF))
    n_small = 0
    if small is not None:
        n_small = devices
        operands.append(small)
        in_specs.append(pl.BlockSpec(memory_space=pltpu.VMEM))
        message = (small.shape[1] + (8 if late else 0), small.shape[2])
        out_shape.append(jax.ShapeDtypeStruct(message, F32))
        out_specs.append(pl.BlockSpec(memory_space=pltpu.VMEM))
        scratch += [
            pltpu.SemaphoreType.DMA((devices - 1,)),
            pltpu.SemaphoreType.DMA((devices - 1,)),
            pltpu.VMEM((devices - 1,) + message, F32),
        ]
    if late:
        windows, rows, width = late[3].shape
        operands += list(late) + list(spread_tables(width, width // devices))
        in_specs += [pl.BlockSpec(memory_space=pl.ANY)] * 5
        in_specs += [pl.BlockSpec(memory_space=pltpu.VMEM)] * 3
        out_shape.append(jax.ShapeDtypeStruct((windows * rows, width), BF))
        out_specs.append(pl.BlockSpec(memory_space=pl.ANY))
        scratch += [
            pltpu.VMEM((devices,) + message, F32),
            pltpu.VMEM((width, 2 * H * KD), BF),
            pltpu.VMEM((windows * rows, width), F32),
            pltpu.VMEM((rows, width), BF),
            pltpu.VMEM((rows, width), F32),
            pltpu.VMEM((rows, width), BF),
            pltpu.VMEM((1, width), F32),
            pltpu.SemaphoreType.DMA((7,)),
        ]
    if masked:
        lengths, weight, shape = masked
        operands += [lengths, weight]
        in_specs += [pl.BlockSpec(memory_space=pltpu.SMEM), pl.BlockSpec(memory_space=pl.ANY)]
        out_shape.append(jax.ShapeDtypeStruct(shape, BF))
        out_specs.append(pl.BlockSpec(memory_space=pl.ANY))
        scratch += [
            pltpu.VMEM(weight.shape, BF),
            pltpu.VMEM((256, shape[2]), BF),
            pltpu.VMEM((256, shape[2]), BF),
            pltpu.SemaphoreType.DMA((3,)),
        ]
    plan = (
        groups, len(pairs), mode, parts, n_small, made_here, late is not None, masked is not None
    )
    return pl.pallas_call(
        functools.partial(sums_kernel, plan, None),
        out_shape=out_shape,
        in_specs=in_specs,
        out_specs=out_specs,
        scratch_shapes=scratch,
        compiler_params=pltpu.CompilerParams(
            collective_id=collective, has_side_effects=True, vmem_limit_bytes=63 * 2**20
        ),
        name=name,
    )(*operands)


def halves(array, rows, columns, size=128):
    out, spot = [], 0
    while spot < columns:
        size = min(size, (columns - spot) // 2)
        out.append((((array, 0, rows, spot, size),), ((array, 0, rows, spot + size, size),)))
        spot += 2 * size
    return tuple(out)


def full(array, shards):
    rows, columns = shards[array].shape
    return (array, 0, rows, 0, columns)


def columns_of_rows(array, rows, first, columns):
    return (array, 0, rows, first, columns)


def gelu_parts(x):
    below = 0.5 * (1.0 + lax.erf(x * (0.5**0.5)))
    density = jnp.exp(-0.5 * x * x) * (1.0 / math.sqrt(2.0 * math.pi))
    return x * below, below + x * density


def norm_parts(value):
    centered = value - jnp.mean(value, axis=-1, keepdims=True)
    scale = lax.rsqrt(jnp.mean(centered * centered, axis=-1, keepdims=True) + epsilon)
    return centered * scale, scale


def norm_backward(unit, scale, grad, gain):
    grad = grad * gain
    along = jnp.mean(grad * unit, axis=-1, keepdims=True)
    return scale * (grad - jnp.mean(grad, axis=-1, keepdims=True) - unit * along)


def times_rows(x, table):
    return lax.dot_general(x, table, (((1,), (1,)), ((), ())), preferred_element_type=F32)


def weight_pairs(shapes, offset):
    def pieces(n, parts):
        rows, columns = shapes[n]
        if rows % (16 * parts):
            return [(offset + n, 0, rows, 0, columns)]
        size = rows // parts
        return [(offset + n, k * size, size, 0, columns) for k in range(parts)]

    first = pieces(5, 3) + pieces(0, 3) + pieces(4, 3) + pieces(2, 3)
    second = pieces(1, 3) + pieces(3, 6)
    steps = max(len(second), 1)
    spare = len(first) - steps
    pairs, spot = [], 0
    for k in range(steps):
        take = 2 if 3 <= k < 3 + spare else 1
        pairs.append((tuple(first[spot : spot + take]), (second[k],)))
        spot += take
    if spot < len(first):
        pairs.append((tuple(first[spot:]), ()))
    return tuple(pairs)


def on_device(
    inputs,
    skip_input,
    lengths,
    cotangent,
    first_gain,
    query_weight,
    key_weight,
    value_weight,
    content_bias,
    position_bias,
    relative_weight,
    mixing_weight,
    second_gain,
    inner_weight,
    inner_bias,
    outer_weight,
    outer_bias,
    third_gain,
    upsample_weight,
    skip_weight,
    skip_bias,
    depth_weight,
    point_weight,
):
    windows, rows, width = inputs.shape
    scale = float(KD) ** (-0.5)
    nseq, ndp = lax.axis_size("seq"), lax.axis_size("dp")
    devices = nseq * ndp
    parts = nseq // H
    keys_total = rows * nseq
    seq = lax.axis_index("seq")
    head, part = lax.div(seq, parts), lax.rem(seq, parts)
    first = seq * rows
    hidden_width = inner_weight.shape[1]

    r = shard_rows = query_weight.shape[0]
    vectors = (
        first_gain,
        content_bias,
        position_bias,
        second_gain,
        inner_bias,
        outer_bias,
        third_gain,
        skip_bias,
    )
    small_rows = [v.reshape(1, -1) for v in vectors] + [depth_weight.T]
    relative_rows = relative_weight.shape[0]
    if r % 16 == 0:
        small_shard = pack_shards(small_rows + [relative_weight])
    else:
        small_rows = [jnp.pad(v, ((0, 0), (0, 128 - v.shape[1]))) for v in small_rows]
        small_rows.append(jnp.zeros((16 - len(vectors) - 3, 128), BF))
        small_rows.append(
            jnp.pad(relative_weight, ((0, -relative_rows % 16), (0, 128 - relative_weight.shape[1])))
        )
        small_shard = jnp.concatenate(small_rows, axis=0)
    keys_width, values_width = 2 * H * KD, H * VD
    half_hidden, half_width = hidden_width // 2, width // 2
    head_shards = [small_shard, query_weight, key_weight, value_weight]
    head_pairs = (
        ((full(0, head_shards), full(1, head_shards)), (full(2, head_shards),)),
        ((columns_of_rows(3, r, 0, values_width // 2),), (columns_of_rows(3, r, values_width // 2, values_width // 2),)),
    )
    shards = [
        skip_weight,
        mixing_weight,
        inner_weight,
        outer_weight,
        upsample_weight,
        point_weight,
    ]
    if r % 16 == 0:
        (
            small_full,
            weight_query,
            weight_key,
            weight_value,
            weight_skip,
            weight_mixing,
            weight_inner,
            weight_outer,
            weight_upsample,
            weight_point,
            mine,
            other,
            normed_low,
            out_grad,
            conv_grad,
            joined_flat,
            lifted_grad,
            third_grad,
            skip_grad,
            skip_part,
            grad_skip_bias,
        ) = use_links(
            "gather_weights",
            1,
            head_shards + shards,
            head_pairs + weight_pairs([w.shape for w in shards], len(head_shards)),
            values=inputs,
            early=len(head_pairs),
            upper=(lengths, cotangent, skip_input),
        )
        out_grad, joined_flat, skip_part = (
            x.reshape(-1, width) for x in (out_grad, joined_flat, skip_part)
        )
        grad_skip_bias = grad_skip_bias[0]
    else:
        small_full, weight_query, weight_key, weight_value = use_links(
            "gather_heads", 1, head_shards, head_pairs
        )
    small_full = small_full.reshape((devices,) + small_shard.shape).astype(jnp.float32)

    def vector(k):
        return small_full[:, k, : vectors[k].shape[0]].reshape(-1)

    (
        gain_first,
        bias_content,
        bias_position,
        gain_second,
        bias_inner,
        bias_outer,
        gain_third,
        bias_skip,
    ) = map(vector, range(len(vectors)))
    taken = len(vectors)
    weight_depth = (
        small_full[:, taken : taken + 3, :r].transpose(0, 2, 1).reshape(width, 3)
    )
    weight_relative = small_full[:, 16 : 16 + relative_rows, :RPF].reshape(H * KD, RPF)

    lives = jnp.exp(
        jnp.linspace(math.log(3.0), math.log(keys_total), RPF // 2, dtype=jnp.float32)
    )
    rates = (math.log(2.0) / lives)[:, None]
    bias_gap = ((bias_position - bias_content) * scale).reshape(H, KD, 1)
    bias_gap = lax.dynamic_index_in_dim(bias_gap, head, 0, keepdims=False)
    relative = lax.dynamic_index_in_dim(
        weight_relative.reshape(H, KD, RPF), head, 0, keepdims=False
    ).T
    info = jnp.concatenate([lengths, part[None].astype(jnp.int32)])
    groups = [[p + parts * g for g in range(H)] for p in range(parts)]

    def exchange(array):
        return lax.all_to_all(array, "seq", 0, 0, axis_index_groups=groups, tiled=True)

    def swap_part(array, slot):
        return lax.ppermute(array, "seq", [(i, i ^ slot) for i in range(nseq)])

    flat = inputs.reshape(windows * rows, width).astype(jnp.float32)
    if r % 16:
        normed_low, sent = project(
            inputs, gain_first, bias_content, weight_query, weight_key, weight_value
        )
        (
            weight_skip,
            weight_mixing,
            weight_inner,
            weight_outer,
            weight_upsample,
            weight_point,
            mine,
            other,
        ) = use_links(
            "gather_weights", 2, shards, weight_pairs([w.shape for w in shards], 0), sent
        )

    def by_row(array):
        (array,) = tie(array.transpose(1, 3, 0, 2).reshape(windows * rows, -1))
        return array

    mixed_own, mixed_wide, log_total = attention_forward(
        info, rates, bias_gap, relative, mine, other, parts
    )
    if r % 16 == 0:
        skip_flat = skip_input.reshape(windows * 2 * rows, width)
        (
            own_skip,
            mixed_low,
            second_low,
            hidden_low,
            third_low,
            block_low,
            before_low,
            middle_low,
            middle_grad,
            mixed_grad,
            *block_sums,
        ) = sum_terms(
            "block_and_skip",
            6,
            [(skip_flat, joined_flat)],
            halves(0, r, half_width),
            "block",
            (mixed_own,),
            block=(
                inputs,
                third_grad,
                weight_mixing,
                weight_inner,
                weight_outer,
                gain_second[None, :],
                gain_third[None, :],
                bias_inner[None, :],
                bias_outer[None, :],
            ),
        )
        grad_second, grad_third, grad_inner_bias, grad_outer_bias = (s[0] for s in block_sums)
    else:
        mixed_low = by_row(exchange(mixed_own))
        middle = flat + matmul(mixed_low, weight_mixing)
        second, second_norm_back = jax.vjp(layer_norm, middle, gain_second)
        second_low = second.astype(jnp.bfloat16)
        before = matmul(second_low, weight_inner) + bias_inner
        hidden, gelu_back = jax.vjp(smooth_gelu, before)
        hidden_low = hidden.astype(jnp.bfloat16)
        block_out = middle + matmul(hidden_low, weight_outer) + bias_outer
        third, third_back = jax.vjp(norm_gelu, block_out, gain_third)
        third_low = third.astype(jnp.bfloat16)
    fine = jnp.arange(2 * rows, dtype=jnp.int32)[:, None] // 2
    twice = (fine == jnp.arange(rows, dtype=jnp.int32)[None, :]).astype(jnp.bfloat16)
    third_twice = (
        jnp.einsum(
            "ts,wsd->wtd",
            twice,
            third_low.reshape(windows, rows, width),
            preferred_element_type=jnp.float32,
        )
        .astype(jnp.bfloat16)
        .reshape(windows * 2 * rows, width)
    )
    skip_flat = skip_input.reshape(windows * 2 * rows, width)
    if r % 16:
        skip_part = matmul(skip_flat, weight_skip) + bias_skip
    joined_low = (
        (matmul(third_twice, weight_upsample) + skip_part)
        .astype(jnp.bfloat16)
        .reshape(windows, 2 * rows, width)
    )
    joined_rim = extended_2(joined_low, (("seq", 1),), 1)
    taps = weight_depth
    joined_wide = joined_rim.astype(jnp.float32)
    conv_low = depth_apply(joined_wide, taps).astype(jnp.bfloat16)
    conv_flat = conv_low.reshape(windows * 2 * rows, width)
    bins = 2 * first + jnp.arange(2 * rows, dtype=jnp.int32)
    keep = (bins // 2)[None, :] < lengths[:, None]
    keep_wide = keep.astype(jnp.float32)[:, :, None]
    if r % 16:
        outputs = (
            matmul(conv_flat, weight_point).reshape(windows, 2 * rows, width) * keep_wide
        ).astype(jnp.bfloat16)
    if r % 16:
        out_grad = (cotangent * keep.astype(jnp.bfloat16)[:, :, None]).reshape(
            windows * 2 * rows, width
        )
        conv_grad = (
            times_transposed(out_grad, weight_point)
            .astype(jnp.bfloat16)
            .reshape(windows, 2 * rows, width)
        )
        grad_rim = extended_2(conv_grad, (("seq", 1),), 1).astype(jnp.float32)
        joined_grad = (
            grad_rim[:, 2:] * taps[:, 0]
            + grad_rim[:, 1:-1] * taps[:, 1]
            + grad_rim[:, :-2] * taps[:, 2]
        )
        grad_skip_bias = jnp.sum(joined_grad, axis=(0, 1))
        joined_back = joined_grad.astype(jnp.bfloat16)
        joined_flat = joined_back.reshape(windows * 2 * rows, width)
        lifted_grad = (
            jnp.einsum("ts,wtd->wsd", twice, joined_back, preferred_element_type=jnp.float32)
            .astype(jnp.bfloat16)
            .reshape(windows * rows, width)
        )
        third_grad = times_transposed(lifted_grad, weight_upsample)
        skip_grad = (
            times_transposed(joined_flat, weight_skip)
            .astype(jnp.bfloat16)
            .reshape(windows, 2 * rows, width)
        )
    conv_wide = conv_grad.astype(jnp.float32)
    grad_depth = jnp.stack(
        [
            jnp.sum(conv_wide * joined_wide[:, :-2], axis=(0, 1)),
            jnp.sum(conv_wide * joined_wide[:, 1:-1], axis=(0, 1)),
            jnp.sum(conv_wide * joined_wide[:, 2:], axis=(0, 1)),
        ],
        axis=1,
    )
    if r % 16:
        block_grad, grad_third = third_back(third_grad)
        block_low = block_grad.astype(jnp.bfloat16)
        grad_outer_bias = jnp.sum(block_grad, axis=0)
        (before_grad,) = gelu_back(times_transposed(block_low, weight_outer))
        before_low = before_grad.astype(jnp.bfloat16)
        grad_inner_bias = jnp.sum(before_low.astype(jnp.float32), axis=0)
        middle_part, grad_second = second_norm_back(times_transposed(before_low, weight_inner))
        middle_grad = block_grad + middle_part
        middle_low = middle_grad.astype(jnp.bfloat16)
        middle_rows = middle_low.reshape(windows, rows, width)
        mixed_grad = (
            jnp.einsum("vd,wrd->wvr", weight_mixing, middle_rows, preferred_element_type=jnp.float32)
            .astype(jnp.bfloat16)
            .reshape(windows, H, VD, rows)
        )
    if r % 16 == 0:
        own_point, own_outer, own_upsample, arrived_grad, outputs = sum_terms(
            "sum_upper",
            3,
            [(conv_flat, out_grad), (hidden_low, block_low), (third_low, lifted_grad)],
            halves(0, r, half_width)
            + halves(1, outer_weight.shape[0], half_width)
            + halves(2, r, half_width),
            "in",
            (mixed_grad,),
            masked=(lengths, weight_point, skip_input.shape),
        )
    else:
        own_point, own_outer, own_skip, own_upsample, arrived_grad = sum_terms(
            "sum_upper",
            3,
            [
                (conv_flat, out_grad),
                (hidden_low, block_low),
                (skip_flat, joined_flat),
                (third_low, lifted_grad),
            ],
            halves(0, r, half_width)
            + halves(1, outer_weight.shape[0], half_width)
            + halves(2, r, half_width)
            + halves(3, r, half_width),
            "in",
            (mixed_grad,),
        )
    query_own, own_side, other_side, bias_sums, relative_sum = attention_backward(
        info, rates, bias_gap, relative, mine, other, arrived_grad, mixed_wide, log_total, parts
    )

    def at_head(value):
        full = jnp.zeros((H,) + value.shape, jnp.float32)
        return lax.dynamic_update_index_in_dim(full, value, head, 0)

    pieces = [
        at_head(bias_sums[0, :, 0]).reshape(-1),
        at_head(bias_sums[1, :, 0]).reshape(-1),
        at_head(relative_sum).reshape(H * KD, RPF),
        grad_second,
        grad_inner_bias,
        grad_outer_bias,
        grad_third,
        grad_skip_bias,
        grad_depth,
    ]

    def pack(pieces):
        packed = jnp.concatenate([p.reshape(devices, -1) for p in pieces], axis=1)
        return jnp.pad(packed, ((0, 0), (0, -packed.shape[1] % 1024))).reshape(devices, -1, 128)

    lower = [(second_low, before_low), (mixed_low, middle_low)]
    lower_groups = halves(0, r, half_hidden) + halves(1, r, half_width)
    lower_heads = (query_own, own_side, other_side)
    packed_width = keys_width + values_width
    if r % 16 == 0:
        right = jax.ShapeDtypeStruct((windows * rows, packed_width), BF)
        own_inner, own_mixing, own_heads, small_total, input_grad = sum_terms(
            "sum_lower",
            4,
            lower + [(normed_low, right)],
            lower_groups + halves(2, r, packed_width // 2),
            "out",
            lower_heads,
            pack(pieces),
            (weight_query, weight_key, weight_value, inputs, middle_grad, gain_first[None, :]),
        )
        own_first = small_total[-8, : width // devices]
        input_grad = input_grad.reshape(windows, rows, width)
        names = pieces
    else:
        own_inner, own_mixing, heads_grad = sum_terms(
            "sum_lower", 4, lower, lower_groups, "out", lower_heads
        )
        packed_grad = jnp.concatenate(
            [
                by_row(heads_grad[:, :, :KD]),
                by_row(heads_grad[:, :, KD : 2 * KD]),
                by_row(heads_grad[:, :, 2 * KD :]),
            ],
            axis=1,
        )
        (packed_grad,) = tie(packed_grad)
        normed_grad = (
            times_transposed(packed_grad[:, : H * KD], weight_query)
            + times_transposed(packed_grad[:, H * KD : keys_width], weight_key)
            + times_transposed(packed_grad[:, keys_width:], weight_value)
        )
        _, first_norm_back = jax.vjp(layer_norm, flat, gain_first)
        input_part, grad_first = first_norm_back(normed_grad)
        input_grad = (middle_grad + input_part).astype(jnp.bfloat16).reshape(windows, rows, width)
        names = [grad_first] + pieces
        own_heads, small_total = sum_terms(
            "sum_heads",
            5,
            [(normed_low, packed_grad)],
            halves(0, r, packed_width // 2),
            small=pack(names),
        )
    small_total, spot, small_grads = small_total.reshape(-1), 0, []
    for p in names:
        size = p.size // devices
        small_grads.append(
            small_total[spot : spot + size].reshape((p.shape[0] // devices,) + p.shape[1:])
        )
        spot += size
    if len(names) > len(pieces):
        own_first = small_grads.pop(0)
    (
        own_content,
        own_position,
        own_relative,
        own_second,
        own_inner_bias,
        own_outer_bias,
        own_third,
        own_skip_bias,
        own_depth,
    ) = small_grads
    return (
        outputs,
        input_grad,
        skip_grad,
        own_first,
        own_heads[:, : H * KD],
        own_heads[:, H * KD : keys_width],
        own_heads[:, keys_width:],
        own_content,
        own_position,
        own_relative,
        own_mixing,
        own_second,
        own_inner,
        own_inner_bias,
        own_outer,
        own_outer_bias,
        own_third,
        own_upsample,
        own_skip,
        own_skip_bias,
        own_depth,
        own_point,
    )


def solution(mesh):
    in_specs = (
        P("dp", "seq", None),
        P("dp", "seq", None),
        P("dp"),
        P("dp", "seq", None),
        P(("dp", "seq")),
        P(("dp", "seq"), None),
        P(("dp", "seq"), None),
        P(("dp", "seq"), None),
        P(("dp", "seq")),
        P(("dp", "seq")),
        P(("dp", "seq"), None),
        P(("dp", "seq"), None),
        P(("dp", "seq")),
        P(("dp", "seq"), None),
        P(("dp", "seq")),
        P(("dp", "seq"), None),
        P(("dp", "seq")),
        P(("dp", "seq")),
        P(("dp", "seq"), None),
        P(("dp", "seq"), None),
        P(("dp", "seq")),
        P(("dp", "seq"), None),
        P(("dp", "seq"), None),
    )
    out_specs = (
        P("dp", "seq", None),
        P("dp", "seq", None),
        P("dp", "seq", None),
        P(("dp", "seq")),
        P(("dp", "seq"), None),
        P(("dp", "seq"), None),
        P(("dp", "seq"), None),
        P(("dp", "seq")),
        P(("dp", "seq")),
        P(("dp", "seq"), None),
        P(("dp", "seq"), None),
        P(("dp", "seq")),
        P(("dp", "seq"), None),
        P(("dp", "seq")),
        P(("dp", "seq"), None),
        P(("dp", "seq")),
        P(("dp", "seq")),
        P(("dp", "seq"), None),
        P(("dp", "seq"), None),
        P(("dp", "seq")),
        P(("dp", "seq"), None),
        P(("dp", "seq"), None),
    )
    return jax.shard_map(
        on_device, mesh=mesh, in_specs=in_specs, out_specs=out_specs, check_vma=False
    )
```
